32 devices in a mesh: dp: 8 (over y, x, core), tensor: 4 (over z).
Axes of the slice: x: 2, y: 2, z: 4, core: 2. Of those that a mesh axis runs over, the one named last changes fastest.
Arguments:
- char_ids: int32 [512, 8, 50], P(None, 'dp'), may hold values from 0 to 261, as said below
- seq_lengths: int32 [8], P('dp'), may hold values from 40 to 512, as said below
- char_table: bfloat16 [262, 16], replicated, may hold values from -6 to 6
- conv_weight: bfloat16 [112, 2048], P(None, 'tensor'), may hold values from -0.75 to 0.75
- conv_bias: bfloat16 [2048], P('tensor'), may hold values from -3 to 3
- highway_weight: bfloat16 [2, 2, 2048, 2048], P(None, None, None, 'tensor'), may hold values from -0.125 to 0.125
- highway_bias: bfloat16 [2, 2, 2048], P(None, None, 'tensor'), may hold values from -3 to 3
- proj_weight: bfloat16 [2048, 768], P('tensor'), may hold values from -0.125 to 0.125
- proj_bias: bfloat16 [768], replicated, may hold values from -2 to 2
- norm_gain: bfloat16 [3, 768], replicated, may hold values from 0.5 to 1.5
- norm_shift: bfloat16 [3, 768], replicated, may hold values from -2 to 2
- qkv_weight: bfloat16 [768, 3, 768], P(None, None, 'tensor'), may hold values from -0.21875 to 0.21875
- qv_bias: bfloat16 [2, 768], P(None, 'tensor'), may hold values from -2 to 2
- output_projection_weight: bfloat16 [768, 768], P('tensor'), may hold values from -2.5 to 2.5
- out_bias: bfloat16 [768], replicated, may hold values from -2 to 2
- up_weight: bfloat16 [768, 3072], P(None, 'tensor'), may hold values from -0.21875 to 0.21875
- up_bias: bfloat16 [3072], P('tensor'), may hold values from -2 to 2
- down_weight: bfloat16 [3072, 768], P('tensor'), may hold values from -0.109375 to 0.109375
- down_bias: bfloat16 [768], replicated, may hold values from -2 to 2
- out_grad: bfloat16 [512, 8, 768], P('tensor', 'dp'), may hold values from -6 to 6
Outputs:
- encoded: bfloat16 [512, 8, 768], P('tensor', 'dp')
- char_table_grad: float32 [262, 16], replicated
- conv_weight_grad: float32 [112, 2048], replicated
- conv_bias_grad: float32 [2048], replicated
- highway_weight_grad: float32 [2, 2, 2048, 2048], P(None, None, 'dp', 'tensor')
- highway_bias_grad: float32 [2, 2, 2048], replicated
- proj_weight_grad: float32 [2048, 768], P('tensor', 'dp')
- proj_bias_grad: float32 [768], replicated
- norm_gain_grad: float32 [3, 768], replicated
- norm_shift_grad: float32 [3, 768], replicated
- qkv_weight_grad: float32 [768, 3, 768], P('dp', None, 'tensor')
- qv_bias_grad: float32 [2, 768], replicated
- out_weight_grad: float32 [768, 768], P('tensor', 'dp')
- out_bias_grad: float32 [768], replicated
- up_weight_grad: float32 [768, 3072], P('dp', 'tensor')
- up_bias_grad: float32 [3072], replicated
- down_weight_grad: float32 [3072, 768], P('tensor', 'dp')
- down_bias_grad: float32 [768], replicated
The draws below stay inside these ranges and needn't reach their ends.
Inputs may be any that keep to these rules, and one draw needn't show every extreme that they name: `char_ids`: each word has 1 to 50 characters with ids 1 to 261, followed by id 0 in its remaining places. Sequence n holds words in slots 0 to seq_lengths[n] - 1; the later slots are padding and are never attended to. In each aligned group of min(8, 8) consecutive sequences exactly one has 512 words.
All inputs are finite; a program needn't handle non-finite values.
Results may differ from the reference program's by a relative error of at most 0.013.
Values may be sent and summed in bfloat16 or wider, within the bound.
A program may use at most 192 MiB of HBM per device.

```python
import math
import jax
import jax.numpy as jnp
from jax import lax

CHARS = 50
CHAR_DIM = 16
VOCAB = 262
FILTERS = 2048
MAX_WIDTH = 7
HW_LAYERS = 2
D = 768
HEADS = 12
HEAD_DIM = 64
FF = 3072
SLOTS = 512
MIN_LEN = 40
SEQS = 8


def draw_char_ids(key, part):
    key = jax.random.fold_in(key, 11)
    key_len, key_ids = jax.random.split(key)
    word_len = jax.random.randint(key_len, (SLOTS, SEQS, 1), 1, CHARS + 1)
    char_vals = jax.random.randint(key_ids, (SLOTS, SEQS, CHARS), 1, VOCAB)
    place = lax.broadcasted_iota(jnp.int32, (SLOTS, SEQS, CHARS), 2)
    return jnp.where(place < word_len, char_vals, 0).astype(jnp.int32)


def draw_seq_lengths(key, part):
    key = jax.random.fold_in(key, 23)
    key_len, key_pick = jax.random.split(key)
    group_size = min(SEQS, 8)
    groups = SEQS // group_size
    lengths = jax.random.randint(key_len, (groups, group_size), MIN_LEN, SLOTS)
    picked = jax.random.randint(key_pick, (groups, 1), 0, group_size)
    place = lax.broadcasted_iota(jnp.int32, (groups, group_size), 1)
    return jnp.where(place == picked, SLOTS, lengths).reshape(SEQS).astype(jnp.int32)


def shard_levels(own_key, shape, cuts, low, high):
    level = 1.0
    for dim, blocks in cuts:
        draws = jax.random.uniform(jax.random.fold_in(jax.random.fold_in(own_key, 6), dim), (blocks,), jnp.float32, low / len(cuts), high / len(cuts))
        level = level * jnp.repeat(jnp.exp(draws), shape[dim] // blocks).reshape((-1,) + (1,) * (len(shape) - 1 - dim))
    return level


def scatter_about(own_key, extent, deviation, bound, cuts=(), dtype=jnp.bfloat16):
    level = shard_levels(own_key, extent, cuts, -0.22, 0.18) if cuts else 1.0
    result = jax.random.normal(own_key, extent, jnp.float32) * deviation * level
    return jnp.minimum(jnp.maximum(result, -bound), bound).astype(dtype)


def setup_inputs(seed: int = 0) -> dict:
    arg_keys = jax.random.split(jax.random.key(seed), 21)
    return {
        "char_ids": draw_char_ids(jax.random.fold_in(arg_keys[20], 71), 0),
        "seq_lengths": draw_seq_lengths(jax.random.fold_in(arg_keys[20], 71), 0),
        "char_table": scatter_about(arg_keys[2], (VOCAB, CHAR_DIM), 1.0, 6.0),
        "conv_weight": scatter_about(arg_keys[3], (MAX_WIDTH * CHAR_DIM, FILTERS), (4 * CHAR_DIM) ** -0.5, 0.75, ((1, 4),)),
        "conv_bias": scatter_about(arg_keys[4], (FILTERS,), 0.5, 3.0, ((0, 4),)),
        "highway_weight": scatter_about(arg_keys[5], (HW_LAYERS, 2, FILTERS, FILTERS), FILTERS ** -0.5, 0.125, ((3, 4),)),
        "highway_bias": scatter_about(arg_keys[6], (HW_LAYERS, 2, FILTERS), 0.5, 3.0, ((2, 4),)),
        "proj_weight": scatter_about(arg_keys[7], (FILTERS, D), FILTERS ** -0.5, 0.125, ((0, 4),)),
        "proj_bias": scatter_about(arg_keys[8], (D,), 0.3, 2.0),
        "norm_gain": jnp.clip(1.0 + 0.1 * jax.random.normal(arg_keys[9], (3, D), jnp.float32), 0.5, 1.5).astype(jnp.bfloat16),
        "norm_shift": scatter_about(arg_keys[10], (3, D), 0.3, 2.0),
        "qkv_weight": scatter_about(arg_keys[11], (D, 3, D), D ** -0.5, 0.21875, ((2, 4),)),
        "qv_bias": scatter_about(arg_keys[12], (2, D), 0.3, 2.0, ((1, 4),)),
        "output_projection_weight": scatter_about(arg_keys[13], (D, D), (max(D // 128, 1)) ** -0.5, 2.5, ((0, 4),)),
        "out_bias": scatter_about(arg_keys[14], (D,), 0.3, 2.0),
        "up_weight": scatter_about(arg_keys[15], (D, FF), D ** -0.5, 0.21875, ((1, 4),)),
        "up_bias": scatter_about(arg_keys[16], (FF,), 0.3, 2.0, ((0, 4),)),
        "down_weight": scatter_about(arg_keys[17], (FF, D), FF ** -0.5, 0.109375, ((0, 4),)),
        "down_bias": scatter_about(arg_keys[18], (D,), 0.3, 2.0),
        "out_grad": scatter_about(arg_keys[19], (SLOTS, SEQS, D), 1.0, 6.0, ((0, 4), (1, 8))),
    }


highest_precision = lax.Precision.HIGHEST
norm_eps = 1e-06
big_neg = -1e+30

@jax.custom_vjp
def low(v):
    return lax.optimization_barrier(v.astype(jnp.bfloat16)).astype(jnp.float32)

@jax.custom_vjp
def lower_backward(v):
    return v

def low_keep(v):
    return (low(v), None)

def low_pass(kept, grad):
    return (grad,)

def back_keep(v):
    return (v, None)

def back_low(kept, grad):
    return (low(grad),)
low.defvjp(low_keep, low_pass)
lower_backward.defvjp(back_keep, back_low)

def width_counts(block):
    unit = block // 64
    return [unit, unit, 2 * unit, 4 * unit, 8 * unit, 16 * unit, 32 * unit]

def layer_norm(values, gain, shift):
    centered = values - lax.optimization_barrier(jnp.mean(values, axis=-1, keepdims=True))
    variance = lax.optimization_barrier(jnp.mean(centered * centered, axis=-1, keepdims=True))
    return centered * lax.rsqrt(variance + norm_eps) * gain + shift

def char_pool(embedding_rows, conv_w, conv_b):
    block = FILTERS // 4
    blocked_w = conv_w.reshape(MAX_WIDTH * CHAR_DIM, 4, block)
    grouped_bias = conv_b.reshape(4, block)
    pieces = []
    start_offset = 0
    for index, item_count in enumerate(width_counts(block)):
        span_len = index + 1
        positions = CHARS - span_len + 1
        filter_window = jnp.concatenate([embedding_rows[:, shift_by:shift_by + positions, :] for shift_by in range(span_len)], axis=2)
        weight_list = blocked_w[:CHAR_DIM * span_len, :, start_offset:start_offset + item_count]
        convolved_rows = jnp.einsum('rhy,yaz->rhaz', filter_window, weight_list, precision=highest_precision) + grouped_bias[:, start_offset:start_offset + item_count]
        convolved_rows = lower_backward(convolved_rows)
        pieces.append(jax.nn.logsumexp(convolved_rows, axis=1) - math.log(positions))
        start_offset += item_count
    return jnp.concatenate(pieces, axis=2).reshape(embedding_rows.shape[0], FILTERS)

def embed_words(id_block, char_emb, conv_w, conv_b, hw_w, hw_b, proj_w, proj_b):
    embedding_rows = char_emb[id_block]
    hidden = jax.nn.silu(char_pool(embedding_rows, conv_w, conv_b))
    for layer in range(HW_LAYERS):
        sent = low(hidden)
        trans = lower_backward(jnp.dot(sent, hw_w[layer, 0], precision=highest_precision, preferred_element_type=jnp.float32) + hw_b[layer, 0])
        gate_pre = lower_backward(jnp.dot(sent, hw_w[layer, 1], precision=highest_precision, preferred_element_type=jnp.float32) + hw_b[layer, 1])
        gate = jax.nn.sigmoid(gate_pre)
        hidden = gate * jax.nn.silu(trans) + (1.0 - gate) * hidden
    return lower_backward(jnp.dot(low(hidden), proj_w, precision=highest_precision, preferred_element_type=jnp.float32) + proj_b)

def encode_rows(embedded, len_stretch, norm_gains, shifts, qkv_w, qv_b, output_weight, output_bias, up_w, up_b, down_w, down_b):
    slot_count = embedded.shape[0]
    seq_count = embedded.shape[1]
    inputs = layer_norm(embedded, norm_gains[0], shifts[0])
    sent = low(inputs)
    projected = jnp.einsum('snd,dke->snke', sent, qkv_w, precision=highest_precision)
    queries = low(lower_backward(projected[:, :, 0] + qv_b[0])).reshape(slot_count, seq_count, HEADS, HEAD_DIM)
    key_rows = low(lower_backward(projected[:, :, 1])).reshape(slot_count, seq_count, HEADS, HEAD_DIM)
    values = low(lower_backward(projected[:, :, 2] + qv_b[1])).reshape(slot_count, seq_count, HEADS, HEAD_DIM)
    scores = jnp.einsum('qnhd,knhd->nhqk', queries, key_rows, precision=highest_precision) * HEAD_DIM ** (-0.5)
    place = lax.broadcasted_iota(jnp.int32, scores.shape, 3)
    scores = lower_backward(jnp.where(place < len_stretch[:, None, None, None], scores, big_neg))
    probs = jax.nn.softmax(scores, axis=-1)
    attention_result = low(lower_backward(jnp.einsum('nhqk,knhd->qnhd', low(probs), values, precision=highest_precision)))
    attention_result = attention_result.reshape(slot_count, seq_count, D)
    residual_branch = lower_backward(jnp.einsum('lpb,bj->lpj', attention_result, output_weight, precision=highest_precision) + output_bias)
    middle = layer_norm(inputs + residual_branch, norm_gains[1], shifts[1])
    upper = lower_backward(jnp.einsum('snd,df->snf', low(middle), up_w, precision=highest_precision) + up_b)
    activated = low(jax.nn.gelu(upper, approximate=False))
    branch_two = lower_backward(jnp.einsum('snf,fd->snd', activated, down_w, precision=highest_precision) + down_b)
    return layer_norm(middle + branch_two, norm_gains[2], shifts[2])

def stretch_forward(id_stretch, len_stretch, params):
    char_emb, conv_w, conv_b, hw_w, hw_b, proj_w, proj_b, norm_gains, shifts, qkv_w, qv_b, output_weight, output_bias, up_w, up_b, down_w, down_b = params
    group = id_stretch.shape[1]
    word_count = SLOTS * group
    block_words = min(512, word_count)
    id_blocks = id_stretch.reshape(word_count // block_words, block_words, CHARS)

    def embed_block(id_block):
        return embed_words(id_block, char_emb, conv_w, conv_b, hw_w, hw_b, proj_w, proj_b)
    embedded = lax.map(jax.checkpoint(embed_block), id_blocks).reshape(SLOTS, group, D)
    return jax.checkpoint(encode_rows)(embedded, len_stretch, norm_gains, shifts, qkv_w, qv_b, output_weight, output_bias, up_w, up_b, down_w, down_b)

def reference(char_ids, seq_lengths, char_table, conv_weight, conv_bias, highway_weight, highway_bias, proj_weight, proj_bias, norm_gain, norm_shift, qkv_weight, qv_bias, output_projection_weight, out_bias, up_weight, up_bias, down_weight, down_bias, out_grad):
    weight_list = tuple((source.astype(jnp.float32) for source in (char_table, conv_weight, conv_bias, highway_weight, highway_bias, proj_weight, proj_bias, norm_gain, norm_shift, qkv_weight, qv_bias, output_projection_weight, out_bias, up_weight, up_bias, down_weight, down_bias)))
    group = min(SEQS, 8)
    stretches = SEQS // group
    id_stretches = jnp.moveaxis(char_ids.reshape(SLOTS, stretches, group, CHARS), 1, 0)
    len_stretches = seq_lengths.reshape(stretches, group)

    def forward(*params):

        def run_stretch(stretch_pair):
            return stretch_forward(stretch_pair[0], stretch_pair[1], params)
        outputs = lax.map(run_stretch, (id_stretches, len_stretches))
        return jnp.moveaxis(outputs, 0, 1).reshape(SLOTS, SEQS, D)
    encoded, pull_back = jax.vjp(forward, *weight_list)
    table_grad, conv_w_grad, conv_b_grad, hw_w_grad, hw_b_grad, proj_w_grad, proj_b_grad, gain_grad, shift_grad, qkv_grad, qv_grad, out_w_grad, out_b_grad, up_w_grad, up_b_grad, down_w_grad, down_b_grad = pull_back(out_grad.astype(jnp.float32))
    return (encoded.astype(jnp.bfloat16), table_grad, conv_w_grad, conv_b_grad, hw_w_grad, hw_b_grad, proj_w_grad, proj_b_grad, gain_grad, shift_grad, qkv_grad, qv_grad, out_w_grad, out_b_grad, up_w_grad, up_b_grad, down_w_grad, down_b_grad)
```

```python
import functools
import math

import jax
import jax.numpy as jnp
import numpy as np
from jax import lax
from jax.experimental import pallas as pl
from jax.experimental.pallas import tpu as pltpu
from jax.sharding import PartitionSpec as P

HEAD_DIM = 64
WORD_TILE = 16
LANES = 128

norm_eps = 1e-06
big_neg = -1e30
f32 = jnp.float32
bf16 = jnp.bfloat16
MESH = pl.DeviceIdType.MESH
VMEM = pl.BlockSpec(memory_space=pltpu.VMEM)
ANY = pl.BlockSpec(memory_space=pl.ANY)
DMA = pltpu.SemaphoreType.DMA
MIB = 1 << 20


def params(cid, vmem):
    return pltpu.CompilerParams(
        collective_id=cid, has_side_effects=True, vmem_limit_bytes=vmem * MIB
    )


def width_counts(block):
    unit = block // 64
    return [unit, unit, 2 * unit, 4 * unit, 8 * unit, 16 * unit, 32 * unit]


def filter_widths(block):
    return np.concatenate(
        [np.full((n,), i + 1, np.int32) for i, n in enumerate(width_counts(block))]
    )


def dot(a, b, ca, cb):
    return lax.dot_general(a, b, (((ca,), (cb,)), ((), ())), preferred_element_type=f32)


def line_barrier(me, count):
    barrier = pltpu.get_barrier_semaphore()
    for there, ok in ((me - 1, me > 0), (me + 1, me < count - 1)):

        @pl.when(ok)
        def greet():
            pl.semaphore_signal(barrier, inc=1, device_id={"tensor": there}, device_id_type=MESH)

    pl.semaphore_wait(barrier, jnp.minimum(me, 1) + jnp.minimum(count - 1 - me, 1))


def line_copy(view, me, count, right, block, chunk, sems):
    send, recv = sems[:2] if right else sems[2:]
    to = jnp.minimum(me + 1, count - 1) if right else jnp.maximum(me - 1, 0)
    ref = view(block, chunk)
    return pltpu.make_async_remote_copy(
        src_ref=ref,
        dst_ref=ref,
        send_sem=send.at[block, chunk],
        recv_sem=recv.at[block, chunk],
        device_id={"tensor": to},
        device_id_type=MESH,
    )


def gather_step(view, step, chunks, me, count, sems):
    for hop in range(count):
        chunk = step - hop
        here = (chunk >= 0) & (chunk < chunks)
        safe = jnp.clip(chunk, 0, chunks - 1)
        for right in (True, False):
            block = me - hop if right else me + hop
            there = (block >= 0) & (block < count)
            block = jnp.clip(block, 0, count - 1)
            more = me < count - 1 if right else me > 0
            copy = functools.partial(line_copy, view, me, count, right, block, safe, sems)

            @pl.when(here & there)
            def pass_on():
                if hop > 0:
                    copy().wait_recv()

                @pl.when(more)
                def send():
                    copy().start()


def gather_drain(view, chunks, me, count, sems):
    def one(chunk, carry):
        for hop in range(count):
            for right in (True, False):
                block = me - hop if right else me + hop
                there = (block >= 0) & (block < count)
                block = jnp.clip(block, 0, count - 1)
                more = me < count - 1 if right else me > 0
                copy = functools.partial(line_copy, view, me, count, right, block, chunk, sems)

                @pl.when(there & more)
                def sent():
                    copy().wait_send()

        return carry

    lax.fori_loop(0, chunks, one, 0)


def windows(y_ref, start, chars):
    group = lax.broadcasted_iota(jnp.int32, (1, WORD_TILE, LANES), 2) // 16
    tile = pl.ds(start, WORD_TILE)
    value = y_ref[0:chars, tile, :]
    for tap in range(1, 7):
        value = jnp.where(group == tap, y_ref[tap : chars + tap, tile, :], value)
    return value.reshape(chars * WORD_TILE, LANES)


def conv_forward_kernel(count, chars, chunks, y_ref, w_ref, off_ref, log_ref, whole_ref, *sems):
    me = lax.axis_index("tensor")
    words, filters = log_ref.shape
    rows = words // chunks
    line_barrier(me, count)

    def view(block, chunk):
        return whole_ref.at[
            pl.ds(pl.multiple_of(chunk * rows, rows), rows),
            pl.ds(pl.multiple_of(block * filters, filters), filters),
        ]

    def tile_step(index, carry):
        start = pl.multiple_of(index * WORD_TILE, WORD_TILE)
        conv = dot(windows(y_ref, start, chars), w_ref[...], 1, 0)
        conv = conv.reshape(chars, WORD_TILE, filters)
        top = jnp.max(conv, axis=0)
        total = top + jnp.log(jnp.sum(jnp.exp(conv - top[None]), axis=0))
        log_ref[pl.ds(start, WORD_TILE), :] = total
        pooled = total - off_ref[...]
        whole_ref[
            pl.ds(start, WORD_TILE), pl.ds(pl.multiple_of(me * filters, filters), filters)
        ] = (pooled * jax.nn.sigmoid(pooled)).astype(bf16)
        return carry

    per = rows // WORD_TILE

    def chunk_step(step, carry):
        @pl.when(step < chunks)
        def work():
            lax.fori_loop(step * per, step * per + per, tile_step, 0)

        gather_step(view, step, chunks, me, count, sems)
        return carry

    lax.fori_loop(0, chunks + count - 1, chunk_step, 0)
    gather_drain(view, chunks, me, count, sems)


def conv_forward(y, w, off, count, chars, cid):
    words, filters = y.shape[1], w.shape[1]
    chunks = 8
    return pl.pallas_call(
        functools.partial(conv_forward_kernel, count, chars, chunks),
        out_shape=(
            jax.ShapeDtypeStruct((words, filters), f32),
            jax.ShapeDtypeStruct((words, count * filters), bf16),
        ),
        in_specs=[VMEM] * 3,
        out_specs=(VMEM, VMEM),
        scratch_shapes=[DMA((count, chunks))] * 4,
        compiler_params=params(cid, 40),
        name="conv_forward",
    )(y, w, off)


def gather_kernel(count, chunks, x_ref, whole_ref, *sems):
    me = lax.axis_index("tensor")
    words, filters = x_ref.shape
    rows = words // chunks
    whole_ref[:, pl.ds(pl.multiple_of(me * filters, filters), filters)] = x_ref[...]
    line_barrier(me, count)

    def view(block, chunk):
        return whole_ref.at[
            pl.ds(pl.multiple_of(chunk * rows, rows), rows),
            pl.ds(pl.multiple_of(block * filters, filters), filters),
        ]

    def chunk_step(step, carry):
        gather_step(view, step, chunks, me, count, sems)
        return carry

    lax.fori_loop(0, chunks + count - 1, chunk_step, 0)
    gather_drain(view, chunks, me, count, sems)


def gather_features(x, count, cid):
    chunks = 4
    return pl.pallas_call(
        functools.partial(gather_kernel, count, chunks),
        out_shape=jax.ShapeDtypeStruct((x.shape[0], count * x.shape[1]), bf16),
        in_specs=[VMEM],
        out_specs=VMEM,
        scratch_shapes=[DMA((count, chunks))] * 4,
        compiler_params=params(cid, 16),
        name="gather_features",
    )(x)


def sum_kernel(count, chunks, p_ref, out_ref, from_left, from_right, s_right, r_right, s_left, r_left):
    me = lax.axis_index("tensor")
    rows = p_ref.shape[0] // chunks
    line_barrier(me, count)

    def tile(chunk):
        return pl.ds(pl.multiple_of(chunk * rows, rows), rows)

    def copies(right, chunk):
        buf = from_left if right else from_right
        send, recv = (s_right, r_right) if right else (s_left, r_left)
        to = jnp.minimum(me + 1, count - 1) if right else jnp.maximum(me - 1, 0)
        first, passed = [
            functools.partial(
                pltpu.make_async_remote_copy,
                src_ref=src.at[tile(chunk)],
                dst_ref=buf.at[tile(chunk)],
                send_sem=send.at[chunk],
                recv_sem=recv.at[chunk],
                device_id={"tensor": to},
                device_id_type=MESH,
            )
            for src in (p_ref, buf)
        ]
        return buf, first, passed

    def step_fn(step, carry):
        for right in (True, False):
            lag = me if right else count - 1 - me
            chunk = step - lag
            here = (chunk >= 0) & (chunk < chunks)
            chunk = jnp.clip(chunk, 0, chunks - 1)
            buf, first, passed = copies(right, chunk)

            @pl.when(here & (lag == 0))
            def start():
                first().start()

            @pl.when(here & (lag > 0))
            def middle():
                first().wait_recv()
                got = buf[tile(chunk), :].astype(f32)

                @pl.when(lag < count - 1)
                def forward():
                    buf[tile(chunk), :] = (got + p_ref[tile(chunk), :].astype(f32)).astype(bf16)
                    passed().start()

                out_ref[tile(chunk), :] += got

        return carry

    out_ref[...] = p_ref[...].astype(f32)
    lax.fori_loop(0, chunks + count - 1, step_fn, 0)

    def drain(chunk, carry):
        for right in (True, False):
            lag = me if right else count - 1 - me

            @pl.when(lag < count - 1)
            def sent():
                copies(right, chunk)[1]().wait_send()

        return carry

    lax.fori_loop(0, chunks, drain, 0)


def sum_rows(partial, count, cid):
    chunks = 8
    shape = partial.shape
    return pl.pallas_call(
        functools.partial(sum_kernel, count, chunks),
        out_shape=jax.ShapeDtypeStruct(shape, f32),
        in_specs=[VMEM],
        out_specs=VMEM,
        scratch_shapes=[pltpu.VMEM(shape, bf16)] * 2 + [DMA((chunks,))] * 4,
        compiler_params=params(cid, 16),
        name="sum_rows",
    )(partial)


def scatter_kernel(count, chunks, p_ref, out_ref, from_left, from_right, *sems):
    me = lax.axis_index("tensor")
    words, filters = out_ref.shape
    rows = words // chunks
    line_barrier(me, count)

    def copies(right, block, chunk):
        buf = from_left if right else from_right
        send, recv = sems[:2] if right else sems[2:]
        to = jnp.minimum(me + 1, count - 1) if right else jnp.maximum(me - 1, 0)
        tile = pl.ds(pl.multiple_of(chunk * rows, rows), rows)
        lanes = pl.ds(pl.multiple_of(block * filters, filters), filters)
        first, passed = [
            functools.partial(
                pltpu.make_async_remote_copy,
                src_ref=src.at[tile, lanes],
                dst_ref=buf.at[tile, lanes],
                send_sem=send.at[block, chunk],
                recv_sem=recv.at[block, chunk],
                device_id={"tensor": to},
                device_id_type=MESH,
            )
            for src in (p_ref, buf)
        ]
        return buf, tile, lanes, first, passed

    out_ref[...] = p_ref[:, pl.ds(pl.multiple_of(me * filters, filters), filters)].astype(f32)
    messages = chunks * (count - 1)

    def step_fn(step, carry):
        for right in (True, False):
            lag = me if right else count - 1 - me
            number = step - lag
            here = (number >= 0) & (number < messages)
            number = jnp.clip(number, 0, messages - 1)
            chunk = number // (count - 1)
            far = count - 1 - number % (count - 1)
            block = far if right else count - 1 - far
            buf, tile, lanes, first, passed = copies(right, block, chunk)

            @pl.when(here & (lag == 0))
            def start():
                first().start()

            @pl.when(here & (lag > 0) & (far > lag))
            def middle():
                first().wait_recv()
                buf[tile, lanes] = (
                    buf[tile, lanes].astype(f32) + p_ref[tile, lanes].astype(f32)
                ).astype(bf16)
                passed().start()

            @pl.when(here & (lag > 0) & (far == lag))
            def last():
                first().wait_recv()
                out_ref[tile, :] += buf[tile, lanes].astype(f32)

        return carry

    lax.fori_loop(0, messages + count - 1, step_fn, 0)

    def drain(number, carry):
        chunk = number // (count - 1)
        far = count - 1 - number % (count - 1)
        for right in (True, False):
            lag = me if right else count - 1 - me
            block = far if right else count - 1 - far

            @pl.when(far > lag)
            def sent():
                copies(right, block, chunk)[3]().wait_send()

        return carry

    lax.fori_loop(0, messages, drain, 0)


def scatter_features(partial, count, cid):
    chunks = 8
    words, whole = partial.shape
    return pl.pallas_call(
        functools.partial(scatter_kernel, count, chunks),
        out_shape=jax.ShapeDtypeStruct((words, whole // count), f32),
        in_specs=[VMEM],
        out_specs=VMEM,
        scratch_shapes=[pltpu.VMEM((words, whole), bf16)] * 2 + [DMA((count, chunks))] * 4,
        compiler_params=params(cid, 20),
        name="scatter_features",
    )(partial)


def conv_backward_kernel(count, chars, chunks, cuts, ids_ref, y_ref, w_ref, wb_ref, off_ref,
                         log_ref, prev_ref, part_ref, *rest):
    if cuts:
        (hw_ref, tr_ref, dw_ref, table_ref, hw_out, tr_out, pad_ref, got_ref, part_send, part_recv,
         hw0, hw0_in, tr0, tr0_in, hwa1, hwb1, tra1, trb1, hwa2, hwb2, tra2, trb2,
         local_sem, dp_send, dp_recv) = rest
    else:
        dw_ref, table_ref, pad_ref, got_ref, part_send, part_recv = rest
    me = lax.axis_index("tensor")
    place = lax.axis_index("dp")
    words, filters = log_ref.shape
    rows = words // chunks
    padded = y_ref.shape[0]
    cell = [place % 2, (place // 2) % 2, place // 4]
    peers = [{"dp": place + (1 - 2 * cell[bit]) * 2**bit} for bit in range(3)] if cuts else []
    peers += [{"tensor": lax.rem(me + k, count)} for k in range(1, count)]
    barrier = pltpu.get_barrier_semaphore()
    for peer in peers:
        pl.semaphore_signal(barrier, inc=1, device_id=peer, device_id_type=MESH)
    pl.semaphore_wait(barrier, len(peers))

    def part_copy(hop, chunk):
        to = lax.rem(me + hop, count)
        tile = pl.ds(pl.multiple_of(chunk * rows, rows), rows)
        return pltpu.make_async_remote_copy(
            src_ref=part_ref.at[tile, pl.ds(pl.multiple_of(to * filters, filters), filters)],
            dst_ref=got_ref.at[hop - 1, tile],
            send_sem=part_send.at[hop - 1, chunk],
            recv_sem=part_recv.at[hop - 1, chunk],
            device_id={"tensor": to},
            device_id_type=MESH,
        )

    def part_start(chunk, carry):
        for hop in range(1, count):
            part_copy(hop, chunk).start()
        return carry

    lax.fori_loop(0, chunks, part_start, 0)

    stages = []
    if cuts:
        c, x, y = cell
        half = hw_ref.shape[0] // 2
        lane_a, lane_b = tra1.shape[-1], trb1.shape[-1]
        part_a, part_b = pl.ds(0, lane_a), pl.ds(lane_a, lane_b)

        def remote(number, src, dst, bit):
            return pltpu.make_async_remote_copy(
                src_ref=src, dst_ref=dst, send_sem=dp_send.at[number], recv_sem=dp_recv.at[number],
                device_id=peers[bit], device_id_type=MESH,
            )

        keep = [
            pltpu.make_async_copy(hw_ref.at[:, :, :, c], hw0, local_sem.at[0]),
            pltpu.make_async_copy(tr_ref.at[:, :, c], tr0, local_sem.at[1]),
        ]
        stages = [
            [
                remote(0, hw_ref.at[:, :, :, 1 - c], hw0_in, 0),
                remote(1, tr_ref.at[:, :, 1 - c], tr0_in, 0),
            ],
            [
                remote(2, hw0.at[pl.ds(0, half), :, 1 - x], hwa1, 1),
                remote(3, hw0.at[pl.ds(half, half), 1 - y], hwb1, 2),
                remote(4, tr0.at[:, 1 - x, :, part_a], tra1, 1),
                remote(5, tr0.at[1 - y, :, :, part_b], trb1, 2),
            ],
            [
                remote(6, hw0.at[pl.ds(0, half), 1 - y, x], hwa2, 2),
                remote(7, hw0.at[pl.ds(half, half), y, 1 - x], hwb2, 1),
                remote(8, tr0.at[1 - y, x, :, part_a], tra2, 2),
                remote(9, tr0.at[y, 1 - x, :, part_b], trb2, 1),
            ],
        ]

        def add(ref, index, other):
            ref[index] = (ref[index].astype(f32) + other.astype(f32)).astype(bf16)

        def after0():
            for copy in keep:
                copy.wait()
            for copy in stages[0]:
                copy.wait()

            def one(k, carry):
                for i in range(2):
                    for j in range(2):
                        add(hw0, (k, i, j), hw0_in[k, i, j])
                return carry

            lax.fori_loop(0, 2 * half, one, 0)
            for i in range(2):
                for j in range(2):
                    add(tr0, (i, j), tr0_in[i, j])

        def after1():
            for copy in stages[1]:
                copy.wait()

            def one(k, carry):
                for i in range(2):
                    add(hw0, (k, i, x), hwa1[k, i])
                    add(hw0, (k + half, y, i), hwb1[k, i])
                return carry

            lax.fori_loop(0, half, one, 0)
            for i in range(2):
                add(tr0, (i, x, slice(None), part_a), tra1[i])
                add(tr0, (y, i, slice(None), part_b), trb1[i])

        def after2():
            for copy in stages[2]:
                copy.wait()

            def one(k, carry):
                hw_out[k] = hw0[k, y, x].astype(f32) + hwa2[k].astype(f32)
                hw_out[k + half] = hw0[k + half, y, x].astype(f32) + hwb2[k].astype(f32)
                return carry

            lax.fori_loop(0, half, one, 0)
            tr_out[:, part_a] = tr0[y, x, :, part_a].astype(f32) + tra2[...].astype(f32)
            tr_out[:, part_b] = tr0[y, x, :, part_b].astype(f32) + trb2[...].astype(f32)

        for copy in keep + stages[0]:
            copy.start()

    dw_ref[...] = jnp.zeros_like(dw_ref)
    table_ref[...] = jnp.zeros_like(table_ref)
    pad_ref[...] = jnp.zeros_like(pad_ref)
    per = rows // WORD_TILE
    group = lax.broadcasted_iota(jnp.int32, (1, WORD_TILE, LANES), 2) // 16
    vocab = lax.broadcasted_iota(jnp.int32, (table_ref.shape[0], padded * WORD_TILE), 0)

    def tile_step(index, carry):
        @pl.when(index % per == 0)
        def arrived():
            for hop in range(1, count):
                part_copy(hop, index // per).wait_recv()

        start = pl.multiple_of(index * WORD_TILE, WORD_TILE)
        tile = pl.ds(start, WORD_TILE)
        x2 = windows(y_ref, start, chars)
        conv = dot(x2, w_ref[...], 1, 0).reshape(chars, WORD_TILE, filters)
        total = log_ref[tile, :]
        pooled = total - off_ref[...]
        sig = jax.nn.sigmoid(pooled)
        grad = prev_ref[tile, :] + part_ref[
            tile, pl.ds(pl.multiple_of(me * filters, filters), filters)
        ].astype(f32)
        for hop in range(count - 1):
            grad = grad + got_ref[hop, tile, :].astype(f32)
        grad = grad * (sig * (1.0 + pooled * (1.0 - sig)))
        d_conv = (grad[None] * jnp.exp(conv - total[None])).astype(bf16)
        d_conv = d_conv.reshape(chars * WORD_TILE, filters)
        dw_ref[...] += dot(x2, d_conv, 0, 0)
        d_win = dot(d_conv, wb_ref[...], 1, 1).astype(bf16)
        pad_ref[6 : 6 + chars] = d_win.reshape(chars, WORD_TILE, LANES)
        d_emb = pad_ref[6 : 6 + padded]
        for tap in range(1, 7):
            d_emb = jnp.where(group == tap, pad_ref[6 - tap : 6 - tap + padded], d_emb)
        one_hot = jnp.where(vocab == ids_ref[pl.ds(index, 1), :], 1.0, 0.0).astype(bf16)
        table_ref[...] += dot(one_hot, d_emb.reshape(padded * WORD_TILE, LANES), 1, 0)
        return carry

    tiles = words // WORD_TILE
    if cuts:
        lax.fori_loop(0, cuts[0], tile_step, 0)
        after0()
        for copy in stages[1]:
            copy.start()
        lax.fori_loop(cuts[0], cuts[1], tile_step, 0)
        after1()
        for copy in stages[2]:
            copy.start()
        lax.fori_loop(cuts[1], tiles, tile_step, 0)
        after2()
    else:
        lax.fori_loop(0, tiles, tile_step, 0)

    def part_drain(chunk, carry):
        for hop in range(1, count):
            part_copy(hop, chunk).wait_send()
        return carry

    lax.fori_loop(0, chunks, part_drain, 0)


def conv_backward(ids, y, w, wb, off, logs, prev, part, hw, tr, count, chars, cid):
    words, filters = logs.shape
    chunks = 8
    out_shape = [
        jax.ShapeDtypeStruct((LANES, filters), f32),
        jax.ShapeDtypeStruct((264, LANES), f32),
    ]
    scratch = [
        pltpu.VMEM((68, WORD_TILE, LANES), bf16),
        pltpu.VMEM((count - 1, words, filters), bf16),
        DMA((count - 1, chunks)),
        DMA((count - 1, chunks)),
    ]
    operands = [ids, y, w, wb, off, logs, prev, part]
    in_specs = [VMEM] * 8
    cuts = None
    if hw is not None:
        cuts = (10, 24)
        mats, rows, cols = hw.shape[0], hw.shape[-2], hw.shape[-1]
        tr_rows, tr_cols = tr.shape[-2], tr.shape[-1]
        lane_a = 1536
        lane_b = tr_cols - lane_a
        out_shape += [
            jax.ShapeDtypeStruct((mats, rows, cols), f32),
            jax.ShapeDtypeStruct((tr_rows, tr_cols), f32),
        ]
        operands += [hw, tr]
        in_specs += [ANY, ANY]
        half = mats // 2
        scratch += [pltpu.VMEM((mats, 2, 2, rows, cols), bf16)] * 2
        scratch += [pltpu.VMEM((2, 2, tr_rows, tr_cols), bf16)] * 2
        scratch += [pltpu.VMEM((half, 2, rows, cols), bf16)] * 2
        scratch += [pltpu.VMEM((2, tr_rows, lane), bf16) for lane in (lane_a, lane_b)]
        scratch += [pltpu.VMEM((half, rows, cols), bf16)] * 2
        scratch += [pltpu.VMEM((tr_rows, lane), bf16) for lane in (lane_a, lane_b)]
        scratch += [DMA((2,)), DMA((10,)), DMA((10,))]
    return pl.pallas_call(
        functools.partial(conv_backward_kernel, count, chars, chunks, cuts),
        out_shape=tuple(out_shape),
        in_specs=in_specs,
        out_specs=tuple([VMEM] * len(out_shape)),
        scratch_shapes=scratch,
        compiler_params=params(cid, 56),
        name="conv_backward",
    )(*operands)


def small_kernel(dp_count, count, in_ref, out_ref, got, mid, *sems):
    s1, r1, s2, r2, s3, r3 = sems
    me = lax.axis_index("tensor")
    place = lax.axis_index("dp")
    barrier = pltpu.get_barrier_semaphore()

    def dp_peer(hop):
        return lax.rem(place + hop, dp_count)

    def greet(hop, carry):
        pl.semaphore_signal(barrier, inc=1, device_id={"dp": dp_peer(hop)}, device_id_type=MESH)
        return carry

    lax.fori_loop(1, dp_count, greet, 0)
    for hop in range(1, count):
        pl.semaphore_signal(
            barrier, inc=1, device_id={"tensor": lax.rem(me + hop, count)}, device_id_type=MESH
        )
    pl.semaphore_wait(barrier, dp_count + count - 2)

    def scatter(hop):
        return pltpu.make_async_remote_copy(
            src_ref=in_ref.at[dp_peer(hop)], dst_ref=got.at[hop - 1], send_sem=s1.at[hop - 1],
            recv_sem=r1.at[hop - 1], device_id={"dp": dp_peer(hop)}, device_id_type=MESH,
        )

    def across(hop):
        return pltpu.make_async_remote_copy(
            src_ref=mid.at[me], dst_ref=mid.at[me], send_sem=s2.at[hop - 1], recv_sem=r2.at[hop - 1],
            device_id={"tensor": lax.rem(me + hop, count)}, device_id_type=MESH,
        )

    def around(hop):
        return pltpu.make_async_remote_copy(
            src_ref=mid, dst_ref=out_ref.at[place], send_sem=s3.at[hop - 1], recv_sem=r3.at[hop - 1],
            device_id={"dp": dp_peer(hop)}, device_id_type=MESH,
        )

    def loop(fn, stop):
        def one(hop, carry):
            fn(hop)
            return carry

        lax.fori_loop(1, stop, one, 0)

    loop(lambda hop: scatter(hop).start(), dp_count)
    loop(lambda hop: scatter(hop).wait(), dp_count)
    total = lax.fori_loop(
        0, dp_count - 1, lambda k, acc: acc + got[k], in_ref[place]
    )
    mid[me] = total.astype(bf16)
    for hop in range(1, count):
        across(hop).start()
    for hop in range(1, count):
        across(hop).wait()
    loop(lambda hop: around(hop).start(), dp_count)
    out_ref[place] = mid[...]
    loop(lambda hop: around(hop).wait(), dp_count)


def sum_small(packed, dp_count, count, cid):
    shape = packed.shape[1:]
    return pl.pallas_call(
        functools.partial(small_kernel, dp_count, count),
        out_shape=jax.ShapeDtypeStruct((dp_count, count) + shape, bf16),
        in_specs=[VMEM],
        out_specs=VMEM,
        scratch_shapes=[
            pltpu.VMEM((dp_count - 1,) + shape, f32),
            pltpu.VMEM((count,) + shape, bf16),
            DMA((dp_count - 1,)),
            DMA((dp_count - 1,)),
            DMA((count - 1,)),
            DMA((count - 1,)),
            DMA((dp_count - 1,)),
            DMA((dp_count - 1,)),
        ],
        compiler_params=params(cid, 32),
        name="sum_small",
    )(packed)


def layer_norm(values, gain, shift):
    centered = values - jnp.mean(values, axis=-1, keepdims=True)
    variance = jnp.mean(centered * centered, axis=-1, keepdims=True)
    return centered * lax.rsqrt(variance + norm_eps) * gain + shift


def norm_back(values, gain, shift, cotangent):
    unused, pull_back = jax.vjp(layer_norm, values, gain, shift)
    return pull_back(cotangent)


def gelu_exact(values):
    return jax.nn.gelu(values, approximate=False)


def highway_mix(pre_acts, previous):
    gate = jax.nn.sigmoid(pre_acts[:, 1])
    return gate * jax.nn.silu(pre_acts[:, 0]) + (1.0 - gate) * previous


def mm(spec, *operands):
    return jnp.einsum(spec, *operands, preferred_element_type=f32)


def body(
    char_ids,
    seq_lengths,
    char_table,
    conv_weight,
    conv_bias,
    highway_weight,
    highway_bias,
    proj_weight,
    proj_bias,
    norm_gain,
    norm_shift,
    qkv_weight,
    qv_bias,
    output_projection_weight,
    out_bias,
    up_weight,
    up_bias,
    down_weight,
    down_bias,
    out_grad,
):
    words, nseq, chars = char_ids.shape
    assert nseq == 1
    count = lax.axis_size("tensor")
    dp_count = lax.axis_size("dp")
    rank = lax.axis_index("tensor")
    vocab, char_dim = char_table.shape
    taps_dim, filters = conv_weight.shape
    features = proj_weight.shape[1]
    heads = qkv_weight.shape[2] // HEAD_DIM
    gains = norm_gain.astype(f32)
    shifts = norm_shift.astype(f32)

    d_out = lax.all_gather(out_grad[:, 0], "tensor", axis=0, tiled=True).astype(f32)

    padded = chars + 6
    ids = jnp.pad(char_ids[:, 0], ((0, 0), (0, 6)), constant_values=-1)
    ids_tiles = jnp.swapaxes(ids.reshape(words // WORD_TILE, WORD_TILE, padded), 1, 2)
    ids_tiles = ids_tiles.reshape(words // WORD_TILE, padded * WORD_TILE)
    table_wide = jnp.pad(jnp.tile(char_table, (1, 7)), ((0, 0), (0, LANES - taps_dim)))
    one_hot = (ids.T[:, :, None] == lax.broadcasted_iota(jnp.int32, (1, 1, vocab), 2)).astype(bf16)
    pattern = np.zeros((padded, LANES), np.float32)
    pattern[:, taps_dim] = 1.0
    for k in range(1, 7):
        pattern[chars - k, taps_dim + k] = 1.0
    y = (mm("qwv,vl->qwl", one_hot, table_wide) + pattern[:, None, :]).astype(bf16)

    widths = filter_widths(filters)
    off = jnp.asarray(np.log((chars - widths + 1).astype(np.float64)).astype(np.float32))[None]
    tap_of = np.arange(taps_dim)[:, None] // char_dim
    w_taps = jnp.where(tap_of < widths[None], conv_weight, 0).astype(bf16)
    ends = np.where(widths[None] > np.arange(1, 7)[:, None], big_neg, 0.0).astype(np.float32)
    tail = LANES - taps_dim - 7
    w_all = jnp.concatenate(
        [w_taps, conv_bias[None], jnp.asarray(ends, bf16), jnp.zeros((tail, filters), bf16)], axis=0
    )
    w_back = jnp.concatenate([w_taps, jnp.zeros((LANES - taps_dim, filters), bf16)], axis=0)

    logs, whole = conv_forward(y, w_all, off, count, chars, 1)
    hidden = jax.nn.silu(logs - off)
    kept_layers = []
    for layer in range(highway_weight.shape[0]):
        if layer > 0:
            whole = gather_features(hidden.astype(bf16), count, 1 + layer)
        pre_acts = mm("rk,jkf->rjf", whole, highway_weight[layer]) + highway_bias[layer].astype(f32)
        kept_layers.append((hidden, whole, pre_acts))
        hidden = highway_mix(pre_acts, hidden)
    top_sent = hidden.astype(bf16)
    embedded = sum_rows(mm("sk,kd->sd", top_sent, proj_weight).astype(bf16), count, 4)
    embedded = embedded + proj_bias.astype(f32)
    inputs = layer_norm(embedded, gains[0], shifts[0])
    sent = inputs.astype(bf16)
    projected = mm("sd,dkh->skh", sent, qkv_weight)
    queries = (projected[:, 0] + qv_bias[0].astype(f32)).astype(bf16).reshape(words, heads, HEAD_DIM)
    key_rows = projected[:, 1].astype(bf16).reshape(words, heads, HEAD_DIM)
    values = (projected[:, 2] + qv_bias[1].astype(f32)).astype(bf16).reshape(words, heads, HEAD_DIM)
    scale = HEAD_DIM ** (-0.5)
    scores = mm("qhd,khd->hqk", queries, key_rows) * scale
    live = lax.broadcasted_iota(jnp.int32, scores.shape, 2) < seq_lengths[0]
    scores = jnp.where(live, scores, big_neg)
    probs = jax.nn.softmax(scores, axis=2)
    attended = mm("hqk,khd->qhd", probs.astype(bf16), values).astype(bf16).reshape(words, -1)
    branch = sum_rows(mm("sh,hd->sd", attended, output_projection_weight).astype(bf16), count, 5)
    middle_pre = inputs + branch + out_bias.astype(f32)
    middle = layer_norm(middle_pre, gains[1], shifts[1])
    sent_mid = middle.astype(bf16)
    upper = mm("sd,df->sf", sent_mid, up_weight) + up_bias.astype(f32)
    activated = gelu_exact(upper).astype(bf16)
    branch_two = sum_rows(mm("sf,fd->sd", activated, down_weight).astype(bf16), count, 6)
    final_pre = middle + branch_two + down_bias.astype(f32)
    own_rows = words // count
    final_own = lax.dynamic_slice_in_dim(final_pre, rank * own_rows, own_rows, 0)
    encoded = layer_norm(final_own, gains[2], shifts[2]).astype(bf16)[:, None]

    d_pre2, d_gain2, d_shift2 = norm_back(final_pre, gains[2], shifts[2], d_out)
    d_branch_two = d_pre2.astype(bf16)
    down_bias_grad = jnp.sum(d_branch_two.astype(f32), axis=0)
    d_down_t = mm("sd,sf->df", d_branch_two, activated)
    d_activated = mm("sd,fd->sf", d_branch_two, down_weight)
    unused, gelu_pull = jax.vjp(gelu_exact, upper)
    d_upper = gelu_pull(d_activated)[0].astype(bf16)
    up_bias_part = jnp.sum(d_upper.astype(f32), axis=0)
    d_up = mm("sd,sf->df", sent_mid, d_upper)
    d_middle = d_pre2 + sum_rows(mm("sf,df->sd", d_upper, up_weight).astype(bf16), count, 7)
    d_pre1, d_gain1, d_shift1 = norm_back(middle_pre, gains[1], shifts[1], d_middle)
    d_branch = d_pre1.astype(bf16)
    out_bias_grad = jnp.sum(d_branch.astype(f32), axis=0)
    d_out_t = mm("sd,sh->dh", d_branch, attended)
    d_heads = mm("sd,hd->sh", d_branch, output_projection_weight).astype(bf16)
    d_heads = d_heads.reshape(words, heads, HEAD_DIM)
    d_values = mm("hqk,qhd->khd", probs.astype(bf16), d_heads).astype(bf16)
    d_probs = mm("qhd,khd->hqk", d_heads, values)
    d_scores = (probs * (d_probs - jnp.sum(d_probs * probs, axis=2, keepdims=True))).astype(bf16)
    d_queries = (mm("hqk,khd->qhd", d_scores, key_rows) * scale).astype(bf16)
    d_keys = (mm("hqk,qhd->khd", d_scores, queries) * scale).astype(bf16)
    d_proj = jnp.concatenate(
        [part.reshape(words, -1) for part in (d_queries, d_keys, d_values)], axis=1
    )
    proj_sums = jnp.sum(d_proj.astype(f32), axis=0).reshape(3, -1)
    qv_part = jnp.stack([proj_sums[0], proj_sums[2]], axis=0)
    d_qkv = mm("sd,sh->dh", sent, d_proj)
    d_inputs = d_pre1 + sum_rows(
        mm("sh,dh->sd", d_proj, qkv_weight.reshape(features, -1)).astype(bf16), count, 8
    )
    d_embedded, d_gain0, d_shift0 = norm_back(embedded, gains[0], shifts[0], d_inputs)
    grads_emb = d_embedded.astype(bf16)
    proj_bias_grad = jnp.sum(grads_emb.astype(f32), axis=0)
    d_proj_t = mm("sd,sk->dk", grads_emb, top_sent)
    d_hidden = mm("sd,kd->sk", grads_emb, proj_weight)

    hw_parts = []
    hw_bias_parts = []
    for layer in reversed(range(len(kept_layers))):
        previous, whole, pre_acts = kept_layers[layer]
        unused, mix_pull = jax.vjp(highway_mix, pre_acts, previous)
        d_pre, d_previous = mix_pull(d_hidden)
        d_pre = d_pre.astype(bf16)
        hw_parts.insert(0, mm("rk,rjf->jkf", whole, d_pre).astype(bf16))
        hw_bias_parts.insert(0, jnp.sum(d_pre.astype(f32), axis=0))
        partial_sum = mm("rjf,jkf->rk", d_pre, highway_weight[layer]).astype(bf16)
        if layer > 0:
            d_hidden = d_previous + scatter_features(partial_sum, count, 8 + layer)
    hw_bias_part = jnp.concatenate(hw_bias_parts, axis=0)

    mats = 2 * len(kept_layers)
    hw_all = jnp.concatenate(hw_parts, axis=0)
    tr_all = jnp.concatenate(
        [
            d_up.astype(bf16),
            d_down_t.astype(bf16),
            d_proj_t.astype(bf16),
            d_qkv.astype(bf16),
            jnp.zeros((features, 64), bf16),
            d_out_t.astype(bf16),
            jnp.zeros((features, 64), bf16),
        ],
        axis=1,
    )
    small = (ids_tiles, y, w_all, w_back, off, logs, d_previous, partial_sum)
    if dp_count == 8 and (features // dp_count) % 16 == 0:
        d_w_all, table_all, hw_sum, tr_sum = conv_backward(
            *small,
            hw_all.reshape(mats, 2, 2, 2, -1, filters),
            tr_all.reshape(2, 2, 2, features // dp_count, -1),
            count,
            chars,
            10,
        )
    else:
        d_w_all, table_all = conv_backward(*small, None, None, count, chars, 10)
        hw_sum = lax.psum_scatter(hw_all, "dp", scatter_dimension=1, tiled=True).astype(f32)
        tr_sum = lax.psum_scatter(tr_all, "dp", scatter_dimension=0, tiled=True).astype(f32)
    hw_w_grad = hw_sum.reshape(len(kept_layers), 2, -1, filters)
    up_w_grad = tr_sum[:, :768]
    down_w_grad = tr_sum[:, 768:1536].T
    proj_w_grad = tr_sum[:, 1536:2048].T
    qkv_w_grad = tr_sum[:, 2048:2624].reshape(-1, 3, heads * HEAD_DIM)
    out_w_grad = tr_sum[:, 2688:2880].T

    table_part = jnp.sum(
        table_all[:vocab, :taps_dim].reshape(vocab, taps_dim // char_dim, char_dim), axis=1
    )
    pieces = [
        d_w_all[: taps_dim + 1],
        hw_bias_part,
        qv_part,
        up_bias_part,
        table_part,
        proj_bias_grad,
        jnp.stack([d_gain0, d_gain1, d_gain2]),
        jnp.stack([d_shift0, d_shift1, d_shift2]),
        out_bias_grad,
        down_bias_grad,
    ]
    sizes = [piece.size for piece in pieces]
    flat = jnp.concatenate([piece.reshape(-1) for piece in pieces])
    width = -(-flat.size // (dp_count * 16 * LANES)) * LANES
    flat = jnp.pad(flat, (0, dp_count * 16 * width - flat.size))
    summed = sum_small(flat.reshape(dp_count, 16, width), dp_count, count, 11)
    summed = jnp.swapaxes(summed, 0, 1).reshape(count, -1).astype(f32)
    ends_at = np.cumsum(sizes)

    def piece(index):
        return summed[:, ends_at[index] - sizes[index] : ends_at[index]]

    conv_all = jnp.swapaxes(piece(0).reshape(count, taps_dim + 1, filters), 0, 1).reshape(
        taps_dim + 1, -1
    )
    conv_w_grad = jnp.where(
        tap_of < np.tile(widths, count)[None], conv_all[:taps_dim], 0.0
    )
    conv_b_grad = conv_all[taps_dim]
    hw_b_grad = jnp.swapaxes(piece(1).reshape(count, mats, filters), 0, 1).reshape(
        len(kept_layers), 2, -1
    )
    qv_grad = jnp.swapaxes(piece(2).reshape(count, 2, -1), 0, 1).reshape(2, -1)
    up_b_grad = piece(3).reshape(-1)
    table_grad = jnp.sum(piece(4), axis=0).reshape(vocab, char_dim)
    proj_b_grad = piece(5)[0]
    gain_grad = piece(6)[0].reshape(3, features)
    shift_grad = piece(7)[0].reshape(3, features)
    out_b_grad = piece(8)[0]
    down_b_grad = piece(9)[0]
    return (
        encoded,
        table_grad,
        conv_w_grad,
        conv_b_grad,
        hw_w_grad,
        hw_b_grad,
        proj_w_grad,
        proj_b_grad,
        gain_grad,
        shift_grad,
        qkv_w_grad,
        qv_grad,
        out_w_grad,
        out_b_grad,
        up_w_grad,
        up_b_grad,
        down_w_grad,
        down_b_grad,
    )


def solution(mesh):
    return jax.shard_map(
        body,
        mesh=mesh,
        in_specs=(
            P(None, "dp", None),
            P("dp"),
            P(),
            P(None, "tensor"),
            P("tensor"),
            P(None, None, None, "tensor"),
            P(None, None, "tensor"),
            P("tensor", None),
            P(),
            P(),
            P(),
            P(None, None, "tensor"),
            P(None, "tensor"),
            P("tensor", None),
            P(),
            P(None, "tensor"),
            P("tensor"),
            P("tensor", None),
            P(),
            P("tensor", "dp", None),
        ),
        out_specs=(
            P("tensor", "dp", None),
            P(),
            P(),
            P(),
            P(None, None, "dp", "tensor"),
            P(),
            P("tensor", "dp"),
            P(),
            P(),
            P(),
            P("dp", None, "tensor"),
            P(),
            P("tensor", "dp"),
            P(),
            P("dp", "tensor"),
            P(),
            P("tensor", "dp"),
            P(),
        ),
        check_vma=False,
    )
```

```python
import functools
import math

import jax
import jax.numpy as jnp
import numpy as np
from jax import lax
from jax.experimental import pallas as pl
from jax.experimental.pallas import tpu as pltpu
from jax.sharding import PartitionSpec as P

HEAD_DIM = 64
WORD_TILE = 32
LANES = 128

norm_eps = 1e-06
big_neg = -1e30
f32 = jnp.float32
bf16 = jnp.bfloat16
MESH = pl.DeviceIdType.MESH
VMEM = pl.BlockSpec(memory_space=pltpu.VMEM)
ANY = pl.BlockSpec(memory_space=pl.ANY)
DMA = pltpu.SemaphoreType.DMA
MIB = 1 << 20


def params(cid, vmem):
    return pltpu.CompilerParams(
        collective_id=cid, has_side_effects=True, vmem_limit_bytes=vmem * MIB
    )


def width_counts(block):
    unit = block // 64
    return [unit, unit, 2 * unit, 4 * unit, 8 * unit, 16 * unit, 32 * unit]


def filter_widths(block):
    return np.concatenate(
        [np.full((n,), i + 1, np.int32) for i, n in enumerate(width_counts(block))]
    )


def dot(a, b, ca, cb):
    return lax.dot_general(a, b, (((ca,), (cb,)), ((), ())), preferred_element_type=f32)


def line_barrier(me, count):
    barrier = pltpu.get_barrier_semaphore()
    for there, ok in ((me - 1, me > 0), (me + 1, me < count - 1)):

        @pl.when(ok)
        def greet():
            pl.semaphore_signal(barrier, inc=1, device_id={"tensor": there}, device_id_type=MESH)

    pl.semaphore_wait(barrier, jnp.minimum(me, 1) + jnp.minimum(count - 1 - me, 1))


def line_copy(view, me, count, right, block, chunk, sems):
    send, recv = sems[:2] if right else sems[2:]
    to = jnp.minimum(me + 1, count - 1) if right else jnp.maximum(me - 1, 0)
    ref = view(block, chunk)
    return pltpu.make_async_remote_copy(
        src_ref=ref,
        dst_ref=ref,
        send_sem=send.at[block, chunk],
        recv_sem=recv.at[block, chunk],
        device_id={"tensor": to},
        device_id_type=MESH,
    )


def gather_step(view, step, chunks, me, count, sems):
    for hop in range(count):
        chunk = step - hop
        here = (chunk >= 0) & (chunk < chunks)
        safe = jnp.clip(chunk, 0, chunks - 1)
        for right in (True, False):
            block = me - hop if right else me + hop
            there = (block >= 0) & (block < count)
            block = jnp.clip(block, 0, count - 1)
            more = me < count - 1 if right else me > 0
            copy = functools.partial(line_copy, view, me, count, right, block, safe, sems)

            @pl.when(here & there)
            def pass_on():
                if hop > 0:
                    copy().wait_recv()

                @pl.when(more)
                def send():
                    copy().start()


def gather_drain(view, chunks, me, count, sems):
    def one(chunk, carry):
        for hop in range(count):
            for right in (True, False):
                block = me - hop if right else me + hop
                there = (block >= 0) & (block < count)
                block = jnp.clip(block, 0, count - 1)
                more = me < count - 1 if right else me > 0
                copy = functools.partial(line_copy, view, me, count, right, block, chunk, sems)

                @pl.when(there & more)
                def sent():
                    copy().wait_send()

        return carry

    lax.fori_loop(0, chunks, one, 0)


def windows(y_ref, start, chars):
    group = lax.broadcasted_iota(jnp.int32, (1, WORD_TILE, LANES), 2) // 16
    tile = pl.ds(start, WORD_TILE)
    value = y_ref[0:chars, tile, :]
    for tap in range(1, 7):
        value = jnp.where(group == tap, y_ref[tap : chars + tap, tile, :], value)
    return value.reshape(chars * WORD_TILE, LANES)


def conv_forward_kernel(count, chars, chunks, y_ref, w_ref, off_ref, log_ref, whole_ref, *sems):
    me = lax.axis_index("tensor")
    words, filters = log_ref.shape
    rows = words // chunks
    line_barrier(me, count)

    def view(block, chunk):
        return whole_ref.at[
            pl.ds(pl.multiple_of(chunk * rows, rows), rows),
            pl.ds(pl.multiple_of(block * filters, filters), filters),
        ]

    def tile_step(index, carry):
        start = pl.multiple_of(index * WORD_TILE, WORD_TILE)
        conv = dot(windows(y_ref, start, chars), w_ref[...], 1, 0)
        conv = conv.reshape(chars, WORD_TILE, filters)
        top = jnp.max(conv, axis=0)
        total = top + jnp.log(jnp.sum(jnp.exp(conv - top[None]), axis=0))
        log_ref[pl.ds(start, WORD_TILE), :] = total
        pooled = total - off_ref[...]
        whole_ref[
            pl.ds(start, WORD_TILE), pl.ds(pl.multiple_of(me * filters, filters), filters)
        ] = (pooled * jax.nn.sigmoid(pooled)).astype(bf16)
        return carry

    per = rows // WORD_TILE

    def chunk_step(step, carry):
        @pl.when(step < chunks)
        def work():
            lax.fori_loop(step * per, step * per + per, tile_step, 0)

        gather_step(view, step, chunks, me, count, sems)
        return carry

    lax.fori_loop(0, chunks + count - 1, chunk_step, 0)
    gather_drain(view, chunks, me, count, sems)


def conv_forward(y, w, off, count, chars, cid):
    words, filters = y.shape[1], w.shape[1]
    chunks = 8
    return pl.pallas_call(
        functools.partial(conv_forward_kernel, count, chars, chunks),
        out_shape=(
            jax.ShapeDtypeStruct((words, filters), f32),
            jax.ShapeDtypeStruct((words, count * filters), bf16),
        ),
        in_specs=[VMEM] * 3,
        out_specs=(VMEM, VMEM),
        scratch_shapes=[DMA((count, chunks))] * 4,
        compiler_params=params(cid, 40),
        name="conv_forward",
    )(y, w, off)


def gather_kernel(count, chunks, x_ref, whole_ref, *sems):
    me = lax.axis_index("tensor")
    words, filters = x_ref.shape
    rows = words // chunks
    whole_ref[:, pl.ds(pl.multiple_of(me * filters, filters), filters)] = x_ref[...]
    line_barrier(me, count)

    def view(block, chunk):
        return whole_ref.at[
            pl.ds(pl.multiple_of(chunk * rows, rows), rows),
            pl.ds(pl.multiple_of(block * filters, filters), filters),
        ]

    def chunk_step(step, carry):
        gather_step(view, step, chunks, me, count, sems)
        return carry

    lax.fori_loop(0, chunks + count - 1, chunk_step, 0)
    gather_drain(view, chunks, me, count, sems)


def gather_features(x, count, cid):
    chunks = 4
    return pl.pallas_call(
        functools.partial(gather_kernel, count, chunks),
        out_shape=jax.ShapeDtypeStruct((x.shape[0], count * x.shape[1]), bf16),
        in_specs=[VMEM],
        out_specs=VMEM,
        scratch_shapes=[DMA((count, chunks))] * 4,
        compiler_params=params(cid, 16),
        name="gather_features",
    )(x)


def sum_kernel(count, chunks, spacing, p_ref, out_ref, from_left, from_right, s_right, r_right, s_left, r_left):
    me = lax.axis_index("tensor")
    rows = p_ref.shape[0] // chunks
    line_barrier(me, count)

    def tile(chunk):
        return pl.ds(pl.multiple_of(chunk * rows, rows), rows)

    def copies(right, chunk):
        buf = from_left if right else from_right
        send, recv = (s_right, r_right) if right else (s_left, r_left)
        to = jnp.minimum(me + 1, count - 1) if right else jnp.maximum(me - 1, 0)
        first, passed = [
            functools.partial(
                pltpu.make_async_remote_copy,
                src_ref=src.at[tile(chunk)],
                dst_ref=buf.at[tile(chunk)],
                send_sem=send.at[chunk],
                recv_sem=recv.at[chunk],
                device_id={"tensor": to},
                device_id_type=MESH,
            )
            for src in (p_ref, buf)
        ]
        return buf, first, passed

    def step_fn(step, carry):
        for right in (True, False):
            lag = me if right else count - 1 - me
            chunk = step - spacing * lag
            here = (chunk >= 0) & (chunk < chunks)
            chunk = jnp.clip(chunk, 0, chunks - 1)
            buf, first, passed = copies(right, chunk)

            @pl.when(here & (lag == 0))
            def start():
                first().start()

            @pl.when(here & (lag > 0))
            def middle():
                first().wait_recv()
                got = buf[tile(chunk), :].astype(f32)

                @pl.when(lag < count - 1)
                def forward():
                    buf[tile(chunk), :] = (got + p_ref[tile(chunk), :].astype(f32)).astype(bf16)
                    passed().start()

                out_ref[tile(chunk), :] += got

        return carry

    out_ref[...] = p_ref[...].astype(f32)
    lax.fori_loop(0, chunks + spacing * (count - 1), step_fn, 0)

    def drain(chunk, carry):
        for right in (True, False):
            lag = me if right else count - 1 - me

            @pl.when(lag < count - 1)
            def sent():
                copies(right, chunk)[1]().wait_send()

        return carry

    lax.fori_loop(0, chunks, drain, 0)


def sum_rows(partial, count, cid):
    chunks = 16
    shape = partial.shape
    return pl.pallas_call(
        functools.partial(sum_kernel, count, chunks, 3),
        out_shape=jax.ShapeDtypeStruct(shape, f32),
        in_specs=[VMEM],
        out_specs=VMEM,
        scratch_shapes=[pltpu.VMEM(shape, bf16)] * 2 + [DMA((chunks,))] * 4,
        compiler_params=params(cid, 16),
        name="sum_rows",
    )(partial)


class LineScatter:
    def __init__(self, count, me, chunks, spacing, p_ref, out_ref, from_left, from_right, sems):
        self.count, self.me, self.chunks, self.spacing = count, me, chunks, spacing
        self.p_ref, self.out_ref = p_ref, out_ref
        self.from_left, self.from_right, self.sems = from_left, from_right, sems
        self.messages = chunks * (count - 1)
        self.steps = self.messages + spacing * (count - 1)

    def place(self, right, number):
        count, me = self.count, self.me
        lag = me if right else count - 1 - me
        chunk = number // (count - 1)
        far = count - 1 - number % (count - 1)
        block = far if right else count - 1 - far
        words, filters = self.out_ref.shape
        rows = words // self.chunks
        tile = pl.ds(pl.multiple_of(chunk * rows, rows), rows)
        lanes = pl.ds(pl.multiple_of(block * filters, filters), filters)
        buf = self.from_left if right else self.from_right
        send, recv = self.sems[:2] if right else self.sems[2:]
        to = jnp.minimum(me + 1, count - 1) if right else jnp.maximum(me - 1, 0)
        first, passed = [
            functools.partial(
                pltpu.make_async_remote_copy,
                src_ref=src.at[tile, lanes],
                dst_ref=buf.at[tile, lanes],
                send_sem=send.at[block, chunk],
                recv_sem=recv.at[block, chunk],
                device_id={"tensor": to},
                device_id_type=MESH,
            )
            for src in (self.p_ref, buf)
        ]
        return lag, far, tile, lanes, buf, first, passed

    def step(self, step):
        for right in (True, False):
            lag = self.me if right else self.count - 1 - self.me
            number = step - self.spacing * lag
            here = (number >= 0) & (number < self.messages)
            number = jnp.clip(number, 0, self.messages - 1)
            lag, far, tile, lanes, buf, first, passed = self.place(right, number)

            @pl.when(here & (lag == 0))
            def start():
                first().start()

            @pl.when(here & (lag > 0) & (far > lag))
            def middle():
                first().wait_recv()
                buf[tile, lanes] = (
                    buf[tile, lanes].astype(f32) + self.p_ref[tile, lanes].astype(f32)
                ).astype(bf16)
                passed().start()

            @pl.when(here & (lag > 0) & (far == lag))
            def last():
                first().wait_recv()
                self.out_ref[tile, :] += buf[tile, lanes].astype(f32)

    def drain(self):
        def one(number, carry):
            for right in (True, False):
                lag, far, tile, lanes, buf, first, passed = self.place(right, number)

                @pl.when(far > lag)
                def sent():
                    first().wait_send()

            return carry

        lax.fori_loop(0, self.messages, one, 0)


class DpSum:
    def __init__(self, cell, peers, x_first, sems, base):
        self.c, self.x, self.y = cell
        self.peers, self.x_first, self.base = peers, x_first, base
        self.send, self.recv = sems
        self.src = self.in0 = self.in1 = self.mid = self.in2 = self.out = None

    def remote(self, number, src, dst, bit):
        return pltpu.make_async_remote_copy(
            src_ref=src,
            dst_ref=dst,
            send_sem=self.send.at[self.base + number],
            recv_sem=self.recv.at[self.base + number],
            device_id=self.peers[bit],
            device_id_type=MESH,
        )

    def copy0(self):
        return self.remote(0, self.src.at[:, :, 1 - self.c], self.in0, 0)

    def copy1(self):
        if self.x_first:
            return self.remote(1, self.src.at[:, 1 - self.x, self.c], self.in1, 1)
        return self.remote(1, self.src.at[1 - self.y, :, self.c], self.in1, 2)

    def copy2(self):
        own = self.y if self.x_first else self.x
        return self.remote(2, self.mid.at[1 - own], self.in2, 2 if self.x_first else 1)

    def finish0(self):
        self.copy0().wait()

        def one(k, carry):
            i, j = k // 2, k % 2
            self.src[i, j, self.c] = (
                self.src[i, j, self.c].astype(f32) + self.in0[i, j].astype(f32)
            ).astype(bf16)
            return carry

        lax.fori_loop(0, 4, one, 0)

    def finish1(self):
        self.copy1().wait()

        def one(k, carry):
            kept = self.src[k, self.x, self.c] if self.x_first else self.src[self.y, k, self.c]
            self.mid[k] = (kept.astype(f32) + self.in1[k].astype(f32)).astype(bf16)
            return carry

        lax.fori_loop(0, 2, one, 0)

    def finish2(self):
        self.copy2().wait()
        own = self.y if self.x_first else self.x
        self.out[...] = self.mid[own].astype(f32) + self.in2[...].astype(f32)


def dp_cell(place):
    cell = [place % 2, (place // 2) % 2, place // 4]
    return cell, [{"dp": place + (1 - 2 * cell[bit]) * 2**bit} for bit in range(3)]


def greet_all(peers):
    barrier = pltpu.get_barrier_semaphore()
    for peer in peers:
        pl.semaphore_signal(barrier, inc=1, device_id=peer, device_id_type=MESH)
    pl.semaphore_wait(barrier, len(peers))


def mix_back(d_hidden, trans, gate_pre, previous):
    gate = jax.nn.sigmoid(gate_pre)
    sig = jax.nn.sigmoid(trans)
    act = trans * sig
    d_trans = (d_hidden * gate * (sig * (1.0 + trans * (1.0 - sig)))).astype(bf16)
    d_gate = (d_hidden * (act - previous) * gate * (1.0 - gate)).astype(bf16)
    return d_trans, d_gate, (1.0 - gate) * d_hidden


def weight_grad_piece(piece, whole_ref, d_refs, outs):
    rows = outs[0].shape[-2]
    lanes = pl.ds(pl.multiple_of(piece * rows, rows), rows)
    index = (piece // 4, (piece // 2) % 2, piece % 2)
    for d_ref, out in zip(d_refs, outs):
        out[index] = dot(whole_ref[:, lanes], d_ref[...], 0, 0).astype(bf16)


def highway_back_kernel(count, chunks, reduce, *refs):
    (d_h2_ref, t1_ref, g1_ref, h1_ref, t0_ref, g0_ref, h0_ref, whole1_ref, w_ref) = refs[:9]
    refs = refs[9:]
    if reduce:
        tra_ref, trb_ref = refs[:2]
        refs = refs[2:]
    part0_ref, prev0_ref, dt0_ref, dg0_ref, sums_ref = refs[:5]
    refs = refs[5:]
    if reduce:
        mids = refs[:4]
        hw_a, hw_b = refs[4:6]
        in0s, in1s = refs[6:10], refs[10:14]
        dp_sems = refs[14:16]
        refs = refs[16:]
    else:
        hw_a, hw_b = refs[:2]
        refs = refs[2:]
    part1_ref, from_left, from_right, d_h1_ref, dt1_ref, dg1_ref = refs[:6]
    sems = refs[6:]
    me = lax.axis_index("tensor")
    words, filters = d_h2_ref.shape
    ring = [{"tensor": lax.rem(me + k, count)} for k in range(1, count)]
    items = []
    if reduce:
        cell, peers = dp_cell(lax.axis_index("dp"))
        greet_all(peers + ring)
        for k, src in enumerate((hw_a, hw_b, tra_ref, trb_ref)):
            item = DpSum(cell, peers, k % 2 == 0, dp_sems, 3 * k)
            item.src, item.in0, item.in1, item.mid = src, in0s[k], in1s[k], mids[k]
            items.append(item)
        for item in items[2:]:
            item.copy0().start()
    else:
        greet_all(ring)

    def back(layer, d_h_ref, t_ref, g_ref, h_ref, dt_ref, dg_ref, prev_ref, p_ref):
        dt, dg, prev = mix_back(d_h_ref[...], t_ref[...], g_ref[...], h_ref[...])
        dt_ref[...] = dt
        dg_ref[...] = dg
        prev_ref[...] = prev
        for j, d in enumerate((dt, dg)):
            sums_ref[2 * layer + j : 2 * layer + j + 1, :] = jnp.sum(
                d.astype(f32), axis=0, keepdims=True
            )

        def one(block, carry):
            lanes = pl.ds(pl.multiple_of(block * filters, filters), filters)
            p_ref[:, lanes] = (
                dot(dt_ref[...], w_ref[layer, 0, lanes, :], 1, 1)
                + dot(dg_ref[...], w_ref[layer, 1, lanes, :], 1, 1)
            ).astype(bf16)
            return carry

        lax.fori_loop(0, count, one, 0)

    back(1, d_h2_ref, t1_ref, g1_ref, h1_ref, dt1_ref, dg1_ref, d_h1_ref, part1_ref)
    d_h1_ref[...] += part1_ref[
        :, pl.ds(pl.multiple_of(me * filters, filters), filters)
    ].astype(f32)
    scatter = LineScatter(
        count, me, chunks, 3, part1_ref, d_h1_ref, from_left, from_right, sems
    )

    def step_fn(step, carry):
        scatter.step(step)

        @pl.when(step < 8)
        def grads():
            weight_grad_piece(step, whole1_ref, (dt1_ref, dg1_ref), (hw_a, hw_b))

        if reduce:

            @pl.when(step == 8)
            def start0():
                for item in items[:2]:
                    item.copy0().start()
                for item in items[2:]:
                    item.finish0()
                    item.copy1().start()

            @pl.when(step == 16)
            def start1():
                for item in items[:2]:
                    item.finish0()
                    item.copy1().start()

        return carry

    lax.fori_loop(0, scatter.steps, step_fn, 0)
    back(0, d_h1_ref, t0_ref, g0_ref, h0_ref, dt0_ref, dg0_ref, prev0_ref, part0_ref)
    for item in items:
        item.finish1()
    scatter.drain()


def highway_back(d_h2, t1, g1, h1, t0, g0, h0, whole1, weight, tra, trb, count, cid):
    words, filters = d_h2.shape
    chunks = 8
    reduce = tra is not None
    rows = whole1.shape[1] // 8
    shape = jax.ShapeDtypeStruct
    out_shape = [
        shape(whole1.shape, bf16),
        shape((words, filters), f32),
        shape((words, filters), bf16),
        shape((words, filters), bf16),
        shape((4, filters), f32),
    ]
    operands = [d_h2, t1, g1, h1, t0, g0, h0, whole1, weight]
    hw_shape = (2, 2, 2, rows, filters)
    scratch = []
    if reduce:
        operands += [tra, trb]
        tails = [hw_shape[-2:], hw_shape[-2:], tra.shape[-2:], trb.shape[-2:]]
        out_shape += [shape((2,) + tail, bf16) for tail in tails]
        scratch += [pltpu.VMEM(hw_shape, bf16)] * 2
        scratch += [pltpu.VMEM((2, 2) + tail, bf16) for tail in tails]
        scratch += [pltpu.VMEM((2,) + tail, bf16) for tail in tails]
        scratch += [DMA((12,))] * 2
    else:
        out_shape += [shape(hw_shape, bf16)] * 2
    scratch += [pltpu.VMEM(whole1.shape, bf16)] * 3
    scratch += [pltpu.VMEM((words, filters), f32)] + [pltpu.VMEM((words, filters), bf16)] * 2
    scratch += [DMA((count, chunks))] * 4
    return pl.pallas_call(
        functools.partial(highway_back_kernel, count, chunks, reduce),
        out_shape=tuple(out_shape),
        in_specs=[VMEM] * len(operands),
        out_specs=tuple([VMEM] * len(out_shape)),
        scratch_shapes=scratch,
        compiler_params=params(cid, 58),
        name="highway_back",
    )(*operands)


def conv_backward_kernel(count, chars, chunks, cuts, *refs):
    (ids_ref, y_ref, w_ref, wb_ref, off_ref, log_ref, prev_ref, part_ref, whole_ref, dt_ref,
     dg_ref) = refs[:11]
    refs = refs[11:]
    if cuts:
        mids_in = refs[:4]
        dw_ref, table_ref = refs[4:6]
        outs = refs[6:12]
        hw_a, hw_b = refs[12:14]
        in0s, in1s, mids, in2s = refs[14:16], refs[16:18], refs[18:20], refs[20:26]
        dp_sems = refs[26:28]
        refs = refs[28:]
    else:
        dw_ref, table_ref, hw_a, hw_b = refs[:4]
        refs = refs[4:]
    pad_ref, got_ref, part_send, part_recv = refs
    me = lax.axis_index("tensor")
    words, filters = log_ref.shape
    rows = words // chunks
    padded = y_ref.shape[0]
    peers = [{"tensor": lax.rem(me + k, count)} for k in range(1, count)]
    items = []
    if cuts:
        cell, dp_peers = dp_cell(lax.axis_index("dp"))
        greet_all(dp_peers + peers)
        for k in range(6):
            item = DpSum(cell, dp_peers, k % 2 == 0, dp_sems, 3 * k)
            item.in2, item.out = in2s[k], outs[k]
            if k < 2:
                item.src, item.in0, item.in1 = (hw_a, hw_b)[k], in0s[k], in1s[k]
                item.mid = mids[k]
            else:
                item.mid = mids_in[k - 2]
            items.append(item)
    else:
        greet_all(peers)

    def part_copy(hop, chunk):
        to = lax.rem(me + hop, count)
        tile = pl.ds(pl.multiple_of(chunk * rows, rows), rows)
        return pltpu.make_async_remote_copy(
            src_ref=part_ref.at[tile, pl.ds(pl.multiple_of(to * filters, filters), filters)],
            dst_ref=got_ref.at[hop - 1, tile],
            send_sem=part_send.at[hop - 1, chunk],
            recv_sem=part_recv.at[hop - 1, chunk],
            device_id={"tensor": to},
            device_id_type=MESH,
        )

    def part_start(chunk, carry):
        for hop in range(1, count):
            part_copy(hop, chunk).start()
        return carry

    lax.fori_loop(0, chunks, part_start, 0)
    for item in items[2:]:
        item.copy2().start()

    def grads(piece, carry):
        weight_grad_piece(piece, whole_ref, (dt_ref, dg_ref), (hw_a, hw_b))
        return carry

    lax.fori_loop(0, 8, grads, 0)
    for item in items[:2]:
        item.copy0().start()

    dw_ref[...] = jnp.zeros_like(dw_ref)
    table_ref[...] = jnp.zeros_like(table_ref)
    pad_ref[...] = jnp.zeros_like(pad_ref)
    per = rows // WORD_TILE
    group = lax.broadcasted_iota(jnp.int32, (1, WORD_TILE, LANES), 2) // 16
    vocab = lax.broadcasted_iota(jnp.int32, (table_ref.shape[0], padded * WORD_TILE), 0)

    def tile_step(index, carry):
        @pl.when(index % per == 0)
        def arrived():
            for hop in range(1, count):
                part_copy(hop, index // per).wait_recv()

        start = pl.multiple_of(index * WORD_TILE, WORD_TILE)
        tile = pl.ds(start, WORD_TILE)
        x2 = windows(y_ref, start, chars)
        conv = dot(x2, w_ref[...], 1, 0).reshape(chars, WORD_TILE, filters)
        total = log_ref[tile, :]
        pooled = total - off_ref[...]
        sig = jax.nn.sigmoid(pooled)
        grad = prev_ref[tile, :] + part_ref[
            tile, pl.ds(pl.multiple_of(me * filters, filters), filters)
        ].astype(f32)
        for hop in range(count - 1):
            grad = grad + got_ref[hop, tile, :].astype(f32)
        grad = grad * (sig * (1.0 + pooled * (1.0 - sig)))
        d_conv = (grad[None] * jnp.exp(conv - total[None])).astype(bf16)
        d_conv = d_conv.reshape(chars * WORD_TILE, filters)
        dw_ref[...] += dot(x2, d_conv, 0, 0)
        d_win = dot(d_conv, wb_ref[...], 1, 1).astype(bf16)
        pad_ref[6 : 6 + chars] = d_win.reshape(chars, WORD_TILE, LANES)
        d_emb = pad_ref[6 : 6 + padded]
        for tap in range(1, 7):
            d_emb = jnp.where(group == tap, pad_ref[6 - tap : 6 - tap + padded], d_emb)
        one_hot = jnp.where(vocab == ids_ref[pl.ds(index, 1), :], 1.0, 0.0).astype(bf16)
        table_ref[...] += dot(one_hot, d_emb.reshape(padded * WORD_TILE, LANES), 1, 0)
        return carry

    tiles = words // WORD_TILE
    if cuts:
        lax.fori_loop(0, cuts[0], tile_step, 0)
        for item in items[:2]:
            item.finish0()
            item.copy1().start()
        lax.fori_loop(cuts[0], cuts[1], tile_step, 0)
        for item in items[:2]:
            item.finish1()
            item.copy2().start()
        lax.fori_loop(cuts[1], tiles, tile_step, 0)
        for item in items:
            item.finish2()
    else:
        lax.fori_loop(0, tiles, tile_step, 0)

    def part_drain(chunk, carry):
        for hop in range(1, count):
            part_copy(hop, chunk).wait_send()
        return carry

    lax.fori_loop(0, chunks, part_drain, 0)


def conv_backward(ids, y, w, wb, off, logs, prev, part, whole, dt, dg, mids, count, chars, cid):
    words, filters = logs.shape
    chunks = 8
    shape = jax.ShapeDtypeStruct
    hw_shape = (2, 2, 2, whole.shape[1] // 8, filters)
    out_shape = [shape((LANES, filters), f32), shape((264, LANES), f32)]
    scratch = []
    operands = [ids, y, w, wb, off, logs, prev, part, whole, dt, dg] + list(mids)
    cuts = None
    if mids:
        cuts = (6, 12)
        own = [hw_shape[-2:]] * 2
        tails = own + [mid.shape[-2:] for mid in mids]
        out_shape += [shape(tail, f32) for tail in tails]
        scratch += [pltpu.VMEM(hw_shape, bf16)] * 2
        scratch += [pltpu.VMEM((2, 2) + tail, bf16) for tail in own]
        scratch += [pltpu.VMEM((2,) + tail, bf16) for tail in own + own]
        scratch += [pltpu.VMEM(tail, bf16) for tail in tails]
        scratch += [DMA((18,))] * 2
    else:
        out_shape += [shape(hw_shape, bf16)] * 2
    scratch += [
        pltpu.VMEM((68, WORD_TILE, LANES), bf16),
        pltpu.VMEM((count - 1, words, filters), bf16),
        DMA((count - 1, chunks)),
        DMA((count - 1, chunks)),
    ]
    return pl.pallas_call(
        functools.partial(conv_backward_kernel, count, chars, chunks, cuts),
        out_shape=tuple(out_shape),
        in_specs=[VMEM] * len(operands),
        out_specs=tuple([VMEM] * len(out_shape)),
        scratch_shapes=scratch,
        compiler_params=params(cid, 58),
        name="conv_backward",
    )(*operands)


def small_kernel(dp_count, count, in_ref, out_ref, got, mid, *sems):
    s1, r1, s2, r2, s3, r3 = sems
    me = lax.axis_index("tensor")
    place = lax.axis_index("dp")
    barrier = pltpu.get_barrier_semaphore()

    def dp_peer(hop):
        return lax.rem(place + hop, dp_count)

    def greet(hop, carry):
        pl.semaphore_signal(barrier, inc=1, device_id={"dp": dp_peer(hop)}, device_id_type=MESH)
        return carry

    lax.fori_loop(1, dp_count, greet, 0)
    for hop in range(1, count):
        pl.semaphore_signal(
            barrier, inc=1, device_id={"tensor": lax.rem(me + hop, count)}, device_id_type=MESH
        )
    pl.semaphore_wait(barrier, dp_count + count - 2)

    def scatter(hop):
        return pltpu.make_async_remote_copy(
            src_ref=in_ref.at[dp_peer(hop)], dst_ref=got.at[hop - 1], send_sem=s1.at[hop - 1],
            recv_sem=r1.at[hop - 1], device_id={"dp": dp_peer(hop)}, device_id_type=MESH,
        )

    def across(hop):
        return pltpu.make_async_remote_copy(
            src_ref=mid.at[me], dst_ref=mid.at[me], send_sem=s2.at[hop - 1], recv_sem=r2.at[hop - 1],
            device_id={"tensor": lax.rem(me + hop, count)}, device_id_type=MESH,
        )

    def around(hop):
        return pltpu.make_async_remote_copy(
            src_ref=mid, dst_ref=out_ref.at[place], send_sem=s3.at[hop - 1], recv_sem=r3.at[hop - 1],
            device_id={"dp": dp_peer(hop)}, device_id_type=MESH,
        )

    def loop(fn, stop):
        def one(hop, carry):
            fn(hop)
            return carry

        lax.fori_loop(1, stop, one, 0)

    loop(lambda hop: scatter(hop).start(), dp_count)
    loop(lambda hop: scatter(hop).wait(), dp_count)
    total = lax.fori_loop(
        0, dp_count - 1, lambda k, acc: acc + got[k], in_ref[place]
    )
    mid[me] = total.astype(bf16)
    for hop in range(1, count):
        across(hop).start()
    for hop in range(1, count):
        across(hop).wait()
    loop(lambda hop: around(hop).start(), dp_count)
    out_ref[place] = mid[...]
    loop(lambda hop: around(hop).wait(), dp_count)


def sum_small(packed, dp_count, count, cid):
    shape = packed.shape[1:]
    return pl.pallas_call(
        functools.partial(small_kernel, dp_count, count),
        out_shape=jax.ShapeDtypeStruct((dp_count, count) + shape, bf16),
        in_specs=[VMEM],
        out_specs=VMEM,
        scratch_shapes=[
            pltpu.VMEM((dp_count - 1,) + shape, f32),
            pltpu.VMEM((count,) + shape, bf16),
            DMA((dp_count - 1,)),
            DMA((dp_count - 1,)),
            DMA((count - 1,)),
            DMA((count - 1,)),
            DMA((dp_count - 1,)),
            DMA((dp_count - 1,)),
        ],
        compiler_params=params(cid, 32),
        name="sum_small",
    )(packed)


def layer_norm(values, gain, shift):
    centered = values - jnp.mean(values, axis=-1, keepdims=True)
    variance = jnp.mean(centered * centered, axis=-1, keepdims=True)
    return centered * lax.rsqrt(variance + norm_eps) * gain + shift


def norm_back(values, gain, shift, cotangent):
    unused, pull_back = jax.vjp(layer_norm, values, gain, shift)
    return pull_back(cotangent)


def gelu_exact(values):
    return jax.nn.gelu(values, approximate=False)


def mm(spec, *operands):
    return jnp.einsum(spec, *operands, preferred_element_type=f32)


def body(
    char_ids,
    seq_lengths,
    char_table,
    conv_weight,
    conv_bias,
    highway_weight,
    highway_bias,
    proj_weight,
    proj_bias,
    norm_gain,
    norm_shift,
    qkv_weight,
    qv_bias,
    output_projection_weight,
    out_bias,
    up_weight,
    up_bias,
    down_weight,
    down_bias,
    out_grad,
):
    words, nseq, chars = char_ids.shape
    assert nseq == 1
    count = lax.axis_size("tensor")
    dp_count = lax.axis_size("dp")
    rank = lax.axis_index("tensor")
    vocab, char_dim = char_table.shape
    taps_dim, filters = conv_weight.shape
    features = proj_weight.shape[1]
    heads = qkv_weight.shape[2] // HEAD_DIM
    gains = norm_gain.astype(f32)
    shifts = norm_shift.astype(f32)

    d_out = lax.all_gather(out_grad[:, 0], "tensor", axis=0, tiled=True).astype(f32)

    padded = chars + 6
    ids = jnp.pad(char_ids[:, 0], ((0, 0), (0, 6)), constant_values=-1)
    ids_tiles = jnp.swapaxes(ids.reshape(words // WORD_TILE, WORD_TILE, padded), 1, 2)
    ids_tiles = ids_tiles.reshape(words // WORD_TILE, padded * WORD_TILE)
    table_wide = jnp.pad(jnp.tile(char_table, (1, 7)), ((0, 0), (0, LANES - taps_dim)))
    one_hot = (ids.T[:, :, None] == lax.broadcasted_iota(jnp.int32, (1, 1, vocab), 2)).astype(bf16)
    pattern = np.zeros((padded, LANES), np.float32)
    pattern[:, taps_dim] = 1.0
    for k in range(1, 7):
        pattern[chars - k, taps_dim + k] = 1.0
    y = (mm("qwv,vl->qwl", one_hot, table_wide) + pattern[:, None, :]).astype(bf16)

    widths = filter_widths(filters)
    off = jnp.asarray(np.log((chars - widths + 1).astype(np.float64)).astype(np.float32))[None]
    tap_of = np.arange(taps_dim)[:, None] // char_dim
    w_taps = jnp.where(tap_of < widths[None], conv_weight, 0).astype(bf16)
    ends = np.where(widths[None] > np.arange(1, 7)[:, None], big_neg, 0.0).astype(np.float32)
    tail = LANES - taps_dim - 7
    w_all = jnp.concatenate(
        [w_taps, conv_bias[None], jnp.asarray(ends, bf16), jnp.zeros((tail, filters), bf16)], axis=0
    )
    w_back = jnp.concatenate([w_taps, jnp.zeros((LANES - taps_dim, filters), bf16)], axis=0)

    logs, whole = conv_forward(y, w_all, off, count, chars, 1)
    hidden = jax.nn.silu(logs - off)
    kept_layers = []
    for layer in range(highway_weight.shape[0]):
        if layer > 0:
            whole = gather_features(hidden.astype(bf16), count, 1 + layer)
        trans, gate_pre = [
            mm("rk,kf->rf", whole, highway_weight[layer, j]) + highway_bias[layer, j].astype(f32)
            for j in range(2)
        ]
        kept_layers.append((hidden, whole, trans, gate_pre))
        gate = jax.nn.sigmoid(gate_pre)
        hidden = gate * jax.nn.silu(trans) + (1.0 - gate) * hidden
    top_sent = hidden.astype(bf16)
    embedded = sum_rows(mm("sk,kd->sd", top_sent, proj_weight).astype(bf16), count, 4)
    embedded = embedded + proj_bias.astype(f32)
    inputs = layer_norm(embedded, gains[0], shifts[0])
    sent = inputs.astype(bf16)
    projected = mm("sd,dkh->skh", sent, qkv_weight)
    queries = (projected[:, 0] + qv_bias[0].astype(f32)).astype(bf16).reshape(words, heads, HEAD_DIM)
    key_rows = projected[:, 1].astype(bf16).reshape(words, heads, HEAD_DIM)
    values = (projected[:, 2] + qv_bias[1].astype(f32)).astype(bf16).reshape(words, heads, HEAD_DIM)
    scale = HEAD_DIM ** (-0.5)
    scores = mm("qhd,khd->hqk", queries, key_rows) * scale
    live = lax.broadcasted_iota(jnp.int32, scores.shape, 2) < seq_lengths[0]
    scores = jnp.where(live, scores, big_neg)
    probs = jax.nn.softmax(scores, axis=2)
    attended = mm("hqk,khd->qhd", probs.astype(bf16), values).astype(bf16).reshape(words, -1)
    branch = sum_rows(mm("sh,hd->sd", attended, output_projection_weight).astype(bf16), count, 5)
    middle_pre = inputs + branch + out_bias.astype(f32)
    middle = layer_norm(middle_pre, gains[1], shifts[1])
    sent_mid = middle.astype(bf16)
    upper = mm("sd,df->sf", sent_mid, up_weight) + up_bias.astype(f32)
    activated = gelu_exact(upper).astype(bf16)
    branch_two = sum_rows(mm("sf,fd->sd", activated, down_weight).astype(bf16), count, 6)
    final_pre = middle + branch_two + down_bias.astype(f32)
    own_rows = words // count
    final_own = lax.dynamic_slice_in_dim(final_pre, rank * own_rows, own_rows, 0)
    encoded = layer_norm(final_own, gains[2], shifts[2]).astype(bf16)[:, None]

    d_pre2, d_gain2, d_shift2 = norm_back(final_pre, gains[2], shifts[2], d_out)
    d_branch_two = d_pre2.astype(bf16)
    down_bias_grad = jnp.sum(d_branch_two.astype(f32), axis=0)
    d_down_t = mm("sd,sf->df", d_branch_two, activated)
    d_activated = mm("sd,fd->sf", d_branch_two, down_weight)
    unused, gelu_pull = jax.vjp(gelu_exact, upper)
    d_upper = gelu_pull(d_activated)[0].astype(bf16)
    up_bias_part = jnp.sum(d_upper.astype(f32), axis=0)
    d_up = mm("sd,sf->df", sent_mid, d_upper)
    d_middle = d_pre2 + sum_rows(mm("sf,df->sd", d_upper, up_weight).astype(bf16), count, 7)
    d_pre1, d_gain1, d_shift1 = norm_back(middle_pre, gains[1], shifts[1], d_middle)
    d_branch = d_pre1.astype(bf16)
    out_bias_grad = jnp.sum(d_branch.astype(f32), axis=0)
    d_out_t = mm("sd,sh->dh", d_branch, attended)
    d_heads = mm("sd,hd->sh", d_branch, output_projection_weight).astype(bf16)
    d_heads = d_heads.reshape(words, heads, HEAD_DIM)
    d_values = mm("hqk,qhd->khd", probs.astype(bf16), d_heads).astype(bf16)
    d_probs = mm("qhd,khd->hqk", d_heads, values)
    d_scores = (probs * (d_probs - jnp.sum(d_probs * probs, axis=2, keepdims=True))).astype(bf16)
    d_queries = (mm("hqk,khd->qhd", d_scores, key_rows) * scale).astype(bf16)
    d_keys = (mm("hqk,qhd->khd", d_scores, queries) * scale).astype(bf16)
    d_proj = jnp.concatenate(
        [part.reshape(words, -1) for part in (d_queries, d_keys, d_values)], axis=1
    )
    proj_sums = jnp.sum(d_proj.astype(f32), axis=0).reshape(3, -1)
    qv_part = jnp.stack([proj_sums[0], proj_sums[2]], axis=0)
    d_qkv = mm("sd,sh->dh", sent, d_proj)
    d_inputs = d_pre1 + sum_rows(
        mm("sh,dh->sd", d_proj, qkv_weight.reshape(features, -1)).astype(bf16), count, 8
    )
    d_embedded, d_gain0, d_shift0 = norm_back(embedded, gains[0], shifts[0], d_inputs)
    grads_emb = d_embedded.astype(bf16)
    proj_bias_grad = jnp.sum(grads_emb.astype(f32), axis=0)
    d_proj_t = mm("sd,sk->dk", grads_emb, top_sent)
    d_hidden = mm("sd,kd->sk", grads_emb, proj_weight)

    tr_a = jnp.concatenate([d_up.astype(bf16), d_down_t.astype(bf16)], axis=1)
    tr_b = jnp.concatenate(
        [
            d_proj_t.astype(bf16),
            d_qkv.astype(bf16),
            jnp.zeros((features, 64), bf16),
            d_out_t.astype(bf16),
            jnp.zeros((features, 64), bf16),
        ],
        axis=1,
    )
    (h0, whole0, t0, g0), (h1, whole1, t1, g1) = kept_layers
    mats = 4
    back_args = (d_hidden, t1, g1, h1, t0, g0, h0, whole1, highway_weight)
    conv_args = (ids_tiles, y, w_all, w_back, off, logs)
    if dp_count == 8 and (features // dp_count) % 16 == 0:
        blocks = (2, 2, 2, features // dp_count, -1)
        part0, prev0, dt0, dg0, hw_bias_part, *mids = highway_back(
            *back_args, tr_a.reshape(blocks), tr_b.reshape(blocks), count, 9
        )
        d_w_all, table_all, *sums = conv_backward(
            *conv_args, prev0, part0, whole0, dt0, dg0, mids, count, chars, 10
        )
        hw_sum = jnp.stack(sums[:4])
        tr_a, tr_b = sums[4:]
    else:
        part0, prev0, dt0, dg0, hw_bias_part, *hw1 = highway_back(*back_args, None, None, count, 9)
        d_w_all, table_all, *hw0 = conv_backward(
            *conv_args, prev0, part0, whole0, dt0, dg0, (), count, chars, 10
        )
        hw_sum = jnp.stack([part.reshape(-1, filters) for part in hw0 + hw1])
        hw_sum = lax.psum_scatter(hw_sum, "dp", scatter_dimension=1, tiled=True).astype(f32)
        tr_a, tr_b = [
            lax.psum_scatter(part, "dp", scatter_dimension=0, tiled=True).astype(f32)
            for part in (tr_a, tr_b)
        ]
    hw_w_grad = hw_sum.reshape(2, 2, -1, filters)
    up_w_grad = tr_a[:, :768]
    down_w_grad = tr_a[:, 768:].T
    proj_w_grad = tr_b[:, :512].T
    qkv_w_grad = tr_b[:, 512:1088].reshape(-1, 3, heads * HEAD_DIM)
    out_w_grad = tr_b[:, 1152:1344].T

    table_part = jnp.sum(
        table_all[:vocab, :taps_dim].reshape(vocab, taps_dim // char_dim, char_dim), axis=1
    )
    pieces = [
        d_w_all[: taps_dim + 1],
        hw_bias_part,
        qv_part,
        up_bias_part,
        table_part,
        proj_bias_grad,
        jnp.stack([d_gain0, d_gain1, d_gain2]),
        jnp.stack([d_shift0, d_shift1, d_shift2]),
        out_bias_grad,
        down_bias_grad,
    ]
    sizes = [piece.size for piece in pieces]
    flat = jnp.concatenate([piece.reshape(-1) for piece in pieces])
    width = -(-flat.size // (dp_count * 16 * LANES)) * LANES
    flat = jnp.pad(flat, (0, dp_count * 16 * width - flat.size))
    summed = sum_small(flat.reshape(dp_count, 16, width), dp_count, count, 11)
    summed = jnp.swapaxes(summed, 0, 1).reshape(count, -1).astype(f32)
    ends_at = np.cumsum(sizes)

    def piece(index):
        return summed[:, ends_at[index] - sizes[index] : ends_at[index]]

    conv_all = jnp.swapaxes(piece(0).reshape(count, taps_dim + 1, filters), 0, 1).reshape(
        taps_dim + 1, -1
    )
    conv_w_grad = jnp.where(
        tap_of < np.tile(widths, count)[None], conv_all[:taps_dim], 0.0
    )
    conv_b_grad = conv_all[taps_dim]
    hw_b_grad = jnp.swapaxes(piece(1).reshape(count, mats, filters), 0, 1).reshape(2, 2, -1)
    qv_grad = jnp.swapaxes(piece(2).reshape(count, 2, -1), 0, 1).reshape(2, -1)
    up_b_grad = piece(3).reshape(-1)
    table_grad = jnp.sum(piece(4), axis=0).reshape(vocab, char_dim)
    proj_b_grad = piece(5)[0]
    gain_grad = piece(6)[0].reshape(3, features)
    shift_grad = piece(7)[0].reshape(3, features)
    out_b_grad = piece(8)[0]
    down_b_grad = piece(9)[0]
    return (
        encoded,
        table_grad,
        conv_w_grad,
        conv_b_grad,
        hw_w_grad,
        hw_b_grad,
        proj_w_grad,
        proj_b_grad,
        gain_grad,
        shift_grad,
        qkv_w_grad,
        qv_grad,
        out_w_grad,
        out_b_grad,
        up_w_grad,
        up_b_grad,
        down_w_grad,
        down_b_grad,
    )


def solution(mesh):
    return jax.shard_map(
        body,
        mesh=mesh,
        in_specs=(
            P(None, "dp", None),
            P("dp"),
            P(),
            P(None, "tensor"),
            P("tensor"),
            P(None, None, None, "tensor"),
            P(None, None, "tensor"),
            P("tensor", None),
            P(),
            P(),
            P(),
            P(None, None, "tensor"),
            P(None, "tensor"),
            P("tensor", None),
            P(),
            P(None, "tensor"),
            P("tensor"),
            P("tensor", None),
            P(),
            P("tensor", "dp", None),
        ),
        out_specs=(
            P("tensor", "dp", None),
            P(),
            P(),
            P(),
            P(None, None, "dp", "tensor"),
            P(),
            P("tensor", "dp"),
            P(),
            P(),
            P(),
            P("dp", None, "tensor"),
            P(),
            P("tensor", "dp"),
            P(),
            P("dp", "tensor"),
            P(),
            P("tensor", "dp"),
            P(),
        ),
        check_vma=False,
    )
```

```python
import functools
import math

import jax
import jax.numpy as jnp
import numpy as np
from jax import lax
from jax.experimental import pallas as pl
from jax.experimental.pallas import tpu as pltpu
from jax.sharding import PartitionSpec as P

HEAD_DIM = 64
WORD_TILE = 32
LANES = 128

norm_eps = 1e-06
big_neg = -1e30
f32 = jnp.float32
bf16 = jnp.bfloat16
MESH = pl.DeviceIdType.MESH
VMEM = pl.BlockSpec(memory_space=pltpu.VMEM)
ANY = pl.BlockSpec(memory_space=pl.ANY)
DMA = pltpu.SemaphoreType.DMA
MIB = 1 << 20


def params(cid, vmem):
    return pltpu.CompilerParams(
        collective_id=cid, has_side_effects=True, vmem_limit_bytes=vmem * MIB
    )


def width_counts(block):
    unit = block // 64
    return [unit, unit, 2 * unit, 4 * unit, 8 * unit, 16 * unit, 32 * unit]


def filter_widths(block):
    return np.concatenate(
        [np.full((n,), i + 1, np.int32) for i, n in enumerate(width_counts(block))]
    )


def dot(a, b, ca, cb):
    return lax.dot_general(a, b, (((ca,), (cb,)), ((), ())), preferred_element_type=f32)


def line_barrier(me, count):
    barrier = pltpu.get_barrier_semaphore()
    for there, ok in ((me - 1, me > 0), (me + 1, me < count - 1)):

        @pl.when(ok)
        def greet():
            pl.semaphore_signal(barrier, inc=1, device_id={"tensor": there}, device_id_type=MESH)

    pl.semaphore_wait(barrier, jnp.minimum(me, 1) + jnp.minimum(count - 1 - me, 1))


def line_copy(view, me, count, right, block, chunk, sems):
    send, recv = sems[:2] if right else sems[2:]
    to = jnp.minimum(me + 1, count - 1) if right else jnp.maximum(me - 1, 0)
    ref = view(block, chunk)
    return pltpu.make_async_remote_copy(
        src_ref=ref,
        dst_ref=ref,
        send_sem=send.at[block, chunk],
        recv_sem=recv.at[block, chunk],
        device_id={"tensor": to},
        device_id_type=MESH,
    )


def gather_step(view, step, chunks, me, count, sems):
    for hop in range(count):
        chunk = step - hop
        here = (chunk >= 0) & (chunk < chunks)
        safe = jnp.clip(chunk, 0, chunks - 1)
        for right in (True, False):
            block = me - hop if right else me + hop
            there = (block >= 0) & (block < count)
            block = jnp.clip(block, 0, count - 1)
            more = me < count - 1 if right else me > 0
            copy = functools.partial(line_copy, view, me, count, right, block, safe, sems)

            @pl.when(here & there)
            def pass_on():
                if hop > 0:
                    copy().wait_recv()

                @pl.when(more)
                def send():
                    copy().start()


def gather_drain(view, chunks, me, count, sems):
    def one(chunk, carry):
        for hop in range(count):
            for right in (True, False):
                block = me - hop if right else me + hop
                there = (block >= 0) & (block < count)
                block = jnp.clip(block, 0, count - 1)
                more = me < count - 1 if right else me > 0
                copy = functools.partial(line_copy, view, me, count, right, block, chunk, sems)

                @pl.when(there & more)
                def sent():
                    copy().wait_send()

        return carry

    lax.fori_loop(0, chunks, one, 0)


def windows(y_ref, start, chars):
    group = lax.broadcasted_iota(jnp.int32, (1, WORD_TILE, LANES), 2) // 16
    tile = pl.ds(start, WORD_TILE)
    value = y_ref[0:chars, tile, :]
    for tap in range(1, 7):
        value = jnp.where(group == tap, y_ref[tap : chars + tap, tile, :], value)
    return value.reshape(chars * WORD_TILE, LANES)


def conv_forward_kernel(count, chars, chunks, y_ref, w_ref, off_ref, log_ref, whole_ref, x_hbm,
                        p_hbm, x_buf, p_buf, keep_sem, *sems):
    me = lax.axis_index("tensor")
    words, filters = log_ref.shape
    rows = words // chunks
    tiles = words // WORD_TILE
    line_barrier(me, count)

    def view(block, chunk):
        return whole_ref.at[
            pl.ds(pl.multiple_of(chunk * rows, rows), rows),
            pl.ds(pl.multiple_of(block * filters, filters), filters),
        ]

    def keep(index):
        slot = index % 2
        return [
            pltpu.make_async_copy(buf.at[slot], hbm.at[index], keep_sem.at[k, slot])
            for k, (buf, hbm) in enumerate(((x_buf, x_hbm), (p_buf, p_hbm)))
        ]

    def tile_step(index, carry):
        slot = index % 2

        @pl.when(index >= 2)
        def free():
            for copy in keep(index - 2):
                copy.wait()

        start = pl.multiple_of(index * WORD_TILE, WORD_TILE)
        x2 = windows(y_ref, start, chars)
        x_buf[slot] = x2
        conv = dot(x2, w_ref[...], 1, 0).reshape(chars, WORD_TILE, filters)
        top = jnp.max(conv, axis=0)
        exps = jnp.exp(conv - top[None])
        sums = jnp.sum(exps, axis=0)
        p_buf[slot] = (exps * (1.0 / sums)[None]).astype(bf16)
        for copy in keep(index):
            copy.start()
        total = top + jnp.log(sums)
        log_ref[pl.ds(start, WORD_TILE), :] = total
        pooled = total - off_ref[...]
        whole_ref[
            pl.ds(start, WORD_TILE), pl.ds(pl.multiple_of(me * filters, filters), filters)
        ] = (pooled * jax.nn.sigmoid(pooled)).astype(bf16)
        return carry

    per = rows // WORD_TILE

    def chunk_step(step, carry):
        @pl.when(step < chunks)
        def work():
            lax.fori_loop(step * per, step * per + per, tile_step, 0)

        gather_step(view, step, chunks, me, count, sems)
        return carry

    lax.fori_loop(0, chunks + count - 1, chunk_step, 0)
    for index in (tiles - 2, tiles - 1):
        for copy in keep(index):
            copy.wait()
    gather_drain(view, chunks, me, count, sems)


def conv_forward(y, w, off, count, chars, cid):
    words, filters = y.shape[1], w.shape[1]
    chunks = 8
    tiles = words // WORD_TILE
    shape = jax.ShapeDtypeStruct
    return pl.pallas_call(
        functools.partial(conv_forward_kernel, count, chars, chunks),
        out_shape=(
            shape((words, filters), f32),
            shape((words, count * filters), bf16),
            shape((tiles, chars * WORD_TILE, LANES), bf16),
            shape((tiles, chars, WORD_TILE, filters), bf16),
        ),
        in_specs=[VMEM] * 3,
        out_specs=(VMEM, VMEM, ANY, ANY),
        scratch_shapes=[
            pltpu.VMEM((2, chars * WORD_TILE, LANES), bf16),
            pltpu.VMEM((2, chars, WORD_TILE, filters), bf16),
            DMA((2, 2)),
        ]
        + [DMA((count, chunks))] * 4,
        compiler_params=params(cid, 50),
        name="conv_forward",
    )(y, w, off)


def gather_kernel(count, chunks, x_ref, whole_ref, *sems):
    me = lax.axis_index("tensor")
    words, filters = x_ref.shape
    rows = words // chunks
    whole_ref[:, pl.ds(pl.multiple_of(me * filters, filters), filters)] = x_ref[...]
    line_barrier(me, count)

    def view(block, chunk):
        return whole_ref.at[
            pl.ds(pl.multiple_of(chunk * rows, rows), rows),
            pl.ds(pl.multiple_of(block * filters, filters), filters),
        ]

    def chunk_step(step, carry):
        gather_step(view, step, chunks, me, count, sems)
        return carry

    lax.fori_loop(0, chunks + count - 1, chunk_step, 0)
    gather_drain(view, chunks, me, count, sems)


def gather_features(x, count, cid):
    chunks = 4
    return pl.pallas_call(
        functools.partial(gather_kernel, count, chunks),
        out_shape=jax.ShapeDtypeStruct((x.shape[0], count * x.shape[1]), bf16),
        in_specs=[VMEM],
        out_specs=VMEM,
        scratch_shapes=[DMA((count, chunks))] * 4,
        compiler_params=params(cid, 16),
        name="gather_features",
    )(x)


class LineSum:
    def __init__(self, count, me, chunks, spacing, number, p_ref, out_ref, buffers, sems):
        self.count, self.me, self.chunks, self.spacing = count, me, chunks, spacing
        self.number, self.p_ref, self.out_ref = number, p_ref, out_ref
        self.buffers, self.sems = buffers, sems
        self.steps = chunks + spacing * (count - 1)

    def place(self, right, chunk):
        count, me, number = self.count, self.me, self.number
        lag = me if right else count - 1 - me
        rows = self.p_ref.shape[0] // self.chunks
        tile = pl.ds(pl.multiple_of(chunk * rows, rows), rows)
        buf = self.buffers[0 if right else 1]
        send, recv = self.sems[:2] if right else self.sems[2:]
        to = jnp.minimum(me + 1, count - 1) if right else jnp.maximum(me - 1, 0)
        first, passed = [
            functools.partial(
                pltpu.make_async_remote_copy,
                src_ref=src,
                dst_ref=buf.at[number, tile],
                send_sem=send.at[number, chunk],
                recv_sem=recv.at[number, chunk],
                device_id={"tensor": to},
                device_id_type=MESH,
            )
            for src in (self.p_ref.at[tile], buf.at[number, tile])
        ]
        return lag, tile, buf, first, passed

    def step(self, step):
        for right in (True, False):
            lag = self.me if right else self.count - 1 - self.me
            chunk = step - self.spacing * lag
            here = (chunk >= 0) & (chunk < self.chunks)
            chunk = jnp.clip(chunk, 0, self.chunks - 1)
            lag, tile, buf, first, passed = self.place(right, chunk)

            @pl.when(here & (lag == 0))
            def start():
                first().start()

            @pl.when(here & (lag > 0))
            def middle():
                first().wait_recv()
                got = buf[self.number, tile, :].astype(f32)

                @pl.when(lag < self.count - 1)
                def forward():
                    buf[self.number, tile, :] = (got + self.p_ref[tile, :].astype(f32)).astype(bf16)
                    passed().start()

                self.out_ref[tile, :] += got

    def drain(self):
        def one(chunk, carry):
            for right in (True, False):
                lag, tile, buf, first, passed = self.place(right, chunk)

                @pl.when(lag < self.count - 1)
                def sent():
                    first().wait_send()

            return carry

        lax.fori_loop(0, self.chunks, one, 0)

    def run(self, done, extra=()):
        rows = self.p_ref.shape[0] // self.chunks
        fill = self.spacing * (self.count - 1)

        def one(step, carry):
            self.step(step)
            for k, work in enumerate(extra):
                pl.when(step == k)(work)

            @pl.when(step >= fill)
            def finish():
                chunk = jnp.maximum(step - fill, 0)
                done(pl.ds(pl.multiple_of(chunk * rows, rows), rows))

            return carry

        lax.fori_loop(0, self.steps, one, 0)
        self.drain()


def norm_parts(values):
    centered = values - jnp.mean(values, axis=-1, keepdims=True)
    root = lax.rsqrt(jnp.mean(centered * centered, axis=-1, keepdims=True) + norm_eps)
    return centered * root, root


def norm_back(values, gain, cotangent):
    nv, root = norm_parts(values)
    scaled = cotangent * gain
    inner = jnp.mean(scaled, axis=-1, keepdims=True)
    along = jnp.mean(scaled * nv, axis=-1, keepdims=True)
    return root * (scaled - inner - nv * along), cotangent * nv


def gelu_parts(values):
    cdf = 0.5 * (1.0 + lax.erf(values * 0.7071067811865476))
    slope = cdf + values * jnp.exp(-0.5 * values * values) * 0.3989422804014327
    return values * cdf, slope


def column_sum(values):
    return jnp.sum(values, axis=0, keepdims=True)


def encoder_kernel(count, chunks, spacing, *refs):
    (top_ref, pw_ref, qw_ref, ow_ref, uw_ref, dw_ref, vec_ref, ub_ref, qb_ref, og_ref,
     live_ref) = refs[:11]
    enc_ref, dh2_ref, tra_ref, trb_ref, sums_ref, qsum_ref = refs[11:17]
    (emb, inp, midpre, mid, fin, slope, dmid, din, sent, sent_mid, act, d_two, d_up, d_branch,
     d_emb, qkv, attended, probs, d_heads, d_proj, part, grad_all, enc_all, from_left,
     from_right) = refs[17:42]
    line_sems, gather_sems = refs[42:46], refs[46:50]
    me = lax.axis_index("tensor")
    words, features = emb.shape
    heads = attended.shape[1] // HEAD_DIM
    hidden = heads * HEAD_DIM
    scale = HEAD_DIM ** (-0.5)
    own = words // count
    own_tile = pl.ds(pl.multiple_of(me * own, own), own)
    grad_all[own_tile, :] = og_ref[...]
    sums_ref[...] = jnp.zeros_like(sums_ref)
    trb_ref[...] = jnp.zeros_like(trb_ref)
    line_barrier(me, count)

    def line(number, out_ref):
        return LineSum(
            count, me, chunks, spacing, number, part, out_ref, (from_left, from_right), line_sems
        )

    def gather_view(block, chunk):
        return grad_all.at[pl.ds(pl.multiple_of(block * own, own), own)]

    def tiles(size, work):
        def one(index, carry):
            work(pl.ds(pl.multiple_of(index * size, size), size))
            return carry

        lax.fori_loop(0, words // size, one, 0)

    def send_product(lhs, rhs, side, out_ref):
        def work(tile):
            value = dot(lhs[tile, :], rhs[...], 1, side).astype(bf16)
            part[tile, :] = value
            out_ref[tile, :] = value.astype(f32)

        tiles(256, work)

    def grads(lhs, rhs, out_ref, lane):
        def half(k):
            def work():
                depth = features // 2
                value = dot(lhs[:, depth * k : depth * k + depth], rhs[...], 0, 0).astype(bf16)
                for i in range(2):
                    for j in range(2):
                        start = (2 * i + j) * (depth // 4)
                        out_ref[k, i, j, :, lane : lane + rhs.shape[1]] = value[
                            start : start + depth // 4
                        ]

            return work

        return [half(0), half(1)]

    def row(index):
        return vec_ref[index : index + 1, :]

    def add_sum(index, value):
        sums_ref[index : index + 1, :] += column_sum(value)

    send_product(top_ref, pw_ref, 0, emb)

    def first_norm(tile):
        value = emb[tile, :] + row(0)
        emb[tile, :] = value
        value = norm_parts(value)[0] * row(3) + row(6)
        inp[tile, :] = value
        sent[tile, :] = value.astype(bf16)

    line(0, emb).run(first_norm)

    def project(tile):
        qkv[tile, :] = (dot(sent[tile, :], qw_ref[...], 1, 0) + qb_ref[...]).astype(bf16)

    tiles(256, project)

    gather_step(gather_view, 0, 1, me, count, gather_sems)
    for head in range(heads):
        lanes = slice(head * HEAD_DIM, (head + 1) * HEAD_DIM)
        keys = slice(hidden + head * HEAD_DIM, hidden + (head + 1) * HEAD_DIM)
        vals = slice(2 * hidden + head * HEAD_DIM, 2 * hidden + (head + 1) * HEAD_DIM)

        def attend(tile):
            scores = dot(qkv[tile, lanes], qkv[:, keys], 1, 1) * scale
            scores = jnp.where(live_ref[...] > 0.0, scores, big_neg)
            exps = jnp.exp(scores - jnp.max(scores, axis=1, keepdims=True))
            value = exps / jnp.sum(exps, axis=1, keepdims=True)
            probs[head, tile, :] = value
            attended[tile, lanes] = dot(value.astype(bf16), qkv[:, vals], 1, 0).astype(bf16)

        tiles(128, attend)
        if head + 1 < count:
            gather_step(gather_view, head + 1, 1, me, count, gather_sems)
    for step in range(heads + 1, count):
        gather_step(gather_view, step, 1, me, count, gather_sems)
    send_product(attended, ow_ref, 0, midpre)

    def second_norm(tile):
        value = midpre[tile, :] + inp[tile, :] + row(1)
        midpre[tile, :] = value
        value = norm_parts(value)[0] * row(4) + row(7)
        mid[tile, :] = value
        sent_mid[tile, :] = value.astype(bf16)

    line(1, midpre).run(second_norm)

    def feed(tile):
        value, back = gelu_parts(dot(sent_mid[tile, :], uw_ref[...], 1, 0) + ub_ref[...])
        act[tile, :] = value.astype(bf16)
        slope[tile, :] = back

    tiles(128, feed)
    send_product(act, dw_ref, 0, fin)

    def third_norm(tile):
        value = fin[tile, :] + mid[tile, :] + row(2)
        cotangent = grad_all[tile, :].astype(f32)
        enc_all[tile, :] = (norm_parts(value)[0] * row(5) + row(8)).astype(bf16)
        back, gain = norm_back(value, row(5), cotangent)
        fin[tile, :] = back
        low = back.astype(bf16)
        d_two[tile, :] = low
        add_sum(2, low.astype(f32))
        add_sum(5, gain)
        add_sum(8, cotangent)

    line(2, fin).run(third_norm)
    enc_ref[...] = enc_all[own_tile, :]

    def feed_back(tile):
        value = (dot(d_two[tile, :], dw_ref[...], 1, 1) * slope[tile, :]).astype(bf16)
        d_up[tile, :] = value
        add_sum(9, value.astype(f32))

    tiles(128, feed_back)
    send_product(d_up, uw_ref, 1, dmid)
    def second_back(tile):
        cotangent = dmid[tile, :] + fin[tile, :]
        back, gain = norm_back(midpre[tile, :], row(4), cotangent)
        dmid[tile, :] = back
        low = back.astype(bf16)
        d_branch[tile, :] = low
        add_sum(1, low.astype(f32))
        add_sum(4, gain)
        add_sum(7, cotangent)

    work = grads(d_two, act, tra_ref, features) + grads(sent_mid, d_up, tra_ref, 0)
    line(3, dmid).run(second_back, work)

    def heads_back(tile):
        d_heads[tile, :] = dot(d_branch[tile, :], ow_ref[...], 1, 1).astype(bf16)

    tiles(256, heads_back)
    for head in range(heads):
        lanes = slice(head * HEAD_DIM, (head + 1) * HEAD_DIM)
        keys = slice(hidden + head * HEAD_DIM, hidden + (head + 1) * HEAD_DIM)
        vals = slice(2 * hidden + head * HEAD_DIM, 2 * hidden + (head + 1) * HEAD_DIM)
        weights = probs[head]
        d_out = d_heads[:, lanes]
        d_proj[:, vals] = dot(weights.astype(bf16), d_out, 0, 0).astype(bf16)
        d_probs = dot(d_out, qkv[:, vals], 1, 1)
        inner = jnp.sum(d_probs * weights, axis=1, keepdims=True)
        d_scores = (weights * (d_probs - inner)).astype(bf16)
        d_proj[:, lanes] = (dot(d_scores, qkv[:, keys], 1, 0) * scale).astype(bf16)
        d_proj[:, keys] = (dot(d_scores, qkv[:, lanes], 0, 0) * scale).astype(bf16)
    send_product(d_proj, qw_ref, 1, din)
    qsum_ref[...] = column_sum(d_proj[...].astype(f32))

    def first_back(tile):
        cotangent = din[tile, :] + dmid[tile, :]
        back, gain = norm_back(emb[tile, :], row(3), cotangent)
        low = back.astype(bf16)
        d_emb[tile, :] = low
        add_sum(0, low.astype(f32))
        add_sum(3, gain)
        add_sum(6, cotangent)

    work = grads(sent, d_proj, trb_ref, top_ref.shape[1])
    work += grads(d_branch, attended, trb_ref, 1152)
    line(4, din).run(first_back, work)

    def last(tile):
        dh2_ref[tile, :] = dot(d_emb[tile, :], pw_ref[...], 1, 1)

    tiles(256, last)
    for work in grads(d_emb, top_ref, trb_ref, 0):
        work()
    gather_drain(gather_view, 1, me, count, gather_sems)


def encoder(top, weights, vec, up_b, qkv_b, out_grad, live, count, cid):
    words, filters = top.shape
    features = weights[0].shape[1]
    three = weights[1].shape[1]
    units = weights[3].shape[1]
    hidden = three // 3
    chunks, spacing = 16, 3
    shape = jax.ShapeDtypeStruct
    rows = features // 8
    wide = [(words, features)]
    scratch = [pltpu.VMEM((words, n), f32) for n in [features] * 5 + [units] + [features] * 2]
    scratch += [
        pltpu.VMEM((words, n), bf16)
        for n in (features, features, units, features, units, features, features, three, hidden)
    ]
    scratch += [pltpu.VMEM((hidden // HEAD_DIM, words, words), f32)]
    scratch += [pltpu.VMEM((words, n), bf16) for n in (hidden, three, features, features, features)]
    scratch += [pltpu.VMEM((5, words, features), bf16)] * 2
    scratch += [DMA((5, chunks))] * 4 + [DMA((count, 1))] * 4
    return pl.pallas_call(
        functools.partial(encoder_kernel, count, chunks, spacing),
        out_shape=(
            shape((words // count, features), bf16),
            shape((words, filters), f32),
            shape((2, 2, 2, rows, features + units), bf16),
            shape((2, 2, 2, rows, 1408), bf16),
            shape((16, features), f32),
            shape((1, three), f32),
        ),
        in_specs=[VMEM] * 11,
        out_specs=(VMEM,) * 6,
        scratch_shapes=scratch,
        compiler_params=params(cid, 58),
        name="encoder",
    )(top, *weights, vec, up_b, qkv_b, out_grad, live)


class LineScatter:
    def __init__(self, count, me, chunks, spacing, p_ref, out_ref, from_left, from_right, sems):
        self.count, self.me, self.chunks, self.spacing = count, me, chunks, spacing
        self.p_ref, self.out_ref = p_ref, out_ref
        self.from_left, self.from_right, self.sems = from_left, from_right, sems
        self.messages = chunks * (count - 1)
        self.steps = self.messages + spacing * (count - 1)

    def place(self, right, number):
        count, me = self.count, self.me
        lag = me if right else count - 1 - me
        chunk = number // (count - 1)
        far = count - 1 - number % (count - 1)
        block = far if right else count - 1 - far
        words, filters = self.out_ref.shape
        rows = words // self.chunks
        tile = pl.ds(pl.multiple_of(chunk * rows, rows), rows)
        lanes = pl.ds(pl.multiple_of(block * filters, filters), filters)
        buf = self.from_left if right else self.from_right
        send, recv = self.sems[:2] if right else self.sems[2:]
        to = jnp.minimum(me + 1, count - 1) if right else jnp.maximum(me - 1, 0)
        first, passed = [
            functools.partial(
                pltpu.make_async_remote_copy,
                src_ref=src.at[tile, lanes],
                dst_ref=buf.at[tile, lanes],
                send_sem=send.at[block, chunk],
                recv_sem=recv.at[block, chunk],
                device_id={"tensor": to},
                device_id_type=MESH,
            )
            for src in (self.p_ref, buf)
        ]
        return lag, far, tile, lanes, buf, first, passed

    def step(self, step):
        for right in (True, False):
            lag = self.me if right else self.count - 1 - self.me
            number = step - self.spacing * lag
            here = (number >= 0) & (number < self.messages)
            number = jnp.clip(number, 0, self.messages - 1)
            lag, far, tile, lanes, buf, first, passed = self.place(right, number)

            @pl.when(here & (lag == 0))
            def start():
                first().start()

            @pl.when(here & (lag > 0) & (far > lag))
            def middle():
                first().wait_recv()
                buf[tile, lanes] = (
                    buf[tile, lanes].astype(f32) + self.p_ref[tile, lanes].astype(f32)
                ).astype(bf16)
                passed().start()

            @pl.when(here & (lag > 0) & (far == lag))
            def last():
                first().wait_recv()
                self.out_ref[tile, :] += buf[tile, lanes].astype(f32)

    def due(self, chunk):
        return (chunk + self.spacing) * (self.count - 1)

    def finished(self, step, work, after=0):
        each = self.count - 1
        since = step - after - self.spacing * each

        @pl.when((since >= 0) & (since % each == 0) & (since < self.messages))
        def call():
            work(jnp.maximum(since, 0) // each)

    def drain(self):
        def one(number, carry):
            for right in (True, False):
                lag, far, tile, lanes, buf, first, passed = self.place(right, number)

                @pl.when(far > lag)
                def sent():
                    first().wait_send()

            return carry

        lax.fori_loop(0, self.messages, one, 0)


class DpSum:
    def __init__(self, cell, peers, x_first, sems, base):
        self.c, self.x, self.y = cell
        self.peers, self.x_first, self.base = peers, x_first, base
        self.send, self.recv = sems
        self.src = self.half = self.in0 = self.in1 = self.mid = self.in2 = None

    def remote(self, number, src, dst, bit):
        return pltpu.make_async_remote_copy(
            src_ref=src,
            dst_ref=dst,
            send_sem=self.send.at[self.base + number],
            recv_sem=self.recv.at[self.base + number],
            device_id=self.peers[bit],
            device_id_type=MESH,
        )

    def copy0(self):
        return self.remote(0, self.src.at[:, :, 1 - self.c], self.in0, 0)

    def copy1(self):
        if self.x_first:
            return self.remote(1, self.half.at[:, 1 - self.x], self.in1, 1)
        return self.remote(1, self.half.at[1 - self.y], self.in1, 2)

    def copy2(self):
        own = self.y if self.x_first else self.x
        return self.remote(2, self.mid.at[1 - own], self.in2, 2 if self.x_first else 1)

    def finish0(self):
        self.copy0().wait()

        def one(k, carry):
            i, j = k // 2, k % 2
            self.half[i, j] = (self.half[i, j].astype(f32) + self.in0[i, j].astype(f32)).astype(bf16)
            return carry

        lax.fori_loop(0, 4, one, 0)

    def finish1(self):
        self.copy1().wait()

        def one(k, carry):
            kept = self.half[k, self.x] if self.x_first else self.half[self.y, k]
            self.mid[k] = (kept.astype(f32) + self.in1[k].astype(f32)).astype(bf16)
            return carry

        lax.fori_loop(0, 2, one, 0)

    def finish2(self):
        self.copy2().wait()
        own = self.y if self.x_first else self.x
        return self.mid[own].astype(f32) + self.in2[...].astype(f32)


def dp_cell(place):
    cell = [place % 2, (place // 2) % 2, place // 4]
    return cell, [{"dp": place + (1 - 2 * cell[bit]) * 2**bit} for bit in range(3)]


def greet_all(peers):
    barrier = pltpu.get_barrier_semaphore()
    for peer in peers:
        pl.semaphore_signal(barrier, inc=1, device_id=peer, device_id_type=MESH)
    pl.semaphore_wait(barrier, len(peers))


def mix_back(d_hidden, trans, gate_pre, previous):
    gate = jax.nn.sigmoid(gate_pre)
    sig = jax.nn.sigmoid(trans)
    act = trans * sig
    d_trans = (d_hidden * gate * (sig * (1.0 + trans * (1.0 - sig)))).astype(bf16)
    d_gate = (d_hidden * (act - previous) * gate * (1.0 - gate)).astype(bf16)
    return d_trans, d_gate, (1.0 - gate) * d_hidden


def weight_grad_piece(piece, whole_ref, d_refs, outs):
    rows = outs[0].shape[-2]
    lanes = pl.ds(pl.multiple_of(piece * rows, rows), rows)
    index = (piece // 4, (piece // 2) % 2, piece % 2)
    for d_ref, out in zip(d_refs, outs):
        out[index] = dot(whole_ref[:, lanes], d_ref[...], 0, 0).astype(bf16)


def highway_back_kernel(count, chunks, reduce, *refs):
    d_h2_ref, t1_ref, g1_ref, h1_ref = refs[:4]
    late_hbm = refs[4:9]
    refs = refs[9:]
    if reduce:
        tr_hbm = refs[:2]
        refs = refs[2:]
    part0_ref, prev0_ref, dt0_ref, dg0_ref, sums_ref = refs[:5]
    refs = refs[5:]
    if reduce:
        mids = refs[:4]
        hw_refs, tr_half = refs[4:6], refs[6:8]
        in0s, in1s = refs[8:12], refs[12:16]
        dp_sems = refs[16:18]
        refs = refs[18:]
    else:
        hw_refs = refs[:2]
        refs = refs[2:]
    part1_ref, from_left, from_right, d_h1_ref, dt1_ref, dg1_ref = refs[:6]
    t0_ref, g0_ref, h0_ref, whole1_ref, w_ref, late_sem = refs[6:12]
    sems = refs[12:]
    me = lax.axis_index("tensor")
    words, filters = d_h2_ref.shape
    w_hbm = late_hbm[4]
    loads = [
        pltpu.make_async_copy(w_hbm.at[1], w_ref.at[1], late_sem.at[0]),
        pltpu.make_async_copy(late_hbm[3], whole1_ref, late_sem.at[1]),
        pltpu.make_async_copy(w_hbm.at[0], w_ref.at[0], late_sem.at[2]),
        pltpu.make_async_copy(late_hbm[0], t0_ref, late_sem.at[3]),
        pltpu.make_async_copy(late_hbm[1], g0_ref, late_sem.at[4]),
        pltpu.make_async_copy(late_hbm[2], h0_ref, late_sem.at[5]),
    ]
    for copy in loads:
        copy.start()
    items = []
    if reduce:
        cell, peers = dp_cell(lax.axis_index("dp"))
        keep = [
            pltpu.make_async_copy(tr_hbm[k].at[:, :, cell[0]], tr_half[k], late_sem.at[6 + k])
            for k in range(2)
        ]
        for copy in keep:
            copy.start()
    ring = [{"tensor": lax.rem(me + k, count)} for k in range(1, count)]
    sums_ref[...] = jnp.zeros_like(sums_ref)

    def mix(layer, d_h_ref, t_ref, g_ref, h_ref, dt_ref, dg_ref, prev_ref, tile):
        dt, dg, prev = mix_back(d_h_ref[tile, :], t_ref[tile, :], g_ref[tile, :], h_ref[tile, :])
        dt_ref[tile, :] = dt
        dg_ref[tile, :] = dg
        prev_ref[tile, :] = prev
        for j, d in enumerate((dt, dg)):
            sums_ref[2 * layer + j : 2 * layer + j + 1, :] += jnp.sum(
                d.astype(f32), axis=0, keepdims=True
            )

    def products(layer, dt_ref, dg_ref, p_ref, part):
        tile = slice(part * (words // 2), (part + 1) * (words // 2))

        def one(block, carry):
            lanes = pl.ds(pl.multiple_of(block * filters, filters), filters)
            p_ref[tile, lanes] = (
                dot(dt_ref[tile, :], w_ref[layer, 0, lanes, :], 1, 1)
                + dot(dg_ref[tile, :], w_ref[layer, 1, lanes, :], 1, 1)
            ).astype(bf16)
            return carry

        lax.fori_loop(0, count, one, 0)

    rows = words // chunks

    def tile_of(index):
        return pl.ds(pl.multiple_of(index * rows, rows), rows)

    def first(index, carry):
        mix(1, d_h2_ref, t1_ref, g1_ref, h1_ref, dt1_ref, dg1_ref, d_h1_ref, tile_of(index))
        return carry

    def own_part(part):
        tile = slice(part * (words // 2), (part + 1) * (words // 2))
        d_h1_ref[tile, :] += part1_ref[
            tile, pl.ds(pl.multiple_of(me * filters, filters), filters)
        ].astype(f32)

    lax.fori_loop(0, chunks, first, 0)
    loads[0].wait()
    products(1, dt1_ref, dg1_ref, part1_ref, 0)
    own_part(0)
    if reduce:
        greet_all(peers + ring)
        for k in range(4):
            item = DpSum(cell, peers, k % 2 == 0, dp_sems, 3 * k)
            if k < 2:
                item.src, item.half = hw_refs[k], hw_refs[k].at[:, :, cell[0]]
            else:
                item.src, item.half = tr_hbm[k - 2], tr_half[k - 2]
            item.in0, item.in1, item.mid = in0s[k], in1s[k], mids[k]
            items.append(item)
        for item in items[2:]:
            item.copy0().start()
    else:
        greet_all(ring)
    scatter = LineScatter(
        count, me, chunks, 3, part1_ref, d_h1_ref, from_left, from_right, sems
    )

    def step_fn(step, carry):
        scatter.step(step)

        @pl.when(step == 0)
        def rest():
            products(1, dt1_ref, dg1_ref, part1_ref, 1)
            own_part(1)
            loads[1].wait()

        @pl.when((step > 0) & (step <= 8))
        def grads():
            weight_grad_piece(step - 1, whole1_ref, (dt1_ref, dg1_ref), hw_refs)

        @pl.when(step == 9)
        def late():
            for copy in loads[2:]:
                copy.wait()

        if reduce:

            @pl.when(step == 9)
            def start0():
                for item in items[:2]:
                    item.copy0().start()
                for copy in keep:
                    copy.wait()
                for item in items[2:]:
                    item.finish0()
                    item.copy1().start()

            @pl.when(step == 15)
            def start1():
                for item in items[:2]:
                    item.finish0()
                    item.copy1().start()

        scatter.finished(
            step,
            lambda chunk: mix(
                0, d_h1_ref, t0_ref, g0_ref, h0_ref, dt0_ref, dg0_ref, prev0_ref, tile_of(chunk)
            ),
        )

        @pl.when(step == scatter.due(chunks // 2 - 1) + 1)
        def early():
            products(0, dt0_ref, dg0_ref, part0_ref, 0)

        return carry

    lax.fori_loop(0, scatter.steps, step_fn, 0)
    products(0, dt0_ref, dg0_ref, part0_ref, 1)
    for item in items:
        item.finish1()
    scatter.drain()


def highway_back(d_h2, t1, g1, h1, t0, g0, h0, whole1, weight, tra, trb, count, cid):
    words, filters = d_h2.shape
    chunks = 8
    reduce = tra is not None
    rows = whole1.shape[1] // 8
    shape = jax.ShapeDtypeStruct
    out_shape = [
        shape(whole1.shape, bf16),
        shape((words, filters), f32),
        shape((words, filters), bf16),
        shape((words, filters), bf16),
        shape((4, filters), f32),
    ]
    operands = [d_h2, t1, g1, h1, t0, g0, h0, whole1, weight]
    in_specs = [VMEM] * 4 + [ANY] * 5
    hw_shape = (2, 2, 2, rows, filters)
    scratch = []
    if reduce:
        operands += [tra, trb]
        in_specs += [ANY] * 2
        tails = [hw_shape[-2:], hw_shape[-2:], tra.shape[-2:], trb.shape[-2:]]
        out_shape += [shape((2,) + tail, bf16) for tail in tails]
        scratch += [pltpu.VMEM(hw_shape, bf16)] * 2
        scratch += [pltpu.VMEM((2, 2) + tail, bf16) for tail in tails[2:]]
        scratch += [pltpu.VMEM((2, 2) + tail, bf16) for tail in tails]
        scratch += [pltpu.VMEM((2,) + tail, bf16) for tail in tails]
        scratch += [DMA((12,))] * 2
    else:
        out_shape += [shape(hw_shape, bf16)] * 2
    scratch += [pltpu.VMEM(whole1.shape, bf16)] * 3
    scratch += [pltpu.VMEM((words, filters), f32)] + [pltpu.VMEM((words, filters), bf16)] * 2
    scratch += [pltpu.VMEM((words, filters), f32)] * 3
    scratch += [pltpu.VMEM(whole1.shape, bf16), pltpu.VMEM(weight.shape, bf16), DMA((8,))]
    scratch += [DMA((count, chunks))] * 4
    return pl.pallas_call(
        functools.partial(highway_back_kernel, count, chunks, reduce),
        out_shape=tuple(out_shape),
        in_specs=in_specs,
        out_specs=tuple([VMEM] * len(out_shape)),
        scratch_shapes=scratch,
        compiler_params=params(cid, 58),
        name="highway_back",
    )(*operands)


def spread_small(send_recv, in_ref, got, mid, out_ref):
    dp_count, count = out_ref.shape[:2]
    s1, r1, s2, r2, s3, r3 = send_recv
    me = lax.axis_index("tensor")
    place = lax.axis_index("dp")

    def remote(src, dst, send, recv, hop, axis, peer):
        return pltpu.make_async_remote_copy(
            src_ref=src, dst_ref=dst, send_sem=send.at[hop - 1], recv_sem=recv.at[hop - 1],
            device_id={axis: peer}, device_id_type=MESH,
        )

    def scatter(hop):
        peer = lax.rem(place + hop, dp_count)
        return remote(in_ref.at[peer], got.at[hop - 1], s1, r1, hop, "dp", peer)

    def across(hop):
        return remote(mid.at[me], mid.at[me], s2, r2, hop, "tensor", lax.rem(me + hop, count))

    def around(hop):
        return remote(mid, out_ref.at[place], s3, r3, hop, "dp", lax.rem(place + hop, dp_count))

    def loop(fn, stop):
        def one(hop, carry):
            fn(hop)
            return carry

        lax.fori_loop(1, stop, one, 0)

    loop(lambda hop: scatter(hop).start(), dp_count)
    loop(lambda hop: scatter(hop).wait(), dp_count)
    total = lax.fori_loop(0, dp_count - 1, lambda k, acc: acc + got[k], in_ref[place])
    mid[me] = total.astype(bf16)
    loop(lambda hop: across(hop).start(), count)
    loop(lambda hop: across(hop).wait(), count)
    loop(lambda hop: around(hop).start(), dp_count)
    out_ref[place] = mid[...]
    loop(lambda hop: around(hop).wait(), dp_count)


def conv_backward_kernel(count, chars, cuts, *refs):
    (ids_ref, x_hbm, p_hbm, wb_ref, off_ref, log_ref, prev_ref, part_ref, whole_hbm, dt_ref,
     dg_ref) = refs[:11]
    refs = refs[11:]
    if cuts:
        mids_in = refs[:4]
        mask_ref, early_ref = refs[4:6]
        hw_out, up_out, down_out, proj_out, qkv_out, o_out = refs[6:12]
        convw_out, convb_out, table_out, early_out = refs[12:16]
        dw_ref, table_ref, hw_a, hw_b = refs[16:20]
        in0s, in1s, mids, in2s = refs[20:22], refs[22:24], refs[24:26], refs[26:32]
        dp_sems = refs[32:34]
        small_ref, small_got, small_mid, small_all = refs[34:38]
        small_sems = refs[38:44]
        refs = refs[44:]
    else:
        dw_ref, table_ref, hw_a, hw_b = refs[:4]
        refs = refs[4:]
    pad_ref, grad_ref, from_left, from_right, x_buf, p_buf, whole_ref, load_sem, whole_sem = refs[:9]
    line_sems = refs[9:]
    me = lax.axis_index("tensor")
    words, filters = log_ref.shape
    tiles = words // WORD_TILE
    padded = ids_ref.shape[1] // WORD_TILE

    def load(index):
        slot = index % 2
        return [
            pltpu.make_async_copy(hbm.at[index], buf.at[slot], load_sem.at[k, slot])
            for k, (buf, hbm) in enumerate(((x_buf, x_hbm), (p_buf, p_hbm)))
        ]

    whole_copy = pltpu.make_async_copy(whole_hbm, whole_ref, whole_sem)
    whole_copy.start()
    for index in range(2):
        for copy in load(index):
            copy.start()
    ring = [{"tensor": lax.rem(me + k, count)} for k in range(1, count)]
    items = []
    if cuts:
        place = lax.axis_index("dp")
        dp_count = small_all.shape[0]
        cell, dp_peers = dp_cell(place)
        greet_all([{"dp": lax.rem(place + k, dp_count)} for k in range(1, dp_count)] + ring)
        for k in range(6):
            item = DpSum(cell, dp_peers, k % 2 == 0, dp_sems, 3 * k)
            item.in2 = in2s[k]
            if k < 2:
                item.src = (hw_a, hw_b)[k]
                item.half = item.src.at[:, :, cell[0]]
                item.in0, item.in1, item.mid = in0s[k], in1s[k], mids[k]
            else:
                item.mid = mids_in[k - 2]
            items.append(item)
        for item in items[2:]:
            item.copy2().start()
    else:
        greet_all(ring)

    dw_ref[...] = jnp.zeros_like(dw_ref)
    table_ref[...] = jnp.zeros_like(table_ref)
    pad_ref[...] = jnp.zeros_like(pad_ref)
    grad_ref[...] = prev_ref[...] + part_ref[
        :, pl.ds(pl.multiple_of(me * filters, filters), filters)
    ].astype(f32)
    chunks = line_sems[0].shape[1]
    per = words // chunks // WORD_TILE
    scatter = LineScatter(
        count, me, chunks, 3, part_ref, grad_ref, from_left, from_right, line_sems
    )
    group = lax.broadcasted_iota(jnp.int32, (1, WORD_TILE, LANES), 2) // 16
    vocab = lax.broadcasted_iota(jnp.int32, (table_ref.shape[0], padded * WORD_TILE), 0)

    def tile_step(index):
        slot = index % 2
        for copy in load(index):
            copy.wait()
        tile = pl.ds(pl.multiple_of(index * WORD_TILE, WORD_TILE), WORD_TILE)
        pooled = log_ref[tile, :] - off_ref[...]
        sig = jax.nn.sigmoid(pooled)
        grad = grad_ref[tile, :] * (sig * (1.0 + pooled * (1.0 - sig)))
        d_conv = (grad[None] * p_buf[slot].astype(f32)).astype(bf16)
        d_conv = d_conv.reshape(chars * WORD_TILE, filters)
        dw_ref[...] += dot(x_buf[slot], d_conv, 0, 0)
        d_win = dot(d_conv, wb_ref[...], 1, 1).astype(bf16)
        pad_ref[6 : 6 + chars] = d_win.reshape(chars, WORD_TILE, LANES)
        d_emb = pad_ref[6 : 6 + padded]
        for tap in range(1, 7):
            d_emb = jnp.where(group == tap, pad_ref[6 - tap : 6 - tap + padded], d_emb)
        one_hot = jnp.where(vocab == ids_ref[pl.ds(index, 1), :], 1.0, 0.0).astype(bf16)
        table_ref[...] += dot(one_hot, d_emb.reshape(padded * WORD_TILE, LANES), 1, 0)

        @pl.when(index + 2 < tiles)
        def more():
            for copy in load(index + 2):
                copy.start()

    def step_fn(step, carry):
        scatter.step(step)

        @pl.when(step == 0)
        def whole():
            whole_copy.wait()

        @pl.when(step < 8)
        def grads():
            weight_grad_piece(step, whole_ref, (dt_ref, dg_ref), (hw_a, hw_b))

        if cuts:

            @pl.when(step == 8)
            def start0():
                for item in items[:2]:
                    item.copy0().start()

            @pl.when(step == cuts[0])
            def start1():
                for item in items[:2]:
                    item.finish0()
                    item.copy1().start()

            @pl.when(step == cuts[1])
            def start2():
                for item in items[:2]:
                    item.finish1()
                    item.copy2().start()

        for k in range(per):
            scatter.finished(step, lambda chunk: tile_step(chunk * per + k), k)
        return carry

    lax.fori_loop(0, scatter.due(chunks - 1) + per, step_fn, 0)
    if cuts:
        for i in range(8):
            small_ref[i, :, 0:filters] = dw_ref[16 * i : 16 * i + 16, :]
            small_ref[i, :, filters : filters + 3 * LANES] = jnp.zeros((16, 3 * LANES), f32)
            for k in range(3):
                lane = filters + k * LANES
                small_ref[i, 0:11, lane : lane + LANES] = table_ref[
                    33 * i + 11 * k : 33 * i + 11 * k + 11, :
                ]
            small_ref[i, :, filters + 3 * LANES :] = early_ref[i]
        spread_small(small_sems, small_ref, small_got, small_mid, small_all)
        for t in range(count):
            lanes = slice(t * filters, (t + 1) * filters)
            for i in range(7):
                band = slice(16 * i, 16 * i + 16)
                convw_out[band, lanes] = small_all[i, t, :, 0:filters].astype(f32) * mask_ref[band, :]
            convb_out[:, lanes] = small_all[7, t, :, 0:filters].astype(f32)[0:1]
        for i in range(8):
            total = small_all[i, 0, :, filters : filters + 3 * LANES].astype(f32)
            for t in range(1, count):
                total += small_all[i, t, :, filters : filters + 3 * LANES].astype(f32)
            for k in range(3):
                table_out[33 * i + 11 * k : 33 * i + 11 * k + 11, :] = total[
                    0:11, k * LANES : (k + 1) * LANES
                ]
            for t in range(count):
                early_out[t, i] = small_all[i, t, :, filters + 3 * LANES :].astype(f32)
        for k in range(4):
            hw_out[k // 2, k % 2] = items[k].finish2()
        total = items[4].finish2()
        units = up_out.shape[1]
        up_out[...] = total[:, :units]
        down_out[...] = total[:, units:].T
        total = items[5].finish2()
        three = qkv_out.shape[1]
        proj_out[...] = total[:, :filters].T
        qkv_out[...] = total[:, filters : filters + three]
        o_out[...] = total[:, 1152 : 1152 + three // 3].T
    scatter.drain()


def conv_backward(ids, x, p, wb, off, logs, prev, part, whole, dt, dg, rest, count, cid):
    words, filters = logs.shape
    chars = p.shape[1]
    chunks = 8
    shape = jax.ShapeDtypeStruct
    hw_shape = (2, 2, 2, whole.shape[1] // 8, filters)
    operands = [ids, x, p, wb, off, logs, prev, part, whole, dt, dg]
    in_specs = [VMEM, ANY, ANY] + [VMEM] * 5 + [ANY, VMEM, VMEM]
    sums = [(LANES, filters), (264, LANES)]
    scratch = []
    cuts = None
    if rest:
        mids, mask, early, units, three = rest
        cuts = (14, 26)
        operands += list(mids) + [mask, early]
        in_specs += [VMEM] * 6
        own = [hw_shape[-2:]] * 2
        tails = own + [mid.shape[-2:] for mid in mids]
        rows = mids[2].shape[-2]
        out_shape = [
            shape((2, 2) + own[0], f32),
            shape((rows, units), f32),
            shape((mids[2].shape[-1] - units, rows), f32),
            shape((filters, rows), f32),
            shape((rows, three), f32),
            shape((three // 3, rows), f32),
            shape((112, count * filters), f32),
            shape((1, count * filters), f32),
            shape(sums[1], f32),
            shape((count,) + early.shape, f32),
        ]
        small = (16, filters + 4 * LANES)
        scratch += [pltpu.VMEM(tail, f32) for tail in sums]
        scratch += [pltpu.VMEM(hw_shape, bf16)] * 2
        scratch += [pltpu.VMEM((2, 2) + tail, bf16) for tail in own]
        scratch += [pltpu.VMEM((2,) + tail, bf16) for tail in own + own]
        scratch += [pltpu.VMEM(tail, bf16) for tail in tails]
        scratch += [DMA((18,))] * 2
        scratch += [
            pltpu.VMEM((8,) + small, f32),
            pltpu.VMEM((7,) + small, f32),
            pltpu.VMEM((count,) + small, bf16),
            pltpu.VMEM((8, count) + small, bf16),
        ]
        scratch += [DMA((7,))] * 2 + [DMA((count - 1,))] * 2 + [DMA((7,))] * 2
    else:
        out_shape = [shape(tail, f32) for tail in sums] + [shape(hw_shape, bf16)] * 2
    scratch += [
        pltpu.VMEM((68, WORD_TILE, LANES), bf16),
        pltpu.VMEM((words, filters), f32),
        pltpu.VMEM(part.shape, bf16),
        pltpu.VMEM(part.shape, bf16),
        pltpu.VMEM((2,) + x.shape[1:], bf16),
        pltpu.VMEM((2,) + p.shape[1:], bf16),
        pltpu.VMEM(whole.shape, bf16),
        DMA((2, 2)),
        DMA,
    ]
    scratch += [DMA((count, chunks))] * 4
    return pl.pallas_call(
        functools.partial(conv_backward_kernel, count, chars, cuts),
        out_shape=tuple(out_shape),
        in_specs=in_specs,
        out_specs=tuple([VMEM] * len(out_shape)),
        scratch_shapes=scratch,
        compiler_params=params(cid, 58),
        name="conv_backward",
    )(*operands)


def small_kernel(dp_count, count, in_ref, out_ref, got, mid, *sems):
    me = lax.axis_index("tensor")
    place = lax.axis_index("dp")
    barrier = pltpu.get_barrier_semaphore()

    def greet(hop, carry):
        peer = lax.rem(place + hop, dp_count)
        pl.semaphore_signal(barrier, inc=1, device_id={"dp": peer}, device_id_type=MESH)
        return carry

    lax.fori_loop(1, dp_count, greet, 0)
    for hop in range(1, count):
        pl.semaphore_signal(
            barrier, inc=1, device_id={"tensor": lax.rem(me + hop, count)}, device_id_type=MESH
        )
    pl.semaphore_wait(barrier, dp_count + count - 2)
    spread_small(sems, in_ref, got, mid, out_ref)


def sum_small(packed, dp_count, count, cid):
    shape = packed.shape[1:]
    return pl.pallas_call(
        functools.partial(small_kernel, dp_count, count),
        out_shape=jax.ShapeDtypeStruct((dp_count, count) + shape, bf16),
        in_specs=[VMEM],
        out_specs=VMEM,
        scratch_shapes=[
            pltpu.VMEM((dp_count - 1,) + shape, f32),
            pltpu.VMEM((count,) + shape, bf16),
            DMA((dp_count - 1,)),
            DMA((dp_count - 1,)),
            DMA((count - 1,)),
            DMA((count - 1,)),
            DMA((dp_count - 1,)),
            DMA((dp_count - 1,)),
        ],
        compiler_params=params(cid, 32),
        name="sum_small",
    )(packed)


def mm(spec, *operands):
    return jnp.einsum(spec, *operands, preferred_element_type=f32)


def body(
    char_ids,
    seq_lengths,
    char_table,
    conv_weight,
    conv_bias,
    highway_weight,
    highway_bias,
    proj_weight,
    proj_bias,
    norm_gain,
    norm_shift,
    qkv_weight,
    qv_bias,
    output_projection_weight,
    out_bias,
    up_weight,
    up_bias,
    down_weight,
    down_bias,
    out_grad,
):
    words, nseq, chars = char_ids.shape
    assert nseq == 1
    count = lax.axis_size("tensor")
    dp_count = lax.axis_size("dp")
    rank = lax.axis_index("tensor")
    vocab, char_dim = char_table.shape
    taps_dim, filters = conv_weight.shape
    features = proj_weight.shape[1]
    heads = qkv_weight.shape[2] // HEAD_DIM

    padded = chars + 6
    ids = jnp.pad(char_ids[:, 0], ((0, 0), (0, 6)), constant_values=-1)
    ids_tiles = jnp.swapaxes(ids.reshape(words // WORD_TILE, WORD_TILE, padded), 1, 2)
    ids_tiles = ids_tiles.reshape(words // WORD_TILE, padded * WORD_TILE)
    table_wide = jnp.pad(jnp.tile(char_table, (1, 7)), ((0, 0), (0, LANES - taps_dim)))
    one_hot = (ids.T[:, :, None] == lax.broadcasted_iota(jnp.int32, (1, 1, vocab), 2)).astype(bf16)
    pattern = np.zeros((padded, LANES), np.float32)
    pattern[:, taps_dim] = 1.0
    for k in range(1, 7):
        pattern[chars - k, taps_dim + k] = 1.0
    y = (mm("qwv,vl->qwl", one_hot, table_wide) + pattern[:, None, :]).astype(bf16)

    widths = filter_widths(filters)
    off = jnp.asarray(np.log((chars - widths + 1).astype(np.float64)).astype(np.float32))[None]
    tap_of = np.arange(taps_dim)[:, None] // char_dim
    w_taps = jnp.where(tap_of < widths[None], conv_weight, 0).astype(bf16)
    ends = np.where(widths[None] > np.arange(1, 7)[:, None], big_neg, 0.0).astype(np.float32)
    tail = LANES - taps_dim - 7
    w_all = jnp.concatenate(
        [w_taps, conv_bias[None], jnp.asarray(ends, bf16), jnp.zeros((tail, filters), bf16)], axis=0
    )
    w_back = jnp.pad(w_taps, ((0, LANES - taps_dim), (0, 0)))

    logs, whole, x_tiles, p_tiles = conv_forward(y, w_all, off, count, chars, 1)
    hidden = jax.nn.silu(logs - off)
    kept_layers = []
    for layer in range(highway_weight.shape[0]):
        if layer > 0:
            whole = gather_features(hidden.astype(bf16), count, 1 + layer)
        trans, gate_pre = [
            mm("rk,kf->rf", whole, highway_weight[layer, j]) + highway_bias[layer, j].astype(f32)
            for j in range(2)
        ]
        kept_layers.append((hidden, whole, trans, gate_pre))
        gate = jax.nn.sigmoid(gate_pre)
        hidden = gate * jax.nn.silu(trans) + (1.0 - gate) * hidden
    vec = jnp.concatenate(
        [jnp.stack([proj_bias, out_bias, down_bias]), norm_gain, norm_shift], axis=0
    ).astype(f32)
    qkv_b = jnp.stack([qv_bias[0], jnp.zeros_like(qv_bias[0]), qv_bias[1]]).reshape(1, -1)
    place = lax.broadcasted_iota(jnp.int32, (1, words), 1)
    live = jnp.where(place < seq_lengths[0], 1.0, 0.0).astype(f32)
    encoded, d_hidden, tr_a, tr_b, row_sums, proj_sums = encoder(
        hidden.astype(bf16),
        (
            proj_weight,
            qkv_weight.reshape(features, -1),
            output_projection_weight,
            up_weight,
            down_weight,
        ),
        jnp.pad(vec, ((0, 7), (0, 0))),
        up_bias.astype(f32)[None],
        qkv_b.astype(f32),
        out_grad[:, 0],
        live,
        count,
        4,
    )
    encoded = encoded[:, None]

    (h0, whole0, t0, g0), (h1, whole1, t1, g1) = kept_layers
    back_args = (d_hidden, t1, g1, h1, t0, g0, h0, whole1, highway_weight)
    conv_args = (ids_tiles, x_tiles, p_tiles, w_back, off, logs)
    taps_mask = tap_of < widths[None]
    three = 3 * heads * HEAD_DIM
    if dp_count == 8 and (features // dp_count) % 16 == 0:
        part0, prev0, dt0, dg0, hw_bias_part, *mids = highway_back(
            *back_args, tr_a, tr_b, count, 9
        )
        early = jnp.concatenate(
            [part.reshape(-1) for part in (hw_bias_part, proj_sums, row_sums[:10])]
        )
        early = jnp.pad(early, (0, 8 * 16 * LANES - early.size)).reshape(8, 16, LANES)
        (hw_w_grad, up_w_grad, down_w_grad, proj_w_grad, qkv_w_grad, out_w_grad, conv_w_grad,
         conv_b_grad, table_all, early) = conv_backward(
            *conv_args, prev0, part0, whole0, dt0, dg0,
            (mids, jnp.asarray(taps_mask, f32), early, up_weight.shape[1], three), count, 10,
        )
        conv_b_grad = conv_b_grad[0]
        early = early.reshape(count, -1)
    else:
        part0, prev0, dt0, dg0, hw_bias_part, *hw1 = highway_back(*back_args, None, None, count, 9)
        d_w_all, table_all, *hw0 = conv_backward(
            *conv_args, prev0, part0, whole0, dt0, dg0, (), count, 10
        )
        hw_sum = jnp.stack([part.reshape(-1, filters) for part in hw0 + hw1])
        hw_sum = lax.psum_scatter(hw_sum, "dp", scatter_dimension=1, tiled=True).astype(f32)
        tr_a, tr_b = [
            lax.psum_scatter(
                part.reshape(features, -1), "dp", scatter_dimension=0, tiled=True
            ).astype(f32)
            for part in (tr_a, tr_b)
        ]
        hw_w_grad = hw_sum.reshape(2, 2, -1, filters)
        units = up_weight.shape[1]
        up_w_grad = tr_a[:, :units]
        down_w_grad = tr_a[:, units:].T
        proj_w_grad = tr_b[:, :filters].T
        qkv_w_grad = tr_b[:, filters : filters + three]
        out_w_grad = tr_b[:, 1152 : 1152 + heads * HEAD_DIM].T
        pieces = [d_w_all[: taps_dim + 1], table_all, hw_bias_part, proj_sums, row_sums[:10]]
        flat = jnp.concatenate([part.reshape(-1) for part in pieces])
        width = -(-flat.size // (dp_count * 16 * LANES)) * LANES
        flat = jnp.pad(flat, (0, dp_count * 16 * width - flat.size))
        summed = sum_small(flat.reshape(dp_count, 16, width), dp_count, count, 11)
        summed = jnp.swapaxes(summed, 0, 1).reshape(count, -1).astype(f32)
        conv_size, table_size = pieces[0].size, table_all.size
        conv_all = summed[:, :conv_size].reshape(count, taps_dim + 1, filters)
        conv_all = jnp.swapaxes(conv_all, 0, 1)
        conv_w_grad = jnp.where(taps_mask[:, None], conv_all[:taps_dim], 0.0)
        conv_w_grad = conv_w_grad.reshape(taps_dim, -1)
        conv_b_grad = conv_all[taps_dim].reshape(-1)
        table_all = jnp.sum(summed[:, conv_size : conv_size + table_size], axis=0)
        table_all = table_all.reshape(-1, LANES)
        early = summed[:, conv_size + table_size :]

    qkv_w_grad = qkv_w_grad.reshape(-1, 3, heads * HEAD_DIM)
    table_grad = jnp.sum(
        table_all[:vocab, :taps_dim].reshape(vocab, taps_dim // char_dim, char_dim), axis=1
    )
    hw_b_grad = jnp.swapaxes(early[:, : 4 * filters].reshape(count, 4, filters), 0, 1)
    hw_b_grad = hw_b_grad.reshape(2, 2, -1)
    early = early[:, 4 * filters :]
    qv_grad = jnp.swapaxes(early[:, :three].reshape(count, 3, -1), 0, 1)[::2].reshape(2, -1)
    rows = early[:, three : three + 10 * features].reshape(count, 10, features)
    proj_b_grad, out_b_grad, down_b_grad = rows[0, 0], rows[0, 1], rows[0, 2]
    gain_grad = rows[0, 3:6]
    shift_grad = rows[0, 6:9]
    up_b_grad = rows[:, 9].reshape(-1)
    return (
        encoded,
        table_grad,
        conv_w_grad,
        conv_b_grad,
        hw_w_grad,
        hw_b_grad,
        proj_w_grad,
        proj_b_grad,
        gain_grad,
        shift_grad,
        qkv_w_grad,
        qv_grad,
        out_w_grad,
        out_b_grad,
        up_w_grad,
        up_b_grad,
        down_w_grad,
        down_b_grad,
    )


def solution(mesh):
    return jax.shard_map(
        body,
        mesh=mesh,
        in_specs=(
            P(None, "dp", None),
            P("dp"),
            P(),
            P(None, "tensor"),
            P("tensor"),
            P(None, None, None, "tensor"),
            P(None, None, "tensor"),
            P("tensor", None),
            P(),
            P(),
            P(),
            P(None, None, "tensor"),
            P(None, "tensor"),
            P("tensor", None),
            P(),
            P(None, "tensor"),
            P("tensor"),
            P("tensor", None),
            P(),
            P("tensor", "dp", None),
        ),
        out_specs=(
            P("tensor", "dp", None),
            P(),
            P(),
            P(),
            P(None, None, "dp", "tensor"),
            P(),
            P("tensor", "dp"),
            P(),
            P(),
            P(),
            P("dp", None, "tensor"),
            P(),
            P("tensor", "dp"),
            P(),
            P("dp", "tensor"),
            P(),
            P("tensor", "dp"),
            P(),
        ),
        check_vma=False,
    )
```

```python
import functools
import math

import jax
import jax.numpy as jnp
import numpy as np
from jax import lax
from jax.experimental import pallas as pl
from jax.experimental.pallas import tpu as pltpu
from jax.sharding import PartitionSpec as P

HEAD_DIM = 64
WORD_TILE = 32
LANES = 128

norm_eps = 1e-06
big_neg = -1e30
f32 = jnp.float32
bf16 = jnp.bfloat16
MESH = pl.DeviceIdType.MESH
VMEM = pl.BlockSpec(memory_space=pltpu.VMEM)
ANY = pl.BlockSpec(memory_space=pl.ANY)
DMA = pltpu.SemaphoreType.DMA
MIB = 1 << 20


def params(cid, vmem):
    return pltpu.CompilerParams(
        collective_id=cid, has_side_effects=True, vmem_limit_bytes=vmem * MIB
    )


def width_counts(block):
    unit = block // 64
    return [unit, unit, 2 * unit, 4 * unit, 8 * unit, 16 * unit, 32 * unit]


def filter_widths(block):
    return np.concatenate(
        [np.full((n,), i + 1, np.int32) for i, n in enumerate(width_counts(block))]
    )


def dot(a, b, ca, cb):
    return lax.dot_general(a, b, (((ca,), (cb,)), ((), ())), preferred_element_type=f32)


def line_barrier(me, count):
    barrier = pltpu.get_barrier_semaphore()
    for there, ok in ((me - 1, me > 0), (me + 1, me < count - 1)):

        @pl.when(ok)
        def greet():
            pl.semaphore_signal(barrier, inc=1, device_id={"tensor": there}, device_id_type=MESH)

    pl.semaphore_wait(barrier, jnp.minimum(me, 1) + jnp.minimum(count - 1 - me, 1))


def line_copy(view, me, count, right, block, chunk, sems):
    send, recv = sems[:2] if right else sems[2:]
    to = jnp.minimum(me + 1, count - 1) if right else jnp.maximum(me - 1, 0)
    ref = view(block, chunk)
    return pltpu.make_async_remote_copy(
        src_ref=ref,
        dst_ref=ref,
        send_sem=send.at[block, chunk],
        recv_sem=recv.at[block, chunk],
        device_id={"tensor": to},
        device_id_type=MESH,
    )


def gather_step(view, step, chunks, me, count, sems):
    for hop in range(count):
        chunk = step - hop
        here = (chunk >= 0) & (chunk < chunks)
        safe = jnp.clip(chunk, 0, chunks - 1)
        for right in (True, False):
            block = me - hop if right else me + hop
            there = (block >= 0) & (block < count)
            block = jnp.clip(block, 0, count - 1)
            more = me < count - 1 if right else me > 0
            copy = functools.partial(line_copy, view, me, count, right, block, safe, sems)

            @pl.when(here & there)
            def pass_on():
                if hop > 0:
                    copy().wait_recv()

                @pl.when(more)
                def send():
                    copy().start()


def gather_drain(view, chunks, me, count, sems):
    def one(chunk, carry):
        for hop in range(count):
            for right in (True, False):
                block = me - hop if right else me + hop
                there = (block >= 0) & (block < count)
                block = jnp.clip(block, 0, count - 1)
                more = me < count - 1 if right else me > 0
                copy = functools.partial(line_copy, view, me, count, right, block, chunk, sems)

                @pl.when(there & more)
                def sent():
                    copy().wait_send()

        return carry

    lax.fori_loop(0, chunks, one, 0)


FLAT_QV = 60
FLAT_HIGHWAY = 63


def flat_row(ref, start, blocks):
    return jnp.concatenate(
        [ref[start + k : start + k + 1, :] for k in range(blocks)], axis=1
    ).astype(f32)


def embed_forward_kernel(count, chars, *refs):
    (ids_ref, chars_ref, pattern_ref, w_ref, off_ref, flat_ref, hw_hbm) = refs[:7]
    log_ref, whole0_ref, whole1_ref, top_ref, x_hbm, p_hbm = refs[7:13]
    kept = refs[13:19]
    y_buf, x_buf, p_buf, hw_ref, table_ref, hb_ref, keep_sem, late_sem = refs[19:27]
    bufs = refs[27:33]
    sems0, sems1 = refs[33:37], refs[37:41]
    t_refs, g_refs, h_refs = (bufs[0], bufs[3]), (bufs[1], bufs[4]), (bufs[2], bufs[5])
    wholes = (whole0_ref, whole1_ref)
    me = lax.axis_index("tensor")
    words, filters = log_ref.shape
    tiles = words // WORD_TILE
    half = words // 2
    padded = ids_ref.shape[1] // WORD_TILE
    own = pl.ds(pl.multiple_of(me * filters, filters), filters)
    loads = [
        pltpu.make_async_copy(hw_hbm.at[layer], hw_ref.at[layer], late_sem.at[layer])
        for layer in range(2)
    ]
    for copy in loads:
        copy.start()
    stores = [
        pltpu.make_async_copy(buf, out, late_sem.at[2 + k])
        for k, (buf, out) in enumerate(zip(bufs, kept))
    ]
    y_buf[...] = jnp.zeros_like(y_buf)
    table_ref[...] = jnp.zeros_like(table_ref)
    depth, vocab_size = chars_ref.shape
    for tap in range(7):
        table_ref[depth * tap : depth * tap + depth, 0:vocab_size] = chars_ref[...]
    for k in range(4):
        start = FLAT_HIGHWAY + k * (filters // LANES)
        hb_ref[k : k + 1, :] = flat_row(flat_ref, start, filters // LANES)
    line_barrier(me, count)

    def view_of(whole):
        def view(block, chunk):
            return whole.at[
                pl.ds(pl.multiple_of(chunk * WORD_TILE, WORD_TILE), WORD_TILE),
                pl.ds(pl.multiple_of(block * filters, filters), filters),
            ]

        return view

    views = [view_of(whole) for whole in wholes]

    def keep(index):
        slot = index % 2
        return [
            pltpu.make_async_copy(buf.at[slot], hbm.at[index], keep_sem.at[k, slot])
            for k, (buf, hbm) in enumerate(((x_buf, x_hbm), (p_buf, p_hbm)))
        ]

    group = lax.broadcasted_iota(jnp.int32, (1, WORD_TILE, LANES), 2) // 16
    vocab = lax.broadcasted_iota(jnp.int32, (table_ref.shape[1], padded * WORD_TILE), 0)

    def tile_step(index):
        slot = index % 2

        @pl.when(index >= 2)
        def free():
            for copy in keep(index - 2):
                copy.wait()

        one_hot = jnp.where(vocab == ids_ref[pl.ds(index, 1), :], 1.0, 0.0).astype(bf16)
        found = dot(table_ref[...], one_hot, 1, 0).astype(bf16).T
        y_buf[0:padded] = found.reshape(padded, WORD_TILE, LANES)
        value = jnp.where(group == 7, pattern_ref[...], y_buf[0:chars])
        for tap in range(1, 7):
            value = jnp.where(group == tap, y_buf[tap : chars + tap], value)
        x2 = value.reshape(chars * WORD_TILE, LANES)
        x_buf[slot] = x2
        conv = dot(x2, w_ref[...], 1, 0).reshape(chars, WORD_TILE, filters)
        top = jnp.max(conv, axis=0)
        exps = jnp.exp(conv - top[None])
        sums = jnp.sum(exps, axis=0)
        p_buf[slot] = (exps * (1.0 / sums)[None]).astype(bf16)
        for copy in keep(index):
            copy.start()
        tile = pl.ds(pl.multiple_of(index * WORD_TILE, WORD_TILE), WORD_TILE)
        total = top + jnp.log(sums)
        log_ref[tile, :] = total
        pooled = total - off_ref[...]
        hidden = pooled * jax.nn.sigmoid(pooled)
        h_refs[0][tile, :] = hidden
        whole0_ref[tile, own] = hidden.astype(bf16)

    def layer_step(layer, part):
        rows = slice(part * half, (part + 1) * half)
        for j, out in enumerate((t_refs[layer], g_refs[layer])):
            bias = hb_ref[2 * layer + j : 2 * layer + j + 1, :]
            out[rows, :] = dot(wholes[layer][rows, :], hw_ref[layer, j], 1, 0) + bias

        def mix(index, carry):
            tile = pl.ds(pl.multiple_of(part * half + index * WORD_TILE, WORD_TILE), WORD_TILE)
            trans = t_refs[layer][tile, :]
            gate = jax.nn.sigmoid(g_refs[layer][tile, :])
            hidden = gate * (trans * jax.nn.sigmoid(trans)) + (1.0 - gate) * h_refs[layer][tile, :]
            if layer == 0:
                h_refs[1][tile, :] = hidden
                whole1_ref[tile, own] = hidden.astype(bf16)
            else:
                top_ref[tile, :] = hidden.astype(bf16)
            return carry

        lax.fori_loop(0, half // WORD_TILE, mix, 0)

    shift = tiles // 2 + count - 1
    last = shift + tiles + count - 1

    def step_fn(step, carry):
        @pl.when(step < tiles)
        def convolve():
            tile_step(step)

        @pl.when(step < tiles + count - 1)
        def first_gather():
            gather_step(views[0], step, tiles, me, count, sems0)

        @pl.when(step == shift)
        def first_half():
            loads[0].wait()
            layer_step(0, 0)

        @pl.when(step == shift + tiles // 2)
        def second_half():
            layer_step(0, 1)
            for copy in stores[:3]:
                copy.start()

        @pl.when(step >= shift)
        def second_gather():
            gather_step(views[1], step - shift, tiles, me, count, sems1)

        @pl.when(step == 2 * shift - 1)
        def third_half():
            loads[1].wait()
            layer_step(1, 0)

        return carry

    lax.fori_loop(0, last, step_fn, 0)
    layer_step(1, 1)
    for copy in stores[3:]:
        copy.start()
    for index in (tiles - 2, tiles - 1):
        for copy in keep(index):
            copy.wait()
    for sems, view in zip((sems0, sems1), views):
        gather_drain(view, tiles, me, count, sems)
    for copy in stores:
        copy.wait()


def embed_forward(ids, table, pattern, w, off, flat_vec, weight, count, chars, cid):
    filters = w.shape[1]
    tiles = ids.shape[0]
    words = tiles * WORD_TILE
    shape = jax.ShapeDtypeStruct
    flat = (words, filters)
    return pl.pallas_call(
        functools.partial(embed_forward_kernel, count, chars),
        out_shape=(
            shape(flat, f32),
            shape((words, count * filters), bf16),
            shape((words, count * filters), bf16),
            shape(flat, bf16),
            shape((tiles, chars * WORD_TILE, LANES), bf16),
            shape((tiles, chars, WORD_TILE, filters), bf16),
        )
        + (shape(flat, f32),) * 6,
        in_specs=[VMEM] * 6 + [ANY],
        out_specs=(VMEM,) * 4 + (ANY,) * 8,
        scratch_shapes=[
            pltpu.VMEM((chars + 6, WORD_TILE, LANES), bf16),
            pltpu.VMEM((2, chars * WORD_TILE, LANES), bf16),
            pltpu.VMEM((2, chars, WORD_TILE, filters), bf16),
            pltpu.VMEM(weight.shape, bf16),
            pltpu.VMEM((LANES, 264), bf16),
            pltpu.VMEM((8, filters), f32),
            DMA((2, 2)),
            DMA((8,)),
        ]
        + [pltpu.VMEM(flat, f32)] * 6
        + [DMA((count, tiles))] * 8,
        compiler_params=params(cid, 58),
        name="embed_forward",
    )(ids, table, pattern, w, off, flat_vec, weight)


class LineSum:
    def __init__(self, count, me, chunks, spacing, number, p_ref, out_ref, buffers, sems):
        self.count, self.me, self.chunks, self.spacing = count, me, chunks, spacing
        self.number, self.p_ref, self.out_ref = number, p_ref, out_ref
        self.buffers, self.sems = buffers, sems
        self.steps = chunks + spacing * (count - 1)

    def place(self, right, chunk):
        count, me, number = self.count, self.me, self.number
        lag = me if right else count - 1 - me
        rows = self.p_ref.shape[0] // self.chunks
        tile = pl.ds(pl.multiple_of(chunk * rows, rows), rows)
        buf = self.buffers[0 if right else 1]
        send, recv = self.sems[:2] if right else self.sems[2:]
        to = jnp.minimum(me + 1, count - 1) if right else jnp.maximum(me - 1, 0)
        first, passed = [
            functools.partial(
                pltpu.make_async_remote_copy,
                src_ref=src,
                dst_ref=buf.at[number, tile],
                send_sem=send.at[number, chunk],
                recv_sem=recv.at[number, chunk],
                device_id={"tensor": to},
                device_id_type=MESH,
            )
            for src in (self.p_ref.at[tile], buf.at[number, tile])
        ]
        return lag, tile, buf, first, passed

    def step(self, step):
        for right in (True, False):
            lag = self.me if right else self.count - 1 - self.me
            chunk = step - self.spacing * lag
            here = (chunk >= 0) & (chunk < self.chunks)
            chunk = jnp.clip(chunk, 0, self.chunks - 1)
            lag, tile, buf, first, passed = self.place(right, chunk)

            @pl.when(here & (lag == 0))
            def start():
                first().start()

            @pl.when(here & (lag > 0))
            def middle():
                first().wait_recv()
                got = buf[self.number, tile, :].astype(f32)

                @pl.when(lag < self.count - 1)
                def forward():
                    buf[self.number, tile, :] = (got + self.p_ref[tile, :].astype(f32)).astype(bf16)
                    passed().start()

                self.out_ref[tile, :] += got

    def drain(self):
        def one(chunk, carry):
            for right in (True, False):
                lag, tile, buf, first, passed = self.place(right, chunk)

                @pl.when(lag < self.count - 1)
                def sent():
                    first().wait_send()

            return carry

        lax.fori_loop(0, self.chunks, one, 0)

    def run(self, done, extra=()):
        rows = self.p_ref.shape[0] // self.chunks
        fill = self.spacing * (self.count - 1)

        def one(step, carry):
            self.step(step)
            for k, work in enumerate(extra):
                pl.when(step == k)(work)

            @pl.when(step >= fill)
            def finish():
                chunk = jnp.maximum(step - fill, 0)
                done(pl.ds(pl.multiple_of(chunk * rows, rows), rows))

            return carry

        lax.fori_loop(0, self.steps, one, 0)
        self.drain()


def norm_parts(values):
    centered = values - jnp.mean(values, axis=-1, keepdims=True)
    root = lax.rsqrt(jnp.mean(centered * centered, axis=-1, keepdims=True) + norm_eps)
    return centered * root, root


def norm_back(values, gain, cotangent):
    nv, root = norm_parts(values)
    scaled = cotangent * gain
    inner = jnp.mean(scaled, axis=-1, keepdims=True)
    along = jnp.mean(scaled * nv, axis=-1, keepdims=True)
    return root * (scaled - inner - nv * along), cotangent * nv


def gelu_parts(values):
    cdf = 0.5 * (1.0 + lax.erf(values * 0.7071067811865476))
    slope = cdf + values * jnp.exp(-0.5 * values * values) * 0.3989422804014327
    return values * cdf, slope


def column_sum(values):
    return jnp.sum(values, axis=0, keepdims=True)


def encoder_kernel(count, chunks, spacing, *refs):
    top_ref, pw_ref, qw_ref, ow_ref, uw_ref, dw_ref, flat_ref, og_ref, len_ref = refs[:9]
    enc_ref, dh2_ref, tra_ref, trb_ref, sums_ref, qsum_ref, vec_ref, qb_ref = refs[9:17]
    (emb, inp, midpre, mid, fin, slope, dmid, din, sent, sent_mid, act, d_two, d_up, d_branch,
     d_emb, qkv, attended, probs, d_heads, d_proj, part, grad_all, enc_all, from_left,
     from_right) = refs[17:42]
    line_sems, gather_sems = refs[42:46], refs[46:50]
    me = lax.axis_index("tensor")
    words, features = emb.shape
    heads = attended.shape[1] // HEAD_DIM
    hidden = heads * HEAD_DIM
    scale = HEAD_DIM ** (-0.5)
    own = words // count
    own_tile = pl.ds(pl.multiple_of(me * own, own), own)
    grad_all[own_tile, :] = og_ref[...]
    sums_ref[...] = jnp.zeros_like(sums_ref)
    trb_ref[...] = jnp.zeros_like(trb_ref)
    for k in range(10):
        vec_ref[k : k + 1, :] = flat_row(flat_ref, k * (features // LANES), features // LANES)
    ends = [flat_ref[FLAT_QV + k : FLAT_QV + k + 1, :].astype(f32) for k in range(3)]
    qb_ref[...] = jnp.zeros_like(qb_ref)
    qb_ref[:, 0:128] = ends[0]
    qb_ref[:, 128:192] = ends[1][:, 0:64]
    qb_ref[:, 384:448] = ends[1][:, 64:128]
    qb_ref[:, 448:576] = ends[2]
    live = lax.broadcasted_iota(jnp.int32, (1, words), 1) < len_ref[0]
    line_barrier(me, count)

    def line(number, out_ref):
        return LineSum(
            count, me, chunks, spacing, number, part, out_ref, (from_left, from_right), line_sems
        )

    def gather_view(block, chunk):
        return grad_all.at[pl.ds(pl.multiple_of(block * own, own), own)]

    def tiles(size, work):
        def one(index, carry):
            work(pl.ds(pl.multiple_of(index * size, size), size))
            return carry

        lax.fori_loop(0, words // size, one, 0)

    def send_product(lhs, rhs, side, out_ref):
        def work(tile):
            value = dot(lhs[tile, :], rhs[...], 1, side).astype(bf16)
            part[tile, :] = value
            out_ref[tile, :] = value.astype(f32)

        tiles(256, work)

    def grads(lhs, rhs, out_ref, lane):
        def half(k):
            def work():
                depth = features // 2
                value = dot(lhs[:, depth * k : depth * k + depth], rhs[...], 0, 0).astype(bf16)
                for i in range(2):
                    for j in range(2):
                        start = (2 * i + j) * (depth // 4)
                        out_ref[k, i, j, :, lane : lane + rhs.shape[1]] = value[
                            start : start + depth // 4
                        ]

            return work

        return [half(0), half(1)]

    def row(index):
        return vec_ref[index : index + 1, :]

    def add_sum(index, value):
        sums_ref[index : index + 1, :] += column_sum(value)

    send_product(top_ref, pw_ref, 0, emb)

    def first_norm(tile):
        value = emb[tile, :] + row(0)
        emb[tile, :] = value
        value = norm_parts(value)[0] * row(3) + row(6)
        inp[tile, :] = value
        sent[tile, :] = value.astype(bf16)

    line(0, emb).run(first_norm)

    def project(tile):
        qkv[tile, :] = (dot(sent[tile, :], qw_ref[...], 1, 1) + qb_ref[...]).astype(bf16)

    tiles(256, project)

    gather_step(gather_view, 0, 1, me, count, gather_sems)
    for head in range(heads):
        lanes = slice(head * HEAD_DIM, (head + 1) * HEAD_DIM)
        keys = slice(hidden + head * HEAD_DIM, hidden + (head + 1) * HEAD_DIM)
        vals = slice(2 * hidden + head * HEAD_DIM, 2 * hidden + (head + 1) * HEAD_DIM)

        def attend(tile):
            scores = dot(qkv[tile, lanes], qkv[:, keys], 1, 1) * scale
            scores = jnp.where(live, scores, big_neg)
            exps = jnp.exp(scores - jnp.max(scores, axis=1, keepdims=True))
            value = exps / jnp.sum(exps, axis=1, keepdims=True)
            probs[head, tile, :] = value
            attended[tile, lanes] = dot(value.astype(bf16), qkv[:, vals], 1, 0).astype(bf16)

        tiles(128, attend)
        if head + 1 < count:
            gather_step(gather_view, head + 1, 1, me, count, gather_sems)
    for step in range(heads + 1, count):
        gather_step(gather_view, step, 1, me, count, gather_sems)
    send_product(attended, ow_ref, 0, midpre)

    def second_norm(tile):
        value = midpre[tile, :] + inp[tile, :] + row(1)
        midpre[tile, :] = value
        value = norm_parts(value)[0] * row(4) + row(7)
        mid[tile, :] = value
        sent_mid[tile, :] = value.astype(bf16)

    line(1, midpre).run(second_norm)

    def feed(tile):
        value, back = gelu_parts(dot(sent_mid[tile, :], uw_ref[...], 1, 0) + row(9))
        act[tile, :] = value.astype(bf16)
        slope[tile, :] = back

    tiles(128, feed)
    send_product(act, dw_ref, 0, fin)

    def third_norm(tile):
        value = fin[tile, :] + mid[tile, :] + row(2)
        cotangent = grad_all[tile, :].astype(f32)
        enc_all[tile, :] = (norm_parts(value)[0] * row(5) + row(8)).astype(bf16)
        back, gain = norm_back(value, row(5), cotangent)
        fin[tile, :] = back
        low = back.astype(bf16)
        d_two[tile, :] = low
        add_sum(2, low.astype(f32))
        add_sum(5, gain)
        add_sum(8, cotangent)

    line(2, fin).run(third_norm)
    enc_ref[...] = enc_all[own_tile, :]

    def feed_back(tile):
        value = (dot(d_two[tile, :], dw_ref[...], 1, 1) * slope[tile, :]).astype(bf16)
        d_up[tile, :] = value
        add_sum(9, value.astype(f32))

    tiles(128, feed_back)
    send_product(d_up, uw_ref, 1, dmid)
    def second_back(tile):
        cotangent = dmid[tile, :] + fin[tile, :]
        back, gain = norm_back(midpre[tile, :], row(4), cotangent)
        dmid[tile, :] = back
        low = back.astype(bf16)
        d_branch[tile, :] = low
        add_sum(1, low.astype(f32))
        add_sum(4, gain)
        add_sum(7, cotangent)

    work = grads(d_two, act, tra_ref, features) + grads(sent_mid, d_up, tra_ref, 0)
    line(3, dmid).run(second_back, work)

    def heads_back(tile):
        d_heads[tile, :] = dot(d_branch[tile, :], ow_ref[...], 1, 1).astype(bf16)

    tiles(256, heads_back)
    for head in range(heads):
        lanes = slice(head * HEAD_DIM, (head + 1) * HEAD_DIM)
        keys = slice(hidden + head * HEAD_DIM, hidden + (head + 1) * HEAD_DIM)
        vals = slice(2 * hidden + head * HEAD_DIM, 2 * hidden + (head + 1) * HEAD_DIM)
        weights = probs[head]
        d_out = d_heads[:, lanes]
        d_proj[:, vals] = dot(weights.astype(bf16), d_out, 0, 0).astype(bf16)
        d_probs = dot(d_out, qkv[:, vals], 1, 1)
        inner = jnp.sum(d_probs * weights, axis=1, keepdims=True)
        d_scores = (weights * (d_probs - inner)).astype(bf16)
        d_proj[:, lanes] = (dot(d_scores, qkv[:, keys], 1, 0) * scale).astype(bf16)
        d_proj[:, keys] = (dot(d_scores, qkv[:, lanes], 0, 0) * scale).astype(bf16)
    send_product(d_proj, qw_ref, 0, din)
    qsum_ref[...] = column_sum(d_proj[...].astype(f32))

    def first_back(tile):
        cotangent = din[tile, :] + dmid[tile, :]
        back, gain = norm_back(emb[tile, :], row(3), cotangent)
        low = back.astype(bf16)
        d_emb[tile, :] = low
        add_sum(0, low.astype(f32))
        add_sum(3, gain)
        add_sum(6, cotangent)

    work = grads(sent, d_proj, trb_ref, top_ref.shape[1])
    work += grads(d_branch, attended, trb_ref, 1152)
    line(4, din).run(first_back, work)

    def last(tile):
        dh2_ref[tile, :] = dot(d_emb[tile, :], pw_ref[...], 1, 1)

    tiles(256, last)
    for work in grads(d_emb, top_ref, trb_ref, 0):
        work()
    gather_drain(gather_view, 1, me, count, gather_sems)


def encoder(top, weights, flat, out_grad, lengths, count, cid):
    words, filters = top.shape
    features = weights[0].shape[1]
    three = weights[1].shape[0]
    units = weights[3].shape[1]
    hidden = three // 3
    chunks, spacing = 16, 3
    shape = jax.ShapeDtypeStruct
    rows = features // 8
    scratch = [pltpu.VMEM((16, features), f32), pltpu.VMEM((1, three), f32)]
    scratch += [pltpu.VMEM((words, n), f32) for n in [features] * 5 + [units] + [features] * 2]
    scratch += [
        pltpu.VMEM((words, n), bf16)
        for n in (features, features, units, features, units, features, features, three, hidden)
    ]
    scratch += [pltpu.VMEM((hidden // HEAD_DIM, words, words), f32)]
    scratch += [pltpu.VMEM((words, n), bf16) for n in (hidden, three, features, features, features)]
    scratch += [pltpu.VMEM((5, words, features), bf16)] * 2
    scratch += [DMA((5, chunks))] * 4 + [DMA((count, 1))] * 4
    return pl.pallas_call(
        functools.partial(encoder_kernel, count, chunks, spacing),
        out_shape=(
            shape((words // count, features), bf16),
            shape((words, filters), f32),
            shape((2, 2, 2, rows, features + units), bf16),
            shape((2, 2, 2, rows, 1408), bf16),
            shape((16, features), f32),
            shape((1, three), f32),
        ),
        in_specs=[VMEM] * 8 + [pl.BlockSpec(memory_space=pltpu.SMEM)],
        out_specs=(VMEM,) * 6,
        scratch_shapes=scratch,
        compiler_params=params(cid, 58),
        name="encoder",
    )(top, *weights, flat, out_grad, lengths)


class LineScatter:
    def __init__(self, count, me, chunks, spacing, p_ref, out_ref, from_left, from_right, sems):
        self.count, self.me, self.chunks, self.spacing = count, me, chunks, spacing
        self.p_ref, self.out_ref = p_ref, out_ref
        self.from_left, self.from_right, self.sems = from_left, from_right, sems
        self.messages = chunks * (count - 1)
        self.steps = self.messages + spacing * (count - 1)

    def place(self, right, number):
        count, me = self.count, self.me
        lag = me if right else count - 1 - me
        chunk = number // (count - 1)
        far = count - 1 - number % (count - 1)
        block = far if right else count - 1 - far
        words, filters = self.out_ref.shape
        rows = words // self.chunks
        tile = pl.ds(pl.multiple_of(chunk * rows, rows), rows)
        lanes = pl.ds(pl.multiple_of(block * filters, filters), filters)
        buf = self.from_left if right else self.from_right
        send, recv = self.sems[:2] if right else self.sems[2:]
        to = jnp.minimum(me + 1, count - 1) if right else jnp.maximum(me - 1, 0)
        first, passed = [
            functools.partial(
                pltpu.make_async_remote_copy,
                src_ref=src.at[tile, lanes],
                dst_ref=buf.at[tile, lanes],
                send_sem=send.at[block, chunk],
                recv_sem=recv.at[block, chunk],
                device_id={"tensor": to},
                device_id_type=MESH,
            )
            for src in (self.p_ref, buf)
        ]
        return lag, far, tile, lanes, buf, first, passed

    def step(self, step):
        for right in (True, False):
            lag = self.me if right else self.count - 1 - self.me
            number = step - self.spacing * lag
            here = (number >= 0) & (number < self.messages)
            number = jnp.clip(number, 0, self.messages - 1)
            lag, far, tile, lanes, buf, first, passed = self.place(right, number)

            @pl.when(here & (lag == 0))
            def start():
                first().start()

            @pl.when(here & (lag > 0) & (far > lag))
            def middle():
                first().wait_recv()
                buf[tile, lanes] = (
                    buf[tile, lanes].astype(f32) + self.p_ref[tile, lanes].astype(f32)
                ).astype(bf16)
                passed().start()

            @pl.when(here & (lag > 0) & (far == lag))
            def last():
                first().wait_recv()
                self.out_ref[tile, :] += buf[tile, lanes].astype(f32)

    def due(self, chunk):
        return (chunk + self.spacing) * (self.count - 1)

    def finished(self, step, work, after=0):
        each = self.count - 1
        since = step - after - self.spacing * each

        @pl.when((since >= 0) & (since % each == 0) & (since < self.messages))
        def call():
            work(jnp.maximum(since, 0) // each)

    def drain(self):
        def one(number, carry):
            for right in (True, False):
                lag, far, tile, lanes, buf, first, passed = self.place(right, number)

                @pl.when(far > lag)
                def sent():
                    first().wait_send()

            return carry

        lax.fori_loop(0, self.messages, one, 0)


class DpSum:
    def __init__(self, cell, peers, x_first, sems, base):
        self.c, self.x, self.y = cell
        self.peers, self.x_first, self.base = peers, x_first, base
        self.send, self.recv = sems
        self.src = self.half = self.in0 = self.in1 = self.mid = self.in2 = None

    def remote(self, number, src, dst, bit):
        return pltpu.make_async_remote_copy(
            src_ref=src,
            dst_ref=dst,
            send_sem=self.send.at[self.base + number],
            recv_sem=self.recv.at[self.base + number],
            device_id=self.peers[bit],
            device_id_type=MESH,
        )

    def copy0(self):
        return self.remote(0, self.src.at[:, :, 1 - self.c], self.in0, 0)

    def copy1(self):
        if self.x_first:
            return self.remote(1, self.half.at[:, 1 - self.x], self.in1, 1)
        return self.remote(1, self.half.at[1 - self.y], self.in1, 2)

    def copy2(self):
        own = self.y if self.x_first else self.x
        return self.remote(2, self.mid.at[1 - own], self.in2, 2 if self.x_first else 1)

    def finish0(self):
        self.copy0().wait()

        def one(k, carry):
            i, j = k // 2, k % 2
            self.half[i, j] = (self.half[i, j].astype(f32) + self.in0[i, j].astype(f32)).astype(bf16)
            return carry

        lax.fori_loop(0, 4, one, 0)

    def finish1(self):
        self.copy1().wait()

        def one(k, carry):
            kept = self.half[k, self.x] if self.x_first else self.half[self.y, k]
            self.mid[k] = (kept.astype(f32) + self.in1[k].astype(f32)).astype(bf16)
            return carry

        lax.fori_loop(0, 2, one, 0)

    def finish2(self):
        self.copy2().wait()
        own = self.y if self.x_first else self.x
        return self.mid[own].astype(f32) + self.in2[...].astype(f32)


def dp_cell(place):
    cell = [place % 2, (place // 2) % 2, place // 4]
    return cell, [{"dp": place + (1 - 2 * cell[bit]) * 2**bit} for bit in range(3)]


def greet_all(peers):
    barrier = pltpu.get_barrier_semaphore()
    for peer in peers:
        pl.semaphore_signal(barrier, inc=1, device_id=peer, device_id_type=MESH)
    pl.semaphore_wait(barrier, len(peers))


def mix_back(d_hidden, trans, gate_pre, previous):
    gate = jax.nn.sigmoid(gate_pre)
    sig = jax.nn.sigmoid(trans)
    act = trans * sig
    d_trans = (d_hidden * gate * (sig * (1.0 + trans * (1.0 - sig)))).astype(bf16)
    d_gate = (d_hidden * (act - previous) * gate * (1.0 - gate)).astype(bf16)
    return d_trans, d_gate, (1.0 - gate) * d_hidden


def weight_grad_piece(piece, whole_ref, d_refs, outs):
    rows = outs[0].shape[-2]
    lanes = pl.ds(pl.multiple_of(piece * rows, rows), rows)
    index = (piece // 4, (piece // 2) % 2, piece % 2)
    for d_ref, out in zip(d_refs, outs):
        out[index] = dot(whole_ref[:, lanes], d_ref[...], 0, 0).astype(bf16)


def highway_back_kernel(count, chunks, reduce, *refs):
    d_h2_ref, t1_ref, g1_ref, h1_ref = refs[:4]
    late_hbm = refs[4:9]
    refs = refs[9:]
    if reduce:
        tr_hbm = refs[:2]
        refs = refs[2:]
    part0_ref, prev0_ref, dt0_ref, dg0_ref, sums_ref = refs[:5]
    refs = refs[5:]
    if reduce:
        tr_outs = refs[2:4]
        hw_refs, tr_half = refs[4:6], refs[6:8]
        in0s, in1s = refs[8:12], refs[12:16]
        mids, in2s = list(refs[:2]) + list(refs[16:18]), refs[18:20]
        dp_sems = refs[20:22]
        refs = refs[22:]
    else:
        hw_refs = refs[:2]
        refs = refs[2:]
    part1_ref, from_left, from_right, d_h1_ref, dt1_ref, dg1_ref = refs[:6]
    t0_ref, g0_ref, h0_ref, whole1_ref, w_ref, late_sem = refs[6:12]
    sems = refs[12:]
    me = lax.axis_index("tensor")
    words, filters = d_h2_ref.shape
    w_hbm = late_hbm[4]
    loads = [
        pltpu.make_async_copy(w_hbm.at[1], w_ref.at[1], late_sem.at[0]),
        pltpu.make_async_copy(late_hbm[3], whole1_ref, late_sem.at[1]),
        pltpu.make_async_copy(w_hbm.at[0], w_ref.at[0], late_sem.at[2]),
        pltpu.make_async_copy(late_hbm[0], t0_ref, late_sem.at[3]),
        pltpu.make_async_copy(late_hbm[1], g0_ref, late_sem.at[4]),
        pltpu.make_async_copy(late_hbm[2], h0_ref, late_sem.at[5]),
    ]
    for copy in loads:
        copy.start()
    items = []
    if reduce:
        cell, peers = dp_cell(lax.axis_index("dp"))
        keep = [
            pltpu.make_async_copy(tr_hbm[k].at[:, :, cell[0]], tr_half[k], late_sem.at[6 + k])
            for k in range(2)
        ]
        for copy in keep:
            copy.start()
    ring = [{"tensor": lax.rem(me + k, count)} for k in range(1, count)]
    sums_ref[...] = jnp.zeros_like(sums_ref)

    def mix(layer, d_h_ref, t_ref, g_ref, h_ref, dt_ref, dg_ref, prev_ref, tile):
        dt, dg, prev = mix_back(d_h_ref[tile, :], t_ref[tile, :], g_ref[tile, :], h_ref[tile, :])
        dt_ref[tile, :] = dt
        dg_ref[tile, :] = dg
        prev_ref[tile, :] = prev
        for j, d in enumerate((dt, dg)):
            sums_ref[2 * layer + j : 2 * layer + j + 1, :] += jnp.sum(
                d.astype(f32), axis=0, keepdims=True
            )

    def products(layer, dt_ref, dg_ref, p_ref, part):
        tile = slice(part * (words // 2), (part + 1) * (words // 2))

        def one(block, carry):
            lanes = pl.ds(pl.multiple_of(block * filters, filters), filters)
            p_ref[tile, lanes] = (
                dot(dt_ref[tile, :], w_ref[layer, 0, lanes, :], 1, 1)
                + dot(dg_ref[tile, :], w_ref[layer, 1, lanes, :], 1, 1)
            ).astype(bf16)
            return carry

        lax.fori_loop(0, count, one, 0)

    rows = words // chunks

    def tile_of(index):
        return pl.ds(pl.multiple_of(index * rows, rows), rows)

    def first(index, carry):
        mix(1, d_h2_ref, t1_ref, g1_ref, h1_ref, dt1_ref, dg1_ref, d_h1_ref, tile_of(index))
        return carry

    def own_part(part):
        tile = slice(part * (words // 2), (part + 1) * (words // 2))
        d_h1_ref[tile, :] += part1_ref[
            tile, pl.ds(pl.multiple_of(me * filters, filters), filters)
        ].astype(f32)

    lax.fori_loop(0, chunks, first, 0)
    loads[0].wait()
    products(1, dt1_ref, dg1_ref, part1_ref, 0)
    own_part(0)
    if reduce:
        greet_all(peers + ring)
        for k in range(4):
            item = DpSum(cell, peers, k % 2 == 0, dp_sems, 3 * k)
            if k < 2:
                item.src, item.half = hw_refs[k], hw_refs[k].at[:, :, cell[0]]
            else:
                item.src, item.half = tr_hbm[k - 2], tr_half[k - 2]
            item.in0, item.in1, item.mid = in0s[k], in1s[k], mids[k]
            if k >= 2:
                item.in2 = in2s[k - 2]
            items.append(item)
        for item in items[2:]:
            item.copy0().start()
    else:
        greet_all(ring)
    scatter = LineScatter(
        count, me, chunks, 3, part1_ref, d_h1_ref, from_left, from_right, sems
    )

    def step_fn(step, carry):
        scatter.step(step)

        @pl.when(step == 0)
        def rest():
            products(1, dt1_ref, dg1_ref, part1_ref, 1)
            own_part(1)
            loads[1].wait()

        @pl.when((step > 0) & (step <= 8))
        def grads():
            weight_grad_piece(step - 1, whole1_ref, (dt1_ref, dg1_ref), hw_refs)

        @pl.when(step == 9)
        def late():
            for copy in loads[2:]:
                copy.wait()

        if reduce:

            @pl.when(step == 4)
            def encoder1():
                for copy in keep:
                    copy.wait()
                for item in items[2:]:
                    item.finish0()
                    item.copy1().start()

            @pl.when(step == 9)
            def highway0():
                for item in items[:2]:
                    item.copy0().start()

            @pl.when(step == 15)
            def highway1():
                for item in items[:2]:
                    item.finish0()
                    item.copy1().start()

            @pl.when(step == 20)
            def encoder2():
                for item in items[2:]:
                    item.finish1()
                    item.copy2().start()

        scatter.finished(
            step,
            lambda chunk: mix(
                0, d_h1_ref, t0_ref, g0_ref, h0_ref, dt0_ref, dg0_ref, prev0_ref, tile_of(chunk)
            ),
        )

        @pl.when(step == scatter.due(chunks // 2 - 1) + 1)
        def early():
            products(0, dt0_ref, dg0_ref, part0_ref, 0)

        return carry

    lax.fori_loop(0, scatter.steps, step_fn, 0)
    products(0, dt0_ref, dg0_ref, part0_ref, 1)
    for item in items[:2]:
        item.finish1()
    for item, out in zip(items[2:], tr_outs if reduce else ()):
        out[...] = item.finish2().astype(bf16)
    scatter.drain()


def highway_back(d_h2, t1, g1, h1, t0, g0, h0, whole1, weight, tra, trb, count, cid):
    words, filters = d_h2.shape
    chunks = 8
    reduce = tra is not None
    rows = whole1.shape[1] // 8
    shape = jax.ShapeDtypeStruct
    out_shape = [
        shape(whole1.shape, bf16),
        shape((words, filters), f32),
        shape((words, filters), bf16),
        shape((words, filters), bf16),
        shape((4, filters), f32),
    ]
    operands = [d_h2, t1, g1, h1, t0, g0, h0, whole1, weight]
    in_specs = [VMEM] * 4 + [ANY] * 5
    hw_shape = (2, 2, 2, rows, filters)
    scratch = []
    if reduce:
        operands += [tra, trb]
        in_specs += [ANY] * 2
        tails = [hw_shape[-2:], hw_shape[-2:], tra.shape[-2:], trb.shape[-2:]]
        out_shape += [shape((2,) + tail, bf16) for tail in tails[:2]]
        out_shape += [shape(tail, bf16) for tail in tails[2:]]
        scratch += [pltpu.VMEM(hw_shape, bf16)] * 2
        scratch += [pltpu.VMEM((2, 2) + tail, bf16) for tail in tails[2:]]
        scratch += [pltpu.VMEM((2, 2) + tail, bf16) for tail in tails]
        scratch += [pltpu.VMEM((2,) + tail, bf16) for tail in tails + tails[2:]]
        scratch += [pltpu.VMEM(tail, bf16) for tail in tails[2:]]
        scratch += [DMA((12,))] * 2
    else:
        out_shape += [shape(hw_shape, bf16)] * 2
    scratch += [pltpu.VMEM(whole1.shape, bf16)] * 3
    scratch += [pltpu.VMEM((words, filters), f32)] + [pltpu.VMEM((words, filters), bf16)] * 2
    scratch += [pltpu.VMEM((words, filters), f32)] * 3
    scratch += [pltpu.VMEM(whole1.shape, bf16), pltpu.VMEM(weight.shape, bf16), DMA((8,))]
    scratch += [DMA((count, chunks))] * 4
    return pl.pallas_call(
        functools.partial(highway_back_kernel, count, chunks, reduce),
        out_shape=tuple(out_shape),
        in_specs=in_specs,
        out_specs=tuple([VMEM] * len(out_shape)),
        scratch_shapes=scratch,
        compiler_params=params(cid, 58),
        name="highway_back",
    )(*operands)


class Spread:
    def __init__(self, sems, in_ref, got, mid, out_ref):
        self.dp_count, self.count = out_ref.shape[:2]
        self.sems, self.in_ref, self.got, self.mid, self.out_ref = sems, in_ref, got, mid, out_ref
        self.me = lax.axis_index("tensor")
        self.place = lax.axis_index("dp")

    def remote(self, src, dst, phase, hop, axis, peer):
        send, recv = self.sems[2 * phase : 2 * phase + 2]
        return pltpu.make_async_remote_copy(
            src_ref=src, dst_ref=dst, send_sem=send.at[hop - 1], recv_sem=recv.at[hop - 1],
            device_id={axis: peer}, device_id_type=MESH,
        )

    def scatter(self, hop):
        peer = lax.rem(self.place + hop, self.dp_count)
        return self.remote(self.in_ref.at[peer], self.got.at[hop - 1], 0, hop, "dp", peer)

    def across(self, hop):
        peer = lax.rem(self.me + hop, self.count)
        return self.remote(self.mid.at[self.me], self.mid.at[self.me], 1, hop, "tensor", peer)

    def around(self, hop):
        peer = lax.rem(self.place + hop, self.dp_count)
        return self.remote(self.mid, self.out_ref.at[self.place], 2, hop, "dp", peer)

    def loop(self, fn, stop):
        def one(hop, carry):
            fn(hop)
            return carry

        lax.fori_loop(1, stop, one, 0)

    def first(self):
        self.loop(lambda hop: self.scatter(hop).start(), self.dp_count)

    def second(self):
        self.loop(lambda hop: self.scatter(hop).wait(), self.dp_count)
        total = lax.fori_loop(
            0,
            self.dp_count - 1,
            lambda k, acc: acc + self.got[k].astype(f32),
            self.in_ref[self.place].astype(f32),
        )
        self.mid[self.me] = total.astype(bf16)
        self.loop(lambda hop: self.across(hop).start(), self.count)

    def third(self):
        self.loop(lambda hop: self.across(hop).wait(), self.count)
        self.loop(lambda hop: self.around(hop).start(), self.dp_count)
        self.out_ref[self.place] = self.mid[...]

    def finish(self):
        self.loop(lambda hop: self.around(hop).wait(), self.dp_count)


def early_parts(rows):
    start = 0
    for source, (count, width) in enumerate(rows):
        for block in range(-(-width // LANES)):
            yield source, block, start, count, min(LANES, width - block * LANES)
            start += count


EARLY = ((4, 512), (1, 576), (10, 768))


def pack_early(ref, *sources):
    ref[...] = jnp.zeros_like(ref)
    for source, block, start, count, width in early_parts(EARLY):
        value = sources[source][0:count, block * LANES : block * LANES + width]
        for k in range(count):
            place = start + k
            ref[place // 16, place % 16 : place % 16 + 1, 0:width] = value[k : k + 1]


def unpack_early(ref, hwb_out, vec_out, upb_out, qv_out):
    for t in range(ref.shape[1]):
        for source, block, start, count, width in early_parts(EARLY):
            for k in range(count):
                place = start + k
                row = ref[place // 16, t, :, :].astype(f32)[place % 16 : place % 16 + 1, 0:width]
                lane = block * LANES
                if source == 0:
                    hwb_out[k : k + 1, t * 512 + lane : t * 512 + lane + width] = row
                elif source == 2 and k == 9:
                    upb_out[:, t * 768 + lane : t * 768 + lane + width] = row
                elif source == 2 and t == 0:
                    vec_out[k : k + 1, lane : lane + width] = row
                elif source == 1:
                    for out, low in ((0, 0), (1, 384)):
                        left, right = max(lane, low), min(lane + width, low + 192)
                        if left < right:
                            place_at = t * 192 + left - low
                            qv_out[out : out + 1, place_at : place_at + right - left] = row[
                                :, left - lane : right - lane
                            ]


def conv_backward_kernel(count, chars, cuts, *refs):
    (ids_ref, x_hbm, p_hbm, w_ref, off_ref, log_ref, prev_ref, part_ref, whole_hbm, dt_ref,
     dg_ref) = refs[:11]
    refs = refs[11:]
    if cuts:
        mids_in = refs[:2]
        hb_sums, proj_sums, row_sums = refs[2:5]
        hw_out, convw_out, convb_out, table_out, hwb_out, vec_out, upb_out, qv_out = refs[5:13]
        dw_ref, table_ref, hw_a, hw_b = refs[13:17]
        in0s, in1s, mids, in2s = refs[17:19], refs[19:21], refs[21:23], refs[23:27]
        dp_sems = refs[27:29]
        spreads = [Spread(refs[33 + 10 * k : 39 + 10 * k], *refs[29 + 10 * k : 33 + 10 * k])
                   for k in range(2)]
        refs = refs[49:]
    else:
        dw_ref, table_ref, hw_a, hw_b = refs[:4]
        refs = refs[4:]
    (pad_ref, stage_ref, grad_ref, from_left, from_right, x_buf, p_buf, whole_ref, wb_ref,
     load_sem, whole_sem) = refs[:11]
    line_sems = refs[11:]
    me = lax.axis_index("tensor")
    words, filters = log_ref.shape
    tiles = words // WORD_TILE
    padded = ids_ref.shape[1] // WORD_TILE

    def load(index):
        slot = index % 2
        return [
            pltpu.make_async_copy(hbm.at[index], buf.at[slot], load_sem.at[k, slot])
            for k, (buf, hbm) in enumerate(((x_buf, x_hbm), (p_buf, p_hbm)))
        ]

    whole_copy = pltpu.make_async_copy(whole_hbm, whole_ref, whole_sem)
    whole_copy.start()
    for index in range(2):
        for copy in load(index):
            copy.start()
    ring = [{"tensor": lax.rem(me + k, count)} for k in range(1, count)]
    items = []
    if cuts:
        place = lax.axis_index("dp")
        dp_count = spreads[0].dp_count
        cell, dp_peers = dp_cell(place)
        greet_all([{"dp": lax.rem(place + k, dp_count)} for k in range(1, dp_count)] + ring)
        for k in range(4):
            item = DpSum(cell, dp_peers, k % 2 == 0, dp_sems, 3 * k)
            item.in2 = in2s[k]
            if k < 2:
                item.src = (hw_a, hw_b)[k]
                item.half = item.src.at[:, :, cell[0]]
                item.in0, item.in1, item.mid = in0s[k], in1s[k], mids[k]
            else:
                item.mid = mids_in[k - 2]
            items.append(item)
        for item in items[2:]:
            item.copy2().start()
        pack_early(spreads[0].in_ref, hb_sums, proj_sums, row_sums)
        spreads[0].first()
    else:
        greet_all(ring)

    row_of = lax.broadcasted_iota(jnp.int32, w_ref.shape, 0)
    wb_ref[...] = jnp.where(row_of < 112, w_ref[...].astype(f32), 0.0).astype(bf16)
    dw_ref[...] = jnp.zeros_like(dw_ref)
    table_ref[...] = jnp.zeros_like(table_ref)
    pad_ref[...] = jnp.zeros_like(pad_ref)
    grad_ref[...] = prev_ref[...] + part_ref[
        :, pl.ds(pl.multiple_of(me * filters, filters), filters)
    ].astype(f32)
    chunks = line_sems[0].shape[1]
    per = words // chunks // WORD_TILE
    scatter = LineScatter(
        count, me, chunks, 3, part_ref, grad_ref, from_left, from_right, line_sems
    )
    group = lax.broadcasted_iota(jnp.int32, (1, WORD_TILE, LANES), 2) // 16
    vocab = lax.broadcasted_iota(jnp.int32, (table_ref.shape[0], padded * WORD_TILE), 0)

    def tile_step(index):
        slot = index % 2
        for copy in load(index):
            copy.wait()
        tile = pl.ds(pl.multiple_of(index * WORD_TILE, WORD_TILE), WORD_TILE)
        pooled = log_ref[tile, :] - off_ref[...]
        sig = jax.nn.sigmoid(pooled)
        grad = grad_ref[tile, :] * (sig * (1.0 + pooled * (1.0 - sig)))
        d_conv = (grad[None] * p_buf[slot].astype(f32)).astype(bf16)
        d_conv = d_conv.reshape(chars * WORD_TILE, filters)
        dw_ref[...] += dot(x_buf[slot], d_conv, 0, 0)
        d_win = dot(d_conv, wb_ref[...], 1, 1).astype(bf16)
        pad_ref[6 : 6 + chars] = d_win.reshape(chars, WORD_TILE, LANES)
        d_emb = pad_ref[6 : 6 + padded]
        for tap in range(1, 7):
            d_emb = jnp.where(group == tap, pad_ref[6 - tap : 6 - tap + padded], d_emb)
        one_hot = jnp.where(vocab == ids_ref[pl.ds(index, 1), :], 1.0, 0.0).astype(bf16)
        table_ref[...] += dot(one_hot, d_emb.reshape(padded * WORD_TILE, LANES), 1, 0)

        @pl.when(index + 2 < tiles)
        def more():
            for copy in load(index + 2):
                copy.start()

    def step_fn(step, carry):
        scatter.step(step)

        @pl.when(step == 0)
        def whole():
            whole_copy.wait()

        @pl.when(step < 8)
        def grads():
            weight_grad_piece(step, whole_ref, (dt_ref, dg_ref), (hw_a, hw_b))

        if cuts:

            @pl.when(step == 4)
            def early2():
                spreads[0].second()

            @pl.when(step == 7)
            def early3():
                spreads[0].third()

            @pl.when(step == 8)
            def start0():
                for item in items[:2]:
                    item.copy0().start()

            @pl.when(step == cuts[0])
            def start1():
                for item in items[:2]:
                    item.finish0()
                    item.copy1().start()

            @pl.when(step == cuts[1])
            def start2():
                for item in items[:2]:
                    item.finish1()
                    item.copy2().start()

        for k in range(per):
            scatter.finished(step, lambda chunk: tile_step(chunk * per + k), k)
        return carry

    lax.fori_loop(0, scatter.due(chunks - 1) + per, step_fn, 0)
    if cuts:
        late = spreads[1]
        taps = table_ref[:, 0:16]
        for tap in range(1, 7):
            taps += table_ref[:, 16 * tap : 16 * tap + 16]
        stage_ref[...] = jnp.zeros_like(stage_ref)
        table_ref[:, 0:16] = taps
        for i in range(8):
            late.in_ref[i, :, 0:filters] = dw_ref[16 * i : 16 * i + 16, :].astype(bf16)
            for k in range(3):
                size = 16 if k < 2 else 1
                stage_ref[0:size, 16 * k : 16 * k + 16] = table_ref[
                    33 * i + 16 * k : 33 * i + 16 * k + size, 0:16
                ]
            late.in_ref[i, :, filters:] = stage_ref[...].astype(bf16)
        late.first()
        spreads[0].finish()
        unpack_early(spreads[0].out_ref, hwb_out, vec_out, upb_out, qv_out)
        late.second()
        late.third()
        for k in range(4):
            hw_out[k // 2, k % 2] = items[k].finish2().astype(bf16)
        late.finish()
        for t in range(count):
            lanes = slice(t * filters, (t + 1) * filters)
            for i in range(7):
                convw_out[16 * i : 16 * i + 16, lanes] = late.out_ref[i, t, :, 0:filters]
            convb_out[:, lanes] = late.out_ref[7, t, :, 0:filters].astype(f32)[0:1]
        for i in range(8):
            total = late.out_ref[i, 0, :, filters:].astype(f32)
            for t in range(1, count):
                total += late.out_ref[i, t, :, filters:].astype(f32)
            for k in range(3):
                size = 16 if k < 2 else 1
                table_out[33 * i + 16 * k : 33 * i + 16 * k + size, :] = total[
                    0:size, 16 * k : 16 * k + 16
                ]
    scatter.drain()


def conv_backward(ids, x, p, w, off, logs, prev, part, whole, dt, dg, rest, count, cid):
    words, filters = logs.shape
    chars = p.shape[1]
    chunks = 8
    shape = jax.ShapeDtypeStruct
    hw_shape = (2, 2, 2, whole.shape[1] // 8, filters)
    operands = [ids, x, p, w, off, logs, prev, part, whole, dt, dg] + list(rest)
    in_specs = [VMEM, ANY, ANY] + [VMEM] * 5 + [ANY, VMEM, VMEM] + [VMEM] * len(rest)
    sums = [(LANES, filters), (264, LANES)]
    scratch = []
    cuts = None
    if rest:
        cuts = (17, 28)
        tail = hw_shape[-2:]
        features = rest[-1].shape[-1]
        out_shape = [
            shape((2, 2) + tail, bf16),
            shape((112, count * filters), bf16),
            shape((1, count * filters), f32),
            shape((264, 16), f32),
            shape((4, count * filters), f32),
            shape((9, features), f32),
            shape((1, count * features), f32),
            shape((2, features), f32),
        ]
        scratch += [pltpu.VMEM(shape_of, f32) for shape_of in sums]
        scratch += [pltpu.VMEM(hw_shape, bf16)] * 2
        scratch += [pltpu.VMEM((2, 2) + tail, bf16)] * 2
        scratch += [pltpu.VMEM((2,) + tail, bf16)] * 4
        scratch += [pltpu.VMEM(tail, bf16)] * 4
        scratch += [DMA((12,))] * 2
        for small, kind in (((16, LANES), f32), ((16, filters + LANES), bf16)):
            scratch += [
                pltpu.VMEM((8,) + small, kind),
                pltpu.VMEM((7,) + small, kind),
                pltpu.VMEM((count,) + small, bf16),
                pltpu.VMEM((8, count) + small, bf16),
            ]
            scratch += [DMA((7,))] * 2 + [DMA((count - 1,))] * 2 + [DMA((7,))] * 2
    else:
        out_shape = [shape(shape_of, f32) for shape_of in sums] + [shape(hw_shape, bf16)] * 2
    scratch += [
        pltpu.VMEM((68, WORD_TILE, LANES), bf16),
        pltpu.VMEM((16, LANES), f32),
        pltpu.VMEM((words, filters), f32),
        pltpu.VMEM(part.shape, bf16),
        pltpu.VMEM(part.shape, bf16),
        pltpu.VMEM((2,) + x.shape[1:], bf16),
        pltpu.VMEM((2,) + p.shape[1:], bf16),
        pltpu.VMEM(whole.shape, bf16),
        pltpu.VMEM(w.shape, bf16),
        DMA((2, 2)),
        DMA,
    ]
    scratch += [DMA((count, chunks))] * 4
    return pl.pallas_call(
        functools.partial(conv_backward_kernel, count, chars, cuts),
        out_shape=tuple(out_shape),
        in_specs=in_specs,
        out_specs=tuple([VMEM] * len(out_shape)),
        scratch_shapes=scratch,
        compiler_params=params(cid, 58),
        name="conv_backward",
    )(*operands)


def small_kernel(dp_count, count, in_ref, out_ref, got, mid, *sems):
    me = lax.axis_index("tensor")
    place = lax.axis_index("dp")
    barrier = pltpu.get_barrier_semaphore()

    def greet(hop, carry):
        peer = lax.rem(place + hop, dp_count)
        pl.semaphore_signal(barrier, inc=1, device_id={"dp": peer}, device_id_type=MESH)
        return carry

    lax.fori_loop(1, dp_count, greet, 0)
    for hop in range(1, count):
        pl.semaphore_signal(
            barrier, inc=1, device_id={"tensor": lax.rem(me + hop, count)}, device_id_type=MESH
        )
    pl.semaphore_wait(barrier, dp_count + count - 2)
    spread = Spread(sems, in_ref, got, mid, out_ref)
    spread.first()
    spread.second()
    spread.third()
    spread.finish()


def sum_small(packed, dp_count, count, cid):
    shape = packed.shape[1:]
    return pl.pallas_call(
        functools.partial(small_kernel, dp_count, count),
        out_shape=jax.ShapeDtypeStruct((dp_count, count) + shape, bf16),
        in_specs=[VMEM],
        out_specs=VMEM,
        scratch_shapes=[
            pltpu.VMEM((dp_count - 1,) + shape, f32),
            pltpu.VMEM((count,) + shape, bf16),
            DMA((dp_count - 1,)),
            DMA((dp_count - 1,)),
            DMA((count - 1,)),
            DMA((count - 1,)),
            DMA((dp_count - 1,)),
            DMA((dp_count - 1,)),
        ],
        compiler_params=params(cid, 32),
        name="sum_small",
    )(packed)


def body(
    char_ids,
    seq_lengths,
    char_table,
    conv_weight,
    conv_bias,
    highway_weight,
    highway_bias,
    proj_weight,
    proj_bias,
    norm_gain,
    norm_shift,
    qkv_weight,
    qv_bias,
    output_projection_weight,
    out_bias,
    up_weight,
    up_bias,
    down_weight,
    down_bias,
    out_grad,
):
    words, nseq, chars = char_ids.shape
    assert nseq == 1
    count = lax.axis_size("tensor")
    dp_count = lax.axis_size("dp")
    rank = lax.axis_index("tensor")
    vocab, char_dim = char_table.shape
    taps_dim, filters = conv_weight.shape
    features = proj_weight.shape[1]
    heads = qkv_weight.shape[2] // HEAD_DIM

    tiles = words // WORD_TILE
    ids_tiles = jnp.swapaxes(char_ids[:, 0].reshape(tiles, WORD_TILE, chars), 1, 2)
    ids_tiles = ids_tiles.reshape(tiles, chars * WORD_TILE)
    flat = [proj_bias, out_bias, down_bias, norm_gain, norm_shift, up_bias, qv_bias, highway_bias]
    flat = jnp.concatenate([part.reshape(-1) for part in flat]).reshape(-1, LANES)

    pattern = np.zeros((chars, WORD_TILE, LANES), np.float32)
    pattern[:, :, taps_dim] = 1.0
    for k in range(1, 7):
        pattern[chars - k, :, taps_dim + k] = 1.0

    widths = filter_widths(filters)
    off = jnp.asarray(np.log((chars - widths + 1).astype(np.float64)).astype(np.float32))[None]
    tap_of = np.arange(taps_dim)[:, None] // char_dim
    w_taps = jnp.where(tap_of < widths[None], conv_weight, 0).astype(bf16)
    ends = np.where(widths[None] > np.arange(1, 7)[:, None], big_neg, 0.0).astype(np.float32)
    tail = LANES - taps_dim - 7
    w_all = jnp.concatenate(
        [w_taps, conv_bias[None], jnp.asarray(ends, bf16), jnp.zeros((tail, filters), bf16)], axis=0
    )

    logs, whole0, whole1, top, x_tiles, p_tiles, t0, g0, h0, t1, g1, h1 = embed_forward(
        ids_tiles,
        char_table.T,
        jnp.asarray(pattern, bf16),
        w_all,
        off,
        flat,
        highway_weight,
        count,
        chars,
        1,
    )
    encoded, d_hidden, tr_a, tr_b, row_sums, proj_sums = encoder(
        top,
        (
            proj_weight,
            jnp.transpose(qkv_weight, (1, 2, 0)).reshape(-1, features),
            output_projection_weight,
            up_weight,
            down_weight,
        ),
        flat,
        out_grad[:, 0],
        seq_lengths,
        count,
        4,
    )
    encoded = encoded[:, None]

    back_args = (d_hidden, t1, g1, h1, t0, g0, h0, whole1, highway_weight)
    conv_args = (ids_tiles, x_tiles, p_tiles, w_all, off, logs)
    taps_mask = np.tile(tap_of < widths[None], (1, count))
    three = 3 * heads * HEAD_DIM
    units = up_weight.shape[1]
    if dp_count == 8 and (features // dp_count) % 16 == 0:
        part0, prev0, dt0, dg0, hw_bias_part, mid_a, mid_b, tr_a, tr_b = highway_back(
            *back_args, tr_a, tr_b, count, 9
        )
        (hw_w_grad, conv_w_grad, conv_b_grad, table_grad, hw_b_grad, rows, up_b_grad,
         qv_grad) = conv_backward(
            *conv_args, prev0, part0, whole0, dt0, dg0,
            (mid_a, mid_b, hw_bias_part, proj_sums, row_sums), count, 10,
        )
        conv_w_grad, conv_b_grad = conv_w_grad.astype(f32), conv_b_grad[0]
        hw_w_grad = hw_w_grad.astype(f32)
        tr_a, tr_b = tr_a.astype(f32), tr_b.astype(f32)
        table_grad = table_grad[:vocab]
        up_b_grad = up_b_grad[0]
    else:
        part0, prev0, dt0, dg0, hw_bias_part, *hw1 = highway_back(*back_args, None, None, count, 9)
        d_w_all, table_all, *hw0 = conv_backward(
            *conv_args, prev0, part0, whole0, dt0, dg0, (), count, 10
        )
        hw_sum = jnp.stack([part.reshape(-1, filters) for part in hw0 + hw1])
        hw_sum = lax.psum_scatter(hw_sum, "dp", scatter_dimension=1, tiled=True).astype(f32)
        tr_a, tr_b = [
            lax.psum_scatter(
                part.reshape(features, -1), "dp", scatter_dimension=0, tiled=True
            ).astype(f32)
            for part in (tr_a, tr_b)
        ]
        hw_w_grad = hw_sum.reshape(2, 2, -1, filters)
        pieces = [d_w_all[: taps_dim + 1], table_all, hw_bias_part, proj_sums, row_sums[:10]]
        flat = jnp.concatenate([part.reshape(-1) for part in pieces])
        width = -(-flat.size // (dp_count * 16 * LANES)) * LANES
        flat = jnp.pad(flat, (0, dp_count * 16 * width - flat.size))
        summed = sum_small(flat.reshape(dp_count, 16, width), dp_count, count, 11)
        summed = jnp.swapaxes(summed, 0, 1).reshape(count, -1).astype(f32)
        conv_size, table_size = pieces[0].size, table_all.size
        conv_all = summed[:, :conv_size].reshape(count, taps_dim + 1, filters)
        conv_all = jnp.swapaxes(conv_all, 0, 1)
        conv_w_grad = conv_all[:taps_dim].reshape(taps_dim, -1)
        conv_b_grad = conv_all[taps_dim].reshape(-1)
        table_all = jnp.sum(summed[:, conv_size : conv_size + table_size], axis=0)
        table_all = table_all.reshape(-1, LANES)
        early = summed[:, conv_size + table_size :]
        table_grad = jnp.sum(
            table_all[:vocab, :taps_dim].reshape(vocab, taps_dim // char_dim, char_dim), axis=1
        )
        hw_b_grad = jnp.swapaxes(early[:, : 4 * filters].reshape(count, 4, filters), 0, 1)
        early = early[:, 4 * filters :]
        qv_grad = jnp.swapaxes(early[:, :three].reshape(count, 3, -1), 0, 1)[::2].reshape(2, -1)
        rows = early[:, three : three + 10 * features].reshape(count, 10, features)
        up_b_grad = rows[:, 9].reshape(-1)
        rows = rows[0]

    conv_w_grad = jnp.where(taps_mask, conv_w_grad, 0.0)
    hw_b_grad = hw_b_grad.reshape(2, 2, -1)
    up_w_grad = tr_a[:, :units]
    down_w_grad = tr_a[:, units:].T
    proj_w_grad = tr_b[:, :filters].T
    qkv_w_grad = tr_b[:, filters : filters + three].reshape(-1, 3, heads * HEAD_DIM)
    out_w_grad = tr_b[:, 1152 : 1152 + heads * HEAD_DIM].T
    proj_b_grad, out_b_grad, down_b_grad = rows[0], rows[1], rows[2]
    gain_grad, shift_grad = rows[3:6], rows[6:9]
    return (
        encoded,
        table_grad,
        conv_w_grad,
        conv_b_grad,
        hw_w_grad,
        hw_b_grad,
        proj_w_grad,
        proj_b_grad,
        gain_grad,
        shift_grad,
        qkv_w_grad,
        qv_grad,
        out_w_grad,
        out_b_grad,
        up_w_grad,
        up_b_grad,
        down_w_grad,
        down_b_grad,
    )


def solution(mesh):
    return jax.shard_map(
        body,
        mesh=mesh,
        in_specs=(
            P(None, "dp", None),
            P("dp"),
            P(),
            P(None, "tensor"),
            P("tensor"),
            P(None, None, None, "tensor"),
            P(None, None, "tensor"),
            P("tensor", None),
            P(),
            P(),
            P(),
            P(None, None, "tensor"),
            P(None, "tensor"),
            P("tensor", None),
            P(),
            P(None, "tensor"),
            P("tensor"),
            P("tensor", None),
            P(),
            P("tensor", "dp", None),
        ),
        out_specs=(
            P("tensor", "dp", None),
            P(),
            P(),
            P(),
            P(None, None, "dp", "tensor"),
            P(),
            P("tensor", "dp"),
            P(),
            P(),
            P(),
            P("dp", None, "tensor"),
            P(),
            P("tensor", "dp"),
            P(),
            P("dp", "tensor"),
            P(),
            P("tensor", "dp"),
            P(),
        ),
        check_vma=False,
    )
```

```python
import functools
import math

import jax
import jax.numpy as jnp
import numpy as np
from jax import lax
from jax.experimental import pallas as pl
from jax.experimental.pallas import tpu as pltpu
from jax.sharding import PartitionSpec as P

HEAD_DIM = 64
WORD_TILE = 32
LANES = 128

norm_eps = 1e-06
big_neg = -1e30
f32 = jnp.float32
bf16 = jnp.bfloat16
MESH = pl.DeviceIdType.MESH
VMEM = pl.BlockSpec(memory_space=pltpu.VMEM)
ANY = pl.BlockSpec(memory_space=pl.ANY)
DMA = pltpu.SemaphoreType.DMA
MIB = 1 << 20


def params(cid, vmem):
    return pltpu.CompilerParams(
        collective_id=cid, has_side_effects=True, vmem_limit_bytes=vmem * MIB
    )


def width_counts(block):
    unit = block // 64
    return [unit, unit, 2 * unit, 4 * unit, 8 * unit, 16 * unit, 32 * unit]


def filter_widths(block):
    return np.concatenate(
        [np.full((n,), i + 1, np.int32) for i, n in enumerate(width_counts(block))]
    )


def dot(a, b, ca, cb):
    return lax.dot_general(a, b, (((ca,), (cb,)), ((), ())), preferred_element_type=f32)


def line_greet(me, count):
    barrier = pltpu.get_barrier_semaphore()
    for there, ok in ((me - 1, me > 0), (me + 1, me < count - 1)):

        @pl.when(ok)
        def greet():
            pl.semaphore_signal(barrier, inc=1, device_id={"tensor": there}, device_id_type=MESH)


def line_meet(me, count):
    pl.semaphore_wait(
        pltpu.get_barrier_semaphore(), jnp.minimum(me, 1) + jnp.minimum(count - 1 - me, 1)
    )


def line_copy(view, me, count, right, block, chunk, sems):
    send, recv = sems[:2] if right else sems[2:]
    to = jnp.minimum(me + 1, count - 1) if right else jnp.maximum(me - 1, 0)
    ref = view(block, chunk)
    return pltpu.make_async_remote_copy(
        src_ref=ref,
        dst_ref=ref,
        send_sem=send.at[block, chunk],
        recv_sem=recv.at[block, chunk],
        device_id={"tensor": to},
        device_id_type=MESH,
    )


def gather_step(view, step, chunks, me, count, sems, spacing=1):
    for hop in range(count):
        chunk = step - spacing * hop
        here = (chunk >= 0) & (chunk < chunks)
        safe = jnp.clip(chunk, 0, chunks - 1)
        for right in (True, False):
            block = me - hop if right else me + hop
            there = (block >= 0) & (block < count)
            block = jnp.clip(block, 0, count - 1)
            more = me < count - 1 if right else me > 0
            copy = functools.partial(line_copy, view, me, count, right, block, safe, sems)

            @pl.when(here & there)
            def pass_on():
                if hop > 0:
                    copy().wait_recv()

                @pl.when(more)
                def send():
                    copy().start()


def gather_drain(view, chunks, me, count, sems):
    def one(chunk, carry):
        for hop in range(count):
            for right in (True, False):
                block = me - hop if right else me + hop
                there = (block >= 0) & (block < count)
                block = jnp.clip(block, 0, count - 1)
                more = me < count - 1 if right else me > 0
                copy = functools.partial(line_copy, view, me, count, right, block, chunk, sems)

                @pl.when(there & more)
                def sent():
                    copy().wait_send()

        return carry

    lax.fori_loop(0, chunks, one, 0)


def embed_forward_kernel(count, chars, *refs):
    (ids_ref, chars_ref, pattern_ref, cw_ref, cb_ref, mask_ref, ends_ref, off_ref, bias_ref,
     hw_hbm) = refs[:10]
    log_ref, whole0_ref, whole1_ref, top_ref, x_hbm, p_hbm = refs[10:16]
    kept = refs[16:22]
    y_buf, x_buf, p_buf, hw_ref, table_ref, w_ref, hb_ref, keep_sem, late_sem = refs[22:31]
    bufs = refs[31:37]
    sems0, sems1 = refs[37:41], refs[41:45]
    t_refs, g_refs, h_refs = (bufs[0], bufs[3]), (bufs[1], bufs[4]), (bufs[2], bufs[5])
    wholes = (whole0_ref, whole1_ref)
    me = lax.axis_index("tensor")
    line_greet(me, count)
    words, filters = log_ref.shape
    tiles = words // WORD_TILE
    half = words // 2
    padded = ids_ref.shape[1] // WORD_TILE
    own = pl.ds(pl.multiple_of(me * filters, filters), filters)
    loads = [
        pltpu.make_async_copy(hw_hbm.at[layer], hw_ref.at[layer], late_sem.at[layer])
        for layer in range(2)
    ]
    for copy in loads:
        copy.start()
    stores = [
        pltpu.make_async_copy(buf, out, late_sem.at[2 + k])
        for k, (buf, out) in enumerate(zip(bufs, kept))
    ]
    y_buf[...] = jnp.zeros_like(y_buf)
    table_ref[...] = jnp.zeros_like(table_ref)
    depth, vocab_size = chars_ref.shape
    for tap in range(7):
        table_ref[depth * tap : depth * tap + depth, 0:vocab_size] = chars_ref[...]
    for layer in range(2):
        hb_ref[2 * layer : 2 * layer + 2, :] = bias_ref[layer].astype(f32)
    taps = cw_ref.shape[0]
    w_ref[0:taps, :] = (cw_ref[...].astype(f32) * mask_ref[...]).astype(bf16)
    first = lax.broadcasted_iota(jnp.int32, ends_ref.shape, 0) == 0
    bias = cb_ref[...].astype(f32).reshape(1, filters)
    w_ref[taps:, :] = jnp.where(first, bias, ends_ref[...]).astype(bf16)
    line_meet(me, count)

    def view_of(whole):
        def view(block, chunk):
            return whole.at[
                pl.ds(pl.multiple_of(chunk * WORD_TILE, WORD_TILE), WORD_TILE),
                pl.ds(pl.multiple_of(block * filters, filters), filters),
            ]

        return view

    views = [view_of(whole) for whole in wholes]

    def keep(index):
        slot = index % 2
        return [
            pltpu.make_async_copy(buf.at[slot], hbm.at[index], keep_sem.at[k, slot])
            for k, (buf, hbm) in enumerate(((x_buf, x_hbm), (p_buf, p_hbm)))
        ]

    group = lax.broadcasted_iota(jnp.int32, (1, WORD_TILE, LANES), 2) // 16
    vocab = lax.broadcasted_iota(jnp.int32, (table_ref.shape[1], padded * WORD_TILE), 0)

    def tile_step(index):
        slot = index % 2

        @pl.when(index >= 2)
        def free():
            for copy in keep(index - 2):
                copy.wait()

        one_hot = jnp.where(vocab == ids_ref[pl.ds(index, 1), :], 1.0, 0.0).astype(bf16)
        found = dot(table_ref[...], one_hot, 1, 0).astype(bf16).T
        y_buf[0:padded] = found.reshape(padded, WORD_TILE, LANES)
        value = jnp.where(group == 7, pattern_ref[...], y_buf[0:chars])
        for tap in range(1, 7):
            value = jnp.where(group == tap, y_buf[tap : chars + tap], value)
        x2 = value.reshape(chars * WORD_TILE, LANES)
        x_buf[slot] = x2
        conv = dot(x2, w_ref[...], 1, 0).reshape(chars, WORD_TILE, filters)
        top = jnp.max(conv, axis=0)
        exps = jnp.exp(conv - top[None])
        sums = jnp.sum(exps, axis=0)
        p_buf[slot] = (exps * (1.0 / sums)[None]).astype(bf16)
        for copy in keep(index):
            copy.start()
        tile = pl.ds(pl.multiple_of(index * WORD_TILE, WORD_TILE), WORD_TILE)
        total = top + jnp.log(sums)
        log_ref[tile, :] = total
        pooled = total - off_ref[...]
        hidden = pooled * jax.nn.sigmoid(pooled)
        h_refs[0][tile, :] = hidden
        whole0_ref[tile, own] = hidden.astype(bf16)

    def layer_step(layer, part):
        rows = slice(part * half, (part + 1) * half)
        for j, out in enumerate((t_refs[layer], g_refs[layer])):
            bias = hb_ref[2 * layer + j : 2 * layer + j + 1, :]
            out[rows, :] = dot(wholes[layer][rows, :], hw_ref[layer, j], 1, 0) + bias

        def mix(index, carry):
            tile = pl.ds(pl.multiple_of(part * half + index * WORD_TILE, WORD_TILE), WORD_TILE)
            trans = t_refs[layer][tile, :]
            gate = jax.nn.sigmoid(g_refs[layer][tile, :])
            hidden = gate * (trans * jax.nn.sigmoid(trans)) + (1.0 - gate) * h_refs[layer][tile, :]
            if layer == 0:
                h_refs[1][tile, :] = hidden
                whole1_ref[tile, own] = hidden.astype(bf16)
            else:
                top_ref[tile, :] = hidden.astype(bf16)
            return carry

        lax.fori_loop(0, half // WORD_TILE, mix, 0)

    spacing = 2
    fill = spacing * (count - 1)
    shift = tiles // 2 + fill
    last = shift + tiles + fill

    def step_fn(step, carry):
        @pl.when(step < tiles)
        def convolve():
            tile_step(step)

        @pl.when(step < tiles + fill)
        def first_gather():
            gather_step(views[0], step, tiles, me, count, sems0, spacing)

        @pl.when(step == shift)
        def first_half():
            loads[0].wait()
            layer_step(0, 0)

        @pl.when(step == shift + tiles // 2)
        def second_half():
            layer_step(0, 1)
            for copy in stores[:3]:
                copy.start()

        @pl.when(step >= shift)
        def second_gather():
            gather_step(views[1], step - shift, tiles, me, count, sems1, spacing)

        @pl.when(step == 2 * shift - 1)
        def third_half():
            loads[1].wait()
            layer_step(1, 0)

        return carry

    lax.fori_loop(0, last, step_fn, 0)
    layer_step(1, 1)
    for copy in stores[3:]:
        copy.start()
    for index in (tiles - 2, tiles - 1):
        for copy in keep(index):
            copy.wait()
    for sems, view in zip((sems0, sems1), views):
        gather_drain(view, tiles, me, count, sems)
    for copy in stores:
        copy.wait()


def embed_forward(ids, table, pattern, conv, off, bias, weight, count, chars, cid):
    filters = conv[0].shape[1]
    tiles = ids.shape[0]
    words = tiles * WORD_TILE
    shape = jax.ShapeDtypeStruct
    flat = (words, filters)
    return pl.pallas_call(
        functools.partial(embed_forward_kernel, count, chars),
        out_shape=(
            shape(flat, f32),
            shape((words, count * filters), bf16),
            shape((words, count * filters), bf16),
            shape(flat, bf16),
            shape((tiles, chars * WORD_TILE, LANES), bf16),
            shape((tiles, chars, WORD_TILE, filters), bf16),
        )
        + (shape(flat, f32),) * 6,
        in_specs=[VMEM] * 9 + [ANY],
        out_specs=(VMEM,) * 4 + (ANY,) * 8,
        scratch_shapes=[
            pltpu.VMEM((chars + 6, WORD_TILE, LANES), bf16),
            pltpu.VMEM((2, chars * WORD_TILE, LANES), bf16),
            pltpu.VMEM((2, chars, WORD_TILE, filters), bf16),
            pltpu.VMEM(weight.shape, bf16),
            pltpu.VMEM((LANES, 264), bf16),
            pltpu.VMEM((LANES, filters), bf16),
            pltpu.VMEM((8, filters), f32),
            DMA((2, 2)),
            DMA((8,)),
        ]
        + [pltpu.VMEM(flat, f32)] * 6
        + [DMA((count, tiles))] * 8,
        compiler_params=params(cid, 58),
        name="embed_forward",
    )(ids, table, pattern, *conv, off, bias, weight)


class LineSum:
    def __init__(self, count, me, chunks, spacing, number, p_ref, out_ref, buffers, sems):
        self.count, self.me, self.chunks, self.spacing = count, me, chunks, spacing
        self.number, self.p_ref, self.out_ref = number, p_ref, out_ref
        self.buffers, self.sems = buffers, sems
        self.steps = chunks + spacing * (count - 1)

    def place(self, right, chunk):
        count, me, number = self.count, self.me, self.number
        lag = me if right else count - 1 - me
        rows = self.p_ref.shape[0] // self.chunks
        tile = pl.ds(pl.multiple_of(chunk * rows, rows), rows)
        buf = self.buffers[0 if right else 1]
        send, recv = self.sems[:2] if right else self.sems[2:]
        to = jnp.minimum(me + 1, count - 1) if right else jnp.maximum(me - 1, 0)
        first, passed = [
            functools.partial(
                pltpu.make_async_remote_copy,
                src_ref=src,
                dst_ref=buf.at[number, tile],
                send_sem=send.at[number, chunk],
                recv_sem=recv.at[number, chunk],
                device_id={"tensor": to},
                device_id_type=MESH,
            )
            for src in (self.p_ref.at[tile], buf.at[number, tile])
        ]
        return lag, tile, buf, first, passed

    def step(self, step):
        for right in (True, False):
            lag = self.me if right else self.count - 1 - self.me
            chunk = step - self.spacing * lag
            here = (chunk >= 0) & (chunk < self.chunks)
            chunk = jnp.clip(chunk, 0, self.chunks - 1)
            lag, tile, buf, first, passed = self.place(right, chunk)

            @pl.when(here & (lag == 0))
            def start():
                first().start()

            @pl.when(here & (lag > 0))
            def middle():
                first().wait_recv()
                got = buf[self.number, tile, :].astype(f32)

                @pl.when(lag < self.count - 1)
                def forward():
                    buf[self.number, tile, :] = (got + self.p_ref[tile, :].astype(f32)).astype(bf16)
                    passed().start()

                self.out_ref[tile, :] += got

    def drain(self):
        def one(chunk, carry):
            for right in (True, False):
                lag, tile, buf, first, passed = self.place(right, chunk)

                @pl.when(lag < self.count - 1)
                def sent():
                    first().wait_send()

            return carry

        lax.fori_loop(0, self.chunks, one, 0)

    def run(self, done, extra=()):
        rows = self.p_ref.shape[0] // self.chunks
        fill = self.spacing * (self.count - 1)

        def one(step, carry):
            self.step(step)
            for k, work in enumerate(extra):
                pl.when(step == k)(work)

            @pl.when(step >= fill)
            def finish():
                chunk = jnp.maximum(step - fill, 0)
                done(pl.ds(pl.multiple_of(chunk * rows, rows), rows))

            return carry

        lax.fori_loop(0, self.steps, one, 0)
        self.drain()


def norm_parts(values):
    centered = values - jnp.mean(values, axis=-1, keepdims=True)
    root = lax.rsqrt(jnp.mean(centered * centered, axis=-1, keepdims=True) + norm_eps)
    return centered * root, root


def norm_back(values, gain, cotangent):
    nv, root = norm_parts(values)
    scaled = cotangent * gain
    inner = jnp.mean(scaled, axis=-1, keepdims=True)
    along = jnp.mean(scaled * nv, axis=-1, keepdims=True)
    return root * (scaled - inner - nv * along), cotangent * nv


def gelu_parts(values):
    cdf = 0.5 * (1.0 + lax.erf(values * 0.7071067811865476))
    slope = cdf + values * jnp.exp(-0.5 * values * values) * 0.3989422804014327
    return values * cdf, slope


def column_sum(values):
    return jnp.sum(values, axis=0, keepdims=True)


def encoder_kernel(count, chunks, spacing, *refs):
    top_ref, pw_ref, qw_ref, ow_ref, uw_ref, dw_ref = refs[:6]
    bias_refs, norm_refs, qv_ref, og_ref, len_ref = refs[6:10], refs[10:12], *refs[12:15]
    enc_ref, dh2_ref, tra_ref, trb_ref, sums_ref, qsum_ref, vec_ref, qb_ref = refs[15:23]
    (emb, inp, midpre, mid, fin, slope, dmid, din, sent, sent_mid, act, d_two, d_up, d_branch,
     d_emb, qkv, attended, probs, d_heads, d_proj, part, grad_all, enc_all, from_left,
     from_right) = refs[23:48]
    line_sems, gather_sems = refs[48:52], refs[52:56]
    me = lax.axis_index("tensor")
    line_greet(me, count)
    words, features = emb.shape
    heads = attended.shape[1] // HEAD_DIM
    hidden = heads * HEAD_DIM
    scale = HEAD_DIM ** (-0.5)
    own = words // count
    own_tile = pl.ds(pl.multiple_of(me * own, own), own)
    grad_all[own_tile, :] = og_ref[...]
    sums_ref[...] = jnp.zeros_like(sums_ref)
    trb_ref[...] = jnp.zeros_like(trb_ref)
    for k, bias_ref in zip((0, 1, 2, 9), bias_refs):
        vec_ref[k : k + 1, :] = bias_ref[...].astype(f32).reshape(1, features)
    for k, norm_ref in zip((3, 6), norm_refs):
        vec_ref[k : k + 3, :] = norm_ref[...].astype(f32)
    qb_ref[...] = jnp.zeros_like(qb_ref)
    ends = qv_ref[...].astype(f32)
    qb_ref[:, 0:hidden] = ends[0:1]
    qb_ref[:, 2 * hidden : 3 * hidden] = ends[1:2]
    live = lax.broadcasted_iota(jnp.int32, (1, words), 1) < len_ref[0]

    def line(number, out_ref):
        return LineSum(
            count, me, chunks, spacing, number, part, out_ref, (from_left, from_right), line_sems
        )

    def gather_view(block, chunk):
        return grad_all.at[pl.ds(pl.multiple_of(block * own, own), own)]

    def tiles(size, work):
        def one(index, carry):
            work(pl.ds(pl.multiple_of(index * size, size), size))
            return carry

        lax.fori_loop(0, words // size, one, 0)

    def send_product(lhs, rhs, side, out_ref):
        def work(tile):
            value = dot(lhs[tile, :], rhs[...], 1, side).astype(bf16)
            part[tile, :] = value
            out_ref[tile, :] = value.astype(f32)

        tiles(256, work)

    def grads(lhs, rhs, out_ref, lane):
        def half(k):
            def work():
                depth = features // 2
                value = dot(lhs[:, depth * k : depth * k + depth], rhs[...], 0, 0).astype(bf16)
                for i in range(2):
                    for j in range(2):
                        start = (2 * i + j) * (depth // 4)
                        out_ref[k, i, j, :, lane : lane + rhs.shape[1]] = value[
                            start : start + depth // 4
                        ]

            return work

        return [half(0), half(1)]

    def row(index):
        return vec_ref[index : index + 1, :]

    def add_sum(index, value):
        sums_ref[index : index + 1, :] += column_sum(value)

    send_product(top_ref, pw_ref, 0, emb)
    line_meet(me, count)

    def first_norm(tile):
        value = emb[tile, :] + row(0)
        emb[tile, :] = value
        value = norm_parts(value)[0] * row(3) + row(6)
        inp[tile, :] = value
        sent[tile, :] = value.astype(bf16)

    line(0, emb).run(first_norm)

    def project(tile):
        qkv[tile, :] = (dot(sent[tile, :], qw_ref[...], 1, 1) + qb_ref[...]).astype(bf16)

    gather_step(gather_view, 0, 1, me, count, gather_sems)
    tiles(256, project)

    for head in range(heads):
        lanes = slice(head * HEAD_DIM, (head + 1) * HEAD_DIM)
        keys = slice(hidden + head * HEAD_DIM, hidden + (head + 1) * HEAD_DIM)
        vals = slice(2 * hidden + head * HEAD_DIM, 2 * hidden + (head + 1) * HEAD_DIM)

        def attend(tile):
            scores = dot(qkv[tile, lanes], qkv[:, keys], 1, 1) * scale
            scores = jnp.where(live, scores, big_neg)
            exps = jnp.exp(scores - jnp.max(scores, axis=1, keepdims=True))
            value = exps / jnp.sum(exps, axis=1, keepdims=True)
            probs[head, tile, :] = value
            attended[tile, lanes] = dot(value.astype(bf16), qkv[:, vals], 1, 0).astype(bf16)

        tiles(128, attend)
        if head == heads - 2:
            gather_step(gather_view, 1, 1, me, count, gather_sems)
    send_product(attended, ow_ref, 0, midpre)

    def pass_grads():
        for step in range(2, count - 1):
            gather_step(gather_view, step, 1, me, count, gather_sems)

    def second_norm(tile):
        value = midpre[tile, :] + inp[tile, :] + row(1)
        midpre[tile, :] = value
        value = norm_parts(value)[0] * row(4) + row(7)
        mid[tile, :] = value
        sent_mid[tile, :] = value.astype(bf16)

    line(1, midpre).run(second_norm, [lambda: None, lambda: None, pass_grads])
    gather_step(gather_view, count - 1, 1, me, count, gather_sems)

    def feed(tile):
        value, back = gelu_parts(dot(sent_mid[tile, :], uw_ref[...], 1, 0) + row(9))
        act[tile, :] = value.astype(bf16)
        slope[tile, :] = back

    tiles(128, feed)
    send_product(act, dw_ref, 0, fin)

    def third_norm(tile):
        value = fin[tile, :] + mid[tile, :] + row(2)
        cotangent = grad_all[tile, :].astype(f32)
        enc_all[tile, :] = (norm_parts(value)[0] * row(5) + row(8)).astype(bf16)
        back, gain = norm_back(value, row(5), cotangent)
        fin[tile, :] = back
        low = back.astype(bf16)
        d_two[tile, :] = low
        add_sum(2, low.astype(f32))
        add_sum(5, gain)
        add_sum(8, cotangent)

    line(2, fin).run(third_norm)
    enc_ref[...] = enc_all[own_tile, :]

    def feed_back(tile):
        value = (dot(d_two[tile, :], dw_ref[...], 1, 1) * slope[tile, :]).astype(bf16)
        d_up[tile, :] = value
        add_sum(9, value.astype(f32))

    tiles(128, feed_back)
    send_product(d_up, uw_ref, 1, dmid)
    def second_back(tile):
        cotangent = dmid[tile, :] + fin[tile, :]
        back, gain = norm_back(midpre[tile, :], row(4), cotangent)
        dmid[tile, :] = back
        low = back.astype(bf16)
        d_branch[tile, :] = low
        add_sum(1, low.astype(f32))
        add_sum(4, gain)
        add_sum(7, cotangent)

    work = grads(d_two, act, tra_ref, features) + grads(sent_mid, d_up, tra_ref, 0)
    line(3, dmid).run(second_back, work)

    def heads_back(tile):
        d_heads[tile, :] = dot(d_branch[tile, :], ow_ref[...], 1, 1).astype(bf16)

    tiles(256, heads_back)
    for head in range(heads):
        lanes = slice(head * HEAD_DIM, (head + 1) * HEAD_DIM)
        keys = slice(hidden + head * HEAD_DIM, hidden + (head + 1) * HEAD_DIM)
        vals = slice(2 * hidden + head * HEAD_DIM, 2 * hidden + (head + 1) * HEAD_DIM)
        weights = probs[head]
        d_out = d_heads[:, lanes]
        d_proj[:, vals] = dot(weights.astype(bf16), d_out, 0, 0).astype(bf16)
        d_probs = dot(d_out, qkv[:, vals], 1, 1)
        inner = jnp.sum(d_probs * weights, axis=1, keepdims=True)
        d_scores = (weights * (d_probs - inner)).astype(bf16)
        d_proj[:, lanes] = (dot(d_scores, qkv[:, keys], 1, 0) * scale).astype(bf16)
        d_proj[:, keys] = (dot(d_scores, qkv[:, lanes], 0, 0) * scale).astype(bf16)
    send_product(d_proj, qw_ref, 0, din)
    qsum_ref[...] = column_sum(d_proj[...].astype(f32))

    def first_back(tile):
        cotangent = din[tile, :] + dmid[tile, :]
        back, gain = norm_back(emb[tile, :], row(3), cotangent)
        low = back.astype(bf16)
        d_emb[tile, :] = low
        add_sum(0, low.astype(f32))
        add_sum(3, gain)
        add_sum(6, cotangent)

    work = grads(sent, d_proj, trb_ref, top_ref.shape[1])
    work += grads(d_branch, attended, trb_ref, 1152)
    line(4, din).run(first_back, work)

    def last(tile):
        dh2_ref[tile, :] = dot(d_emb[tile, :], pw_ref[...], 1, 1)

    tiles(256, last)
    for work in grads(d_emb, top_ref, trb_ref, 0):
        work()
    gather_drain(gather_view, 1, me, count, gather_sems)


def encoder(top, weights, biases, out_grad, lengths, count, cid):
    words, filters = top.shape
    features = weights[0].shape[1]
    three = weights[1].shape[0]
    units = weights[3].shape[1]
    hidden = three // 3
    chunks, spacing = 16, 4
    shape = jax.ShapeDtypeStruct
    rows = features // 8
    scratch = [pltpu.VMEM((16, features), f32), pltpu.VMEM((1, three), f32)]
    scratch += [pltpu.VMEM((words, n), f32) for n in [features] * 5 + [units] + [features] * 2]
    scratch += [
        pltpu.VMEM((words, n), bf16)
        for n in (features, features, units, features, units, features, features, three, hidden)
    ]
    scratch += [pltpu.VMEM((hidden // HEAD_DIM, words, words), f32)]
    scratch += [pltpu.VMEM((words, n), bf16) for n in (hidden, three, features, features, features)]
    scratch += [pltpu.VMEM((5, words, features), bf16)] * 2
    scratch += [DMA((5, chunks))] * 4 + [DMA((count, 1))] * 4
    return pl.pallas_call(
        functools.partial(encoder_kernel, count, chunks, spacing),
        out_shape=(
            shape((words // count, features), bf16),
            shape((words, filters), f32),
            shape((2, 2, 2, rows, features + units), bf16),
            shape((2, 2, 2, rows, 1408), bf16),
            shape((16, features), f32),
            shape((1, three), f32),
        ),
        in_specs=[VMEM] * 14 + [pl.BlockSpec(memory_space=pltpu.SMEM)],
        out_specs=(VMEM,) * 6,
        scratch_shapes=scratch,
        compiler_params=params(cid, 58),
        name="encoder",
    )(top, *weights, *biases, out_grad, lengths)


class LineScatter:
    def __init__(self, count, me, chunks, spacing, p_ref, out_ref, from_left, from_right, sems):
        self.count, self.me, self.chunks, self.spacing = count, me, chunks, spacing
        self.p_ref, self.out_ref = p_ref, out_ref
        self.from_left, self.from_right, self.sems = from_left, from_right, sems
        self.messages = chunks * (count - 1)
        self.steps = self.messages + spacing * (count - 1)

    def place(self, right, number):
        count, me = self.count, self.me
        lag = me if right else count - 1 - me
        chunk = number // (count - 1)
        far = count - 1 - number % (count - 1)
        block = far if right else count - 1 - far
        words, filters = self.out_ref.shape
        rows = words // self.chunks
        tile = pl.ds(pl.multiple_of(chunk * rows, rows), rows)
        lanes = pl.ds(pl.multiple_of(block * filters, filters), filters)
        buf = self.from_left if right else self.from_right
        send, recv = self.sems[:2] if right else self.sems[2:]
        to = jnp.minimum(me + 1, count - 1) if right else jnp.maximum(me - 1, 0)
        first, passed = [
            functools.partial(
                pltpu.make_async_remote_copy,
                src_ref=src.at[tile, lanes],
                dst_ref=buf.at[tile, lanes],
                send_sem=send.at[block, chunk],
                recv_sem=recv.at[block, chunk],
                device_id={"tensor": to},
                device_id_type=MESH,
            )
            for src in (self.p_ref, buf)
        ]
        return lag, far, tile, lanes, buf, first, passed

    def step(self, step):
        for right in (True, False):
            lag = self.me if right else self.count - 1 - self.me
            number = step - self.spacing * lag
            here = (number >= 0) & (number < self.messages)
            number = jnp.clip(number, 0, self.messages - 1)
            lag, far, tile, lanes, buf, first, passed = self.place(right, number)

            @pl.when(here & (lag == 0))
            def start():
                first().start()

            @pl.when(here & (lag > 0) & (far > lag))
            def middle():
                first().wait_recv()
                buf[tile, lanes] = (
                    buf[tile, lanes].astype(f32) + self.p_ref[tile, lanes].astype(f32)
                ).astype(bf16)
                passed().start()

            @pl.when(here & (lag > 0) & (far == lag))
            def last():
                first().wait_recv()
                self.out_ref[tile, :] += buf[tile, lanes].astype(f32)

    def due(self, chunk):
        return (chunk + self.spacing) * (self.count - 1)

    def finished(self, step, work, after=0):
        each = self.count - 1
        since = step - after - self.spacing * each

        @pl.when((since >= 0) & (since % each == 0) & (since < self.messages))
        def call():
            work(jnp.maximum(since, 0) // each)

    def drain(self):
        def one(number, carry):
            for right in (True, False):
                lag, far, tile, lanes, buf, first, passed = self.place(right, number)

                @pl.when(far > lag)
                def sent():
                    first().wait_send()

            return carry

        lax.fori_loop(0, self.messages, one, 0)


class DpSum:
    def __init__(self, cell, peers, x_first, sems, base):
        self.c, self.x, self.y = cell
        self.peers, self.x_first, self.base = peers, x_first, base
        self.send, self.recv = sems
        self.src = self.half = self.in0 = self.in1 = self.mid = self.in2 = None

    def remote(self, number, src, dst, bit):
        return pltpu.make_async_remote_copy(
            src_ref=src,
            dst_ref=dst,
            send_sem=self.send.at[self.base + number],
            recv_sem=self.recv.at[self.base + number],
            device_id=self.peers[bit],
            device_id_type=MESH,
        )

    def copy0(self):
        return self.remote(0, self.src.at[:, :, 1 - self.c], self.in0, 0)

    def copy1(self):
        if self.x_first:
            return self.remote(1, self.half.at[:, 1 - self.x], self.in1, 1)
        return self.remote(1, self.half.at[1 - self.y], self.in1, 2)

    def copy2(self):
        own = self.y if self.x_first else self.x
        return self.remote(2, self.mid.at[1 - own], self.in2, 2 if self.x_first else 1)

    def finish0(self):
        self.copy0().wait()

        def one(k, carry):
            i, j = k // 2, k % 2
            self.half[i, j] = (self.half[i, j].astype(f32) + self.in0[i, j].astype(f32)).astype(bf16)
            return carry

        lax.fori_loop(0, 4, one, 0)

    def finish1(self):
        self.copy1().wait()

        def one(k, carry):
            kept = self.half[k, self.x] if self.x_first else self.half[self.y, k]
            self.mid[k] = (kept.astype(f32) + self.in1[k].astype(f32)).astype(bf16)
            return carry

        lax.fori_loop(0, 2, one, 0)

    def finish2(self):
        self.copy2().wait()
        own = self.y if self.x_first else self.x
        return self.mid[own].astype(f32) + self.in2[...].astype(f32)


def dp_cell(place):
    cell = [place % 2, (place // 2) % 2, place // 4]
    return cell, [{"dp": place + (1 - 2 * cell[bit]) * 2**bit} for bit in range(3)]


def greet_all(peers):
    barrier = pltpu.get_barrier_semaphore()
    for peer in peers:
        pl.semaphore_signal(barrier, inc=1, device_id=peer, device_id_type=MESH)


def meet_all(peers):
    pl.semaphore_wait(pltpu.get_barrier_semaphore(), len(peers))


def mix_back(d_hidden, trans, gate_pre, previous):
    gate = jax.nn.sigmoid(gate_pre)
    sig = jax.nn.sigmoid(trans)
    act = trans * sig
    d_trans = (d_hidden * gate * (sig * (1.0 + trans * (1.0 - sig)))).astype(bf16)
    d_gate = (d_hidden * (act - previous) * gate * (1.0 - gate)).astype(bf16)
    return d_trans, d_gate, (1.0 - gate) * d_hidden


def weight_grad_piece(piece, whole_ref, d_refs, outs):
    rows = outs[0].shape[-2]
    lanes = pl.ds(pl.multiple_of(piece * rows, rows), rows)
    index = (piece // 4, (piece // 2) % 2, piece % 2)
    for d_ref, out in zip(d_refs, outs):
        out[index] = dot(whole_ref[:, lanes], d_ref[...], 0, 0).astype(bf16)


def highway_back_kernel(count, chunks, reduce, *refs):
    d_h2_ref, t1_ref, g1_ref, h1_ref = refs[:4]
    late_hbm = refs[4:9]
    refs = refs[9:]
    if reduce:
        tr_hbm = refs[:2]
        refs = refs[2:]
    part0_ref, prev0_ref, dt0_ref, dg0_ref, sums_ref = refs[:5]
    refs = refs[5:]
    if reduce:
        tr_outs = refs[2:4]
        hw_refs, tr_half = refs[4:6], refs[6:8]
        in0s, in1s = refs[8:12], refs[12:16]
        mids, in2s = list(refs[:2]) + list(refs[16:18]), refs[18:20]
        dp_sems = refs[20:22]
        refs = refs[22:]
    else:
        hw_refs = refs[:2]
        refs = refs[2:]
    part1_ref, from_left, from_right, d_h1_ref, dt1_ref, dg1_ref = refs[:6]
    t0_ref, g0_ref, h0_ref, whole1_ref, w_ref, late_sem = refs[6:12]
    sems = refs[12:]
    me = lax.axis_index("tensor")
    words, filters = d_h2_ref.shape
    w_hbm = late_hbm[4]
    loads = [
        pltpu.make_async_copy(w_hbm.at[1], w_ref.at[1], late_sem.at[0]),
        pltpu.make_async_copy(late_hbm[3], whole1_ref, late_sem.at[1]),
        pltpu.make_async_copy(w_hbm.at[0], w_ref.at[0], late_sem.at[2]),
        pltpu.make_async_copy(late_hbm[0], t0_ref, late_sem.at[3]),
        pltpu.make_async_copy(late_hbm[1], g0_ref, late_sem.at[4]),
        pltpu.make_async_copy(late_hbm[2], h0_ref, late_sem.at[5]),
    ]
    for copy in loads:
        copy.start()
    items = []
    if reduce:
        cell, peers = dp_cell(lax.axis_index("dp"))
        keep = [
            pltpu.make_async_copy(tr_hbm[k].at[:, :, cell[0]], tr_half[k], late_sem.at[6 + k])
            for k in range(2)
        ]
        for copy in keep:
            copy.start()
    ring = [{"tensor": lax.rem(me + k, count)} for k in range(1, count)]
    everyone = (peers if reduce else []) + ring
    greet_all(everyone)
    sums_ref[...] = jnp.zeros_like(sums_ref)

    def mix(layer, d_h_ref, t_ref, g_ref, h_ref, dt_ref, dg_ref, prev_ref, tile):
        dt, dg, prev = mix_back(d_h_ref[tile, :], t_ref[tile, :], g_ref[tile, :], h_ref[tile, :])
        dt_ref[tile, :] = dt
        dg_ref[tile, :] = dg
        prev_ref[tile, :] = prev
        for j, d in enumerate((dt, dg)):
            sums_ref[2 * layer + j : 2 * layer + j + 1, :] += jnp.sum(
                d.astype(f32), axis=0, keepdims=True
            )

    def products(layer, dt_ref, dg_ref, p_ref, part):
        tile = slice(part * (words // 2), (part + 1) * (words // 2))

        def one(block, carry):
            lanes = pl.ds(pl.multiple_of(block * filters, filters), filters)
            p_ref[tile, lanes] = (
                dot(dt_ref[tile, :], w_ref[layer, 0, lanes, :], 1, 1)
                + dot(dg_ref[tile, :], w_ref[layer, 1, lanes, :], 1, 1)
            ).astype(bf16)
            return carry

        lax.fori_loop(0, count, one, 0)

    rows = words // chunks

    def tile_of(index):
        return pl.ds(pl.multiple_of(index * rows, rows), rows)

    def first(index, carry):
        mix(1, d_h2_ref, t1_ref, g1_ref, h1_ref, dt1_ref, dg1_ref, d_h1_ref, tile_of(index))
        return carry

    def own_part(part):
        tile = slice(part * (words // 2), (part + 1) * (words // 2))
        d_h1_ref[tile, :] += part1_ref[
            tile, pl.ds(pl.multiple_of(me * filters, filters), filters)
        ].astype(f32)

    lax.fori_loop(0, chunks // 2, first, 0)
    loads[0].wait()
    products(1, dt1_ref, dg1_ref, part1_ref, 0)
    own_part(0)
    meet_all(everyone)
    if reduce:
        for k in range(4):
            item = DpSum(cell, peers, k % 2 == 0, dp_sems, 3 * k)
            if k < 2:
                item.src, item.half = hw_refs[k], hw_refs[k].at[:, :, cell[0]]
            else:
                item.src, item.half = tr_hbm[k - 2], tr_half[k - 2]
            item.in0, item.in1, item.mid = in0s[k], in1s[k], mids[k]
            if k >= 2:
                item.in2 = in2s[k - 2]
            items.append(item)
        for item in items[2:]:
            item.copy0().start()
    scatter = LineScatter(
        count, me, chunks, 3, part1_ref, d_h1_ref, from_left, from_right, sems
    )

    def step_fn(step, carry):
        scatter.step(step)

        @pl.when(step == 0)
        def rest():
            lax.fori_loop(chunks // 2, chunks, first, 0)
            products(1, dt1_ref, dg1_ref, part1_ref, 1)
            own_part(1)
            loads[1].wait()

        @pl.when((step > 0) & (step <= 8))
        def grads():
            weight_grad_piece(step - 1, whole1_ref, (dt1_ref, dg1_ref), hw_refs)

        @pl.when(step == 9)
        def late():
            for copy in loads[2:]:
                copy.wait()

        if reduce:

            @pl.when(step == 4)
            def encoder1():
                for copy in keep:
                    copy.wait()
                for item in items[2:]:
                    item.finish0()
                    item.copy1().start()

            @pl.when(step == 9)
            def highway0():
                for item in items[:2]:
                    item.copy0().start()

            @pl.when(step == 15)
            def highway1():
                for item in items[:2]:
                    item.finish0()
                    item.copy1().start()

            @pl.when(step == 20)
            def encoder2():
                for item in items[2:]:
                    item.finish1()
                    item.copy2().start()

        scatter.finished(
            step,
            lambda chunk: mix(
                0, d_h1_ref, t0_ref, g0_ref, h0_ref, dt0_ref, dg0_ref, prev0_ref, tile_of(chunk)
            ),
        )

        @pl.when(step == scatter.due(chunks // 2 - 1) + 1)
        def early():
            products(0, dt0_ref, dg0_ref, part0_ref, 0)

        return carry

    lax.fori_loop(0, scatter.steps, step_fn, 0)
    products(0, dt0_ref, dg0_ref, part0_ref, 1)
    for item in items[:2]:
        item.finish1()
    for item, out in zip(items[2:], tr_outs if reduce else ()):
        out[...] = item.finish2().astype(bf16)
    scatter.drain()


def highway_back(d_h2, t1, g1, h1, t0, g0, h0, whole1, weight, tra, trb, count, cid):
    words, filters = d_h2.shape
    chunks = 8
    reduce = tra is not None
    rows = whole1.shape[1] // 8
    shape = jax.ShapeDtypeStruct
    out_shape = [
        shape(whole1.shape, bf16),
        shape((words, filters), f32),
        shape((words, filters), bf16),
        shape((words, filters), bf16),
        shape((4, filters), f32),
    ]
    operands = [d_h2, t1, g1, h1, t0, g0, h0, whole1, weight]
    in_specs = [VMEM] * 4 + [ANY] * 5
    hw_shape = (2, 2, 2, rows, filters)
    scratch = []
    if reduce:
        operands += [tra, trb]
        in_specs += [ANY] * 2
        tails = [hw_shape[-2:], hw_shape[-2:], tra.shape[-2:], trb.shape[-2:]]
        out_shape += [shape((2,) + tail, bf16) for tail in tails[:2]]
        out_shape += [shape(tail, bf16) for tail in tails[2:]]
        scratch += [pltpu.VMEM(hw_shape, bf16)] * 2
        scratch += [pltpu.VMEM((2, 2) + tail, bf16) for tail in tails[2:]]
        scratch += [pltpu.VMEM((2, 2) + tail, bf16) for tail in tails]
        scratch += [pltpu.VMEM((2,) + tail, bf16) for tail in tails + tails[2:]]
        scratch += [pltpu.VMEM(tail, bf16) for tail in tails[2:]]
        scratch += [DMA((12,))] * 2
    else:
        out_shape += [shape(hw_shape, bf16)] * 2
    scratch += [pltpu.VMEM(whole1.shape, bf16)] * 3
    scratch += [pltpu.VMEM((words, filters), f32)] + [pltpu.VMEM((words, filters), bf16)] * 2
    scratch += [pltpu.VMEM((words, filters), f32)] * 3
    scratch += [pltpu.VMEM(whole1.shape, bf16), pltpu.VMEM(weight.shape, bf16), DMA((8,))]
    scratch += [DMA((count, chunks))] * 4
    return pl.pallas_call(
        functools.partial(highway_back_kernel, count, chunks, reduce),
        out_shape=tuple(out_shape),
        in_specs=in_specs,
        out_specs=tuple([VMEM] * len(out_shape)),
        scratch_shapes=scratch,
        compiler_params=params(cid, 58),
        name="highway_back",
    )(*operands)


class Spread:
    def __init__(self, sems, in_ref, got, mid, out_ref):
        self.dp_count, self.count = out_ref.shape[:2]
        self.sems, self.in_ref, self.got, self.mid, self.out_ref = sems, in_ref, got, mid, out_ref
        self.me = lax.axis_index("tensor")
        self.place = lax.axis_index("dp")

    def remote(self, src, dst, phase, hop, axis, peer):
        send, recv = self.sems[2 * phase : 2 * phase + 2]
        return pltpu.make_async_remote_copy(
            src_ref=src, dst_ref=dst, send_sem=send.at[hop - 1], recv_sem=recv.at[hop - 1],
            device_id={axis: peer}, device_id_type=MESH,
        )

    def scatter(self, hop):
        peer = lax.rem(self.place + hop, self.dp_count)
        return self.remote(self.in_ref.at[peer], self.got.at[hop - 1], 0, hop, "dp", peer)

    def across(self, hop):
        peer = lax.rem(self.me + hop, self.count)
        return self.remote(self.mid.at[self.me], self.mid.at[self.me], 1, hop, "tensor", peer)

    def around(self, hop):
        peer = lax.rem(self.place + hop, self.dp_count)
        return self.remote(self.mid, self.out_ref.at[self.place], 2, hop, "dp", peer)

    def loop(self, fn, stop):
        def one(hop, carry):
            fn(hop)
            return carry

        lax.fori_loop(1, stop, one, 0)

    def first(self):
        self.loop(lambda hop: self.scatter(hop).start(), self.dp_count)

    def second(self):
        self.loop(lambda hop: self.scatter(hop).wait(), self.dp_count)
        total = lax.fori_loop(
            0,
            self.dp_count - 1,
            lambda k, acc: acc + self.got[k].astype(f32),
            self.in_ref[self.place].astype(f32),
        )
        self.mid[self.me] = total.astype(bf16)
        self.loop(lambda hop: self.across(hop).start(), self.count)

    def third(self):
        self.loop(lambda hop: self.across(hop).wait(), self.count)
        self.loop(lambda hop: self.around(hop).start(), self.dp_count)
        self.out_ref[self.place] = self.mid[...]

    def finish(self):
        self.loop(lambda hop: self.around(hop).wait(), self.dp_count)


def early_parts(rows):
    start = 0
    for source, (count, width) in enumerate(rows):
        for block in range(-(-width // LANES)):
            yield source, block, start, count, min(LANES, width - block * LANES)
            start += count


EARLY = ((4, 512), (1, 576), (10, 768))


def pack_early(ref, *sources):
    ref[...] = jnp.zeros_like(ref)
    for source, block, start, count, width in early_parts(EARLY):
        value = sources[source][0:count, block * LANES : block * LANES + width]
        for k in range(count):
            place = start + k
            ref[place // 16, place % 16 : place % 16 + 1, 0:width] = value[k : k + 1]


def unpack_early(ref, hwb_out, vec_out, upb_out, qv_out):
    for t in range(ref.shape[1]):
        for source, block, start, count, width in early_parts(EARLY):
            for k in range(count):
                place = start + k
                row = ref[place // 16, t, :, :].astype(f32)[place % 16 : place % 16 + 1, 0:width]
                lane = block * LANES
                if source == 0:
                    hwb_out[k : k + 1, t * 512 + lane : t * 512 + lane + width] = row
                elif source == 2 and k == 9:
                    upb_out[:, t * 768 + lane : t * 768 + lane + width] = row
                elif source == 2 and t == 0:
                    vec_out[k : k + 1, lane : lane + width] = row
                elif source == 1:
                    for out, low in ((0, 0), (1, 384)):
                        left, right = max(lane, low), min(lane + width, low + 192)
                        if left < right:
                            place_at = t * 192 + left - low
                            qv_out[out : out + 1, place_at : place_at + right - left] = row[
                                :, left - lane : right - lane
                            ]


def conv_backward_kernel(count, chars, cuts, *refs):
    (ids_ref, x_hbm, p_hbm, cw_ref, mask_ref, off_ref, log_ref, prev_ref, part_ref, whole_hbm,
     dt_ref, dg_ref) = refs[:12]
    refs = refs[12:]
    if cuts:
        mids_in = refs[:2]
        hb_sums, proj_sums, row_sums = refs[2:5]
        hw_out, convw_out, convb_out, table_out, hwb_out, vec_out, upb_out, qv_out = refs[5:13]
        dw_ref, table_ref, hw_a, hw_b = refs[13:17]
        in0s, in1s, mids, in2s = refs[17:19], refs[19:21], refs[21:23], refs[23:27]
        dp_sems = refs[27:29]
        spreads = [Spread(refs[33 + 10 * k : 39 + 10 * k], *refs[29 + 10 * k : 33 + 10 * k])
                   for k in range(2)]
        refs = refs[49:]
    else:
        dw_ref, table_ref, hw_a, hw_b = refs[:4]
        refs = refs[4:]
    (pad_ref, stage_ref, grad_ref, from_left, from_right, x_buf, p_buf, whole_ref, wb_ref,
     load_sem, whole_sem) = refs[:11]
    line_sems = refs[11:]
    me = lax.axis_index("tensor")
    words, filters = log_ref.shape
    tiles = words // WORD_TILE
    padded = ids_ref.shape[1] // WORD_TILE

    def load(index):
        slot = index % 2
        return [
            pltpu.make_async_copy(hbm.at[index], buf.at[slot], load_sem.at[k, slot])
            for k, (buf, hbm) in enumerate(((x_buf, x_hbm), (p_buf, p_hbm)))
        ]

    whole_copy = pltpu.make_async_copy(whole_hbm, whole_ref, whole_sem)
    whole_copy.start()
    for index in range(2):
        for copy in load(index):
            copy.start()
    ring = [{"tensor": lax.rem(me + k, count)} for k in range(1, count)]
    items = []
    if cuts:
        place = lax.axis_index("dp")
        dp_count = spreads[0].dp_count
        cell, dp_peers = dp_cell(place)
        ring += [{"dp": lax.rem(place + k, dp_count)} for k in range(1, dp_count)]
        for k in range(4):
            item = DpSum(cell, dp_peers, k % 2 == 0, dp_sems, 3 * k)
            item.in2 = in2s[k]
            if k < 2:
                item.src = (hw_a, hw_b)[k]
                item.half = item.src.at[:, :, cell[0]]
                item.in0, item.in1, item.mid = in0s[k], in1s[k], mids[k]
            else:
                item.mid = mids_in[k - 2]
            items.append(item)
        pack_early(spreads[0].in_ref, hb_sums, proj_sums, row_sums)
    greet_all(ring)
    taps = cw_ref.shape[0]
    wb_ref[...] = jnp.zeros_like(wb_ref)
    wb_ref[0:taps, :] = (cw_ref[...].astype(f32) * mask_ref[...]).astype(bf16)
    dw_ref[...] = jnp.zeros_like(dw_ref)
    table_ref[...] = jnp.zeros_like(table_ref)
    pad_ref[...] = jnp.zeros_like(pad_ref)
    grad_ref[...] = prev_ref[...] + part_ref[
        :, pl.ds(pl.multiple_of(me * filters, filters), filters)
    ].astype(f32)
    meet_all(ring)
    for item in items[2:]:
        item.copy2().start()
    if cuts:
        spreads[0].first()
    chunks = line_sems[0].shape[1]
    per = words // chunks // WORD_TILE
    scatter = LineScatter(
        count, me, chunks, 3, part_ref, grad_ref, from_left, from_right, line_sems
    )
    group = lax.broadcasted_iota(jnp.int32, (1, WORD_TILE, LANES), 2) // 16
    vocab = lax.broadcasted_iota(jnp.int32, (table_ref.shape[0], padded * WORD_TILE), 0)

    def tile_step(index):
        slot = index % 2
        for copy in load(index):
            copy.wait()
        tile = pl.ds(pl.multiple_of(index * WORD_TILE, WORD_TILE), WORD_TILE)
        pooled = log_ref[tile, :] - off_ref[...]
        sig = jax.nn.sigmoid(pooled)
        grad = grad_ref[tile, :] * (sig * (1.0 + pooled * (1.0 - sig)))
        d_conv = (grad[None] * p_buf[slot].astype(f32)).astype(bf16)
        d_conv = d_conv.reshape(chars * WORD_TILE, filters)
        dw_ref[...] += dot(x_buf[slot], d_conv, 0, 0)
        d_win = dot(d_conv, wb_ref[...], 1, 1).astype(bf16)
        pad_ref[6 : 6 + chars] = d_win.reshape(chars, WORD_TILE, LANES)
        d_emb = pad_ref[6 : 6 + padded]
        for tap in range(1, 7):
            d_emb = jnp.where(group == tap, pad_ref[6 - tap : 6 - tap + padded], d_emb)
        one_hot = jnp.where(vocab == ids_ref[pl.ds(index, 1), :], 1.0, 0.0).astype(bf16)
        table_ref[...] += dot(one_hot, d_emb.reshape(padded * WORD_TILE, LANES), 1, 0)

        @pl.when(index + 2 < tiles)
        def more():
            for copy in load(index + 2):
                copy.start()

    def step_fn(step, carry):
        scatter.step(step)

        @pl.when(step == 0)
        def whole():
            whole_copy.wait()

        @pl.when(step < 8)
        def grads():
            weight_grad_piece(step, whole_ref, (dt_ref, dg_ref), (hw_a, hw_b))

        if cuts:

            @pl.when(step == 4)
            def early2():
                spreads[0].second()

            @pl.when(step == 7)
            def early3():
                spreads[0].third()

            @pl.when(step == 8)
            def start0():
                for item in items[:2]:
                    item.copy0().start()

            @pl.when(step == cuts[0])
            def start1():
                for item in items[:2]:
                    item.finish0()
                    item.copy1().start()

            @pl.when(step == cuts[1])
            def start2():
                for item in items[:2]:
                    item.finish1()
                    item.copy2().start()

        for k in range(per):
            scatter.finished(step, lambda chunk: tile_step(chunk * per + k), k)
        return carry

    lax.fori_loop(0, scatter.due(chunks - 1) + per, step_fn, 0)
    if cuts:
        late = spreads[1]
        taps = table_ref[:, 0:16]
        for tap in range(1, 7):
            taps += table_ref[:, 16 * tap : 16 * tap + 16]
        stage_ref[...] = jnp.zeros_like(stage_ref)
        table_ref[:, 0:16] = taps
        for i in range(8):
            late.in_ref[i, :, 0:filters] = dw_ref[16 * i : 16 * i + 16, :].astype(bf16)
            for k in range(3):
                size = 16 if k < 2 else 1
                stage_ref[0:size, 16 * k : 16 * k + 16] = table_ref[
                    33 * i + 16 * k : 33 * i + 16 * k + size, 0:16
                ]
            late.in_ref[i, :, filters:] = stage_ref[...].astype(bf16)
        late.first()
        spreads[0].finish()
        unpack_early(spreads[0].out_ref, hwb_out, vec_out, upb_out, qv_out)
        late.second()
        late.third()
        for k in range(4):
            hw_out[k // 2, k % 2] = items[k].finish2().astype(bf16)
        late.finish()
        for t in range(count):
            lanes = slice(t * filters, (t + 1) * filters)
            for i in range(7):
                convw_out[16 * i : 16 * i + 16, lanes] = late.out_ref[i, t, :, 0:filters]
            convb_out[:, lanes] = late.out_ref[7, t, :, 0:filters].astype(f32)[0:1]
        for i in range(8):
            total = late.out_ref[i, 0, :, filters:].astype(f32)
            for t in range(1, count):
                total += late.out_ref[i, t, :, filters:].astype(f32)
            for k in range(3):
                size = 16 if k < 2 else 1
                table_out[33 * i + 16 * k : 33 * i + 16 * k + size, :] = total[
                    0:size, 16 * k : 16 * k + 16
                ]
    scatter.drain()


def conv_backward(ids, x, p, w, mask, off, logs, prev, part, whole, dt, dg, rest, count, cid):
    words, filters = logs.shape
    chars = p.shape[1]
    chunks = 8
    shape = jax.ShapeDtypeStruct
    hw_shape = (2, 2, 2, whole.shape[1] // 8, filters)
    operands = [ids, x, p, w, mask, off, logs, prev, part, whole, dt, dg] + list(rest)
    in_specs = [VMEM, ANY, ANY] + [VMEM] * 6 + [ANY, VMEM, VMEM] + [VMEM] * len(rest)
    sums = [(LANES, filters), (264, LANES)]
    scratch = []
    cuts = None
    if rest:
        cuts = (17, 28)
        tail = hw_shape[-2:]
        features = rest[-1].shape[-1]
        out_shape = [
            shape((2, 2) + tail, bf16),
            shape((112, count * filters), bf16),
            shape((1, count * filters), f32),
            shape((264, 16), f32),
            shape((4, count * filters), f32),
            shape((9, features), f32),
            shape((1, count * features), f32),
            shape((2, features), f32),
        ]
        scratch += [pltpu.VMEM(shape_of, f32) for shape_of in sums]
        scratch += [pltpu.VMEM(hw_shape, bf16)] * 2
        scratch += [pltpu.VMEM((2, 2) + tail, bf16)] * 2
        scratch += [pltpu.VMEM((2,) + tail, bf16)] * 4
        scratch += [pltpu.VMEM(tail, bf16)] * 4
        scratch += [DMA((12,))] * 2
        for small, kind in (((16, LANES), f32), ((16, filters + LANES), bf16)):
            scratch += [
                pltpu.VMEM((8,) + small, kind),
                pltpu.VMEM((7,) + small, kind),
                pltpu.VMEM((count,) + small, bf16),
                pltpu.VMEM((8, count) + small, bf16),
            ]
            scratch += [DMA((7,))] * 2 + [DMA((count - 1,))] * 2 + [DMA((7,))] * 2
    else:
        out_shape = [shape(shape_of, f32) for shape_of in sums] + [shape(hw_shape, bf16)] * 2
    scratch += [
        pltpu.VMEM((68, WORD_TILE, LANES), bf16),
        pltpu.VMEM((16, LANES), f32),
        pltpu.VMEM((words, filters), f32),
        pltpu.VMEM(part.shape, bf16),
        pltpu.VMEM(part.shape, bf16),
        pltpu.VMEM((2,) + x.shape[1:], bf16),
        pltpu.VMEM((2,) + p.shape[1:], bf16),
        pltpu.VMEM(whole.shape, bf16),
        pltpu.VMEM((LANES, filters), bf16),
        DMA((2, 2)),
        DMA,
    ]
    scratch += [DMA((count, chunks))] * 4
    return pl.pallas_call(
        functools.partial(conv_backward_kernel, count, chars, cuts),
        out_shape=tuple(out_shape),
        in_specs=in_specs,
        out_specs=tuple([VMEM] * len(out_shape)),
        scratch_shapes=scratch,
        compiler_params=params(cid, 58),
        name="conv_backward",
    )(*operands)


def small_kernel(dp_count, count, in_ref, out_ref, got, mid, *sems):
    me = lax.axis_index("tensor")
    place = lax.axis_index("dp")
    barrier = pltpu.get_barrier_semaphore()

    def greet(hop, carry):
        peer = lax.rem(place + hop, dp_count)
        pl.semaphore_signal(barrier, inc=1, device_id={"dp": peer}, device_id_type=MESH)
        return carry

    lax.fori_loop(1, dp_count, greet, 0)
    for hop in range(1, count):
        pl.semaphore_signal(
            barrier, inc=1, device_id={"tensor": lax.rem(me + hop, count)}, device_id_type=MESH
        )
    pl.semaphore_wait(barrier, dp_count + count - 2)
    spread = Spread(sems, in_ref, got, mid, out_ref)
    spread.first()
    spread.second()
    spread.third()
    spread.finish()


def sum_small(packed, dp_count, count, cid):
    shape = packed.shape[1:]
    return pl.pallas_call(
        functools.partial(small_kernel, dp_count, count),
        out_shape=jax.ShapeDtypeStruct((dp_count, count) + shape, bf16),
        in_specs=[VMEM],
        out_specs=VMEM,
        scratch_shapes=[
            pltpu.VMEM((dp_count - 1,) + shape, f32),
            pltpu.VMEM((count,) + shape, bf16),
            DMA((dp_count - 1,)),
            DMA((dp_count - 1,)),
            DMA((count - 1,)),
            DMA((count - 1,)),
            DMA((dp_count - 1,)),
            DMA((dp_count - 1,)),
        ],
        compiler_params=params(cid, 32),
        name="sum_small",
    )(packed)


def finish_kernel(units, three, *refs):
    (enc, table, conv_w, mask, conv_b, hw, hw_b, rows, qv, up_b, tr_a, tr_b) = refs[:12]
    (enc_out, table_out, conv_w_out, conv_b_out, hw_out, hw_b_out, proj_out, proj_b_out, gain_out,
     shift_out, qkv_out, qv_out, o_out, o_b_out, up_out, up_b_out, down_out, down_b_out) = refs[12:]
    filters = mask.shape[1]
    enc_out[0] = enc[...]
    table_out[...] = table[...].T[:, 0 : table_out.shape[1]]
    for start in range(0, conv_w.shape[1], filters):
        lanes = slice(start, start + filters)
        conv_w_out[:, lanes] = conv_w[:, lanes].astype(f32) * mask[...]
    conv_b_out[...] = conv_b[...].reshape(conv_b_out.shape)
    for layer in range(2):
        hw_b_out[layer] = hw_b[2 * layer : 2 * layer + 2, :]
        for j in range(2):
            hw_out[layer, j] = hw[layer, j].astype(f32)
    for k, out in enumerate((proj_b_out, o_b_out, down_b_out)):
        out[...] = rows[k : k + 1, :].reshape(out.shape)
    gain_out[...] = rows[3:6, :]
    shift_out[...] = rows[6:9, :]
    qv_out[...] = qv[...]
    up_b_out[...] = up_b[...].reshape(up_b_out.shape)
    up_out[...] = tr_a[:, 0:units].astype(f32)
    down_out[...] = tr_a[:, units:].astype(f32)
    proj_out[...] = tr_b[:, 0:filters].astype(f32)
    hidden = three // 3
    qkv = tr_b[:, filters : filters + three].astype(f32)
    for k in range(3):
        qkv_out[k] = qkv[:, k * hidden : (k + 1) * hidden]
    o_out[...] = tr_b[:, 1152 : 1152 + hidden].astype(f32).T


def finish(encoded, table, conv_w, mask, conv_b, hw, hw_b, rows, qv, up_b, tr_a, tr_b, vocab,
           units, three):
    features, depth, filters = rows.shape[1], tr_a.shape[0], mask.shape[1]
    shapes = [
        (table.shape[1], vocab), conv_w.shape, (conv_w.shape[1],), hw.shape,
        (2, 2, hw_b.shape[1]), (depth, filters), (features,), (3, features), (3, features),
        (3, depth, three // 3), qv.shape, (three // 3, depth), (features,), (depth, units),
        (up_b.shape[1],), (depth, tr_a.shape[1] - units), (features,),
    ]
    (encoded, table, conv_w, conv_b, hw, hw_b, proj, proj_b, gain, shift, qkv, qv, o, o_b, up, up_b,
     down, down_b) = pl.pallas_call(
        functools.partial(finish_kernel, units, three),
        out_shape=tuple(
            [jax.ShapeDtypeStruct((1,) + encoded.shape, bf16)]
            + [jax.ShapeDtypeStruct(shape, f32) for shape in shapes]
        ),
        in_specs=[VMEM] * 12,
        out_specs=(VMEM,) * 18,
        compiler_params=pltpu.CompilerParams(vmem_limit_bytes=32 * MIB),
        name="finish",
    )(encoded, table, conv_w, mask, conv_b, hw, hw_b, rows, qv, up_b, tr_a, tr_b)
    return (
        jnp.transpose(encoded, (1, 0, 2)), table.T, conv_w, conv_b, hw, hw_b, proj.T, proj_b, gain,
        shift, jnp.transpose(qkv, (1, 0, 2)), qv, o, o_b, up, up_b, down.T, down_b,
    )


def body(
    char_ids,
    seq_lengths,
    char_table,
    conv_weight,
    conv_bias,
    highway_weight,
    highway_bias,
    proj_weight,
    proj_bias,
    norm_gain,
    norm_shift,
    qkv_weight,
    qv_bias,
    output_projection_weight,
    out_bias,
    up_weight,
    up_bias,
    down_weight,
    down_bias,
    out_grad,
):
    words, nseq, chars = char_ids.shape
    assert nseq == 1
    count = lax.axis_size("tensor")
    dp_count = lax.axis_size("dp")
    rank = lax.axis_index("tensor")
    vocab, char_dim = char_table.shape
    taps_dim, filters = conv_weight.shape
    features = proj_weight.shape[1]
    heads = qkv_weight.shape[2] // HEAD_DIM

    tiles = words // WORD_TILE
    ids_tiles = jnp.swapaxes(char_ids[:, 0].reshape(tiles, WORD_TILE, chars), 1, 2)
    ids_tiles = ids_tiles.reshape(tiles, chars * WORD_TILE)
    pattern = np.zeros((chars, WORD_TILE, LANES), np.float32)
    pattern[:, :, taps_dim] = 1.0
    for k in range(1, 7):
        pattern[chars - k, :, taps_dim + k] = 1.0

    widths = filter_widths(filters)
    off = jnp.asarray(np.log((chars - widths + 1).astype(np.float64)).astype(np.float32))[None]
    tap_of = np.arange(taps_dim)[:, None] // char_dim
    taps_mask = tap_of < widths[None]
    mask = jnp.asarray(taps_mask, f32)
    ends = np.zeros((LANES - taps_dim, filters), np.float32)
    ends[1:7] = np.where(widths[None] > np.arange(1, 7)[:, None], big_neg, 0.0)

    logs, whole0, whole1, top, x_tiles, p_tiles, t0, g0, h0, t1, g1, h1 = embed_forward(
        ids_tiles,
        char_table.T,
        jnp.asarray(pattern, bf16),
        (conv_weight, conv_bias, mask, jnp.asarray(ends)),
        off,
        highway_bias,
        highway_weight,
        count,
        chars,
        1,
    )
    encoded, d_hidden, tr_a, tr_b, row_sums, proj_sums = encoder(
        top,
        (
            proj_weight,
            jnp.transpose(qkv_weight, (1, 2, 0)).reshape(-1, features),
            output_projection_weight,
            up_weight,
            down_weight,
        ),
        (proj_bias, out_bias, down_bias, up_bias, norm_gain, norm_shift, qv_bias),
        out_grad[:, 0],
        seq_lengths,
        count,
        4,
    )

    back_args = (d_hidden, t1, g1, h1, t0, g0, h0, whole1, highway_weight)
    conv_args = (ids_tiles, x_tiles, p_tiles, conv_weight, mask, off, logs)
    three = 3 * heads * HEAD_DIM
    units = up_weight.shape[1]
    if dp_count == 8 and (features // dp_count) % 16 == 0:
        part0, prev0, dt0, dg0, hw_bias_part, mid_a, mid_b, tr_a, tr_b = highway_back(
            *back_args, tr_a, tr_b, count, 9
        )
        (hw_w_grad, conv_w_grad, conv_b_grad, table_grad, hw_b_grad, rows, up_b_grad,
         qv_grad) = conv_backward(
            *conv_args, prev0, part0, whole0, dt0, dg0,
            (mid_a, mid_b, hw_bias_part, proj_sums, row_sums), count, 10,
        )
        return finish(
            encoded, table_grad, conv_w_grad, mask, conv_b_grad, hw_w_grad, hw_b_grad, rows,
            qv_grad, up_b_grad, tr_a, tr_b, vocab, units, three,
        )
    else:
        part0, prev0, dt0, dg0, hw_bias_part, *hw1 = highway_back(*back_args, None, None, count, 9)
        d_w_all, table_all, *hw0 = conv_backward(
            *conv_args, prev0, part0, whole0, dt0, dg0, (), count, 10
        )
        hw_sum = jnp.stack([part.reshape(-1, filters) for part in hw0 + hw1])
        hw_sum = lax.psum_scatter(hw_sum, "dp", scatter_dimension=1, tiled=True).astype(f32)
        tr_a, tr_b = [
            lax.psum_scatter(
                part.reshape(features, -1), "dp", scatter_dimension=0, tiled=True
            ).astype(f32)
            for part in (tr_a, tr_b)
        ]
        hw_w_grad = hw_sum.reshape(2, 2, -1, filters)
        pieces = [d_w_all[: taps_dim + 1], table_all, hw_bias_part, proj_sums, row_sums[:10]]
        flat = jnp.concatenate([part.reshape(-1) for part in pieces])
        width = -(-flat.size // (dp_count * 16 * LANES)) * LANES
        flat = jnp.pad(flat, (0, dp_count * 16 * width - flat.size))
        summed = sum_small(flat.reshape(dp_count, 16, width), dp_count, count, 11)
        summed = jnp.swapaxes(summed, 0, 1).reshape(count, -1).astype(f32)
        conv_size, table_size = pieces[0].size, table_all.size
        conv_all = summed[:, :conv_size].reshape(count, taps_dim + 1, filters)
        conv_all = jnp.swapaxes(conv_all, 0, 1)
        conv_w_grad = conv_all[:taps_dim].reshape(taps_dim, -1)
        conv_b_grad = conv_all[taps_dim].reshape(-1)
        table_all = jnp.sum(summed[:, conv_size : conv_size + table_size], axis=0)
        table_all = table_all.reshape(-1, LANES)
        early = summed[:, conv_size + table_size :]
        table_grad = jnp.sum(
            table_all[:vocab, :taps_dim].reshape(vocab, taps_dim // char_dim, char_dim), axis=1
        )
        hw_b_grad = jnp.swapaxes(early[:, : 4 * filters].reshape(count, 4, filters), 0, 1)
        early = early[:, 4 * filters :]
        qv_grad = jnp.swapaxes(early[:, :three].reshape(count, 3, -1), 0, 1)[::2].reshape(2, -1)
        rows = early[:, three : three + 10 * features].reshape(count, 10, features)
        up_b_grad = rows[:, 9].reshape(-1)
        rows = rows[0]

    conv_w_grad = jnp.where(np.tile(taps_mask, (1, count)), conv_w_grad, 0.0)
    hw_b_grad = hw_b_grad.reshape(2, 2, -1)
    up_w_grad = tr_a[:, :units]
    down_w_grad = tr_a[:, units:].T
    proj_w_grad = tr_b[:, :filters].T
    qkv_w_grad = tr_b[:, filters : filters + three].reshape(-1, 3, heads * HEAD_DIM)
    out_w_grad = tr_b[:, 1152 : 1152 + heads * HEAD_DIM].T
    proj_b_grad, out_b_grad, down_b_grad = rows[0], rows[1], rows[2]
    gain_grad, shift_grad = rows[3:6], rows[6:9]
    return (
        encoded[:, None],
        table_grad,
        conv_w_grad,
        conv_b_grad,
        hw_w_grad,
        hw_b_grad,
        proj_w_grad,
        proj_b_grad,
        gain_grad,
        shift_grad,
        qkv_w_grad,
        qv_grad,
        out_w_grad,
        out_b_grad,
        up_w_grad,
        up_b_grad,
        down_w_grad,
        down_b_grad,
    )


def solution(mesh):
    return jax.shard_map(
        body,
        mesh=mesh,
        in_specs=(
            P(None, "dp", None),
            P("dp"),
            P(),
            P(None, "tensor"),
            P("tensor"),
            P(None, None, None, "tensor"),
            P(None, None, "tensor"),
            P("tensor", None),
            P(),
            P(),
            P(),
            P(None, None, "tensor"),
            P(None, "tensor"),
            P("tensor", None),
            P(),
            P(None, "tensor"),
            P("tensor"),
            P("tensor", None),
            P(),
            P("tensor", "dp", None),
        ),
        out_specs=(
            P("tensor", "dp", None),
            P(),
            P(),
            P(),
            P(None, None, "dp", "tensor"),
            P(),
            P("tensor", "dp"),
            P(),
            P(),
            P(),
            P("dp", None, "tensor"),
            P(),
            P("tensor", "dp"),
            P(),
            P("dp", "tensor"),
            P(),
            P("tensor", "dp"),
            P(),
        ),
        check_vma=False,
    )
```

```python
import functools
import math

import jax
import jax.numpy as jnp
import numpy as np
from jax import lax
from jax.experimental import pallas as pl
from jax.experimental.pallas import tpu as pltpu
from jax.sharding import PartitionSpec as P

HEAD_DIM = 64
WORD_TILE = 32
LANES = 128

norm_eps = 1e-06
big_neg = -1e30
f32 = jnp.float32
bf16 = jnp.bfloat16
MESH = pl.DeviceIdType.MESH
VMEM = pl.BlockSpec(memory_space=pltpu.VMEM)
ANY = pl.BlockSpec(memory_space=pl.ANY)
DMA = pltpu.SemaphoreType.DMA
MIB = 1 << 20


def params(cid, vmem):
    return pltpu.CompilerParams(
        collective_id=cid, has_side_effects=True, vmem_limit_bytes=vmem * MIB
    )


def width_counts(block):
    unit = block // 64
    return [unit, unit, 2 * unit, 4 * unit, 8 * unit, 16 * unit, 32 * unit]


def filter_widths(block):
    return np.concatenate(
        [np.full((n,), i + 1, np.int32) for i, n in enumerate(width_counts(block))]
    )


def dot(a, b, ca, cb):
    return lax.dot_general(a, b, (((ca,), (cb,)), ((), ())), preferred_element_type=f32)


def line_greet(me, count):
    barrier = pltpu.get_barrier_semaphore()
    for there, ok in ((me - 1, me > 0), (me + 1, me < count - 1)):

        @pl.when(ok)
        def greet():
            pl.semaphore_signal(barrier, inc=1, device_id={"tensor": there}, device_id_type=MESH)


def line_meet(me, count):
    pl.semaphore_wait(
        pltpu.get_barrier_semaphore(), jnp.minimum(me, 1) + jnp.minimum(count - 1 - me, 1)
    )


def line_copy(view, me, count, right, block, chunk, sems):
    send, recv = sems[:2] if right else sems[2:]
    to = jnp.minimum(me + 1, count - 1) if right else jnp.maximum(me - 1, 0)
    ref = view(block, chunk)
    return pltpu.make_async_remote_copy(
        src_ref=ref,
        dst_ref=ref,
        send_sem=send.at[block, chunk],
        recv_sem=recv.at[block, chunk],
        device_id={"tensor": to},
        device_id_type=MESH,
    )


def gather_step(view, step, chunks, me, count, sems, spacing=1):
    for hop in range(count):
        chunk = step - spacing * hop
        here = (chunk >= 0) & (chunk < chunks)
        safe = jnp.clip(chunk, 0, chunks - 1)
        for right in (True, False):
            block = me - hop if right else me + hop
            there = (block >= 0) & (block < count)
            block = jnp.clip(block, 0, count - 1)
            more = me < count - 1 if right else me > 0
            copy = functools.partial(line_copy, view, me, count, right, block, safe, sems)

            @pl.when(here & there)
            def pass_on():
                if hop > 0:
                    copy().wait_recv()

                @pl.when(more)
                def send():
                    copy().start()


def gather_drain(view, chunks, me, count, sems):
    def one(chunk, carry):
        for hop in range(count):
            for right in (True, False):
                block = me - hop if right else me + hop
                there = (block >= 0) & (block < count)
                block = jnp.clip(block, 0, count - 1)
                more = me < count - 1 if right else me > 0
                copy = functools.partial(line_copy, view, me, count, right, block, chunk, sems)

                @pl.when(there & more)
                def sent():
                    copy().wait_send()

        return carry

    lax.fori_loop(0, chunks, one, 0)


def embed_forward_kernel(count, chars, *refs):
    (ids_ref, chars_ref, pattern_ref, cw_ref, cb_ref, mask_ref, ends_ref, off_ref, bias_ref,
     hw_hbm) = refs[:10]
    log_ref, whole0_ref, whole1_ref, top_ref, x_hbm, p_hbm = refs[10:16]
    kept = refs[16:22]
    y_buf, x_buf, p_buf, hw_ref, table_ref, w_ref, hb_ref, keep_sem, late_sem = refs[22:31]
    bufs = refs[31:37]
    sems0, sems1 = refs[37:41], refs[41:45]
    t_refs, g_refs, h_refs = (bufs[0], bufs[3]), (bufs[1], bufs[4]), (bufs[2], bufs[5])
    wholes = (whole0_ref, whole1_ref)
    me = lax.axis_index("tensor")
    line_greet(me, count)
    words, filters = log_ref.shape
    tiles = words // WORD_TILE
    half = words // 2
    padded = ids_ref.shape[1] // WORD_TILE
    own = pl.ds(pl.multiple_of(me * filters, filters), filters)
    loads = [
        pltpu.make_async_copy(hw_hbm.at[layer], hw_ref.at[layer], late_sem.at[layer])
        for layer in range(2)
    ]
    for copy in loads:
        copy.start()
    stores = [
        pltpu.make_async_copy(buf, out, late_sem.at[2 + k])
        for k, (buf, out) in enumerate(zip(bufs, kept))
    ]
    y_buf[...] = jnp.zeros_like(y_buf)
    table_ref[...] = jnp.zeros_like(table_ref)
    depth, vocab_size = chars_ref.shape
    for tap in range(7):
        table_ref[depth * tap : depth * tap + depth, 0:vocab_size] = chars_ref[...]
    for layer in range(2):
        hb_ref[2 * layer : 2 * layer + 2, :] = bias_ref[layer].astype(f32)
    taps = cw_ref.shape[0]
    w_ref[0:taps, :] = (cw_ref[...].astype(f32) * mask_ref[...]).astype(bf16)
    first = lax.broadcasted_iota(jnp.int32, ends_ref.shape, 0) == 0
    bias = cb_ref[...].astype(f32).reshape(1, filters)
    w_ref[taps:, :] = jnp.where(first, bias, ends_ref[...]).astype(bf16)
    line_meet(me, count)

    def view_of(whole):
        def view(block, chunk):
            return whole.at[
                pl.ds(pl.multiple_of(chunk * WORD_TILE, WORD_TILE), WORD_TILE),
                pl.ds(pl.multiple_of(block * filters, filters), filters),
            ]

        return view

    views = [view_of(whole) for whole in wholes]

    def keep(index):
        slot = index % 2
        return [
            pltpu.make_async_copy(buf.at[slot], hbm.at[index], keep_sem.at[k, slot])
            for k, (buf, hbm) in enumerate(((x_buf, x_hbm), (p_buf, p_hbm)))
        ]

    group = lax.broadcasted_iota(jnp.int32, (1, WORD_TILE, LANES), 2) // 16
    vocab = lax.broadcasted_iota(jnp.int32, (table_ref.shape[1], padded * WORD_TILE), 0)

    def tile_step(index):
        slot = index % 2

        @pl.when(index >= 2)
        def free():
            for copy in keep(index - 2):
                copy.wait()

        one_hot = jnp.where(vocab == ids_ref[pl.ds(index, 1), :], 1.0, 0.0).astype(bf16)
        found = dot(table_ref[...], one_hot, 1, 0).astype(bf16).T
        y_buf[0:padded] = found.reshape(padded, WORD_TILE, LANES)
        value = jnp.where(group == 7, pattern_ref[...], y_buf[0:chars])
        for tap in range(1, 7):
            value = jnp.where(group == tap, y_buf[tap : chars + tap], value)
        x2 = value.reshape(chars * WORD_TILE, LANES)
        x_buf[slot] = x2
        conv = dot(x2, w_ref[...], 1, 0).reshape(chars, WORD_TILE, filters)
        top = jnp.max(conv, axis=0)
        exps = jnp.exp(conv - top[None])
        sums = jnp.sum(exps, axis=0)
        p_buf[slot] = (exps * (1.0 / sums)[None]).astype(bf16)
        for copy in keep(index):
            copy.start()
        tile = pl.ds(pl.multiple_of(index * WORD_TILE, WORD_TILE), WORD_TILE)
        total = top + jnp.log(sums)
        log_ref[tile, :] = total
        pooled = total - off_ref[...]
        hidden = pooled * jax.nn.sigmoid(pooled)
        h_refs[0][tile, :] = hidden
        whole0_ref[tile, own] = hidden.astype(bf16)

    def layer_step(layer, part):
        rows = slice(part * half, (part + 1) * half)
        for j, out in enumerate((t_refs[layer], g_refs[layer])):
            bias = hb_ref[2 * layer + j : 2 * layer + j + 1, :]
            out[rows, :] = dot(wholes[layer][rows, :], hw_ref[layer, j], 1, 0) + bias

        def mix(index, carry):
            tile = pl.ds(pl.multiple_of(part * half + index * WORD_TILE, WORD_TILE), WORD_TILE)
            trans = t_refs[layer][tile, :]
            gate = jax.nn.sigmoid(g_refs[layer][tile, :])
            hidden = gate * (trans * jax.nn.sigmoid(trans)) + (1.0 - gate) * h_refs[layer][tile, :]
            if layer == 0:
                h_refs[1][tile, :] = hidden
                whole1_ref[tile, own] = hidden.astype(bf16)
            else:
                top_ref[tile, :] = hidden.astype(bf16)
            return carry

        lax.fori_loop(0, half // WORD_TILE, mix, 0)

    spacing = 2
    fill = spacing * (count - 1)
    shift = tiles // 2 + fill
    last = shift + tiles + fill

    def step_fn(step, carry):
        @pl.when(step < tiles)
        def convolve():
            tile_step(step)

        @pl.when(step < tiles + fill)
        def first_gather():
            gather_step(views[0], step, tiles, me, count, sems0, spacing)

        @pl.when(step == shift)
        def first_half():
            loads[0].wait()
            layer_step(0, 0)

        @pl.when(step == shift + tiles // 2)
        def second_half():
            layer_step(0, 1)
            for copy in stores[:3]:
                copy.start()

        @pl.when(step >= shift)
        def second_gather():
            gather_step(views[1], step - shift, tiles, me, count, sems1, spacing)

        @pl.when(step == 2 * shift - 1)
        def third_half():
            loads[1].wait()
            layer_step(1, 0)

        return carry

    lax.fori_loop(0, last, step_fn, 0)
    layer_step(1, 1)
    for copy in stores[3:]:
        copy.start()
    for index in (tiles - 2, tiles - 1):
        for copy in keep(index):
            copy.wait()
    for sems, view in zip((sems0, sems1), views):
        gather_drain(view, tiles, me, count, sems)
    for copy in stores:
        copy.wait()


def embed_forward(ids, table, pattern, conv, off, bias, weight, count, chars, cid):
    filters = conv[0].shape[1]
    tiles = ids.shape[0]
    words = tiles * WORD_TILE
    shape = jax.ShapeDtypeStruct
    flat = (words, filters)
    return pl.pallas_call(
        functools.partial(embed_forward_kernel, count, chars),
        out_shape=(
            shape(flat, f32),
            shape((words, count * filters), bf16),
            shape((words, count * filters), bf16),
            shape(flat, bf16),
            shape((tiles, chars * WORD_TILE, LANES), bf16),
            shape((tiles, chars, WORD_TILE, filters), bf16),
        )
        + (shape(flat, f32),) * 6,
        in_specs=[VMEM] * 9 + [ANY],
        out_specs=(VMEM,) * 4 + (ANY,) * 8,
        scratch_shapes=[
            pltpu.VMEM((chars + 6, WORD_TILE, LANES), bf16),
            pltpu.VMEM((2, chars * WORD_TILE, LANES), bf16),
            pltpu.VMEM((2, chars, WORD_TILE, filters), bf16),
            pltpu.VMEM(weight.shape, bf16),
            pltpu.VMEM((LANES, 264), bf16),
            pltpu.VMEM((LANES, filters), bf16),
            pltpu.VMEM((8, filters), f32),
            DMA((2, 2)),
            DMA((8,)),
        ]
        + [pltpu.VMEM(flat, f32)] * 6
        + [DMA((count, tiles))] * 8,
        compiler_params=params(cid, 58),
        name="embed_forward",
    )(ids, table, pattern, *conv, off, bias, weight)


class LineSum:
    def __init__(self, count, me, chunks, spacing, first, sums, parts, outs, buffers, sems):
        self.count, self.me, self.chunks, self.spacing = count, me, chunks, spacing
        self.first, self.messages, self.parts, self.outs = first, sums * chunks, parts, outs
        self.buffers, self.sems = buffers, sems
        self.fill = spacing * (count - 1)

    def tile(self, number, size=1):
        rows = self.parts.shape[1] // self.chunks * size
        return pl.ds(pl.multiple_of(number % self.chunks // size * rows, rows), rows)

    def place(self, right, number):
        count, me = self.count, self.me
        k, chunk, tile = self.first + number // self.chunks, number % self.chunks, self.tile(number)
        buf = self.buffers[0 if right else 1]
        send, recv = self.sems[:2] if right else self.sems[2:]
        to = jnp.minimum(me + 1, count - 1) if right else jnp.maximum(me - 1, 0)
        first, passed = [
            functools.partial(
                pltpu.make_async_remote_copy,
                src_ref=src.at[k, tile],
                dst_ref=buf.at[k, tile],
                send_sem=send.at[k, chunk],
                recv_sem=recv.at[k, chunk],
                device_id={"tensor": to},
                device_id_type=MESH,
            )
            for src in (self.parts, buf)
        ]
        return k, tile, buf, first, passed

    def step(self, step):
        for right in (True, False):
            lag = self.me if right else self.count - 1 - self.me
            number = step - self.spacing * lag
            here = (number >= 0) & (number < self.messages)
            number = jnp.clip(number, 0, self.messages - 1)
            k, tile, buf, first, passed = self.place(right, number)

            @pl.when(here & (lag == 0))
            def start():
                first().start()

            @pl.when(here & (lag > 0))
            def middle():
                first().wait_recv()
                got = buf[k, tile, :].astype(f32)

                @pl.when(lag < self.count - 1)
                def forward():
                    buf[k, tile, :] = (got + self.parts[k, tile, :].astype(f32)).astype(bf16)
                    passed().start()

                self.outs[k, tile, :] += got

    def drain(self):
        def one(number, carry):
            for right in (True, False):
                lag = self.me if right else self.count - 1 - self.me
                k, tile, buf, first, passed = self.place(right, number)

                @pl.when(lag < self.count - 1)
                def sent():
                    first().wait_send()

            return carry

        lax.fori_loop(0, self.messages, one, 0)

    def run(self, done, after, extra):
        size = self.chunks // 4

        def one(step, carry):
            self.step(step)
            for k, work in extra.items():
                pl.when(step == k)(work)
            number = step - self.fill
            for k in range(len(done)):

                @pl.when((number >= k * self.chunks) & (number < (k + 1) * self.chunks))
                def finish():
                    done[k](self.tile(jnp.maximum(number, 0)))

                    @pl.when(number % size == size - 1)
                    def quarter():
                        after[k](self.tile(jnp.maximum(number, 0), size))

            return carry

        lax.fori_loop(0, self.messages + self.fill, one, 0)
        self.drain()


def norm_parts(values):
    centered = values - jnp.mean(values, axis=-1, keepdims=True)
    root = lax.rsqrt(jnp.mean(centered * centered, axis=-1, keepdims=True) + norm_eps)
    return centered * root, root


def norm_back(values, gain, cotangent):
    nv, root = norm_parts(values)
    scaled = cotangent * gain
    inner = jnp.mean(scaled, axis=-1, keepdims=True)
    along = jnp.mean(scaled * nv, axis=-1, keepdims=True)
    return root * (scaled - inner - nv * along), cotangent * nv


def gelu_parts(values):
    cdf = 0.5 * (1.0 + lax.erf(values * 0.7071067811865476))
    slope = cdf + values * jnp.exp(-0.5 * values * values) * 0.3989422804014327
    return values * cdf, slope


def column_sum(values):
    return jnp.sum(values, axis=0, keepdims=True)


def encoder_kernel(count, chunks, spacing, *refs):
    top_ref, pw_ref, qw_ref, ow_ref, uw_ref, dw_ref = refs[:6]
    bias_refs, norm_refs, qv_ref, og_ref, len_ref = refs[6:10], refs[10:12], *refs[12:15]
    enc_ref, dh2_ref, tra_ref, trb_ref, sums_ref, qsum_ref, vec_ref, qb_ref = refs[15:23]
    (inp, mid, slope, sent, sent_mid, act, d_two, d_up, d_branch, d_emb, qkv, attended, probs,
     d_heads, d_proj, grad_all, enc_all, outs, parts, from_left, from_right) = refs[23:44]
    line_sems, gather_sems = refs[44:48], refs[48:52]
    emb, midpre, fin, dmid, din = [outs.at[k] for k in range(5)]
    me = lax.axis_index("tensor")
    line_greet(me, count)
    words, features = inp.shape
    heads = attended.shape[1] // HEAD_DIM
    hidden = heads * HEAD_DIM
    scale = HEAD_DIM ** (-0.5)
    own = words // count
    own_tile = pl.ds(pl.multiple_of(me * own, own), own)
    grad_all[own_tile, :] = og_ref[...]
    sums_ref[...] = jnp.zeros_like(sums_ref)
    trb_ref[...] = jnp.zeros_like(trb_ref)
    for k, bias_ref in zip((0, 1, 2, 9), bias_refs):
        vec_ref[k : k + 1, :] = bias_ref[...].astype(f32).reshape(1, features)
    for k, norm_ref in zip((3, 6), norm_refs):
        vec_ref[k : k + 3, :] = norm_ref[...].astype(f32)
    qb_ref[...] = jnp.zeros_like(qb_ref)
    ends = qv_ref[...].astype(f32)
    qb_ref[:, 0:hidden] = ends[0:1]
    qb_ref[:, 2 * hidden : 3 * hidden] = ends[1:2]
    live = lax.broadcasted_iota(jnp.int32, (1, words), 1) < len_ref[0]

    def line(first, sums):
        return LineSum(
            count, me, chunks, spacing, first, sums, parts, outs, (from_left, from_right), line_sems
        )

    def gather_view(block, chunk):
        return grad_all.at[pl.ds(pl.multiple_of(block * own, own), own)]

    def tiles(size, work):
        def one(index, carry):
            work(pl.ds(pl.multiple_of(index * size, size), size))
            return carry

        lax.fori_loop(0, words // size, one, 0)

    def product(lhs, rhs, side, k):
        def work(tile):
            value = dot(lhs[tile, :], rhs[...], 1, side).astype(bf16)
            parts[k, tile, :] = value
            outs[k, tile, :] = value.astype(f32)

        return work

    def grads(lhs, rhs, out_ref, lane):
        def half(k):
            def work():
                depth = features // 2
                value = dot(lhs[:, depth * k : depth * k + depth], rhs[...], 0, 0).astype(bf16)
                for i in range(2):
                    for j in range(2):
                        start = (2 * i + j) * (depth // 4)
                        out_ref[k, i, j, :, lane : lane + rhs.shape[1]] = value[
                            start : start + depth // 4
                        ]

            return work

        return [half(0), half(1)]

    def row(index):
        return vec_ref[index : index + 1, :]

    def add_sum(index, value):
        sums_ref[index : index + 1, :] += column_sum(value)

    tiles(256, product(top_ref, pw_ref, 0, 0))
    line_meet(me, count)

    def first_norm(tile):
        value = emb[tile, :] + row(0)
        emb[tile, :] = value
        value = norm_parts(value)[0] * row(3) + row(6)
        inp[tile, :] = value
        sent[tile, :] = value.astype(bf16)

    def project(tile):
        qkv[tile, :] = (dot(sent[tile, :], qw_ref[...], 1, 1) + qb_ref[...]).astype(bf16)

    line(0, 1).run([first_norm], [project], {})
    gather_step(gather_view, 0, 1, me, count, gather_sems)

    for head in range(heads):
        lanes = slice(head * HEAD_DIM, (head + 1) * HEAD_DIM)
        keys = slice(hidden + head * HEAD_DIM, hidden + (head + 1) * HEAD_DIM)
        vals = slice(2 * hidden + head * HEAD_DIM, 2 * hidden + (head + 1) * HEAD_DIM)

        def attend(tile):
            scores = dot(qkv[tile, lanes], qkv[:, keys], 1, 1) * scale
            scores = jnp.where(live, scores, big_neg)
            exps = jnp.exp(scores - jnp.max(scores, axis=1, keepdims=True))
            value = exps / jnp.sum(exps, axis=1, keepdims=True)
            probs[head, tile, :] = value
            attended[tile, lanes] = dot(value.astype(bf16), qkv[:, vals], 1, 0).astype(bf16)

        tiles(128, attend)
        if head == heads - 2:
            gather_step(gather_view, 1, 1, me, count, gather_sems)
    tiles(256, product(attended, ow_ref, 0, 1))

    def pass_grads():
        for step in range(2, count - 1):
            gather_step(gather_view, step, 1, me, count, gather_sems)

    def second_norm(tile):
        value = midpre[tile, :] + inp[tile, :] + row(1)
        midpre[tile, :] = value
        value = norm_parts(value)[0] * row(4) + row(7)
        mid[tile, :] = value
        sent_mid[tile, :] = value.astype(bf16)


    send_down = product(act, dw_ref, 0, 2)
    send_up = product(d_up, uw_ref, 1, 3)

    def feed(tile):
        value, back = gelu_parts(dot(sent_mid[tile, :], uw_ref[...], 1, 0) + row(9))
        act[tile, :] = value.astype(bf16)
        slope[tile, :] = back
        send_down(tile)

    def third_norm(tile):
        value = fin[tile, :] + mid[tile, :] + row(2)
        cotangent = grad_all[tile, :].astype(f32)
        enc_all[tile, :] = (norm_parts(value)[0] * row(5) + row(8)).astype(bf16)
        back, gain = norm_back(value, row(5), cotangent)
        fin[tile, :] = back
        low = back.astype(bf16)
        d_two[tile, :] = low
        add_sum(2, low.astype(f32))
        add_sum(5, gain)
        add_sum(8, cotangent)

    def feed_back(tile):
        value = (dot(d_two[tile, :], dw_ref[...], 1, 1) * slope[tile, :]).astype(bf16)
        d_up[tile, :] = value
        add_sum(9, value.astype(f32))
        send_up(tile)

    def second_back(tile):
        cotangent = dmid[tile, :] + fin[tile, :]
        back, gain = norm_back(midpre[tile, :], row(4), cotangent)
        dmid[tile, :] = back
        low = back.astype(bf16)
        d_branch[tile, :] = low
        add_sum(1, low.astype(f32))
        add_sum(4, gain)
        add_sum(7, cotangent)

    def heads_back(tile):
        d_heads[tile, :] = dot(d_branch[tile, :], ow_ref[...], 1, 1).astype(bf16)

    extra = {2: pass_grads}
    extra[chunks + 4] = lambda: gather_step(
        gather_view, count - 1, 1, me, count, gather_sems
    )
    work = grads(d_two, act, tra_ref, features) + grads(sent_mid, d_up, tra_ref, 0)
    extra.update({2 * chunks + spacing * (count - 1) + k: w for k, w in enumerate(work)})
    line(1, 3).run(
        [second_norm, third_norm, second_back], [feed, feed_back, heads_back], extra
    )
    enc_ref[...] = enc_all[own_tile, :]

    for head in range(heads):
        lanes = slice(head * HEAD_DIM, (head + 1) * HEAD_DIM)
        keys = slice(hidden + head * HEAD_DIM, hidden + (head + 1) * HEAD_DIM)
        vals = slice(2 * hidden + head * HEAD_DIM, 2 * hidden + (head + 1) * HEAD_DIM)
        weights = probs[head]
        d_out = d_heads[:, lanes]
        d_proj[:, vals] = dot(weights.astype(bf16), d_out, 0, 0).astype(bf16)
        d_probs = dot(d_out, qkv[:, vals], 1, 1)
        inner = jnp.sum(d_probs * weights, axis=1, keepdims=True)
        d_scores = (weights * (d_probs - inner)).astype(bf16)
        d_proj[:, lanes] = (dot(d_scores, qkv[:, keys], 1, 0) * scale).astype(bf16)
        d_proj[:, keys] = (dot(d_scores, qkv[:, lanes], 0, 0) * scale).astype(bf16)
    tiles(256, product(d_proj, qw_ref, 0, 4))
    qsum_ref[...] = column_sum(d_proj[...].astype(f32))

    def first_back(tile):
        cotangent = din[tile, :] + dmid[tile, :]
        back, gain = norm_back(emb[tile, :], row(3), cotangent)
        low = back.astype(bf16)
        d_emb[tile, :] = low
        add_sum(0, low.astype(f32))
        add_sum(3, gain)
        add_sum(6, cotangent)

    def last(tile):
        dh2_ref[tile, :] = dot(d_emb[tile, :], pw_ref[...], 1, 1)

    work = grads(sent, d_proj, trb_ref, top_ref.shape[1])
    work += grads(d_branch, attended, trb_ref, 1152)
    line(4, 1).run([first_back], [last], dict(enumerate(work)))
    for work in grads(d_emb, top_ref, trb_ref, 0):
        work()
    gather_drain(gather_view, 1, me, count, gather_sems)


def encoder(top, weights, biases, out_grad, lengths, count, cid):
    words, filters = top.shape
    features = weights[0].shape[1]
    three = weights[1].shape[0]
    units = weights[3].shape[1]
    hidden = three // 3
    chunks = 16
    spacing = (chunks - chunks // 4) // (count - 1)
    shape = jax.ShapeDtypeStruct
    rows = features // 8
    scratch = [pltpu.VMEM((16, features), f32), pltpu.VMEM((1, three), f32)]
    scratch += [pltpu.VMEM((words, n), f32) for n in (features, features, units)]
    scratch += [
        pltpu.VMEM((words, n), bf16)
        for n in (features, features, units, features, units, features, features, three, hidden)
    ]
    scratch += [pltpu.VMEM((hidden // HEAD_DIM, words, words), f32)]
    scratch += [pltpu.VMEM((words, n), bf16) for n in (hidden, three, features, features)]
    scratch += [pltpu.VMEM((5, words, features), f32)]
    scratch += [pltpu.VMEM((5, words, features), bf16)] * 3
    scratch += [DMA((5, chunks))] * 4 + [DMA((count, 1))] * 4
    return pl.pallas_call(
        functools.partial(encoder_kernel, count, chunks, spacing),
        out_shape=(
            shape((words // count, features), bf16),
            shape((words, filters), f32),
            shape((2, 2, 2, rows, features + units), bf16),
            shape((2, 2, 2, rows, 1408), bf16),
            shape((16, features), f32),
            shape((1, three), f32),
        ),
        in_specs=[VMEM] * 14 + [pl.BlockSpec(memory_space=pltpu.SMEM)],
        out_specs=(VMEM,) * 6,
        scratch_shapes=scratch,
        compiler_params=params(cid, 58),
        name="encoder",
    )(top, *weights, *biases, out_grad, lengths)


class LineScatter:
    def __init__(self, count, me, chunks, spacing, p_ref, out_ref, from_left, from_right, sems):
        self.count, self.me, self.chunks, self.spacing = count, me, chunks, spacing
        self.p_ref, self.out_ref = p_ref, out_ref
        self.from_left, self.from_right, self.sems = from_left, from_right, sems
        self.messages = chunks * (count - 1)
        self.steps = self.messages + spacing * (count - 1)

    def place(self, right, number):
        count, me = self.count, self.me
        lag = me if right else count - 1 - me
        chunk = number // (count - 1)
        far = count - 1 - number % (count - 1)
        block = far if right else count - 1 - far
        words, filters = self.out_ref.shape
        rows = words // self.chunks
        tile = pl.ds(pl.multiple_of(chunk * rows, rows), rows)
        lanes = pl.ds(pl.multiple_of(block * filters, filters), filters)
        buf = self.from_left if right else self.from_right
        send, recv = self.sems[:2] if right else self.sems[2:]
        to = jnp.minimum(me + 1, count - 1) if right else jnp.maximum(me - 1, 0)
        first, passed = [
            functools.partial(
                pltpu.make_async_remote_copy,
                src_ref=src.at[tile, lanes],
                dst_ref=buf.at[tile, lanes],
                send_sem=send.at[block, chunk],
                recv_sem=recv.at[block, chunk],
                device_id={"tensor": to},
                device_id_type=MESH,
            )
            for src in (self.p_ref, buf)
        ]
        return lag, far, tile, lanes, buf, first, passed

    def step(self, step):
        for right in (True, False):
            lag = self.me if right else self.count - 1 - self.me
            number = step - self.spacing * lag
            here = (number >= 0) & (number < self.messages)
            number = jnp.clip(number, 0, self.messages - 1)
            lag, far, tile, lanes, buf, first, passed = self.place(right, number)

            @pl.when(here & (lag == 0))
            def start():
                first().start()

            @pl.when(here & (lag > 0) & (far > lag))
            def middle():
                first().wait_recv()
                buf[tile, lanes] = (
                    buf[tile, lanes].astype(f32) + self.p_ref[tile, lanes].astype(f32)
                ).astype(bf16)
                passed().start()

            @pl.when(here & (lag > 0) & (far == lag))
            def last():
                first().wait_recv()
                self.out_ref[tile, :] += buf[tile, lanes].astype(f32)

    def due(self, chunk):
        return (chunk + self.spacing) * (self.count - 1)

    def finished(self, step, work, after=0):
        each = self.count - 1
        since = step - after - self.spacing * each

        @pl.when((since >= 0) & (since % each == 0) & (since < self.messages))
        def call():
            work(jnp.maximum(since, 0) // each)

    def drain(self):
        def one(number, carry):
            for right in (True, False):
                lag, far, tile, lanes, buf, first, passed = self.place(right, number)

                @pl.when(far > lag)
                def sent():
                    first().wait_send()

            return carry

        lax.fori_loop(0, self.messages, one, 0)


class DpSum:
    def __init__(self, cell, peers, x_first, sems, base):
        self.c, self.x, self.y = cell
        self.peers, self.x_first, self.base = peers, x_first, base
        self.send, self.recv = sems
        self.src = self.half = self.in0 = self.in1 = self.mid = self.in2 = None

    def remote(self, number, src, dst, bit):
        return pltpu.make_async_remote_copy(
            src_ref=src,
            dst_ref=dst,
            send_sem=self.send.at[self.base + number],
            recv_sem=self.recv.at[self.base + number],
            device_id=self.peers[bit],
            device_id_type=MESH,
        )

    def copy0(self):
        return self.remote(0, self.src.at[:, :, 1 - self.c], self.in0, 0)

    def copy1(self):
        if self.x_first:
            return self.remote(1, self.half.at[:, 1 - self.x], self.in1, 1)
        return self.remote(1, self.half.at[1 - self.y], self.in1, 2)

    def copy2(self):
        own = self.y if self.x_first else self.x
        return self.remote(2, self.mid.at[1 - own], self.in2, 2 if self.x_first else 1)

    def finish0(self):
        self.copy0().wait()

        def one(k, carry):
            i, j = k // 2, k % 2
            self.half[i, j] = (self.half[i, j].astype(f32) + self.in0[i, j].astype(f32)).astype(bf16)
            return carry

        lax.fori_loop(0, 4, one, 0)

    def finish1(self):
        self.copy1().wait()

        def one(k, carry):
            kept = self.half[k, self.x] if self.x_first else self.half[self.y, k]
            self.mid[k] = (kept.astype(f32) + self.in1[k].astype(f32)).astype(bf16)
            return carry

        lax.fori_loop(0, 2, one, 0)

    def finish2(self):
        self.copy2().wait()
        own = self.y if self.x_first else self.x
        return self.mid[own].astype(f32) + self.in2[...].astype(f32)


def dp_cell(place):
    cell = [place % 2, (place // 2) % 2, place // 4]
    return cell, [{"dp": place + (1 - 2 * cell[bit]) * 2**bit} for bit in range(3)]


def greet_all(peers):
    barrier = pltpu.get_barrier_semaphore()
    for peer in peers:
        pl.semaphore_signal(barrier, inc=1, device_id=peer, device_id_type=MESH)


def meet_all(peers):
    pl.semaphore_wait(pltpu.get_barrier_semaphore(), len(peers))


def mix_back(d_hidden, trans, gate_pre, previous):
    gate = jax.nn.sigmoid(gate_pre)
    sig = jax.nn.sigmoid(trans)
    act = trans * sig
    d_trans = (d_hidden * gate * (sig * (1.0 + trans * (1.0 - sig)))).astype(bf16)
    d_gate = (d_hidden * (act - previous) * gate * (1.0 - gate)).astype(bf16)
    return d_trans, d_gate, (1.0 - gate) * d_hidden


def weight_grad_piece(piece, whole_ref, d_refs, outs):
    rows = outs[0].shape[-2]
    lanes = pl.ds(pl.multiple_of(piece * rows, rows), rows)
    index = (piece // 4, (piece // 2) % 2, piece % 2)
    for d_ref, out in zip(d_refs, outs):
        out[index] = dot(whole_ref[:, lanes], d_ref[...], 0, 0).astype(bf16)


def highway_back_kernel(count, chunks, reduce, *refs):
    d_h2_ref, t1_ref, g1_ref, h1_ref = refs[:4]
    late_hbm = refs[4:9]
    refs = refs[9:]
    if reduce:
        tr_hbm = refs[:2]
        refs = refs[2:]
    part0_ref, prev0_ref, dt0_ref, dg0_ref, sums_ref = refs[:5]
    refs = refs[5:]
    if reduce:
        tr_outs = refs[2:4]
        hw_refs, tr_half = refs[4:6], refs[6:8]
        in0s, in1s = refs[8:12], refs[12:16]
        mids, in2s = list(refs[:2]) + list(refs[16:18]), refs[18:20]
        dp_sems = refs[20:22]
        refs = refs[22:]
    else:
        hw_refs = refs[:2]
        refs = refs[2:]
    part1_ref, from_left, from_right, d_h1_ref, dt1_ref, dg1_ref = refs[:6]
    t0_ref, g0_ref, h0_ref, whole1_ref, w_ref, late_sem = refs[6:12]
    sems = refs[12:]
    me = lax.axis_index("tensor")
    words, filters = d_h2_ref.shape
    w_hbm = late_hbm[4]
    loads = [
        pltpu.make_async_copy(w_hbm.at[1], w_ref.at[1], late_sem.at[0]),
        pltpu.make_async_copy(late_hbm[3], whole1_ref, late_sem.at[1]),
        pltpu.make_async_copy(w_hbm.at[0], w_ref.at[0], late_sem.at[2]),
        pltpu.make_async_copy(late_hbm[0], t0_ref, late_sem.at[3]),
        pltpu.make_async_copy(late_hbm[1], g0_ref, late_sem.at[4]),
        pltpu.make_async_copy(late_hbm[2], h0_ref, late_sem.at[5]),
    ]
    for copy in loads:
        copy.start()
    items = []
    if reduce:
        cell, peers = dp_cell(lax.axis_index("dp"))
        keep = [
            pltpu.make_async_copy(tr_hbm[k].at[:, :, cell[0]], tr_half[k], late_sem.at[6 + k])
            for k in range(2)
        ]
        for copy in keep:
            copy.start()
    ring = [{"tensor": lax.rem(me + k, count)} for k in range(1, count)]
    everyone = (peers if reduce else []) + ring
    greet_all(everyone)
    sums_ref[...] = jnp.zeros_like(sums_ref)

    def mix(layer, d_h_ref, t_ref, g_ref, h_ref, dt_ref, dg_ref, prev_ref, tile):
        dt, dg, prev = mix_back(d_h_ref[tile, :], t_ref[tile, :], g_ref[tile, :], h_ref[tile, :])
        dt_ref[tile, :] = dt
        dg_ref[tile, :] = dg
        prev_ref[tile, :] = prev
        for j, d in enumerate((dt, dg)):
            sums_ref[2 * layer + j : 2 * layer + j + 1, :] += jnp.sum(
                d.astype(f32), axis=0, keepdims=True
            )

    def products(layer, dt_ref, dg_ref, p_ref, part):
        tile = slice(part * (words // 2), (part + 1) * (words // 2))

        def one(block, carry):
            lanes = pl.ds(pl.multiple_of(block * filters, filters), filters)
            p_ref[tile, lanes] = (
                dot(dt_ref[tile, :], w_ref[layer, 0, lanes, :], 1, 1)
                + dot(dg_ref[tile, :], w_ref[layer, 1, lanes, :], 1, 1)
            ).astype(bf16)
            return carry

        lax.fori_loop(0, count, one, 0)

    rows = words // chunks

    def tile_of(index):
        return pl.ds(pl.multiple_of(index * rows, rows), rows)

    def first(index, carry):
        mix(1, d_h2_ref, t1_ref, g1_ref, h1_ref, dt1_ref, dg1_ref, d_h1_ref, tile_of(index))
        return carry

    def own_part(part):
        tile = slice(part * (words // 2), (part + 1) * (words // 2))
        d_h1_ref[tile, :] += part1_ref[
            tile, pl.ds(pl.multiple_of(me * filters, filters), filters)
        ].astype(f32)

    lax.fori_loop(0, chunks // 2, first, 0)
    loads[0].wait()
    products(1, dt1_ref, dg1_ref, part1_ref, 0)
    own_part(0)
    meet_all(everyone)
    if reduce:
        for k in range(4):
            item = DpSum(cell, peers, k % 2 == 0, dp_sems, 3 * k)
            if k < 2:
                item.src, item.half = hw_refs[k], hw_refs[k].at[:, :, cell[0]]
            else:
                item.src, item.half = tr_hbm[k - 2], tr_half[k - 2]
            item.in0, item.in1, item.mid = in0s[k], in1s[k], mids[k]
            if k >= 2:
                item.in2 = in2s[k - 2]
            items.append(item)
        for item in items[2:]:
            item.copy0().start()
    scatter = LineScatter(
        count, me, chunks, 3, part1_ref, d_h1_ref, from_left, from_right, sems
    )

    def step_fn(step, carry):
        scatter.step(step)

        @pl.when(step == 0)
        def rest():
            lax.fori_loop(chunks // 2, chunks, first, 0)
            products(1, dt1_ref, dg1_ref, part1_ref, 1)
            own_part(1)
            loads[1].wait()

        @pl.when((step > 0) & (step <= 8))
        def grads():
            weight_grad_piece(step - 1, whole1_ref, (dt1_ref, dg1_ref), hw_refs)

        @pl.when(step == 9)
        def late():
            for copy in loads[2:]:
                copy.wait()

        if reduce:

            @pl.when(step == 4)
            def encoder1():
                for copy in keep:
                    copy.wait()
                for item in items[2:]:
                    item.finish0()
                    item.copy1().start()

            @pl.when(step == 9)
            def highway0():
                for item in items[:2]:
                    item.copy0().start()

            @pl.when(step == 15)
            def highway1():
                for item in items[:2]:
                    item.finish0()
                    item.copy1().start()

            @pl.when(step == 20)
            def encoder2():
                for item in items[2:]:
                    item.finish1()
                    item.copy2().start()

        scatter.finished(
            step,
            lambda chunk: mix(
                0, d_h1_ref, t0_ref, g0_ref, h0_ref, dt0_ref, dg0_ref, prev0_ref, tile_of(chunk)
            ),
        )

        @pl.when(step == scatter.due(chunks // 2 - 1) + 1)
        def early():
            products(0, dt0_ref, dg0_ref, part0_ref, 0)

        return carry

    lax.fori_loop(0, scatter.steps, step_fn, 0)
    products(0, dt0_ref, dg0_ref, part0_ref, 1)
    for item in items[:2]:
        item.finish1()
    for item, out in zip(items[2:], tr_outs if reduce else ()):
        out[...] = item.finish2().astype(bf16)
    scatter.drain()


def highway_back(d_h2, t1, g1, h1, t0, g0, h0, whole1, weight, tra, trb, count, cid):
    words, filters = d_h2.shape
    chunks = 8
    reduce = tra is not None
    rows = whole1.shape[1] // 8
    shape = jax.ShapeDtypeStruct
    out_shape = [
        shape(whole1.shape, bf16),
        shape((words, filters), f32),
        shape((words, filters), bf16),
        shape((words, filters), bf16),
        shape((4, filters), f32),
    ]
    operands = [d_h2, t1, g1, h1, t0, g0, h0, whole1, weight]
    in_specs = [VMEM] * 4 + [ANY] * 5
    hw_shape = (2, 2, 2, rows, filters)
    scratch = []
    if reduce:
        operands += [tra, trb]
        in_specs += [ANY] * 2
        tails = [hw_shape[-2:], hw_shape[-2:], tra.shape[-2:], trb.shape[-2:]]
        out_shape += [shape((2,) + tail, bf16) for tail in tails[:2]]
        out_shape += [shape(tail, bf16) for tail in tails[2:]]
        scratch += [pltpu.VMEM(hw_shape, bf16)] * 2
        scratch += [pltpu.VMEM((2, 2) + tail, bf16) for tail in tails[2:]]
        scratch += [pltpu.VMEM((2, 2) + tail, bf16) for tail in tails]
        scratch += [pltpu.VMEM((2,) + tail, bf16) for tail in tails + tails[2:]]
        scratch += [pltpu.VMEM(tail, bf16) for tail in tails[2:]]
        scratch += [DMA((12,))] * 2
    else:
        out_shape += [shape(hw_shape, bf16)] * 2
    scratch += [pltpu.VMEM(whole1.shape, bf16)] * 3
    scratch += [pltpu.VMEM((words, filters), f32)] + [pltpu.VMEM((words, filters), bf16)] * 2
    scratch += [pltpu.VMEM((words, filters), f32)] * 3
    scratch += [pltpu.VMEM(whole1.shape, bf16), pltpu.VMEM(weight.shape, bf16), DMA((8,))]
    scratch += [DMA((count, chunks))] * 4
    return pl.pallas_call(
        functools.partial(highway_back_kernel, count, chunks, reduce),
        out_shape=tuple(out_shape),
        in_specs=in_specs,
        out_specs=tuple([VMEM] * len(out_shape)),
        scratch_shapes=scratch,
        compiler_params=params(cid, 58),
        name="highway_back",
    )(*operands)


class Spread:
    def __init__(self, sems, in_ref, got, mid, out_ref):
        self.dp_count, self.count = out_ref.shape[:2]
        self.sems, self.in_ref, self.got, self.mid, self.out_ref = sems, in_ref, got, mid, out_ref
        self.me = lax.axis_index("tensor")
        self.place = lax.axis_index("dp")

    def remote(self, src, dst, phase, hop, axis, peer):
        send, recv = self.sems[2 * phase : 2 * phase + 2]
        return pltpu.make_async_remote_copy(
            src_ref=src, dst_ref=dst, send_sem=send.at[hop - 1], recv_sem=recv.at[hop - 1],
            device_id={axis: peer}, device_id_type=MESH,
        )

    def scatter(self, hop):
        peer = lax.rem(self.place + hop, self.dp_count)
        return self.remote(self.in_ref.at[peer], self.got.at[hop - 1], 0, hop, "dp", peer)

    def across(self, hop):
        peer = lax.rem(self.me + hop, self.count)
        return self.remote(self.mid.at[self.me], self.mid.at[self.me], 1, hop, "tensor", peer)

    def around(self, hop):
        peer = lax.rem(self.place + hop, self.dp_count)
        return self.remote(self.mid, self.out_ref.at[self.place], 2, hop, "dp", peer)

    def loop(self, fn, stop):
        def one(hop, carry):
            fn(hop)
            return carry

        lax.fori_loop(1, stop, one, 0)

    def first(self):
        self.loop(lambda hop: self.scatter(hop).start(), self.dp_count)

    def second(self):
        self.loop(lambda hop: self.scatter(hop).wait(), self.dp_count)
        total = lax.fori_loop(
            0,
            self.dp_count - 1,
            lambda k, acc: acc + self.got[k].astype(f32),
            self.in_ref[self.place].astype(f32),
        )
        self.mid[self.me] = total.astype(bf16)
        self.loop(lambda hop: self.across(hop).start(), self.count)

    def third(self):
        self.loop(lambda hop: self.across(hop).wait(), self.count)
        self.loop(lambda hop: self.around(hop).start(), self.dp_count)
        self.out_ref[self.place] = self.mid[...]

    def finish(self):
        self.loop(lambda hop: self.around(hop).wait(), self.dp_count)


def early_parts(rows):
    start = 0
    for source, (count, width) in enumerate(rows):
        for block in range(-(-width // LANES)):
            yield source, block, start, count, min(LANES, width - block * LANES)
            start += count


EARLY = ((4, 512), (1, 576), (10, 768))


def pack_early(ref, *sources):
    ref[...] = jnp.zeros_like(ref)
    for source, block, start, count, width in early_parts(EARLY):
        value = sources[source][0:count, block * LANES : block * LANES + width]
        for k in range(count):
            place = start + k
            ref[place // 16, place % 16 : place % 16 + 1, 0:width] = value[k : k + 1]


def unpack_early(ref, hwb_out, vec_out, upb_out, qv_out):
    for t in range(ref.shape[1]):
        for source, block, start, count, width in early_parts(EARLY):
            for k in range(count):
                place = start + k
                row = ref[place // 16, t, :, :].astype(f32)[place % 16 : place % 16 + 1, 0:width]
                lane = block * LANES
                if source == 0:
                    hwb_out[k : k + 1, t * 512 + lane : t * 512 + lane + width] = row
                elif source == 2 and k == 9:
                    upb_out[:, t * 768 + lane : t * 768 + lane + width] = row
                elif source == 2 and t == 0:
                    vec_out[k : k + 1, lane : lane + width] = row
                elif source == 1:
                    for out, low in ((0, 0), (1, 384)):
                        left, right = max(lane, low), min(lane + width, low + 192)
                        if left < right:
                            place_at = t * 192 + left - low
                            qv_out[out : out + 1, place_at : place_at + right - left] = row[
                                :, left - lane : right - lane
                            ]


def conv_backward_kernel(count, chars, cuts, *refs):
    (ids_ref, x_hbm, p_hbm, cw_ref, mask_ref, off_ref, log_ref, prev_ref, part_ref, whole_hbm,
     dt_ref, dg_ref) = refs[:12]
    refs = refs[12:]
    if cuts:
        mids_in = refs[:2]
        hb_sums, proj_sums, row_sums = refs[2:5]
        hw_out, convw_out, convb_out, table_out, hwb_out, vec_out, upb_out, qv_out = refs[5:13]
        dw_ref, table_ref, hw_a, hw_b = refs[13:17]
        in0s, in1s, mids, in2s = refs[17:19], refs[19:21], refs[21:23], refs[23:27]
        dp_sems = refs[27:29]
        spreads = [Spread(refs[33 + 10 * k : 39 + 10 * k], *refs[29 + 10 * k : 33 + 10 * k])
                   for k in range(2)]
        refs = refs[49:]
    else:
        dw_ref, table_ref, hw_a, hw_b = refs[:4]
        refs = refs[4:]
    (pad_ref, stage_ref, grad_ref, from_left, from_right, x_buf, p_buf, whole_ref, wb_ref,
     load_sem, whole_sem) = refs[:11]
    line_sems = refs[11:]
    me = lax.axis_index("tensor")
    words, filters = log_ref.shape
    tiles = words // WORD_TILE
    padded = ids_ref.shape[1] // WORD_TILE

    def load(index):
        slot = index % 2
        return [
            pltpu.make_async_copy(hbm.at[index], buf.at[slot], load_sem.at[k, slot])
            for k, (buf, hbm) in enumerate(((x_buf, x_hbm), (p_buf, p_hbm)))
        ]

    whole_copy = pltpu.make_async_copy(whole_hbm, whole_ref, whole_sem)
    whole_copy.start()
    for index in range(2):
        for copy in load(index):
            copy.start()
    ring = [{"tensor": lax.rem(me + k, count)} for k in range(1, count)]
    items = []
    if cuts:
        place = lax.axis_index("dp")
        dp_count = spreads[0].dp_count
        cell, dp_peers = dp_cell(place)
        ring += [{"dp": lax.rem(place + k, dp_count)} for k in range(1, dp_count)]
        for k in range(4):
            item = DpSum(cell, dp_peers, k % 2 == 0, dp_sems, 3 * k)
            item.in2 = in2s[k]
            if k < 2:
                item.src = (hw_a, hw_b)[k]
                item.half = item.src.at[:, :, cell[0]]
                item.in0, item.in1, item.mid = in0s[k], in1s[k], mids[k]
            else:
                item.mid = mids_in[k - 2]
            items.append(item)
        pack_early(spreads[0].in_ref, hb_sums, proj_sums, row_sums)
    greet_all(ring)
    taps = cw_ref.shape[0]
    wb_ref[...] = jnp.zeros_like(wb_ref)
    wb_ref[0:taps, :] = (cw_ref[...].astype(f32) * mask_ref[...]).astype(bf16)
    dw_ref[...] = jnp.zeros_like(dw_ref)
    table_ref[...] = jnp.zeros_like(table_ref)
    pad_ref[...] = jnp.zeros_like(pad_ref)
    grad_ref[...] = prev_ref[...] + part_ref[
        :, pl.ds(pl.multiple_of(me * filters, filters), filters)
    ].astype(f32)
    meet_all(ring)
    for item in items[2:]:
        item.copy2().start()
    if cuts:
        spreads[0].first()
    chunks = line_sems[0].shape[1]
    per = words // chunks // WORD_TILE
    scatter = LineScatter(
        count, me, chunks, 3, part_ref, grad_ref, from_left, from_right, line_sems
    )
    group = lax.broadcasted_iota(jnp.int32, (1, WORD_TILE, LANES), 2) // 16
    vocab = lax.broadcasted_iota(jnp.int32, (table_ref.shape[0], padded * WORD_TILE), 0)

    def tile_step(index):
        slot = index % 2
        for copy in load(index):
            copy.wait()
        tile = pl.ds(pl.multiple_of(index * WORD_TILE, WORD_TILE), WORD_TILE)
        pooled = log_ref[tile, :] - off_ref[...]
        sig = jax.nn.sigmoid(pooled)
        grad = grad_ref[tile, :] * (sig * (1.0 + pooled * (1.0 - sig)))
        d_conv = (grad[None] * p_buf[slot].astype(f32)).astype(bf16)
        d_conv = d_conv.reshape(chars * WORD_TILE, filters)
        dw_ref[...] += dot(x_buf[slot], d_conv, 0, 0)
        d_win = dot(d_conv, wb_ref[...], 1, 1).astype(bf16)
        pad_ref[6 : 6 + chars] = d_win.reshape(chars, WORD_TILE, LANES)
        d_emb = pad_ref[6 : 6 + padded]
        for tap in range(1, 7):
            d_emb = jnp.where(group == tap, pad_ref[6 - tap : 6 - tap + padded], d_emb)
        one_hot = jnp.where(vocab == ids_ref[pl.ds(index, 1), :], 1.0, 0.0).astype(bf16)
        table_ref[...] += dot(one_hot, d_emb.reshape(padded * WORD_TILE, LANES), 1, 0)

        @pl.when(index + 2 < tiles)
        def more():
            for copy in load(index + 2):
                copy.start()

    def step_fn(step, carry):
        scatter.step(step)

        @pl.when(step == 0)
        def whole():
            whole_copy.wait()

        @pl.when(step < 8)
        def grads():
            weight_grad_piece(step, whole_ref, (dt_ref, dg_ref), (hw_a, hw_b))

        if cuts:

            @pl.when(step == 4)
            def early2():
                spreads[0].second()

            @pl.when(step == 7)
            def early3():
                spreads[0].third()

            @pl.when(step == 8)
            def start0():
                for item in items[:2]:
                    item.copy0().start()

            @pl.when(step == cuts[0])
            def start1():
                for item in items[:2]:
                    item.finish0()
                    item.copy1().start()

            @pl.when(step == cuts[1])
            def start2():
                for item in items[:2]:
                    item.finish1()
                    item.copy2().start()

        for k in range(per):
            scatter.finished(step, lambda chunk: tile_step(chunk * per + k), k)
        return carry

    lax.fori_loop(0, scatter.due(chunks - 1) + per, step_fn, 0)
    if cuts:
        late = spreads[1]
        taps = table_ref[:, 0:16]
        for tap in range(1, 7):
            taps += table_ref[:, 16 * tap : 16 * tap + 16]
        stage_ref[...] = jnp.zeros_like(stage_ref)
        table_ref[:, 0:16] = taps
        for i in range(8):
            late.in_ref[i, :, 0:filters] = dw_ref[16 * i : 16 * i + 16, :].astype(bf16)
            for k in range(3):
                size = 16 if k < 2 else 1
                stage_ref[0:size, 16 * k : 16 * k + 16] = table_ref[
                    33 * i + 16 * k : 33 * i + 16 * k + size, 0:16
                ]
            late.in_ref[i, :, filters:] = stage_ref[...].astype(bf16)
        late.first()
        spreads[0].finish()
        unpack_early(spreads[0].out_ref, hwb_out, vec_out, upb_out, qv_out)
        late.second()
        late.third()
        for k in range(4):
            hw_out[k // 2, k % 2] = items[k].finish2().astype(bf16)
        late.finish()
        for t in range(count):
            lanes = slice(t * filters, (t + 1) * filters)
            for i in range(7):
                convw_out[16 * i : 16 * i + 16, lanes] = late.out_ref[i, t, :, 0:filters]
            convb_out[:, lanes] = late.out_ref[7, t, :, 0:filters].astype(f32)[0:1]
        for i in range(8):
            total = late.out_ref[i, 0, :, filters:].astype(f32)
            for t in range(1, count):
                total += late.out_ref[i, t, :, filters:].astype(f32)
            for k in range(3):
                size = 16 if k < 2 else 1
                table_out[33 * i + 16 * k : 33 * i + 16 * k + size, :] = total[
                    0:size, 16 * k : 16 * k + 16
                ]
    scatter.drain()


def conv_backward(ids, x, p, w, mask, off, logs, prev, part, whole, dt, dg, rest, count, cid):
    words, filters = logs.shape
    chars = p.shape[1]
    chunks = 8
    shape = jax.ShapeDtypeStruct
    hw_shape = (2, 2, 2, whole.shape[1] // 8, filters)
    operands = [ids, x, p, w, mask, off, logs, prev, part, whole, dt, dg] + list(rest)
    in_specs = [VMEM, ANY, ANY] + [VMEM] * 6 + [ANY, VMEM, VMEM] + [VMEM] * len(rest)
    sums = [(LANES, filters), (264, LANES)]
    scratch = []
    cuts = None
    if rest:
        cuts = (17, 28)
        tail = hw_shape[-2:]
        features = rest[-1].shape[-1]
        out_shape = [
            shape((2, 2) + tail, bf16),
            shape((112, count * filters), bf16),
            shape((1, count * filters), f32),
            shape((264, 16), f32),
            shape((4, count * filters), f32),
            shape((9, features), f32),
            shape((1, count * features), f32),
            shape((2, features), f32),
        ]
        scratch += [pltpu.VMEM(shape_of, f32) for shape_of in sums]
        scratch += [pltpu.VMEM(hw_shape, bf16)] * 2
        scratch += [pltpu.VMEM((2, 2) + tail, bf16)] * 2
        scratch += [pltpu.VMEM((2,) + tail, bf16)] * 4
        scratch += [pltpu.VMEM(tail, bf16)] * 4
        scratch += [DMA((12,))] * 2
        for small, kind in (((16, LANES), f32), ((16, filters + LANES), bf16)):
            scratch += [
                pltpu.VMEM((8,) + small, kind),
                pltpu.VMEM((7,) + small, kind),
                pltpu.VMEM((count,) + small, bf16),
                pltpu.VMEM((8, count) + small, bf16),
            ]
            scratch += [DMA((7,))] * 2 + [DMA((count - 1,))] * 2 + [DMA((7,))] * 2
    else:
        out_shape = [shape(shape_of, f32) for shape_of in sums] + [shape(hw_shape, bf16)] * 2
    scratch += [
        pltpu.VMEM((68, WORD_TILE, LANES), bf16),
        pltpu.VMEM((16, LANES), f32),
        pltpu.VMEM((words, filters), f32),
        pltpu.VMEM(part.shape, bf16),
        pltpu.VMEM(part.shape, bf16),
        pltpu.VMEM((2,) + x.shape[1:], bf16),
        pltpu.VMEM((2,) + p.shape[1:], bf16),
        pltpu.VMEM(whole.shape, bf16),
        pltpu.VMEM((LANES, filters), bf16),
        DMA((2, 2)),
        DMA,
    ]
    scratch += [DMA((count, chunks))] * 4
    return pl.pallas_call(
        functools.partial(conv_backward_kernel, count, chars, cuts),
        out_shape=tuple(out_shape),
        in_specs=in_specs,
        out_specs=tuple([VMEM] * len(out_shape)),
        scratch_shapes=scratch,
        compiler_params=params(cid, 58),
        name="conv_backward",
    )(*operands)


def small_kernel(dp_count, count, in_ref, out_ref, got, mid, *sems):
    me = lax.axis_index("tensor")
    place = lax.axis_index("dp")
    barrier = pltpu.get_barrier_semaphore()

    def greet(hop, carry):
        peer = lax.rem(place + hop, dp_count)
        pl.semaphore_signal(barrier, inc=1, device_id={"dp": peer}, device_id_type=MESH)
        return carry

    lax.fori_loop(1, dp_count, greet, 0)
    for hop in range(1, count):
        pl.semaphore_signal(
            barrier, inc=1, device_id={"tensor": lax.rem(me + hop, count)}, device_id_type=MESH
        )
    pl.semaphore_wait(barrier, dp_count + count - 2)
    spread = Spread(sems, in_ref, got, mid, out_ref)
    spread.first()
    spread.second()
    spread.third()
    spread.finish()


def sum_small(packed, dp_count, count, cid):
    shape = packed.shape[1:]
    return pl.pallas_call(
        functools.partial(small_kernel, dp_count, count),
        out_shape=jax.ShapeDtypeStruct((dp_count, count) + shape, bf16),
        in_specs=[VMEM],
        out_specs=VMEM,
        scratch_shapes=[
            pltpu.VMEM((dp_count - 1,) + shape, f32),
            pltpu.VMEM((count,) + shape, bf16),
            DMA((dp_count - 1,)),
            DMA((dp_count - 1,)),
            DMA((count - 1,)),
            DMA((count - 1,)),
            DMA((dp_count - 1,)),
            DMA((dp_count - 1,)),
        ],
        compiler_params=params(cid, 32),
        name="sum_small",
    )(packed)


def finish_kernel(units, three, *refs):
    (enc_out, table_out, conv_w_out, conv_b_out, hw_out, hw_b_out, proj_out, proj_b_out, gain_out,
     shift_out, qkv_out, qv_out, o_out, o_b_out, up_out, up_b_out, down_out,
     down_b_out) = refs[12:30]
    bufs, sem = refs[30:42], refs[42]
    loads = [
        pltpu.make_async_copy(src, dst, sem.at[k])
        for k, (src, dst) in enumerate(zip(refs[:12], bufs))
    ]
    for copy in loads:
        copy.start()
    for copy in loads:
        copy.wait()
    (enc, table, conv_w, mask, conv_b, hw, hw_b, rows, qv, up_b, tr_a, tr_b) = bufs
    filters = mask.shape[1]
    enc_out[0] = enc[...]
    table_out[...] = table[...].T[:, 0 : table_out.shape[1]]
    for start in range(0, conv_w.shape[1], filters):
        lanes = slice(start, start + filters)
        conv_w_out[:, lanes] = conv_w[:, lanes].astype(f32) * mask[...]
    conv_b_out[...] = conv_b[...].reshape(conv_b_out.shape)
    for layer in range(2):
        hw_b_out[layer] = hw_b[2 * layer : 2 * layer + 2, :]
        for j in range(2):
            hw_out[layer, j] = hw[layer, j].astype(f32)
    for k, out in enumerate((proj_b_out, o_b_out, down_b_out)):
        out[...] = rows[k : k + 1, :].reshape(out.shape)
    gain_out[...] = rows[3:6, :]
    shift_out[...] = rows[6:9, :]
    qv_out[...] = qv[...]
    up_b_out[...] = up_b[...].reshape(up_b_out.shape)
    up_out[...] = tr_a[:, 0:units].astype(f32)
    down_out[...] = tr_a[:, units:].astype(f32)
    proj_out[...] = tr_b[:, 0:filters].astype(f32)
    hidden = three // 3
    qkv = tr_b[:, filters : filters + three].astype(f32)
    for k in range(3):
        qkv_out[k] = qkv[:, k * hidden : (k + 1) * hidden]
    o_out[...] = tr_b[:, 1152 : 1152 + hidden].astype(f32).T


def finish(encoded, table, conv_w, mask, conv_b, hw, hw_b, rows, qv, up_b, tr_a, tr_b, vocab,
           units, three):
    features, depth, filters = rows.shape[1], tr_a.shape[0], mask.shape[1]
    shapes = [
        (table.shape[1], vocab), conv_w.shape, (conv_w.shape[1],), hw.shape,
        (2, 2, hw_b.shape[1]), (depth, filters), (features,), (3, features), (3, features),
        (3, depth, three // 3), qv.shape, (three // 3, depth), (features,), (depth, units),
        (up_b.shape[1],), (depth, tr_a.shape[1] - units), (features,),
    ]
    operands = (encoded, table, conv_w, mask, conv_b, hw, hw_b, rows, qv, up_b, tr_a, tr_b)
    (encoded, table, conv_w, conv_b, hw, hw_b, proj, proj_b, gain, shift, qkv, qv, o, o_b, up, up_b,
     down, down_b) = pl.pallas_call(
        functools.partial(finish_kernel, units, three),
        out_shape=tuple(
            [jax.ShapeDtypeStruct((1,) + encoded.shape, bf16)]
            + [jax.ShapeDtypeStruct(shape, f32) for shape in shapes]
        ),
        in_specs=[ANY] * 12,
        out_specs=(VMEM,) * 18,
        scratch_shapes=[pltpu.VMEM(part.shape, part.dtype) for part in operands] + [DMA((12,))],
        compiler_params=pltpu.CompilerParams(vmem_limit_bytes=58 * MIB),
        name="finish",
    )(*operands)
    return (
        jnp.transpose(encoded, (1, 0, 2)), table.T, conv_w, conv_b, hw, hw_b, proj.T, proj_b, gain,
        shift, jnp.transpose(qkv, (1, 0, 2)), qv, o, o_b, up, up_b, down.T, down_b,
    )


def body(
    char_ids,
    seq_lengths,
    char_table,
    conv_weight,
    conv_bias,
    highway_weight,
    highway_bias,
    proj_weight,
    proj_bias,
    norm_gain,
    norm_shift,
    qkv_weight,
    qv_bias,
    output_projection_weight,
    out_bias,
    up_weight,
    up_bias,
    down_weight,
    down_bias,
    out_grad,
):
    words, nseq, chars = char_ids.shape
    assert nseq == 1
    count = lax.axis_size("tensor")
    dp_count = lax.axis_size("dp")
    rank = lax.axis_index("tensor")
    vocab, char_dim = char_table.shape
    taps_dim, filters = conv_weight.shape
    features = proj_weight.shape[1]
    heads = qkv_weight.shape[2] // HEAD_DIM

    tiles = words // WORD_TILE
    ids_tiles = jnp.swapaxes(char_ids[:, 0].reshape(tiles, WORD_TILE, chars), 1, 2)
    ids_tiles = ids_tiles.reshape(tiles, chars * WORD_TILE)
    pattern = np.zeros((chars, WORD_TILE, LANES), np.float32)
    pattern[:, :, taps_dim] = 1.0
    for k in range(1, 7):
        pattern[chars - k, :, taps_dim + k] = 1.0

    widths = filter_widths(filters)
    off = jnp.asarray(np.log((chars - widths + 1).astype(np.float64)).astype(np.float32))[None]
    tap_of = np.arange(taps_dim)[:, None] // char_dim
    taps_mask = tap_of < widths[None]
    mask = jnp.asarray(taps_mask, f32)
    ends = np.zeros((LANES - taps_dim, filters), np.float32)
    ends[1:7] = np.where(widths[None] > np.arange(1, 7)[:, None], big_neg, 0.0)

    logs, whole0, whole1, top, x_tiles, p_tiles, t0, g0, h0, t1, g1, h1 = embed_forward(
        ids_tiles,
        char_table.T,
        jnp.asarray(pattern, bf16),
        (conv_weight, conv_bias, mask, jnp.asarray(ends)),
        off,
        highway_bias,
        highway_weight,
        count,
        chars,
        1,
    )
    encoded, d_hidden, tr_a, tr_b, row_sums, proj_sums = encoder(
        top,
        (
            proj_weight,
            jnp.transpose(qkv_weight, (1, 2, 0)).reshape(-1, features),
            output_projection_weight,
            up_weight,
            down_weight,
        ),
        (proj_bias, out_bias, down_bias, up_bias, norm_gain, norm_shift, qv_bias),
        out_grad[:, 0],
        seq_lengths,
        count,
        4,
    )

    back_args = (d_hidden, t1, g1, h1, t0, g0, h0, whole1, highway_weight)
    conv_args = (ids_tiles, x_tiles, p_tiles, conv_weight, mask, off, logs)
    three = 3 * heads * HEAD_DIM
    units = up_weight.shape[1]
    if dp_count == 8 and (features // dp_count) % 16 == 0:
        part0, prev0, dt0, dg0, hw_bias_part, mid_a, mid_b, tr_a, tr_b = highway_back(
            *back_args, tr_a, tr_b, count, 9
        )
        (hw_w_grad, conv_w_grad, conv_b_grad, table_grad, hw_b_grad, rows, up_b_grad,
         qv_grad) = conv_backward(
            *conv_args, prev0, part0, whole0, dt0, dg0,
            (mid_a, mid_b, hw_bias_part, proj_sums, row_sums), count, 10,
        )
        return finish(
            encoded, table_grad, conv_w_grad, mask, conv_b_grad, hw_w_grad, hw_b_grad, rows,
            qv_grad, up_b_grad, tr_a, tr_b, vocab, units, three,
        )
    else:
        part0, prev0, dt0, dg0, hw_bias_part, *hw1 = highway_back(*back_args, None, None, count, 9)
        d_w_all, table_all, *hw0 = conv_backward(
            *conv_args, prev0, part0, whole0, dt0, dg0, (), count, 10
        )
        hw_sum = jnp.stack([part.reshape(-1, filters) for part in hw0 + hw1])
        hw_sum = lax.psum_scatter(hw_sum, "dp", scatter_dimension=1, tiled=True).astype(f32)
        tr_a, tr_b = [
            lax.psum_scatter(
                part.reshape(features, -1), "dp", scatter_dimension=0, tiled=True
            ).astype(f32)
            for part in (tr_a, tr_b)
        ]
        hw_w_grad = hw_sum.reshape(2, 2, -1, filters)
        pieces = [d_w_all[: taps_dim + 1], table_all, hw_bias_part, proj_sums, row_sums[:10]]
        flat = jnp.concatenate([part.reshape(-1) for part in pieces])
        width = -(-flat.size // (dp_count * 16 * LANES)) * LANES
        flat = jnp.pad(flat, (0, dp_count * 16 * width - flat.size))
        summed = sum_small(flat.reshape(dp_count, 16, width), dp_count, count, 11)
        summed = jnp.swapaxes(summed, 0, 1).reshape(count, -1).astype(f32)
        conv_size, table_size = pieces[0].size, table_all.size
        conv_all = summed[:, :conv_size].reshape(count, taps_dim + 1, filters)
        conv_all = jnp.swapaxes(conv_all, 0, 1)
        conv_w_grad = conv_all[:taps_dim].reshape(taps_dim, -1)
        conv_b_grad = conv_all[taps_dim].reshape(-1)
        table_all = jnp.sum(summed[:, conv_size : conv_size + table_size], axis=0)
        table_all = table_all.reshape(-1, LANES)
        early = summed[:, conv_size + table_size :]
        table_grad = jnp.sum(
            table_all[:vocab, :taps_dim].reshape(vocab, taps_dim // char_dim, char_dim), axis=1
        )
        hw_b_grad = jnp.swapaxes(early[:, : 4 * filters].reshape(count, 4, filters), 0, 1)
        early = early[:, 4 * filters :]
        qv_grad = jnp.swapaxes(early[:, :three].reshape(count, 3, -1), 0, 1)[::2].reshape(2, -1)
        rows = early[:, three : three + 10 * features].reshape(count, 10, features)
        up_b_grad = rows[:, 9].reshape(-1)
        rows = rows[0]

    conv_w_grad = jnp.where(np.tile(taps_mask, (1, count)), conv_w_grad, 0.0)
    hw_b_grad = hw_b_grad.reshape(2, 2, -1)
    up_w_grad = tr_a[:, :units]
    down_w_grad = tr_a[:, units:].T
    proj_w_grad = tr_b[:, :filters].T
    qkv_w_grad = tr_b[:, filters : filters + three].reshape(-1, 3, heads * HEAD_DIM)
    out_w_grad = tr_b[:, 1152 : 1152 + heads * HEAD_DIM].T
    proj_b_grad, out_b_grad, down_b_grad = rows[0], rows[1], rows[2]
    gain_grad, shift_grad = rows[3:6], rows[6:9]
    return (
        encoded[:, None],
        table_grad,
        conv_w_grad,
        conv_b_grad,
        hw_w_grad,
        hw_b_grad,
        proj_w_grad,
        proj_b_grad,
        gain_grad,
        shift_grad,
        qkv_w_grad,
        qv_grad,
        out_w_grad,
        out_b_grad,
        up_w_grad,
        up_b_grad,
        down_w_grad,
        down_b_grad,
    )


def solution(mesh):
    return jax.shard_map(
        body,
        mesh=mesh,
        in_specs=(
            P(None, "dp", None),
            P("dp"),
            P(),
            P(None, "tensor"),
            P("tensor"),
            P(None, None, None, "tensor"),
            P(None, None, "tensor"),
            P("tensor", None),
            P(),
            P(),
            P(),
            P(None, None, "tensor"),
            P(None, "tensor"),
            P("tensor", None),
            P(),
            P(None, "tensor"),
            P("tensor"),
            P("tensor", None),
            P(),
            P("tensor", "dp", None),
        ),
        out_specs=(
            P("tensor", "dp", None),
            P(),
            P(),
            P(),
            P(None, None, "dp", "tensor"),
            P(),
            P("tensor", "dp"),
            P(),
            P(),
            P(),
            P("dp", None, "tensor"),
            P(),
            P("tensor", "dp"),
            P(),
            P("dp", "tensor"),
            P(),
            P("tensor", "dp"),
            P(),
        ),
        check_vma=False,
    )
```

```python
import functools
import math

import jax
import jax.numpy as jnp
import numpy as np
from jax import lax
from jax.experimental import pallas as pl
from jax.experimental.pallas import tpu as pltpu
from jax.sharding import PartitionSpec as P

HEAD_DIM = 64
WORD_TILE = 32
LANES = 128

norm_eps = 1e-06
big_neg = -1e30
f32 = jnp.float32
bf16 = jnp.bfloat16
MESH = pl.DeviceIdType.MESH
VMEM = pl.BlockSpec(memory_space=pltpu.VMEM)
ANY = pl.BlockSpec(memory_space=pl.ANY)
DMA = pltpu.SemaphoreType.DMA
MIB = 1 << 20


def params(cid, vmem):
    return pltpu.CompilerParams(
        collective_id=cid, has_side_effects=True, vmem_limit_bytes=vmem * MIB
    )


def width_counts(block):
    unit = block // 64
    return [unit, unit, 2 * unit, 4 * unit, 8 * unit, 16 * unit, 32 * unit]


def filter_widths(block):
    return np.concatenate(
        [np.full((n,), i + 1, np.int32) for i, n in enumerate(width_counts(block))]
    )


def dot(a, b, ca, cb):
    return lax.dot_general(a, b, (((ca,), (cb,)), ((), ())), preferred_element_type=f32)


def line_greet(me, count):
    barrier = pltpu.get_barrier_semaphore()
    for there, ok in ((me - 1, me > 0), (me + 1, me < count - 1)):

        @pl.when(ok)
        def greet():
            pl.semaphore_signal(barrier, inc=1, device_id={"tensor": there}, device_id_type=MESH)


def line_meet(me, count):
    pl.semaphore_wait(
        pltpu.get_barrier_semaphore(), jnp.minimum(me, 1) + jnp.minimum(count - 1 - me, 1)
    )


def line_copy(view, me, count, right, block, chunk, sems):
    send, recv = sems[:2] if right else sems[2:]
    to = jnp.minimum(me + 1, count - 1) if right else jnp.maximum(me - 1, 0)
    ref = view(block, chunk)
    return pltpu.make_async_remote_copy(
        src_ref=ref,
        dst_ref=ref,
        send_sem=send.at[block, chunk],
        recv_sem=recv.at[block, chunk],
        device_id={"tensor": to},
        device_id_type=MESH,
    )


def gather_step(view, step, chunks, me, count, sems, spacing=1):
    for hop in range(count):
        chunk = step - spacing * hop
        here = (chunk >= 0) & (chunk < chunks)
        safe = jnp.clip(chunk, 0, chunks - 1)
        for right in (True, False):
            block = me - hop if right else me + hop
            there = (block >= 0) & (block < count)
            block = jnp.clip(block, 0, count - 1)
            more = me < count - 1 if right else me > 0
            copy = functools.partial(line_copy, view, me, count, right, block, safe, sems)

            @pl.when(here & there)
            def pass_on():
                if hop > 0:
                    copy().wait_recv()

                @pl.when(more)
                def send():
                    copy().start()


def gather_drain(view, chunks, me, count, sems):
    def one(chunk, carry):
        for hop in range(count):
            for right in (True, False):
                block = me - hop if right else me + hop
                there = (block >= 0) & (block < count)
                block = jnp.clip(block, 0, count - 1)
                more = me < count - 1 if right else me > 0
                copy = functools.partial(line_copy, view, me, count, right, block, chunk, sems)

                @pl.when(there & more)
                def sent():
                    copy().wait_send()

        return carry

    lax.fori_loop(0, chunks, one, 0)


def embed_forward_kernel(count, chars, *refs):
    (ids_ref, chars_ref, pattern_ref, cw_ref, cb_ref, mask_ref, ends_ref, off_ref, bias_ref,
     hw_hbm) = refs[:10]
    log_out, whole0_out, whole1_ref, top_ref, x_hbm, p_hbm = refs[10:16]
    kept = refs[16:22]
    y_buf, x_buf, p_buf, hw_ref, table_ref, w_ref, hb_ref, keep_sem, late_sem = refs[22:31]
    bufs = refs[31:37]
    sems0, sems1 = refs[37:41], refs[41:45]
    log_ref, whole0_ref = refs[45:47]
    t_refs, g_refs, h_refs = (bufs[0], bufs[3]), (bufs[1], bufs[4]), (bufs[2], bufs[5])
    wholes = (whole0_ref, whole1_ref)
    me = lax.axis_index("tensor")
    line_greet(me, count)
    words, filters = log_ref.shape
    tiles = words // WORD_TILE
    padded = ids_ref.shape[1] // WORD_TILE
    own = pl.ds(pl.multiple_of(me * filters, filters), filters)
    loads = [
        pltpu.make_async_copy(hw_hbm.at[layer], hw_ref.at[layer], late_sem.at[layer])
        for layer in range(2)
    ]
    for copy in loads:
        copy.start()
    stores = [
        pltpu.make_async_copy(buf, out, late_sem.at[2 + k])
        for k, (buf, out) in enumerate(zip(bufs, kept))
    ]
    logs_copy = pltpu.make_async_copy(log_ref, log_out, late_sem.at[8])
    whole_copy = pltpu.make_async_copy(whole0_ref, whole0_out, late_sem.at[9])
    y_buf[...] = jnp.zeros_like(y_buf)
    table_ref[...] = jnp.zeros_like(table_ref)
    depth, vocab_size = chars_ref.shape
    for tap in range(7):
        table_ref[depth * tap : depth * tap + depth, 0:vocab_size] = chars_ref[...]
    for layer in range(2):
        hb_ref[2 * layer : 2 * layer + 2, :] = bias_ref[layer].astype(f32)
    taps = cw_ref.shape[0]
    w_ref[0:taps, :] = (cw_ref[...].astype(f32) * mask_ref[...]).astype(bf16)
    first = lax.broadcasted_iota(jnp.int32, ends_ref.shape, 0) == 0
    bias = cb_ref[...].astype(f32).reshape(1, filters)
    w_ref[taps:, :] = jnp.where(first, bias, ends_ref[...]).astype(bf16)
    line_meet(me, count)

    def view_of(whole):
        def view(block, chunk):
            return whole.at[
                pl.ds(pl.multiple_of(chunk * WORD_TILE, WORD_TILE), WORD_TILE),
                pl.ds(pl.multiple_of(block * filters, filters), filters),
            ]

        return view

    views = [view_of(whole) for whole in wholes]

    def keep(index):
        slot = index % 2
        return [
            pltpu.make_async_copy(buf.at[slot], hbm.at[index], keep_sem.at[k, slot])
            for k, (buf, hbm) in enumerate(((x_buf, x_hbm), (p_buf, p_hbm)))
        ]

    lane_group = lax.broadcasted_iota(jnp.int32, (1, WORD_TILE, LANES), 2) // 16
    vocab = lax.broadcasted_iota(jnp.int32, (table_ref.shape[1], padded * WORD_TILE), 0)

    def tile_step(index):
        slot = index % 2

        @pl.when(index >= 2)
        def free():
            for copy in keep(index - 2):
                copy.wait()

        one_hot = jnp.where(vocab == ids_ref[pl.ds(index, 1), :], 1.0, 0.0).astype(bf16)
        found = dot(table_ref[...], one_hot, 1, 0).astype(bf16).T
        y_buf[0:padded] = found.reshape(padded, WORD_TILE, LANES)
        value = jnp.where(lane_group == 7, pattern_ref[...], y_buf[0:chars])
        for tap in range(1, 7):
            value = jnp.where(lane_group == tap, y_buf[tap : chars + tap], value)
        x2 = value.reshape(chars * WORD_TILE, LANES)
        x_buf[slot] = x2
        conv = dot(x2, w_ref[...], 1, 0).reshape(chars, WORD_TILE, filters)
        top = jnp.max(conv, axis=0)
        exps = jnp.exp(conv - top[None])
        sums = jnp.sum(exps, axis=0)
        p_buf[slot] = (exps * (1.0 / sums)[None]).astype(bf16)
        for copy in keep(index):
            copy.start()
        tile = pl.ds(pl.multiple_of(index * WORD_TILE, WORD_TILE), WORD_TILE)
        total = top + jnp.log(sums)
        log_ref[tile, :] = total
        pooled = total - off_ref[...]
        hidden = pooled * jax.nn.sigmoid(pooled)
        h_refs[0][tile, :] = hidden
        whole0_ref[tile, own] = hidden.astype(bf16)

    size = words // 4
    group = tiles // 4

    def layer_step(layer, quarter):
        start = quarter * size
        rows = pl.ds(pl.multiple_of(start, size), size)
        for j, out in enumerate((t_refs[layer], g_refs[layer])):
            bias = hb_ref[2 * layer + j : 2 * layer + j + 1, :]
            out[rows, :] = dot(wholes[layer][rows, :], hw_ref[layer, j], 1, 0) + bias

        def mix(index, carry):
            tile = pl.ds(pl.multiple_of(start + index * WORD_TILE, WORD_TILE), WORD_TILE)
            trans = t_refs[layer][tile, :]
            gate = jax.nn.sigmoid(g_refs[layer][tile, :])
            hidden = gate * (trans * jax.nn.sigmoid(trans)) + (1.0 - gate) * h_refs[layer][tile, :]
            if layer == 0:
                h_refs[1][tile, :] = hidden
                whole1_ref[tile, own] = hidden.astype(bf16)
            else:
                top_ref[tile, :] = hidden.astype(bf16)
            return carry

        lax.fori_loop(0, size // WORD_TILE, mix, 0)

    spacing = 2
    fill = spacing * (count - 1)
    shift = group + fill
    last = shift + tiles + fill

    def step_fn(step, carry):
        @pl.when(step < tiles)
        def convolve():
            tile_step(step)

        @pl.when(step < tiles + fill)
        def first_gather():
            gather_step(views[0], step, tiles, me, count, sems0, spacing)

        @pl.when(step == shift)
        def weights0():
            loads[0].wait()

        since = step - shift

        @pl.when((since >= 0) & (since < tiles) & (since % group == 0))
        def layer0():
            layer_step(0, jnp.maximum(since, 0) // group)

        @pl.when(since == tiles - group)
        def leave():
            for copy in stores[:3] + [logs_copy, whole_copy]:
                copy.start()

        @pl.when(step >= shift)
        def second_gather():
            gather_step(views[1], step - shift, tiles, me, count, sems1, spacing)

        since = step - shift - fill - group + 1

        @pl.when(since == 0)
        def weights1():
            loads[1].wait()

        @pl.when((since >= 0) & (since % group == 0))
        def layer1():
            layer_step(1, jnp.maximum(since, 0) // group)

        return carry

    lax.fori_loop(0, last, step_fn, 0)
    for copy in stores[3:]:
        copy.start()
    for index in (tiles - 2, tiles - 1):
        for copy in keep(index):
            copy.wait()
    for sems, view in zip((sems0, sems1), views):
        gather_drain(view, tiles, me, count, sems)
    for copy in stores + [logs_copy, whole_copy]:
        copy.wait()


def embed_forward(ids, table, pattern, conv, off, bias, weight, count, chars, cid):
    filters = conv[0].shape[1]
    tiles = ids.shape[0]
    words = tiles * WORD_TILE
    shape = jax.ShapeDtypeStruct
    flat = (words, filters)
    return pl.pallas_call(
        functools.partial(embed_forward_kernel, count, chars),
        out_shape=(
            shape(flat, f32),
            shape((words, count * filters), bf16),
            shape((words, count * filters), bf16),
            shape(flat, bf16),
            shape((tiles, chars * WORD_TILE, LANES), bf16),
            shape((tiles, chars, WORD_TILE, filters), bf16),
        )
        + (shape(flat, f32),) * 6,
        in_specs=[VMEM] * 9 + [ANY],
        out_specs=(ANY, ANY, VMEM, VMEM) + (ANY,) * 8,
        scratch_shapes=[
            pltpu.VMEM((chars + 6, WORD_TILE, LANES), bf16),
            pltpu.VMEM((2, chars * WORD_TILE, LANES), bf16),
            pltpu.VMEM((2, chars, WORD_TILE, filters), bf16),
            pltpu.VMEM(weight.shape, bf16),
            pltpu.VMEM((LANES, 264), bf16),
            pltpu.VMEM((LANES, filters), bf16),
            pltpu.VMEM((8, filters), f32),
            DMA((2, 2)),
            DMA((10,)),
        ]
        + [pltpu.VMEM(flat, f32)] * 6
        + [DMA((count, tiles))] * 8
        + [pltpu.VMEM(flat, f32), pltpu.VMEM((words, count * filters), bf16)],
        compiler_params=params(cid, 58),
        name="embed_forward",
    )(ids, table, pattern, *conv, off, bias, weight)


class LineSum:
    def __init__(self, count, me, chunks, spacing, first, sums, parts, outs, buffers, sems):
        self.count, self.me, self.chunks, self.spacing = count, me, chunks, spacing
        self.first, self.messages, self.parts, self.outs = first, sums * chunks, parts, outs
        self.buffers, self.sems = buffers, sems
        self.fill = spacing * (count - 1)

    def tile(self, number, size=1):
        rows = self.parts.shape[1] // self.chunks * size
        return pl.ds(pl.multiple_of(number % self.chunks // size * rows, rows), rows)

    def place(self, right, number):
        count, me = self.count, self.me
        k, chunk, tile = self.first + number // self.chunks, number % self.chunks, self.tile(number)
        buf = self.buffers[0 if right else 1]
        send, recv = self.sems[:2] if right else self.sems[2:]
        to = jnp.minimum(me + 1, count - 1) if right else jnp.maximum(me - 1, 0)
        first, passed = [
            functools.partial(
                pltpu.make_async_remote_copy,
                src_ref=src.at[k, tile],
                dst_ref=buf.at[k, tile],
                send_sem=send.at[k, chunk],
                recv_sem=recv.at[k, chunk],
                device_id={"tensor": to},
                device_id_type=MESH,
            )
            for src in (self.parts, buf)
        ]
        return k, tile, buf, first, passed

    def step(self, step):
        for right in (True, False):
            lag = self.me if right else self.count - 1 - self.me
            number = step - self.spacing * lag
            here = (number >= 0) & (number < self.messages)
            number = jnp.clip(number, 0, self.messages - 1)
            k, tile, buf, first, passed = self.place(right, number)

            @pl.when(here & (lag == 0))
            def start():
                first().start()

            @pl.when(here & (lag > 0))
            def middle():
                first().wait_recv()
                got = buf[k, tile, :].astype(f32)

                @pl.when(lag < self.count - 1)
                def forward():
                    buf[k, tile, :] = (got + self.parts[k, tile, :].astype(f32)).astype(bf16)
                    passed().start()

                self.outs[k, tile, :] += got

    def drain(self):
        def one(number, carry):
            for right in (True, False):
                lag = self.me if right else self.count - 1 - self.me
                k, tile, buf, first, passed = self.place(right, number)

                @pl.when(lag < self.count - 1)
                def sent():
                    first().wait_send()

            return carry

        lax.fori_loop(0, self.messages, one, 0)

    def run(self, before, done, after, extra):
        size = self.chunks // 4

        def one(step, carry):
            @pl.when((step < self.chunks) & (step % size == 0))
            def prepare():
                before(self.tile(jnp.minimum(step, self.chunks - 1), size))

            self.step(step)
            for k, work in extra.items():
                pl.when(step == k)(work)
            number = step - self.fill
            for k in range(len(done)):

                @pl.when((number >= k * self.chunks) & (number < (k + 1) * self.chunks))
                def finish():
                    done[k](self.tile(jnp.maximum(number, 0)))

                    @pl.when(number % size == size - 1)
                    def quarter():
                        after[k](self.tile(jnp.maximum(number, 0), size))

            return carry

        lax.fori_loop(0, self.messages + self.fill, one, 0)
        self.drain()


def norm_parts(values):
    centered = values - jnp.mean(values, axis=-1, keepdims=True)
    root = lax.rsqrt(jnp.mean(centered * centered, axis=-1, keepdims=True) + norm_eps)
    return centered * root, root


def norm_back(values, gain, cotangent):
    nv, root = norm_parts(values)
    scaled = cotangent * gain
    inner = jnp.mean(scaled, axis=-1, keepdims=True)
    along = jnp.mean(scaled * nv, axis=-1, keepdims=True)
    return root * (scaled - inner - nv * along), cotangent * nv


def gelu_parts(values):
    cdf = 0.5 * (1.0 + lax.erf(values * 0.7071067811865476))
    slope = cdf + values * jnp.exp(-0.5 * values * values) * 0.3989422804014327
    return values * cdf, slope


def column_sum(values):
    return jnp.sum(values, axis=0, keepdims=True)


def mix_back(d_hidden, trans, gate_pre, previous):
    gate = jax.nn.sigmoid(gate_pre)
    sig = jax.nn.sigmoid(trans)
    act = trans * sig
    d_trans = (d_hidden * gate * (sig * (1.0 + trans * (1.0 - sig)))).astype(bf16)
    d_gate = (d_hidden * (act - previous) * gate * (1.0 - gate)).astype(bf16)
    return d_trans, d_gate, (1.0 - gate) * d_hidden


def encoder_kernel(count, chunks, spacing, *refs):
    top_ref, pw_ref, qw_ref, ow_ref, uw_ref, dw_ref = refs[:6]
    bias_refs, norm_refs, qv_ref, og_ref, len_ref = refs[6:10], refs[10:12], *refs[12:15]
    mix_refs = refs[15:18]
    refs = refs[3:]
    enc_ref, prev_ref, dt_ref, dg_ref, mix_sums = refs[15:20]
    refs = refs[3:]
    tra_out, trb_ref, sums_ref, qsum_ref, vec_ref, qb_ref = refs[17:23]
    (inp, mid, slope, sent, sent_mid, act, d_two, d_up, d_branch, d_emb, qkv, attended, probs,
     d_heads, d_proj, grad_all, enc_all, outs, parts, from_left, from_right) = refs[23:44]
    line_sems, gather_sems = refs[44:48], refs[48:52]
    tra_ref, tra_sem = refs[52:54]
    tra_copy = pltpu.make_async_copy(tra_ref, tra_out, tra_sem)
    emb, midpre, fin, dmid, din = [outs.at[k] for k in range(5)]
    me = lax.axis_index("tensor")
    line_greet(me, count)
    words, features = inp.shape
    heads = attended.shape[1] // HEAD_DIM
    hidden = heads * HEAD_DIM
    scale = HEAD_DIM ** (-0.5)
    own = words // count
    own_tile = pl.ds(pl.multiple_of(me * own, own), own)
    grad_all[own_tile, :] = og_ref[...]
    sums_ref[...] = jnp.zeros_like(sums_ref)
    mix_sums[...] = jnp.zeros_like(mix_sums)
    trb_ref[...] = jnp.zeros_like(trb_ref)
    for k, bias_ref in zip((0, 1, 2, 9), bias_refs):
        vec_ref[k : k + 1, :] = bias_ref[...].astype(f32).reshape(1, features)
    for k, norm_ref in zip((3, 6), norm_refs):
        vec_ref[k : k + 3, :] = norm_ref[...].astype(f32)
    qb_ref[...] = jnp.zeros_like(qb_ref)
    ends = qv_ref[...].astype(f32)
    qb_ref[:, 0:hidden] = ends[0:1]
    qb_ref[:, 2 * hidden : 3 * hidden] = ends[1:2]
    live = lax.broadcasted_iota(jnp.int32, (1, words), 1) < len_ref[0]

    def line(first, sums):
        return LineSum(
            count, me, chunks, spacing, first, sums, parts, outs, (from_left, from_right), line_sems
        )

    def gather_view(block, chunk):
        return grad_all.at[pl.ds(pl.multiple_of(block * own, own), own)]

    def tiles(size, work):
        def one(index, carry):
            work(pl.ds(pl.multiple_of(index * size, size), size))
            return carry

        lax.fori_loop(0, words // size, one, 0)

    def product(lhs, rhs, side, k):
        def work(tile):
            value = dot(lhs[tile, :], rhs[...], 1, side).astype(bf16)
            parts[k, tile, :] = value
            outs[k, tile, :] = value.astype(f32)

        return work

    def grads(lhs, rhs, out_ref, lane):
        def half(k):
            def work():
                depth = features // 2
                value = dot(lhs[:, depth * k : depth * k + depth], rhs[...], 0, 0).astype(bf16)
                for i in range(2):
                    for j in range(2):
                        start = (2 * i + j) * (depth // 4)
                        out_ref[k, i, j, :, lane : lane + rhs.shape[1]] = value[
                            start : start + depth // 4
                        ]

            return work

        return [half(0), half(1)]

    def row(index):
        return vec_ref[index : index + 1, :]

    def add_sum(index, value):
        sums_ref[index : index + 1, :] += column_sum(value)

    line_meet(me, count)

    def first_norm(tile):
        value = emb[tile, :] + row(0)
        emb[tile, :] = value
        value = norm_parts(value)[0] * row(3) + row(6)
        inp[tile, :] = value
        sent[tile, :] = value.astype(bf16)

    def project(tile):
        qkv[tile, :] = (dot(sent[tile, :], qw_ref[...], 1, 1) + qb_ref[...]).astype(bf16)

    line(0, 1).run(product(top_ref, pw_ref, 0, 0), [first_norm], [project], {})
    gather_step(gather_view, 0, 1, me, count, gather_sems)

    for head in range(heads):
        lanes = slice(head * HEAD_DIM, (head + 1) * HEAD_DIM)
        keys = slice(hidden + head * HEAD_DIM, hidden + (head + 1) * HEAD_DIM)
        vals = slice(2 * hidden + head * HEAD_DIM, 2 * hidden + (head + 1) * HEAD_DIM)

        def attend(tile):
            scores = dot(qkv[tile, lanes], qkv[:, keys], 1, 1) * scale
            scores = jnp.where(live, scores, big_neg)
            exps = jnp.exp(scores - jnp.max(scores, axis=1, keepdims=True))
            value = exps * (1.0 / jnp.sum(exps, axis=1, keepdims=True))
            probs[head, tile, :] = value
            attended[tile, lanes] = dot(value.astype(bf16), qkv[:, vals], 1, 0).astype(bf16)

        tiles(256, attend)
        if head == heads - 2:
            gather_step(gather_view, 1, 1, me, count, gather_sems)

    def pass_grads():
        for step in range(2, count - 1):
            gather_step(gather_view, step, 1, me, count, gather_sems)

    def second_norm(tile):
        value = midpre[tile, :] + inp[tile, :] + row(1)
        midpre[tile, :] = value
        value = norm_parts(value)[0] * row(4) + row(7)
        mid[tile, :] = value
        sent_mid[tile, :] = value.astype(bf16)


    send_down = product(act, dw_ref, 0, 2)
    send_up = product(d_up, uw_ref, 1, 3)

    def feed(tile):
        value, back = gelu_parts(dot(sent_mid[tile, :], uw_ref[...], 1, 0) + row(9))
        act[tile, :] = value.astype(bf16)
        slope[tile, :] = back
        send_down(tile)

    def third_norm(tile):
        value = fin[tile, :] + mid[tile, :] + row(2)
        cotangent = grad_all[tile, :].astype(f32)
        enc_all[tile, :] = (norm_parts(value)[0] * row(5) + row(8)).astype(bf16)
        back, gain = norm_back(value, row(5), cotangent)
        fin[tile, :] = back
        low = back.astype(bf16)
        d_two[tile, :] = low
        add_sum(2, low.astype(f32))
        add_sum(5, gain)
        add_sum(8, cotangent)

    def feed_back(tile):
        value = (dot(d_two[tile, :], dw_ref[...], 1, 1) * slope[tile, :]).astype(bf16)
        d_up[tile, :] = value
        add_sum(9, value.astype(f32))
        send_up(tile)

    def second_back(tile):
        cotangent = dmid[tile, :] + fin[tile, :]
        back, gain = norm_back(midpre[tile, :], row(4), cotangent)
        dmid[tile, :] = back
        low = back.astype(bf16)
        d_branch[tile, :] = low
        add_sum(1, low.astype(f32))
        add_sum(4, gain)
        add_sum(7, cotangent)

    def heads_back(tile):
        d_heads[tile, :] = dot(d_branch[tile, :], ow_ref[...], 1, 1).astype(bf16)

    extra = {2: pass_grads}
    extra[chunks + 4] = lambda: gather_step(
        gather_view, count - 1, 1, me, count, gather_sems
    )
    work = grads(d_two, act, tra_ref, features) + grads(sent_mid, d_up, tra_ref, 0)
    extra.update({2 * chunks + spacing * (count - 1) + k: w for k, w in enumerate(work)})
    line(1, 3).run(
        product(attended, ow_ref, 0, 1),
        [second_norm, third_norm, second_back], [feed, feed_back, heads_back], extra
    )
    tra_copy.start()
    enc_ref[...] = enc_all[own_tile, :]

    for head in range(heads):
        lanes = slice(head * HEAD_DIM, (head + 1) * HEAD_DIM)
        keys = slice(hidden + head * HEAD_DIM, hidden + (head + 1) * HEAD_DIM)
        vals = slice(2 * hidden + head * HEAD_DIM, 2 * hidden + (head + 1) * HEAD_DIM)
        weights = probs[head]
        d_out = d_heads[:, lanes]
        d_proj[:, vals] = dot(weights.astype(bf16), d_out, 0, 0).astype(bf16)
        d_probs = dot(d_out, qkv[:, vals], 1, 1)
        inner = jnp.sum(d_probs * weights, axis=1, keepdims=True)
        d_scores = (weights * (d_probs - inner)).astype(bf16)
        d_proj[:, lanes] = (dot(d_scores, qkv[:, keys], 1, 0) * scale).astype(bf16)
        d_proj[:, keys] = (dot(d_scores, qkv[:, lanes], 0, 0) * scale).astype(bf16)
    qsum_ref[...] = column_sum(d_proj[...].astype(f32))

    def first_back(tile):
        cotangent = din[tile, :] + dmid[tile, :]
        back, gain = norm_back(emb[tile, :], row(3), cotangent)
        low = back.astype(bf16)
        d_emb[tile, :] = low
        add_sum(0, low.astype(f32))
        add_sum(3, gain)
        add_sum(6, cotangent)

    def last(tile):
        d_hidden = dot(d_emb[tile, :], pw_ref[...], 1, 1)
        d_trans, d_gate, prev_ref[tile, :] = mix_back(d_hidden, *[ref[tile, :] for ref in mix_refs])
        dt_ref[tile, :] = d_trans
        dg_ref[tile, :] = d_gate
        mix_sums[0:1, :] += column_sum(d_trans.astype(f32))
        mix_sums[1:2, :] += column_sum(d_gate.astype(f32))

    work = grads(sent, d_proj, trb_ref, top_ref.shape[1])
    work += grads(d_branch, attended, trb_ref, 1152)
    line(4, 1).run(
        product(d_proj, qw_ref, 0, 4), [first_back], [last], {5 + k: w for k, w in enumerate(work)}
    )
    for work in grads(d_emb, top_ref, trb_ref, 0):
        work()
    gather_drain(gather_view, 1, me, count, gather_sems)
    tra_copy.wait()


def encoder(top, weights, biases, out_grad, lengths, mix, count, cid):
    words, filters = top.shape
    features = weights[0].shape[1]
    three = weights[1].shape[0]
    units = weights[3].shape[1]
    hidden = three // 3
    chunks = 16
    spacing = (chunks - chunks // 4) // (count - 1)
    shape = jax.ShapeDtypeStruct
    rows = features // 8
    scratch = [pltpu.VMEM((16, features), f32), pltpu.VMEM((1, three), f32)]
    scratch += [pltpu.VMEM((words, n), f32) for n in (features, features, units)]
    scratch += [
        pltpu.VMEM((words, n), bf16)
        for n in (features, features, units, features, units, features, features, three, hidden)
    ]
    scratch += [pltpu.VMEM((hidden // HEAD_DIM, words, words), f32)]
    scratch += [pltpu.VMEM((words, n), bf16) for n in (hidden, three, features, features)]
    scratch += [pltpu.VMEM((5, words, features), f32)]
    scratch += [pltpu.VMEM((5, words, features), bf16)] * 3
    scratch += [DMA((5, chunks))] * 4 + [DMA((count, 1))] * 4
    scratch += [pltpu.VMEM((2, 2, 2, rows, features + units), bf16), DMA]
    return pl.pallas_call(
        functools.partial(encoder_kernel, count, chunks, spacing),
        out_shape=(
            shape((words // count, features), bf16),
            shape((words, filters), f32),
            shape((words, filters), bf16),
            shape((words, filters), bf16),
            shape((2, filters), f32),
            shape((2, 2, 2, rows, features + units), bf16),
            shape((2, 2, 2, rows, 1408), bf16),
            shape((16, features), f32),
            shape((1, three), f32),
        ),
        in_specs=[VMEM] * 14 + [pl.BlockSpec(memory_space=pltpu.SMEM)] + [VMEM] * 3,
        out_specs=(VMEM,) * 5 + (ANY, VMEM, VMEM, VMEM),
        scratch_shapes=scratch,
        compiler_params=params(cid, 58),
        name="encoder",
    )(top, *weights, *biases, out_grad, lengths, *mix)


class LineScatter:
    def __init__(self, count, me, chunks, spacing, p_ref, out_ref, from_left, from_right, sems):
        self.count, self.me, self.chunks, self.spacing = count, me, chunks, spacing
        self.p_ref, self.out_ref = p_ref, out_ref
        self.from_left, self.from_right, self.sems = from_left, from_right, sems
        self.messages = chunks * (count - 1)
        self.steps = self.messages + spacing * (count - 1)

    def place(self, right, number):
        count, me = self.count, self.me
        lag = me if right else count - 1 - me
        chunk = number // (count - 1)
        far = count - 1 - number % (count - 1)
        block = far if right else count - 1 - far
        words, filters = self.out_ref.shape
        rows = words // self.chunks
        tile = pl.ds(pl.multiple_of(chunk * rows, rows), rows)
        lanes = pl.ds(pl.multiple_of(block * filters, filters), filters)
        buf = self.from_left if right else self.from_right
        send, recv = self.sems[:2] if right else self.sems[2:]
        to = jnp.minimum(me + 1, count - 1) if right else jnp.maximum(me - 1, 0)
        first, passed = [
            functools.partial(
                pltpu.make_async_remote_copy,
                src_ref=src.at[tile, lanes],
                dst_ref=buf.at[tile, lanes],
                send_sem=send.at[block, chunk],
                recv_sem=recv.at[block, chunk],
                device_id={"tensor": to},
                device_id_type=MESH,
            )
            for src in (self.p_ref, buf)
        ]
        return lag, far, tile, lanes, buf, first, passed

    def step(self, step):
        for right in (True, False):
            lag = self.me if right else self.count - 1 - self.me
            number = step - self.spacing * lag
            here = (number >= 0) & (number < self.messages)
            number = jnp.clip(number, 0, self.messages - 1)
            lag, far, tile, lanes, buf, first, passed = self.place(right, number)

            @pl.when(here & (lag == 0))
            def start():
                first().start()

            @pl.when(here & (lag > 0) & (far > lag))
            def middle():
                first().wait_recv()
                buf[tile, lanes] = (
                    buf[tile, lanes].astype(f32) + self.p_ref[tile, lanes].astype(f32)
                ).astype(bf16)
                passed().start()

            @pl.when(here & (lag > 0) & (far == lag))
            def last():
                first().wait_recv()
                self.out_ref[tile, :] += buf[tile, lanes].astype(f32)

    def due(self, chunk):
        return (chunk + self.spacing) * (self.count - 1)

    def finished(self, step, work, after=0):
        each = self.count - 1
        since = step - after - self.spacing * each

        @pl.when((since >= 0) & (since % each == 0) & (since < self.messages))
        def call():
            work(jnp.maximum(since, 0) // each)

    def drain(self):
        def one(number, carry):
            for right in (True, False):
                lag, far, tile, lanes, buf, first, passed = self.place(right, number)

                @pl.when(far > lag)
                def sent():
                    first().wait_send()

            return carry

        lax.fori_loop(0, self.messages, one, 0)


class DpSum:
    def __init__(self, cell, peers, x_first, sems, base):
        self.c, self.x, self.y = cell
        self.peers, self.x_first, self.base = peers, x_first, base
        self.send, self.recv = sems
        self.src = self.half = self.in0 = self.in1 = self.mid = self.in2 = None

    def remote(self, number, src, dst, bit):
        return pltpu.make_async_remote_copy(
            src_ref=src,
            dst_ref=dst,
            send_sem=self.send.at[self.base + number],
            recv_sem=self.recv.at[self.base + number],
            device_id=self.peers[bit],
            device_id_type=MESH,
        )

    def copy0(self):
        return self.remote(0, self.src.at[:, :, 1 - self.c], self.in0, 0)

    def copy1(self):
        if self.x_first:
            return self.remote(1, self.half.at[:, 1 - self.x], self.in1, 1)
        return self.remote(1, self.half.at[1 - self.y], self.in1, 2)

    def copy2(self):
        own = self.y if self.x_first else self.x
        return self.remote(2, self.mid.at[1 - own], self.in2, 2 if self.x_first else 1)

    def finish0(self):
        self.copy0().wait()

        def one(k, carry):
            i, j = k // 2, k % 2
            self.half[i, j] = (self.half[i, j].astype(f32) + self.in0[i, j].astype(f32)).astype(bf16)
            return carry

        lax.fori_loop(0, 4, one, 0)

    def finish1(self):
        self.copy1().wait()

        def one(k, carry):
            kept = self.half[k, self.x] if self.x_first else self.half[self.y, k]
            self.mid[k] = (kept.astype(f32) + self.in1[k].astype(f32)).astype(bf16)
            return carry

        lax.fori_loop(0, 2, one, 0)

    def finish2(self):
        self.copy2().wait()
        own = self.y if self.x_first else self.x
        return self.mid[own].astype(f32) + self.in2[...].astype(f32)


def dp_cell(place):
    cell = [place % 2, (place // 2) % 2, place // 4]
    return cell, [{"dp": place + (1 - 2 * cell[bit]) * 2**bit} for bit in range(3)]


def greet_all(peers):
    barrier = pltpu.get_barrier_semaphore()
    for peer in peers:
        pl.semaphore_signal(barrier, inc=1, device_id=peer, device_id_type=MESH)


def meet_all(peers):
    pl.semaphore_wait(pltpu.get_barrier_semaphore(), len(peers))


def weight_grad_piece(piece, whole_ref, d_refs, outs):
    rows = outs[0].shape[-2]
    lanes = pl.ds(pl.multiple_of(piece * rows, rows), rows)
    index = (piece // 4, (piece // 2) % 2, piece % 2)
    for d_ref, out in zip(d_refs, outs):
        out[index] = dot(whole_ref[:, lanes], d_ref[...], 0, 0).astype(bf16)


def highway_back_kernel(count, chunks, reduce, *refs):
    prev1_hbm, dt1_ref, dg1_ref, sums1_ref = refs[:4]
    late_hbm = refs[4:9]
    refs = refs[9:]
    if reduce:
        tr_hbm = refs[:2]
        refs = refs[2:]
    part0_ref, prev0_ref, dt0_ref, dg0_ref, sums_ref = refs[:5]
    refs = refs[5:]
    if reduce:
        tr_outs = refs[2:4]
        hw_refs, tr_half = refs[4:6], refs[6:8]
        in0s, in1s = refs[8:12], refs[12:16]
        mids, in2s = list(refs[:2]) + list(refs[16:18]), refs[18:20]
        dp_sems = refs[20:22]
        refs = refs[22:]
    else:
        hw_refs = refs[:2]
        refs = refs[2:]
    part1_ref, from_left, from_right, d_h1_ref = refs[:4]
    t0_ref, g0_ref, h0_ref, whole1_ref, w_ref, late_sem = refs[4:10]
    sems = refs[10:]
    me = lax.axis_index("tensor")
    words, filters = dt1_ref.shape
    prev_load = pltpu.make_async_copy(prev1_hbm, d_h1_ref, late_sem.at[8])
    prev_load.start()
    w_hbm = late_hbm[4]
    loads = [
        pltpu.make_async_copy(w_hbm.at[1], w_ref.at[1], late_sem.at[0]),
        pltpu.make_async_copy(late_hbm[3], whole1_ref, late_sem.at[1]),
        pltpu.make_async_copy(w_hbm.at[0], w_ref.at[0], late_sem.at[2]),
        pltpu.make_async_copy(late_hbm[0], t0_ref, late_sem.at[3]),
        pltpu.make_async_copy(late_hbm[1], g0_ref, late_sem.at[4]),
        pltpu.make_async_copy(late_hbm[2], h0_ref, late_sem.at[5]),
    ]
    for copy in loads:
        copy.start()
    items = []
    if reduce:
        cell, peers = dp_cell(lax.axis_index("dp"))
        keep = [
            pltpu.make_async_copy(tr_hbm[k].at[:, :, cell[0]], tr_half[k], late_sem.at[6 + k])
            for k in range(2)
        ]
        for copy in keep:
            copy.start()
    ring = [{"tensor": lax.rem(me + k, count)} for k in range(1, count)]
    everyone = (peers if reduce else []) + ring
    greet_all(everyone)
    sums_ref[0:2, :] = jnp.zeros_like(sums1_ref)
    sums_ref[2:4, :] = sums1_ref[...]

    def mix(layer, d_h_ref, t_ref, g_ref, h_ref, dt_ref, dg_ref, prev_ref, tile):
        dt, dg, prev = mix_back(d_h_ref[tile, :], t_ref[tile, :], g_ref[tile, :], h_ref[tile, :])
        dt_ref[tile, :] = dt
        dg_ref[tile, :] = dg
        prev_ref[tile, :] = prev
        for j, d in enumerate((dt, dg)):
            sums_ref[2 * layer + j : 2 * layer + j + 1, :] += jnp.sum(
                d.astype(f32), axis=0, keepdims=True
            )

    def products(layer, dt_ref, dg_ref, p_ref, part):
        tile = slice(part * (words // 2), (part + 1) * (words // 2))

        def one(block, carry):
            lanes = pl.ds(pl.multiple_of(block * filters, filters), filters)
            p_ref[tile, lanes] = (
                dot(dt_ref[tile, :], w_ref[layer, 0, lanes, :], 1, 1)
                + dot(dg_ref[tile, :], w_ref[layer, 1, lanes, :], 1, 1)
            ).astype(bf16)
            return carry

        lax.fori_loop(0, count, one, 0)

    rows = words // chunks

    def tile_of(index):
        return pl.ds(pl.multiple_of(index * rows, rows), rows)

    def own_part(part):
        tile = slice(part * (words // 2), (part + 1) * (words // 2))
        d_h1_ref[tile, :] += part1_ref[
            tile, pl.ds(pl.multiple_of(me * filters, filters), filters)
        ].astype(f32)

    loads[0].wait()
    products(1, dt1_ref, dg1_ref, part1_ref, 0)
    prev_load.wait()
    own_part(0)
    meet_all(everyone)
    if reduce:
        for k in range(4):
            item = DpSum(cell, peers, k % 2 == 0, dp_sems, 3 * k)
            if k < 2:
                item.src, item.half = hw_refs[k], hw_refs[k].at[:, :, cell[0]]
            else:
                item.src, item.half = tr_hbm[k - 2], tr_half[k - 2]
            item.in0, item.in1, item.mid = in0s[k], in1s[k], mids[k]
            if k >= 2:
                item.in2 = in2s[k - 2]
            items.append(item)
        for item in items[2:]:
            item.copy0().start()
    scatter = LineScatter(
        count, me, chunks, 3, part1_ref, d_h1_ref, from_left, from_right, sems
    )

    def step_fn(step, carry):
        scatter.step(step)

        @pl.when(step == 0)
        def rest():
            products(1, dt1_ref, dg1_ref, part1_ref, 1)
            own_part(1)
            loads[1].wait()

        @pl.when((step > 0) & (step <= 8))
        def grads():
            weight_grad_piece(step - 1, whole1_ref, (dt1_ref, dg1_ref), hw_refs)

        @pl.when(step == 9)
        def late():
            for copy in loads[2:]:
                copy.wait()

        if reduce:

            @pl.when(step == 4)
            def encoder1():
                for copy in keep:
                    copy.wait()
                for item in items[2:]:
                    item.finish0()
                    item.copy1().start()

            @pl.when(step == 9)
            def highway0():
                for item in items[:2]:
                    item.copy0().start()

            @pl.when(step == 15)
            def highway1():
                for item in items[:2]:
                    item.finish0()
                    item.copy1().start()

            @pl.when(step == 20)
            def encoder2():
                for item in items[2:]:
                    item.finish1()
                    item.copy2().start()

        scatter.finished(
            step,
            lambda chunk: mix(
                0, d_h1_ref, t0_ref, g0_ref, h0_ref, dt0_ref, dg0_ref, prev0_ref, tile_of(chunk)
            ),
        )

        @pl.when(step == scatter.due(chunks // 2 - 1) + 1)
        def early():
            products(0, dt0_ref, dg0_ref, part0_ref, 0)

        return carry

    lax.fori_loop(0, scatter.steps, step_fn, 0)
    products(0, dt0_ref, dg0_ref, part0_ref, 1)
    for item in items[:2]:
        item.finish1()
    for item, out in zip(items[2:], tr_outs if reduce else ()):
        out[...] = item.finish2().astype(bf16)
    scatter.drain()


def highway_back(prev1, dt1, dg1, sums1, t0, g0, h0, whole1, weight, tra, trb, count, cid):
    words, filters = dt1.shape
    chunks = 8
    reduce = tra is not None
    rows = whole1.shape[1] // 8
    shape = jax.ShapeDtypeStruct
    out_shape = [
        shape(whole1.shape, bf16),
        shape((words, filters), f32),
        shape((words, filters), bf16),
        shape((words, filters), bf16),
        shape((4, filters), f32),
    ]
    operands = [prev1, dt1, dg1, sums1, t0, g0, h0, whole1, weight]
    in_specs = [ANY] + [VMEM] * 3 + [ANY] * 5
    hw_shape = (2, 2, 2, rows, filters)
    scratch = []
    if reduce:
        operands += [tra, trb]
        in_specs += [ANY] * 2
        tails = [hw_shape[-2:], hw_shape[-2:], tra.shape[-2:], trb.shape[-2:]]
        out_shape += [shape((2,) + tail, bf16) for tail in tails[:2]]
        out_shape += [shape(tail, bf16) for tail in tails[2:]]
        scratch += [pltpu.VMEM(hw_shape, bf16)] * 2
        scratch += [pltpu.VMEM((2, 2) + tail, bf16) for tail in tails[2:]]
        scratch += [pltpu.VMEM((2, 2) + tail, bf16) for tail in tails]
        scratch += [pltpu.VMEM((2,) + tail, bf16) for tail in tails + tails[2:]]
        scratch += [pltpu.VMEM(tail, bf16) for tail in tails[2:]]
        scratch += [DMA((12,))] * 2
    else:
        out_shape += [shape(hw_shape, bf16)] * 2
    scratch += [pltpu.VMEM(whole1.shape, bf16)] * 3
    scratch += [pltpu.VMEM((words, filters), f32)] * 4
    scratch += [pltpu.VMEM(whole1.shape, bf16), pltpu.VMEM(weight.shape, bf16), DMA((9,))]
    scratch += [DMA((count, chunks))] * 4
    return pl.pallas_call(
        functools.partial(highway_back_kernel, count, chunks, reduce),
        out_shape=tuple(out_shape),
        in_specs=in_specs,
        out_specs=tuple([VMEM] * len(out_shape)),
        scratch_shapes=scratch,
        compiler_params=params(cid, 58),
        name="highway_back",
    )(*operands)


class Spread:
    def __init__(self, sems, in_ref, got, mid, out_ref):
        self.dp_count, self.count = out_ref.shape[:2]
        self.sems, self.in_ref, self.got, self.mid, self.out_ref = sems, in_ref, got, mid, out_ref
        self.me = lax.axis_index("tensor")
        self.place = lax.axis_index("dp")

    def remote(self, src, dst, phase, hop, axis, peer):
        send, recv = self.sems[2 * phase : 2 * phase + 2]
        index = (hop - 1,) if phase < 2 else hop
        return pltpu.make_async_remote_copy(
            src_ref=src, dst_ref=dst, send_sem=send.at[index], recv_sem=recv.at[index],
            device_id={axis: peer}, device_id_type=MESH,
        )

    def scatter(self, hop):
        peer = lax.rem(self.place + hop, self.dp_count)
        return self.remote(self.in_ref.at[peer], self.got.at[hop - 1], 0, hop, "dp", peer)

    def across(self, hop):
        peer = lax.rem(self.me + hop, self.count)
        return self.remote(self.mid.at[self.me], self.mid.at[self.me], 1, hop, "tensor", peer)

    def around(self, hop, rank):
        peer = lax.rem(self.place + hop, self.dp_count)
        dst = self.out_ref.at[self.place, rank]
        return self.remote(self.mid.at[rank], dst, 2, (rank, hop - 1), "dp", peer)

    def hand_on(self, rank):
        self.loop(lambda hop: self.around(hop, rank).start(), self.dp_count)
        self.out_ref[self.place, rank] = self.mid[rank]

    def loop(self, fn, stop):
        def one(hop, carry):
            fn(hop)
            return carry

        lax.fori_loop(1, stop, one, 0)

    def first(self):
        self.loop(lambda hop: self.scatter(hop).start(), self.dp_count)

    def second(self):
        self.loop(lambda hop: self.scatter(hop).wait(), self.dp_count)
        total = lax.fori_loop(
            0,
            self.dp_count - 1,
            lambda k, acc: acc + self.got[k].astype(f32),
            self.in_ref[self.place].astype(f32),
        )
        self.mid[self.me] = total.astype(bf16)
        self.loop(lambda hop: self.across(hop).start(), self.count)
        self.hand_on(self.me)

    def third(self):
        def one(hop):
            self.across(hop).wait()
            self.hand_on(lax.rem(self.me + self.count - hop, self.count))

        self.loop(one, self.count)

    def finish(self):
        for rank in range(self.count):
            self.loop(lambda hop: self.around(hop, rank).wait(), self.dp_count)


def early_parts(rows):
    start = 0
    for source, (count, width) in enumerate(rows):
        for block in range(-(-width // LANES)):
            yield source, block, start, count, min(LANES, width - block * LANES)
            start += count


EARLY = ((4, 512), (1, 576), (10, 768))


def pack_early(ref, *sources):
    ref[...] = jnp.zeros_like(ref)
    for source, block, start, count, width in early_parts(EARLY):
        value = sources[source][0:count, block * LANES : block * LANES + width]
        for k in range(count):
            place = start + k
            ref[place // 16, place % 16 : place % 16 + 1, 0:width] = value[k : k + 1]


def unpack_early(ref, hwb_out, vec_out, upb_out, qv_out):
    for t in range(ref.shape[1]):
        for source, block, start, count, width in early_parts(EARLY):
            for k in range(count):
                place = start + k
                row = ref[place // 16, t, :, :].astype(f32)[place % 16 : place % 16 + 1, 0:width]
                lane = block * LANES
                if source == 0:
                    hwb_out[k : k + 1, t * 512 + lane : t * 512 + lane + width] = row
                elif source == 2 and k == 9:
                    upb_out[:, t * 768 + lane : t * 768 + lane + width] = row
                elif source == 2 and t == 0:
                    vec_out[k : k + 1, lane : lane + width] = row
                elif source == 1:
                    for out, low in ((0, 0), (1, 384)):
                        left, right = max(lane, low), min(lane + width, low + 192)
                        if left < right:
                            place_at = t * 192 + left - low
                            qv_out[out : out + 1, place_at : place_at + right - left] = row[
                                :, left - lane : right - lane
                            ]


def conv_backward_kernel(count, chars, cuts, *refs):
    (ids_ref, x_hbm, p_hbm, cw_ref, mask_ref, off_ref, log_ref, prev_ref, part_ref, whole_hbm,
     dt_ref, dg_ref) = refs[:12]
    refs = refs[12:]
    if cuts:
        mids_in = refs[:2]
        hb_sums, proj_sums, row_sums = refs[2:5]
        hw_out, convw_out, convb_out, table_out, hwb_out, vec_out, upb_out, qv_out = refs[5:13]
        dw_ref, table_ref, hw_a, hw_b = refs[13:17]
        in0s, in1s, mids, in2s = refs[17:19], refs[19:21], refs[21:23], refs[23:27]
        dp_sems = refs[27:29]
        spreads = [Spread(refs[33 + 10 * k : 39 + 10 * k], *refs[29 + 10 * k : 33 + 10 * k])
                   for k in range(2)]
        refs = refs[49:]
    else:
        dw_ref, table_ref, hw_a, hw_b = refs[:4]
        refs = refs[4:]
    (pad_ref, stage_ref, grad_ref, from_left, from_right, x_buf, p_buf, whole_ref, wb_ref,
     load_sem, whole_sem) = refs[:11]
    line_sems = refs[11:]
    me = lax.axis_index("tensor")
    words, filters = log_ref.shape
    tiles = words // WORD_TILE
    padded = ids_ref.shape[1] // WORD_TILE

    def load(index):
        slot = index % 2
        return [
            pltpu.make_async_copy(hbm.at[index], buf.at[slot], load_sem.at[k, slot])
            for k, (buf, hbm) in enumerate(((x_buf, x_hbm), (p_buf, p_hbm)))
        ]

    whole_copy = pltpu.make_async_copy(whole_hbm, whole_ref, whole_sem)
    whole_copy.start()
    for index in range(2):
        for copy in load(index):
            copy.start()
    ring = [{"tensor": lax.rem(me + k, count)} for k in range(1, count)]
    items = []
    if cuts:
        place = lax.axis_index("dp")
        dp_count = spreads[0].dp_count
        cell, dp_peers = dp_cell(place)
        ring += [{"dp": lax.rem(place + k, dp_count)} for k in range(1, dp_count)]
        for k in range(4):
            item = DpSum(cell, dp_peers, k % 2 == 0, dp_sems, 3 * k)
            item.in2 = in2s[k]
            if k < 2:
                item.src = (hw_a, hw_b)[k]
                item.half = item.src.at[:, :, cell[0]]
                item.in0, item.in1, item.mid = in0s[k], in1s[k], mids[k]
            else:
                item.mid = mids_in[k - 2]
            items.append(item)
        pack_early(spreads[0].in_ref, hb_sums, proj_sums, row_sums)
    greet_all(ring)
    taps = cw_ref.shape[0]
    wb_ref[...] = jnp.zeros_like(wb_ref)
    wb_ref[0:taps, :] = (cw_ref[...].astype(f32) * mask_ref[...]).astype(bf16)
    dw_ref[...] = jnp.zeros_like(dw_ref)
    table_ref[...] = jnp.zeros_like(table_ref)
    pad_ref[...] = jnp.zeros_like(pad_ref)
    grad_ref[...] = prev_ref[...] + part_ref[
        :, pl.ds(pl.multiple_of(me * filters, filters), filters)
    ].astype(f32)
    meet_all(ring)
    for item in items[2:]:
        item.copy2().start()
    if cuts:
        spreads[0].first()
    chunks = line_sems[0].shape[1]
    per = words // chunks // WORD_TILE
    scatter = LineScatter(
        count, me, chunks, 3, part_ref, grad_ref, from_left, from_right, line_sems
    )
    group = lax.broadcasted_iota(jnp.int32, (1, WORD_TILE, LANES), 2) // 16
    vocab = lax.broadcasted_iota(jnp.int32, (table_ref.shape[0], padded * WORD_TILE), 0)

    def tile_step(index):
        slot = index % 2
        for copy in load(index):
            copy.wait()
        tile = pl.ds(pl.multiple_of(index * WORD_TILE, WORD_TILE), WORD_TILE)
        pooled = log_ref[tile, :] - off_ref[...]
        sig = jax.nn.sigmoid(pooled)
        grad = grad_ref[tile, :] * (sig * (1.0 + pooled * (1.0 - sig)))
        d_conv = (grad[None] * p_buf[slot].astype(f32)).astype(bf16)
        d_conv = d_conv.reshape(chars * WORD_TILE, filters)
        dw_ref[...] += dot(x_buf[slot], d_conv, 0, 0)
        d_win = dot(d_conv, wb_ref[...], 1, 1).astype(bf16)
        pad_ref[6 : 6 + chars] = d_win.reshape(chars, WORD_TILE, LANES)
        d_emb = pad_ref[6 : 6 + padded]
        for tap in range(1, 7):
            d_emb = jnp.where(group == tap, pad_ref[6 - tap : 6 - tap + padded], d_emb)
        one_hot = jnp.where(vocab == ids_ref[pl.ds(index, 1), :], 1.0, 0.0).astype(bf16)
        table_ref[...] += dot(one_hot, d_emb.reshape(padded * WORD_TILE, LANES), 1, 0)

        @pl.when(index + 2 < tiles)
        def more():
            for copy in load(index + 2):
                copy.start()

    def step_fn(step, carry):
        scatter.step(step)

        @pl.when(step == 0)
        def whole():
            whole_copy.wait()

        @pl.when(step < 8)
        def grads():
            weight_grad_piece(step, whole_ref, (dt_ref, dg_ref), (hw_a, hw_b))

        if cuts:

            @pl.when(step == 4)
            def early2():
                spreads[0].second()

            @pl.when(step == 7)
            def early3():
                spreads[0].third()

            @pl.when(step == 8)
            def start0():
                for item in items[:2]:
                    item.copy0().start()

            @pl.when(step == cuts[0])
            def start1():
                for item in items[:2]:
                    item.finish0()
                    item.copy1().start()

            @pl.when(step == cuts[1])
            def start2():
                for item in items[:2]:
                    item.finish1()
                    item.copy2().start()

        for k in range(per):
            scatter.finished(step, lambda chunk: tile_step(chunk * per + k), k)
        return carry

    lax.fori_loop(0, scatter.due(chunks - 1) + per, step_fn, 0)
    if cuts:
        late = spreads[1]
        taps = table_ref[:, 0:16]
        for tap in range(1, 7):
            taps += table_ref[:, 16 * tap : 16 * tap + 16]
        stage_ref[...] = jnp.zeros_like(stage_ref)
        table_ref[:, 0:16] = taps
        for i in range(8):
            late.in_ref[i, :, 0:filters] = dw_ref[16 * i : 16 * i + 16, :].astype(bf16)
            for k in range(3):
                size = 16 if k < 2 else 1
                stage_ref[0:size, 16 * k : 16 * k + 16] = table_ref[
                    33 * i + 16 * k : 33 * i + 16 * k + size, 0:16
                ]
            late.in_ref[i, :, filters:] = stage_ref[...].astype(bf16)
        late.first()
        spreads[0].finish()
        unpack_early(spreads[0].out_ref, hwb_out, vec_out, upb_out, qv_out)
        late.second()
        late.third()
        for k in range(4):
            hw_out[k // 2, k % 2] = items[k].finish2().astype(bf16)
        late.finish()
        for t in range(count):
            lanes = slice(t * filters, (t + 1) * filters)
            for i in range(7):
                convw_out[16 * i : 16 * i + 16, lanes] = late.out_ref[i, t, :, 0:filters]
            convb_out[:, lanes] = late.out_ref[7, t, :, 0:filters].astype(f32)[0:1]
        for i in range(8):
            total = late.out_ref[i, 0, :, filters:].astype(f32)
            for t in range(1, count):
                total += late.out_ref[i, t, :, filters:].astype(f32)
            for k in range(3):
                size = 16 if k < 2 else 1
                table_out[33 * i + 16 * k : 33 * i + 16 * k + size, :] = total[
                    0:size, 16 * k : 16 * k + 16
                ]
    scatter.drain()


def conv_backward(ids, x, p, w, mask, off, logs, prev, part, whole, dt, dg, rest, count, cid):
    words, filters = logs.shape
    chars = p.shape[1]
    chunks = 8
    shape = jax.ShapeDtypeStruct
    hw_shape = (2, 2, 2, whole.shape[1] // 8, filters)
    operands = [ids, x, p, w, mask, off, logs, prev, part, whole, dt, dg] + list(rest)
    in_specs = [VMEM, ANY, ANY] + [VMEM] * 6 + [ANY, VMEM, VMEM] + [VMEM] * len(rest)
    sums = [(LANES, filters), (264, LANES)]
    scratch = []
    cuts = None
    if rest:
        cuts = (17, 28)
        tail = hw_shape[-2:]
        features = rest[-1].shape[-1]
        out_shape = [
            shape((2, 2) + tail, bf16),
            shape((112, count * filters), bf16),
            shape((1, count * filters), f32),
            shape((264, 16), f32),
            shape((4, count * filters), f32),
            shape((9, features), f32),
            shape((1, count * features), f32),
            shape((2, features), f32),
        ]
        scratch += [pltpu.VMEM(shape_of, f32) for shape_of in sums]
        scratch += [pltpu.VMEM(hw_shape, bf16)] * 2
        scratch += [pltpu.VMEM((2, 2) + tail, bf16)] * 2
        scratch += [pltpu.VMEM((2,) + tail, bf16)] * 4
        scratch += [pltpu.VMEM(tail, bf16)] * 4
        scratch += [DMA((12,))] * 2
        for small, kind in (((16, LANES), f32), ((16, filters + LANES), bf16)):
            scratch += [
                pltpu.VMEM((8,) + small, kind),
                pltpu.VMEM((7,) + small, kind),
                pltpu.VMEM((count,) + small, bf16),
                pltpu.VMEM((8, count) + small, bf16),
            ]
            scratch += [DMA((7,))] * 2 + [DMA((count - 1,))] * 2 + [DMA((count, 7))] * 2
    else:
        out_shape = [shape(shape_of, f32) for shape_of in sums] + [shape(hw_shape, bf16)] * 2
    scratch += [
        pltpu.VMEM((68, WORD_TILE, LANES), bf16),
        pltpu.VMEM((16, LANES), f32),
        pltpu.VMEM((words, filters), f32),
        pltpu.VMEM(part.shape, bf16),
        pltpu.VMEM(part.shape, bf16),
        pltpu.VMEM((2,) + x.shape[1:], bf16),
        pltpu.VMEM((2,) + p.shape[1:], bf16),
        pltpu.VMEM(whole.shape, bf16),
        pltpu.VMEM((LANES, filters), bf16),
        DMA((2, 2)),
        DMA,
    ]
    scratch += [DMA((count, chunks))] * 4
    return pl.pallas_call(
        functools.partial(conv_backward_kernel, count, chars, cuts),
        out_shape=tuple(out_shape),
        in_specs=in_specs,
        out_specs=tuple([VMEM] * len(out_shape)),
        scratch_shapes=scratch,
        compiler_params=params(cid, 58),
        name="conv_backward",
    )(*operands)


def small_kernel(dp_count, count, in_ref, out_ref, got, mid, *sems):
    me = lax.axis_index("tensor")
    place = lax.axis_index("dp")
    barrier = pltpu.get_barrier_semaphore()

    def greet(hop, carry):
        peer = lax.rem(place + hop, dp_count)
        pl.semaphore_signal(barrier, inc=1, device_id={"dp": peer}, device_id_type=MESH)
        return carry

    lax.fori_loop(1, dp_count, greet, 0)
    for hop in range(1, count):
        pl.semaphore_signal(
            barrier, inc=1, device_id={"tensor": lax.rem(me + hop, count)}, device_id_type=MESH
        )
    pl.semaphore_wait(barrier, dp_count + count - 2)
    spread = Spread(sems, in_ref, got, mid, out_ref)
    spread.first()
    spread.second()
    spread.third()
    spread.finish()


def sum_small(packed, dp_count, count, cid):
    shape = packed.shape[1:]
    return pl.pallas_call(
        functools.partial(small_kernel, dp_count, count),
        out_shape=jax.ShapeDtypeStruct((dp_count, count) + shape, bf16),
        in_specs=[VMEM],
        out_specs=VMEM,
        scratch_shapes=[
            pltpu.VMEM((dp_count - 1,) + shape, f32),
            pltpu.VMEM((count,) + shape, bf16),
            DMA((dp_count - 1,)),
            DMA((dp_count - 1,)),
            DMA((count - 1,)),
            DMA((count - 1,)),
            DMA((count, dp_count - 1)),
            DMA((count, dp_count - 1)),
        ],
        compiler_params=params(cid, 32),
        name="sum_small",
    )(packed)


def finish_kernel(units, three, *refs):
    (enc_out, table_out, conv_w_out, conv_b_out, hw_out, hw_b_out, proj_out, proj_b_out, gain_out,
     shift_out, qkv_out, qv_out, o_out, o_b_out, up_out, up_b_out, down_out,
     down_b_out) = refs[12:30]
    bufs, sem = refs[30:42], refs[42]
    loads = [
        pltpu.make_async_copy(src, dst, sem.at[k])
        for k, (src, dst) in enumerate(zip(refs[:12], bufs))
    ]
    for copy in loads:
        copy.start()
    for copy in loads:
        copy.wait()
    (enc, table, conv_w, mask, conv_b, hw, hw_b, rows, qv, up_b, tr_a, tr_b) = bufs
    filters = mask.shape[1]
    enc_out[0] = enc[...]
    table_out[...] = table[...].T[:, 0 : table_out.shape[1]]
    for start in range(0, conv_w.shape[1], filters):
        lanes = slice(start, start + filters)
        conv_w_out[:, lanes] = conv_w[:, lanes].astype(f32) * mask[...]
    conv_b_out[...] = conv_b[...].reshape(conv_b_out.shape)
    for layer in range(2):
        hw_b_out[layer] = hw_b[2 * layer : 2 * layer + 2, :]
        for j in range(2):
            hw_out[layer, j] = hw[layer, j].astype(f32)
    for k, out in enumerate((proj_b_out, o_b_out, down_b_out)):
        out[...] = rows[k : k + 1, :].reshape(out.shape)
    gain_out[...] = rows[3:6, :]
    shift_out[...] = rows[6:9, :]
    qv_out[...] = qv[...]
    up_b_out[...] = up_b[...].reshape(up_b_out.shape)
    up_out[...] = tr_a[:, 0:units].astype(f32)
    down_out[...] = tr_a[:, units:].astype(f32)
    proj_out[...] = tr_b[:, 0:filters].astype(f32)
    hidden = three // 3
    qkv = tr_b[:, filters : filters + three].astype(f32)
    for k in range(3):
        qkv_out[k] = qkv[:, k * hidden : (k + 1) * hidden]
    o_out[...] = tr_b[:, 1152 : 1152 + hidden].astype(f32).T


def finish(encoded, table, conv_w, mask, conv_b, hw, hw_b, rows, qv, up_b, tr_a, tr_b, vocab,
           units, three):
    features, depth, filters = rows.shape[1], tr_a.shape[0], mask.shape[1]
    shapes = [
        (table.shape[1], vocab), conv_w.shape, (conv_w.shape[1],), hw.shape,
        (2, 2, hw_b.shape[1]), (depth, filters), (features,), (3, features), (3, features),
        (3, depth, three // 3), qv.shape, (three // 3, depth), (features,), (depth, units),
        (up_b.shape[1],), (depth, tr_a.shape[1] - units), (features,),
    ]
    operands = (encoded, table, conv_w, mask, conv_b, hw, hw_b, rows, qv, up_b, tr_a, tr_b)
    (encoded, table, conv_w, conv_b, hw, hw_b, proj, proj_b, gain, shift, qkv, qv, o, o_b, up, up_b,
     down, down_b) = pl.pallas_call(
        functools.partial(finish_kernel, units, three),
        out_shape=tuple(
            [jax.ShapeDtypeStruct((1,) + encoded.shape, bf16)]
            + [jax.ShapeDtypeStruct(shape, f32) for shape in shapes]
        ),
        in_specs=[ANY] * 12,
        out_specs=(VMEM,) * 18,
        scratch_shapes=[pltpu.VMEM(part.shape, part.dtype) for part in operands] + [DMA((12,))],
        compiler_params=pltpu.CompilerParams(vmem_limit_bytes=58 * MIB),
        name="finish",
    )(*operands)
    return (
        jnp.transpose(encoded, (1, 0, 2)), table.T, conv_w, conv_b, hw, hw_b, proj.T, proj_b, gain,
        shift, jnp.transpose(qkv, (1, 0, 2)), qv, o, o_b, up, up_b, down.T, down_b,
    )


def body(
    char_ids,
    seq_lengths,
    char_table,
    conv_weight,
    conv_bias,
    highway_weight,
    highway_bias,
    proj_weight,
    proj_bias,
    norm_gain,
    norm_shift,
    qkv_weight,
    qv_bias,
    output_projection_weight,
    out_bias,
    up_weight,
    up_bias,
    down_weight,
    down_bias,
    out_grad,
):
    words, nseq, chars = char_ids.shape
    assert nseq == 1
    count = lax.axis_size("tensor")
    dp_count = lax.axis_size("dp")
    rank = lax.axis_index("tensor")
    vocab, char_dim = char_table.shape
    taps_dim, filters = conv_weight.shape
    features = proj_weight.shape[1]
    heads = qkv_weight.shape[2] // HEAD_DIM

    tiles = words // WORD_TILE
    ids_tiles = jnp.swapaxes(char_ids[:, 0].reshape(tiles, WORD_TILE, chars), 1, 2)
    ids_tiles = ids_tiles.reshape(tiles, chars * WORD_TILE)
    pattern = np.zeros((chars, WORD_TILE, LANES), np.float32)
    pattern[:, :, taps_dim] = 1.0
    for k in range(1, 7):
        pattern[chars - k, :, taps_dim + k] = 1.0

    widths = filter_widths(filters)
    off = jnp.asarray(np.log((chars - widths + 1).astype(np.float64)).astype(np.float32))[None]
    tap_of = np.arange(taps_dim)[:, None] // char_dim
    taps_mask = tap_of < widths[None]
    mask = jnp.asarray(taps_mask, f32)
    ends = np.zeros((LANES - taps_dim, filters), np.float32)
    ends[1:7] = np.where(widths[None] > np.arange(1, 7)[:, None], big_neg, 0.0)

    logs, whole0, whole1, top, x_tiles, p_tiles, t0, g0, h0, t1, g1, h1 = embed_forward(
        ids_tiles,
        char_table.T,
        jnp.asarray(pattern, bf16),
        (conv_weight, conv_bias, mask, jnp.asarray(ends)),
        off,
        highway_bias,
        highway_weight,
        count,
        chars,
        1,
    )
    encoded, prev1, dt1, dg1, sums1, tr_a, tr_b, row_sums, proj_sums = encoder(
        top,
        (
            proj_weight,
            jnp.transpose(qkv_weight, (1, 2, 0)).reshape(-1, features),
            output_projection_weight,
            up_weight,
            down_weight,
        ),
        (proj_bias, out_bias, down_bias, up_bias, norm_gain, norm_shift, qv_bias),
        out_grad[:, 0],
        seq_lengths,
        (t1, g1, h1),
        count,
        4,
    )

    back_args = (prev1, dt1, dg1, sums1, t0, g0, h0, whole1, highway_weight)
    conv_args = (ids_tiles, x_tiles, p_tiles, conv_weight, mask, off, logs)
    three = 3 * heads * HEAD_DIM
    units = up_weight.shape[1]
    if dp_count == 8 and (features // dp_count) % 16 == 0:
        part0, prev0, dt0, dg0, hw_bias_part, mid_a, mid_b, tr_a, tr_b = highway_back(
            *back_args, tr_a, tr_b, count, 9
        )
        (hw_w_grad, conv_w_grad, conv_b_grad, table_grad, hw_b_grad, rows, up_b_grad,
         qv_grad) = conv_backward(
            *conv_args, prev0, part0, whole0, dt0, dg0,
            (mid_a, mid_b, hw_bias_part, proj_sums, row_sums), count, 10,
        )
        return finish(
            encoded, table_grad, conv_w_grad, mask, conv_b_grad, hw_w_grad, hw_b_grad, rows,
            qv_grad, up_b_grad, tr_a, tr_b, vocab, units, three,
        )
    else:
        part0, prev0, dt0, dg0, hw_bias_part, *hw1 = highway_back(*back_args, None, None, count, 9)
        d_w_all, table_all, *hw0 = conv_backward(
            *conv_args, prev0, part0, whole0, dt0, dg0, (), count, 10
        )
        hw_sum = jnp.stack([part.reshape(-1, filters) for part in hw0 + hw1])
        hw_sum = lax.psum_scatter(hw_sum, "dp", scatter_dimension=1, tiled=True).astype(f32)
        tr_a, tr_b = [
            lax.psum_scatter(
                part.reshape(features, -1), "dp", scatter_dimension=0, tiled=True
            ).astype(f32)
            for part in (tr_a, tr_b)
        ]
        hw_w_grad = hw_sum.reshape(2, 2, -1, filters)
        pieces = [d_w_all[: taps_dim + 1], table_all, hw_bias_part, proj_sums, row_sums[:10]]
        flat = jnp.concatenate([part.reshape(-1) for part in pieces])
        width = -(-flat.size // (dp_count * 16 * LANES)) * LANES
        flat = jnp.pad(flat, (0, dp_count * 16 * width - flat.size))
        summed = sum_small(flat.reshape(dp_count, 16, width), dp_count, count, 11)
        summed = jnp.swapaxes(summed, 0, 1).reshape(count, -1).astype(f32)
        conv_size, table_size = pieces[0].size, table_all.size
        conv_all = summed[:, :conv_size].reshape(count, taps_dim + 1, filters)
        conv_all = jnp.swapaxes(conv_all, 0, 1)
        conv_w_grad = conv_all[:taps_dim].reshape(taps_dim, -1)
        conv_b_grad = conv_all[taps_dim].reshape(-1)
        table_all = jnp.sum(summed[:, conv_size : conv_size + table_size], axis=0)
        table_all = table_all.reshape(-1, LANES)
        early = summed[:, conv_size + table_size :]
        table_grad = jnp.sum(
            table_all[:vocab, :taps_dim].reshape(vocab, taps_dim // char_dim, char_dim), axis=1
        )
        hw_b_grad = jnp.swapaxes(early[:, : 4 * filters].reshape(count, 4, filters), 0, 1)
        early = early[:, 4 * filters :]
        qv_grad = jnp.swapaxes(early[:, :three].reshape(count, 3, -1), 0, 1)[::2].reshape(2, -1)
        rows = early[:, three : three + 10 * features].reshape(count, 10, features)
        up_b_grad = rows[:, 9].reshape(-1)
        rows = rows[0]

    conv_w_grad = jnp.where(np.tile(taps_mask, (1, count)), conv_w_grad, 0.0)
    hw_b_grad = hw_b_grad.reshape(2, 2, -1)
    up_w_grad = tr_a[:, :units]
    down_w_grad = tr_a[:, units:].T
    proj_w_grad = tr_b[:, :filters].T
    qkv_w_grad = tr_b[:, filters : filters + three].reshape(-1, 3, heads * HEAD_DIM)
    out_w_grad = tr_b[:, 1152 : 1152 + heads * HEAD_DIM].T
    proj_b_grad, out_b_grad, down_b_grad = rows[0], rows[1], rows[2]
    gain_grad, shift_grad = rows[3:6], rows[6:9]
    return (
        encoded[:, None],
        table_grad,
        conv_w_grad,
        conv_b_grad,
        hw_w_grad,
        hw_b_grad,
        proj_w_grad,
        proj_b_grad,
        gain_grad,
        shift_grad,
        qkv_w_grad,
        qv_grad,
        out_w_grad,
        out_b_grad,
        up_w_grad,
        up_b_grad,
        down_w_grad,
        down_b_grad,
    )


def solution(mesh):
    return jax.shard_map(
        body,
        mesh=mesh,
        in_specs=(
            P(None, "dp", None),
            P("dp"),
            P(),
            P(None, "tensor"),
            P("tensor"),
            P(None, None, None, "tensor"),
            P(None, None, "tensor"),
            P("tensor", None),
            P(),
            P(),
            P(),
            P(None, None, "tensor"),
            P(None, "tensor"),
            P("tensor", None),
            P(),
            P(None, "tensor"),
            P("tensor"),
            P("tensor", None),
            P(),
            P("tensor", "dp", None),
        ),
        out_specs=(
            P("tensor", "dp", None),
            P(),
            P(),
            P(),
            P(None, None, "dp", "tensor"),
            P(),
            P("tensor", "dp"),
            P(),
            P(),
            P(),
            P("dp", None, "tensor"),
            P(),
            P("tensor", "dp"),
            P(),
            P("dp", "tensor"),
            P(),
            P("tensor", "dp"),
            P(),
        ),
        check_vma=False,
    )
```

```python
import functools
import math

import jax
import jax.numpy as jnp
import numpy as np
from jax import lax
from jax.experimental import pallas as pl
from jax.experimental.pallas import tpu as pltpu
from jax.sharding import PartitionSpec as P

HEAD_DIM = 64
WORD_TILE = 32
LANES = 128

norm_eps = 1e-06
big_neg = -1e30
f32 = jnp.float32
bf16 = jnp.bfloat16
MESH = pl.DeviceIdType.MESH
VMEM = pl.BlockSpec(memory_space=pltpu.VMEM)
ANY = pl.BlockSpec(memory_space=pl.ANY)
DMA = pltpu.SemaphoreType.DMA
MIB = 1 << 20


def params(cid, vmem):
    return pltpu.CompilerParams(
        collective_id=cid, has_side_effects=True, vmem_limit_bytes=vmem * MIB
    )


def width_counts(block):
    unit = block // 64
    return [unit, unit, 2 * unit, 4 * unit, 8 * unit, 16 * unit, 32 * unit]


def filter_widths(block):
    return np.concatenate(
        [np.full((n,), i + 1, np.int32) for i, n in enumerate(width_counts(block))]
    )


def dot(a, b, ca, cb):
    return lax.dot_general(a, b, (((ca,), (cb,)), ((), ())), preferred_element_type=f32)


def line_greet(me, count):
    barrier = pltpu.get_barrier_semaphore()
    for there, ok in ((me - 1, me > 0), (me + 1, me < count - 1)):

        @pl.when(ok)
        def greet():
            pl.semaphore_signal(barrier, inc=1, device_id={"tensor": there}, device_id_type=MESH)


def line_meet(me, count):
    pl.semaphore_wait(
        pltpu.get_barrier_semaphore(), jnp.minimum(me, 1) + jnp.minimum(count - 1 - me, 1)
    )


def line_copy(view, me, count, right, block, chunk, sems):
    send, recv = sems[:2] if right else sems[2:]
    to = jnp.minimum(me + 1, count - 1) if right else jnp.maximum(me - 1, 0)
    ref = view(block, chunk)
    return pltpu.make_async_remote_copy(
        src_ref=ref,
        dst_ref=ref,
        send_sem=send.at[block, chunk],
        recv_sem=recv.at[block, chunk],
        device_id={"tensor": to},
        device_id_type=MESH,
    )


def gather_step(view, step, chunks, me, count, sems, spacing=1):
    for hop in range(count):
        chunk = step - spacing * hop
        here = (chunk >= 0) & (chunk < chunks)
        safe = jnp.clip(chunk, 0, chunks - 1)
        for right in (True, False):
            block = me - hop if right else me + hop
            there = (block >= 0) & (block < count)
            block = jnp.clip(block, 0, count - 1)
            more = me < count - 1 if right else me > 0
            copy = functools.partial(line_copy, view, me, count, right, block, safe, sems)

            @pl.when(here & there)
            def pass_on():
                if hop > 0:
                    copy().wait_recv()

                @pl.when(more)
                def send():
                    copy().start()


def gather_drain(view, chunks, me, count, sems):
    def one(chunk, carry):
        for hop in range(count):
            for right in (True, False):
                block = me - hop if right else me + hop
                there = (block >= 0) & (block < count)
                block = jnp.clip(block, 0, count - 1)
                more = me < count - 1 if right else me > 0
                copy = functools.partial(line_copy, view, me, count, right, block, chunk, sems)

                @pl.when(there & more)
                def sent():
                    copy().wait_send()

        return carry

    lax.fori_loop(0, chunks, one, 0)


def embed_forward_kernel(count, chars, *refs):
    (ids_ref, chars_ref, pattern_ref, cw_ref, cb_ref, mask_ref, ends_ref, off_ref, bias_ref,
     hw_hbm) = refs[:10]
    log_out, whole0_out, whole1_ref, top_ref, x_hbm, p_hbm = refs[10:16]
    kept = refs[16:22]
    y_buf, x_buf, p_buf, hw_ref, table_ref, w_ref, hb_ref, keep_sem, late_sem = refs[22:31]
    bufs = refs[31:37]
    sems0, sems1 = refs[37:41], refs[41:45]
    log_ref, whole0_ref = refs[45:47]
    t_refs, g_refs, h_refs = (bufs[0], bufs[3]), (bufs[1], bufs[4]), (bufs[2], bufs[5])
    wholes = (whole0_ref, whole1_ref)
    me = lax.axis_index("tensor")
    line_greet(me, count)
    words, filters = log_ref.shape
    tiles = words // WORD_TILE
    padded = ids_ref.shape[1] // WORD_TILE
    own = pl.ds(pl.multiple_of(me * filters, filters), filters)
    loads = [
        pltpu.make_async_copy(hw_hbm.at[layer], hw_ref.at[layer], late_sem.at[layer])
        for layer in range(2)
    ]
    for copy in loads:
        copy.start()
    stores = [
        pltpu.make_async_copy(buf, out, late_sem.at[2 + k])
        for k, (buf, out) in enumerate(zip(bufs, kept))
    ]
    logs_copy = pltpu.make_async_copy(log_ref, log_out, late_sem.at[8])
    whole_copy = pltpu.make_async_copy(whole0_ref, whole0_out, late_sem.at[9])
    y_buf[...] = jnp.zeros_like(y_buf)
    table_ref[...] = jnp.zeros_like(table_ref)
    depth, vocab_size = chars_ref.shape
    for tap in range(7):
        table_ref[depth * tap : depth * tap + depth, 0:vocab_size] = chars_ref[...]
    for layer in range(2):
        hb_ref[2 * layer : 2 * layer + 2, :] = bias_ref[layer].astype(f32)
    taps = cw_ref.shape[0]
    w_ref[0:taps, :] = (cw_ref[...].astype(f32) * mask_ref[...]).astype(bf16)
    first = lax.broadcasted_iota(jnp.int32, ends_ref.shape, 0) == 0
    bias = cb_ref[...].astype(f32).reshape(1, filters)
    w_ref[taps:, :] = jnp.where(first, bias, ends_ref[...]).astype(bf16)
    line_meet(me, count)

    def view_of(whole):
        def view(block, chunk):
            return whole.at[
                pl.ds(pl.multiple_of(chunk * WORD_TILE, WORD_TILE), WORD_TILE),
                pl.ds(pl.multiple_of(block * filters, filters), filters),
            ]

        return view

    views = [view_of(whole) for whole in wholes]

    def keep(index):
        slot = index % 2
        return [
            pltpu.make_async_copy(buf.at[slot], hbm.at[index], keep_sem.at[k, slot])
            for k, (buf, hbm) in enumerate(((x_buf, x_hbm), (p_buf, p_hbm)))
        ]

    lane_group = lax.broadcasted_iota(jnp.int32, (1, WORD_TILE, LANES), 2) // 16
    vocab = lax.broadcasted_iota(jnp.int32, (table_ref.shape[1], padded * WORD_TILE), 0)

    def tile_step(index):
        slot = index % 2

        @pl.when(index >= 2)
        def free():
            for copy in keep(index - 2):
                copy.wait()

        one_hot = jnp.where(vocab == ids_ref[pl.ds(index, 1), :], 1.0, 0.0).astype(bf16)
        found = dot(table_ref[...], one_hot, 1, 0).astype(bf16).T
        y_buf[0:padded] = found.reshape(padded, WORD_TILE, LANES)
        value = jnp.where(lane_group == 7, pattern_ref[...], y_buf[0:chars])
        for tap in range(1, 7):
            value = jnp.where(lane_group == tap, y_buf[tap : chars + tap], value)
        x2 = value.reshape(chars * WORD_TILE, LANES)
        x_buf[slot] = x2
        conv = dot(x2, w_ref[...], 1, 0).reshape(chars, WORD_TILE, filters)
        top = jnp.max(conv, axis=0)
        exps = jnp.exp(conv - top[None])
        sums = jnp.sum(exps, axis=0)
        p_buf[slot] = (exps * (1.0 / sums)[None]).astype(bf16)
        for copy in keep(index):
            copy.start()
        tile = pl.ds(pl.multiple_of(index * WORD_TILE, WORD_TILE), WORD_TILE)
        total = top + jnp.log(sums)
        log_ref[tile, :] = total
        pooled = total - off_ref[...]
        hidden = pooled * jax.nn.sigmoid(pooled)
        h_refs[0][tile, :] = hidden
        whole0_ref[tile, own] = hidden.astype(bf16)

    size = words // 4
    group = tiles // 4

    def layer_step(layer, quarter):
        start = quarter * size
        rows = pl.ds(pl.multiple_of(start, size), size)
        for j, out in enumerate((t_refs[layer], g_refs[layer])):
            bias = hb_ref[2 * layer + j : 2 * layer + j + 1, :]
            out[rows, :] = dot(wholes[layer][rows, :], hw_ref[layer, j], 1, 0) + bias

        def mix(index, carry):
            tile = pl.ds(pl.multiple_of(start + index * WORD_TILE, WORD_TILE), WORD_TILE)
            trans = t_refs[layer][tile, :]
            gate = jax.nn.sigmoid(g_refs[layer][tile, :])
            hidden = gate * (trans * jax.nn.sigmoid(trans)) + (1.0 - gate) * h_refs[layer][tile, :]
            if layer == 0:
                h_refs[1][tile, :] = hidden
                whole1_ref[tile, own] = hidden.astype(bf16)
            else:
                top_ref[tile, :] = hidden.astype(bf16)
            return carry

        lax.fori_loop(0, size // WORD_TILE, mix, 0)

    spacing = 2
    fill = spacing * (count - 1)
    shift = group + fill
    last = shift + tiles + fill

    def step_fn(step, carry):
        @pl.when(step < tiles)
        def convolve():
            tile_step(step)

        @pl.when(step < tiles + fill)
        def first_gather():
            gather_step(views[0], step, tiles, me, count, sems0, spacing)

        @pl.when(step == shift)
        def weights0():
            loads[0].wait()

        since = step - shift

        @pl.when((since >= 0) & (since < tiles) & (since % group == 0))
        def layer0():
            layer_step(0, jnp.maximum(since, 0) // group)

        @pl.when(since == tiles - group)
        def leave():
            for copy in stores[:3] + [logs_copy, whole_copy]:
                copy.start()

        @pl.when(step >= shift)
        def second_gather():
            gather_step(views[1], step - shift, tiles, me, count, sems1, spacing)

        since = step - shift - fill - group + 1

        @pl.when(since == 0)
        def weights1():
            loads[1].wait()

        @pl.when((since >= 0) & (since % group == 0))
        def layer1():
            layer_step(1, jnp.maximum(since, 0) // group)

        return carry

    lax.fori_loop(0, last, step_fn, 0)
    for copy in stores[3:]:
        copy.start()
    for index in (tiles - 2, tiles - 1):
        for copy in keep(index):
            copy.wait()
    for sems, view in zip((sems0, sems1), views):
        gather_drain(view, tiles, me, count, sems)
    for copy in stores + [logs_copy, whole_copy]:
        copy.wait()


def embed_forward(ids, table, pattern, conv, off, bias, weight, count, chars, cid):
    filters = conv[0].shape[1]
    tiles = ids.shape[0]
    words = tiles * WORD_TILE
    shape = jax.ShapeDtypeStruct
    flat = (words, filters)
    return pl.pallas_call(
        functools.partial(embed_forward_kernel, count, chars),
        out_shape=(
            shape(flat, f32),
            shape((words, count * filters), bf16),
            shape((words, count * filters), bf16),
            shape(flat, bf16),
            shape((tiles, chars * WORD_TILE, LANES), bf16),
            shape((tiles, chars, WORD_TILE, filters), bf16),
        )
        + (shape(flat, f32),) * 6,
        in_specs=[VMEM] * 9 + [ANY],
        out_specs=(ANY, ANY, VMEM, VMEM) + (ANY,) * 8,
        scratch_shapes=[
            pltpu.VMEM((chars + 6, WORD_TILE, LANES), bf16),
            pltpu.VMEM((2, chars * WORD_TILE, LANES), bf16),
            pltpu.VMEM((2, chars, WORD_TILE, filters), bf16),
            pltpu.VMEM(weight.shape, bf16),
            pltpu.VMEM((LANES, 264), bf16),
            pltpu.VMEM((LANES, filters), bf16),
            pltpu.VMEM((8, filters), f32),
            DMA((2, 2)),
            DMA((10,)),
        ]
        + [pltpu.VMEM(flat, f32)] * 6
        + [DMA((count, tiles))] * 8
        + [pltpu.VMEM(flat, f32), pltpu.VMEM((words, count * filters), bf16)],
        compiler_params=params(cid, 58),
        name="embed_forward",
    )(ids, table, pattern, *conv, off, bias, weight)


class LineSum:
    def __init__(self, count, me, chunks, spacing, first, sums, parts, outs, buffers, sems):
        self.count, self.me, self.chunks, self.spacing = count, me, chunks, spacing
        self.first, self.messages, self.parts, self.outs = first, sums * chunks, parts, outs
        self.buffers, self.sems = buffers, sems
        self.fill = spacing * (count - 1)

    def tile(self, number, size=1):
        rows = self.parts.shape[1] // self.chunks * size
        return pl.ds(pl.multiple_of(number % self.chunks // size * rows, rows), rows)

    def place(self, right, number):
        count, me = self.count, self.me
        k, chunk, tile = self.first + number // self.chunks, number % self.chunks, self.tile(number)
        buf = self.buffers[0 if right else 1]
        send, recv = self.sems[:2] if right else self.sems[2:]
        to = jnp.minimum(me + 1, count - 1) if right else jnp.maximum(me - 1, 0)
        first, passed = [
            functools.partial(
                pltpu.make_async_remote_copy,
                src_ref=src.at[k, tile],
                dst_ref=buf.at[k, tile],
                send_sem=send.at[k, chunk],
                recv_sem=recv.at[k, chunk],
                device_id={"tensor": to},
                device_id_type=MESH,
            )
            for src in (self.parts, buf)
        ]
        return k, tile, buf, first, passed

    def step(self, step):
        for right in (True, False):
            lag = self.me if right else self.count - 1 - self.me
            number = step - self.spacing * lag
            here = (number >= 0) & (number < self.messages)
            number = jnp.clip(number, 0, self.messages - 1)
            k, tile, buf, first, passed = self.place(right, number)

            @pl.when(here & (lag == 0))
            def start():
                first().start()

            @pl.when(here & (lag > 0))
            def middle():
                first().wait_recv()
                got = buf[k, tile, :].astype(f32)

                @pl.when(lag < self.count - 1)
                def forward():
                    buf[k, tile, :] = (got + self.parts[k, tile, :].astype(f32)).astype(bf16)
                    passed().start()

                self.outs[k, tile, :] += got

    def drain(self):
        def one(number, carry):
            for right in (True, False):
                lag = self.me if right else self.count - 1 - self.me
                k, tile, buf, first, passed = self.place(right, number)

                @pl.when(lag < self.count - 1)
                def sent():
                    first().wait_send()

            return carry

        lax.fori_loop(0, self.messages, one, 0)

    def run(self, before, done, after, extra):
        size = self.chunks // 4

        def one(step, carry):
            @pl.when((step < self.chunks) & (step % size == 0))
            def prepare():
                before(self.tile(jnp.minimum(step, self.chunks - 1), size))

            self.step(step)
            for k, work in extra.items():
                pl.when(step == k)(work)
            number = step - self.fill
            for k in range(len(done)):

                @pl.when((number >= k * self.chunks) & (number < (k + 1) * self.chunks))
                def finish():
                    done[k](self.tile(jnp.maximum(number, 0)))

                    @pl.when(number % size == size - 1)
                    def quarter():
                        after[k](self.tile(jnp.maximum(number, 0), size))

            return carry

        lax.fori_loop(0, self.messages + self.fill, one, 0)
        self.drain()


def norm_parts(values):
    centered = values - jnp.mean(values, axis=-1, keepdims=True)
    root = lax.rsqrt(jnp.mean(centered * centered, axis=-1, keepdims=True) + norm_eps)
    return centered * root, root


def norm_back(values, gain, cotangent):
    nv, root = norm_parts(values)
    scaled = cotangent * gain
    inner = jnp.mean(scaled, axis=-1, keepdims=True)
    along = jnp.mean(scaled * nv, axis=-1, keepdims=True)
    return root * (scaled - inner - nv * along), cotangent * nv


def gelu_parts(values):
    cdf = 0.5 * (1.0 + lax.erf(values * 0.7071067811865476))
    slope = cdf + values * jnp.exp(-0.5 * values * values) * 0.3989422804014327
    return values * cdf, slope


def column_sum(values):
    return jnp.sum(values, axis=0, keepdims=True)


def mix_back(d_hidden, trans, gate_pre, previous):
    gate = jax.nn.sigmoid(gate_pre)
    sig = jax.nn.sigmoid(trans)
    act = trans * sig
    d_trans = (d_hidden * gate * (sig * (1.0 + trans * (1.0 - sig)))).astype(bf16)
    d_gate = (d_hidden * (act - previous) * gate * (1.0 - gate)).astype(bf16)
    return d_trans, d_gate, (1.0 - gate) * d_hidden


def encoder_kernel(count, chunks, spacing, *refs):
    top_ref, pw_ref, qw_ref, ow_ref, uw_ref, dw_ref = refs[:6]
    bias_refs, norm_refs, qv_ref, og_ref, len_ref = refs[6:10], refs[10:12], *refs[12:15]
    mix_refs = refs[15:18]
    refs = refs[3:]
    enc_ref, prev_ref, dt_ref, dg_ref, mix_sums = refs[15:20]
    refs = refs[3:]
    tra_out, trb_ref, sums_ref, qsum_ref, vec_ref, qb_ref = refs[17:23]
    (inp, mid, slope, sent, sent_mid, act, d_two, d_up, d_branch, d_emb, qkv, attended, probs,
     d_heads, d_proj, grad_all, enc_all, outs, parts, from_left, from_right) = refs[23:44]
    line_sems, gather_sems = refs[44:48], refs[48:52]
    tra_ref, tra_sem = refs[52:54]
    tra_copy = pltpu.make_async_copy(tra_ref, tra_out, tra_sem)
    emb, midpre, fin, dmid, din = [outs.at[k] for k in range(5)]
    me = lax.axis_index("tensor")
    line_greet(me, count)
    words, features = inp.shape
    heads = attended.shape[1] // HEAD_DIM
    hidden = heads * HEAD_DIM
    scale = HEAD_DIM ** (-0.5)
    own = words // count
    own_tile = pl.ds(pl.multiple_of(me * own, own), own)
    grad_all[own_tile, :] = og_ref[...]
    sums_ref[...] = jnp.zeros_like(sums_ref)
    mix_sums[...] = jnp.zeros_like(mix_sums)
    trb_ref[...] = jnp.zeros_like(trb_ref)
    for k, bias_ref in zip((0, 1, 2, 9), bias_refs):
        vec_ref[k : k + 1, :] = bias_ref[...].astype(f32).reshape(1, features)
    for k, norm_ref in zip((3, 6), norm_refs):
        vec_ref[k : k + 3, :] = norm_ref[...].astype(f32)
    qb_ref[...] = jnp.zeros_like(qb_ref)
    ends = qv_ref[...].astype(f32)
    qb_ref[:, 0:hidden] = ends[0:1]
    qb_ref[:, 2 * hidden : 3 * hidden] = ends[1:2]
    live = lax.broadcasted_iota(jnp.int32, (1, words), 1) < len_ref[0]

    def line(first, sums):
        return LineSum(
            count, me, chunks, spacing, first, sums, parts, outs, (from_left, from_right), line_sems
        )

    def gather_view(block, chunk):
        return grad_all.at[pl.ds(pl.multiple_of(block * own, own), own)]

    def tiles(size, work):
        def one(index, carry):
            work(pl.ds(pl.multiple_of(index * size, size), size))
            return carry

        lax.fori_loop(0, words // size, one, 0)

    def product(lhs, rhs, side, k):
        def work(tile):
            value = dot(lhs[tile, :], rhs[...], 1, side).astype(bf16)
            parts[k, tile, :] = value
            outs[k, tile, :] = value.astype(f32)

        return work

    def grads(lhs, rhs, out_ref, lane):
        def half(k):
            def work():
                depth = features // 2
                value = dot(lhs[:, depth * k : depth * k + depth], rhs[...], 0, 0).astype(bf16)
                for i in range(2):
                    for j in range(2):
                        start = (2 * i + j) * (depth // 4)
                        out_ref[k, i, j, :, lane : lane + rhs.shape[1]] = value[
                            start : start + depth // 4
                        ]

            return work

        return [half(0), half(1)]

    def row(index):
        return vec_ref[index : index + 1, :]

    def add_sum(index, value):
        sums_ref[index : index + 1, :] += column_sum(value)

    line_meet(me, count)

    def first_norm(tile):
        value = emb[tile, :] + row(0)
        emb[tile, :] = value
        value = norm_parts(value)[0] * row(3) + row(6)
        inp[tile, :] = value
        sent[tile, :] = value.astype(bf16)

    def project(tile):
        qkv[tile, :] = (dot(sent[tile, :], qw_ref[...], 1, 1) + qb_ref[...]).astype(bf16)

    line(0, 1).run(product(top_ref, pw_ref, 0, 0), [first_norm], [project], {})
    gather_step(gather_view, 0, 1, me, count, gather_sems)

    for head in range(heads):
        lanes = slice(head * HEAD_DIM, (head + 1) * HEAD_DIM)
        keys = slice(hidden + head * HEAD_DIM, hidden + (head + 1) * HEAD_DIM)
        vals = slice(2 * hidden + head * HEAD_DIM, 2 * hidden + (head + 1) * HEAD_DIM)

        def attend(tile):
            scores = dot(qkv[tile, lanes], qkv[:, keys], 1, 1) * scale
            scores = jnp.where(live, scores, big_neg)
            exps = jnp.exp(scores - jnp.max(scores, axis=1, keepdims=True))
            value = exps * (1.0 / jnp.sum(exps, axis=1, keepdims=True))
            probs[head, tile, :] = value
            attended[tile, lanes] = dot(value.astype(bf16), qkv[:, vals], 1, 0).astype(bf16)

        tiles(256, attend)
        if head == heads - 2:
            gather_step(gather_view, 1, 1, me, count, gather_sems)

    def pass_grads():
        for step in range(2, count - 1):
            gather_step(gather_view, step, 1, me, count, gather_sems)

    def second_norm(tile):
        value = midpre[tile, :] + inp[tile, :] + row(1)
        midpre[tile, :] = value
        value = norm_parts(value)[0] * row(4) + row(7)
        mid[tile, :] = value
        sent_mid[tile, :] = value.astype(bf16)


    send_down = product(act, dw_ref, 0, 2)
    send_up = product(d_up, uw_ref, 1, 3)

    def feed(tile):
        value, back = gelu_parts(dot(sent_mid[tile, :], uw_ref[...], 1, 0) + row(9))
        act[tile, :] = value.astype(bf16)
        slope[tile, :] = back
        send_down(tile)

    def third_norm(tile):
        value = fin[tile, :] + mid[tile, :] + row(2)
        cotangent = grad_all[tile, :].astype(f32)
        enc_all[tile, :] = (norm_parts(value)[0] * row(5) + row(8)).astype(bf16)
        back, gain = norm_back(value, row(5), cotangent)
        fin[tile, :] = back
        low = back.astype(bf16)
        d_two[tile, :] = low
        add_sum(2, low.astype(f32))
        add_sum(5, gain)
        add_sum(8, cotangent)

    def feed_back(tile):
        value = (dot(d_two[tile, :], dw_ref[...], 1, 1) * slope[tile, :]).astype(bf16)
        d_up[tile, :] = value
        add_sum(9, value.astype(f32))
        send_up(tile)

    def second_back(tile):
        cotangent = dmid[tile, :] + fin[tile, :]
        back, gain = norm_back(midpre[tile, :], row(4), cotangent)
        dmid[tile, :] = back
        low = back.astype(bf16)
        d_branch[tile, :] = low
        add_sum(1, low.astype(f32))
        add_sum(4, gain)
        add_sum(7, cotangent)

    def heads_back(tile):
        d_heads[tile, :] = dot(d_branch[tile, :], ow_ref[...], 1, 1).astype(bf16)

    extra = {2: pass_grads}
    extra[chunks + 4] = lambda: gather_step(
        gather_view, count - 1, 1, me, count, gather_sems
    )
    work = grads(d_two, act, tra_ref, features) + grads(sent_mid, d_up, tra_ref, 0)
    extra.update({2 * chunks + spacing * (count - 1) + k: w for k, w in enumerate(work)})
    line(1, 3).run(
        product(attended, ow_ref, 0, 1),
        [second_norm, third_norm, second_back], [feed, feed_back, heads_back], extra
    )
    tra_copy.start()
    enc_ref[...] = enc_all[own_tile, :]

    for head in range(heads):
        lanes = slice(head * HEAD_DIM, (head + 1) * HEAD_DIM)
        keys = slice(hidden + head * HEAD_DIM, hidden + (head + 1) * HEAD_DIM)
        vals = slice(2 * hidden + head * HEAD_DIM, 2 * hidden + (head + 1) * HEAD_DIM)
        weights = probs[head]
        d_out = d_heads[:, lanes]
        d_proj[:, vals] = dot(weights.astype(bf16), d_out, 0, 0).astype(bf16)
        d_probs = dot(d_out, qkv[:, vals], 1, 1)
        inner = jnp.sum(d_probs * weights, axis=1, keepdims=True)
        d_scores = (weights * (d_probs - inner)).astype(bf16)
        d_proj[:, lanes] = (dot(d_scores, qkv[:, keys], 1, 0) * scale).astype(bf16)
        d_proj[:, keys] = (dot(d_scores, qkv[:, lanes], 0, 0) * scale).astype(bf16)
    qsum_ref[...] = column_sum(d_proj[...].astype(f32))

    def first_back(tile):
        cotangent = din[tile, :] + dmid[tile, :]
        back, gain = norm_back(emb[tile, :], row(3), cotangent)
        low = back.astype(bf16)
        d_emb[tile, :] = low
        add_sum(0, low.astype(f32))
        add_sum(3, gain)
        add_sum(6, cotangent)

    def last(tile):
        d_hidden = dot(d_emb[tile, :], pw_ref[...], 1, 1)
        d_trans, d_gate, prev_ref[tile, :] = mix_back(d_hidden, *[ref[tile, :] for ref in mix_refs])
        dt_ref[tile, :] = d_trans
        dg_ref[tile, :] = d_gate
        mix_sums[0:1, :] += column_sum(d_trans.astype(f32))
        mix_sums[1:2, :] += column_sum(d_gate.astype(f32))

    work = grads(sent, d_proj, trb_ref, top_ref.shape[1])
    work += grads(d_branch, attended, trb_ref, 1152)
    line(4, 1).run(
        product(d_proj, qw_ref, 0, 4), [first_back], [last], {5 + k: w for k, w in enumerate(work)}
    )
    for work in grads(d_emb, top_ref, trb_ref, 0):
        work()
    gather_drain(gather_view, 1, me, count, gather_sems)
    tra_copy.wait()


def encoder(top, weights, biases, out_grad, lengths, mix, count, cid):
    words, filters = top.shape
    features = weights[0].shape[1]
    three = weights[1].shape[0]
    units = weights[3].shape[1]
    hidden = three // 3
    chunks = 16
    spacing = (chunks - chunks // 4) // (count - 1)
    shape = jax.ShapeDtypeStruct
    rows = features // 8
    scratch = [pltpu.VMEM((16, features), f32), pltpu.VMEM((1, three), f32)]
    scratch += [pltpu.VMEM((words, n), f32) for n in (features, features, units)]
    scratch += [
        pltpu.VMEM((words, n), bf16)
        for n in (features, features, units, features, units, features, features, three, hidden)
    ]
    scratch += [pltpu.VMEM((hidden // HEAD_DIM, words, words), f32)]
    scratch += [pltpu.VMEM((words, n), bf16) for n in (hidden, three, features, features)]
    scratch += [pltpu.VMEM((5, words, features), f32)]
    scratch += [pltpu.VMEM((5, words, features), bf16)] * 3
    scratch += [DMA((5, chunks))] * 4 + [DMA((count, 1))] * 4
    scratch += [pltpu.VMEM((2, 2, 2, rows, features + units), bf16), DMA]
    return pl.pallas_call(
        functools.partial(encoder_kernel, count, chunks, spacing),
        out_shape=(
            shape((words // count, features), bf16),
            shape((words, filters), f32),
            shape((words, filters), bf16),
            shape((words, filters), bf16),
            shape((2, filters), f32),
            shape((2, 2, 2, rows, features + units), bf16),
            shape((2, 2, 2, rows, 1408), bf16),
            shape((16, features), f32),
            shape((1, three), f32),
        ),
        in_specs=[VMEM] * 14 + [pl.BlockSpec(memory_space=pltpu.SMEM)] + [VMEM] * 3,
        out_specs=(VMEM,) * 5 + (ANY, VMEM, VMEM, VMEM),
        scratch_shapes=scratch,
        compiler_params=params(cid, 58),
        name="encoder",
    )(top, *weights, *biases, out_grad, lengths, *mix)


class LineScatter:
    def __init__(self, count, me, chunks, spacing, p_ref, out_ref, from_left, from_right, sems):
        self.count, self.me, self.chunks, self.spacing = count, me, chunks, spacing
        self.p_ref, self.out_ref = p_ref, out_ref
        self.from_left, self.from_right, self.sems = from_left, from_right, sems
        self.messages = chunks * (count - 1)
        self.steps = self.messages + spacing * (count - 1)

    def place(self, right, number):
        count, me = self.count, self.me
        lag = me if right else count - 1 - me
        chunk = number // (count - 1)
        far = count - 1 - number % (count - 1)
        block = far if right else count - 1 - far
        words, filters = self.out_ref.shape
        rows = words // self.chunks
        tile = pl.ds(pl.multiple_of(chunk * rows, rows), rows)
        lanes = pl.ds(pl.multiple_of(block * filters, filters), filters)
        buf = self.from_left if right else self.from_right
        send, recv = self.sems[:2] if right else self.sems[2:]
        to = jnp.minimum(me + 1, count - 1) if right else jnp.maximum(me - 1, 0)
        first, passed = [
            functools.partial(
                pltpu.make_async_remote_copy,
                src_ref=src.at[tile, lanes],
                dst_ref=buf.at[tile, lanes],
                send_sem=send.at[block, chunk],
                recv_sem=recv.at[block, chunk],
                device_id={"tensor": to},
                device_id_type=MESH,
            )
            for src in (self.p_ref, buf)
        ]
        return lag, far, tile, lanes, buf, first, passed

    def step(self, step):
        for right in (True, False):
            lag = self.me if right else self.count - 1 - self.me
            number = step - self.spacing * lag
            here = (number >= 0) & (number < self.messages)
            number = jnp.clip(number, 0, self.messages - 1)
            lag, far, tile, lanes, buf, first, passed = self.place(right, number)

            @pl.when(here & (lag == 0))
            def start():
                first().start()

            @pl.when(here & (lag > 0) & (far > lag))
            def middle():
                first().wait_recv()
                buf[tile, lanes] = (
                    buf[tile, lanes].astype(f32) + self.p_ref[tile, lanes].astype(f32)
                ).astype(bf16)
                passed().start()

            @pl.when(here & (lag > 0) & (far == lag))
            def last():
                first().wait_recv()
                self.out_ref[tile, :] += buf[tile, lanes].astype(f32)

    def due(self, chunk):
        return (chunk + self.spacing) * (self.count - 1)

    def finished(self, step, work, after=0):
        each = self.count - 1
        since = step - after - self.spacing * each

        @pl.when((since >= 0) & (since % each == 0) & (since < self.messages))
        def call():
            work(jnp.maximum(since, 0) // each)

    def drain(self):
        def one(number, carry):
            for right in (True, False):
                lag, far, tile, lanes, buf, first, passed = self.place(right, number)

                @pl.when(far > lag)
                def sent():
                    first().wait_send()

            return carry

        lax.fori_loop(0, self.messages, one, 0)


class DpSum:
    def __init__(self, cell, peers, x_first, sems, base):
        self.c, self.x, self.y = cell
        self.peers, self.x_first, self.base = peers, x_first, base
        self.send, self.recv = sems
        self.src = self.half = self.in0 = self.in1 = self.mid = self.in2 = None

    def remote(self, number, src, dst, bit):
        return pltpu.make_async_remote_copy(
            src_ref=src,
            dst_ref=dst,
            send_sem=self.send.at[self.base + number],
            recv_sem=self.recv.at[self.base + number],
            device_id=self.peers[bit],
            device_id_type=MESH,
        )

    def copy0(self):
        return self.remote(0, self.src.at[:, :, 1 - self.c], self.in0, 0)

    def copy1(self):
        if self.x_first:
            return self.remote(1, self.half.at[:, 1 - self.x], self.in1, 1)
        return self.remote(1, self.half.at[1 - self.y], self.in1, 2)

    def copy2(self):
        own = self.y if self.x_first else self.x
        return self.remote(2, self.mid.at[1 - own], self.in2, 2 if self.x_first else 1)

    def finish0(self):
        self.copy0().wait()

        def one(k, carry):
            i, j = k // 2, k % 2
            self.half[i, j] = (self.half[i, j].astype(f32) + self.in0[i, j].astype(f32)).astype(bf16)
            return carry

        lax.fori_loop(0, 4, one, 0)

    def finish1(self):
        self.copy1().wait()

        def one(k, carry):
            kept = self.half[k, self.x] if self.x_first else self.half[self.y, k]
            self.mid[k] = (kept.astype(f32) + self.in1[k].astype(f32)).astype(bf16)
            return carry

        lax.fori_loop(0, 2, one, 0)

    def finish2(self):
        self.copy2().wait()
        own = self.y if self.x_first else self.x
        return self.mid[own].astype(f32) + self.in2[...].astype(f32)


def dp_cell(place):
    cell = [place % 2, (place // 2) % 2, place // 4]
    return cell, [{"dp": place + (1 - 2 * cell[bit]) * 2**bit} for bit in range(3)]


def greet_all(peers):
    barrier = pltpu.get_barrier_semaphore()
    for peer in peers:
        pl.semaphore_signal(barrier, inc=1, device_id=peer, device_id_type=MESH)


def meet_all(peers):
    pl.semaphore_wait(pltpu.get_barrier_semaphore(), len(peers))


def weight_grad_piece(piece, whole_ref, d_refs, outs):
    rows = outs[0].shape[-2]
    lanes = pl.ds(pl.multiple_of(piece * rows, rows), rows)
    index = (piece // 4, (piece // 2) % 2, piece % 2)
    for d_ref, out in zip(d_refs, outs):
        out[index] = dot(whole_ref[:, lanes], d_ref[...], 0, 0).astype(bf16)


def highway_back_kernel(count, chunks, reduce, *refs):
    prev1_hbm, dt1_ref, dg1_ref, sums1_ref = refs[:4]
    late_hbm = refs[4:9]
    refs = refs[9:]
    if reduce:
        tr_hbm = refs[:2]
        refs = refs[2:]
    part0_ref, prev0_ref, dt0_ref, dg0_ref, sums_ref = refs[:5]
    refs = refs[5:]
    if reduce:
        tr_outs = refs[2:4]
        hw_refs, tr_half = refs[4:6], refs[6:8]
        in0s, in1s = refs[8:12], refs[12:16]
        mids, in2s = list(refs[:2]) + list(refs[16:18]), refs[18:20]
        dp_sems = refs[20:22]
        refs = refs[22:]
    else:
        hw_refs = refs[:2]
        refs = refs[2:]
    part1_ref, from_left, from_right, d_h1_ref = refs[:4]
    t0_ref, g0_ref, h0_ref, whole1_ref, w_ref, late_sem = refs[4:10]
    sems = refs[10:]
    me = lax.axis_index("tensor")
    words, filters = dt1_ref.shape
    prev_load = pltpu.make_async_copy(prev1_hbm, d_h1_ref, late_sem.at[8])
    prev_load.start()
    w_hbm = late_hbm[4]
    loads = [
        pltpu.make_async_copy(w_hbm.at[1], w_ref.at[1], late_sem.at[0]),
        pltpu.make_async_copy(late_hbm[3], whole1_ref, late_sem.at[1]),
        pltpu.make_async_copy(w_hbm.at[0], w_ref.at[0], late_sem.at[2]),
        pltpu.make_async_copy(late_hbm[0], t0_ref, late_sem.at[3]),
        pltpu.make_async_copy(late_hbm[1], g0_ref, late_sem.at[4]),
        pltpu.make_async_copy(late_hbm[2], h0_ref, late_sem.at[5]),
    ]
    for copy in loads:
        copy.start()
    items = []
    if reduce:
        cell, peers = dp_cell(lax.axis_index("dp"))
        keep = [
            pltpu.make_async_copy(tr_hbm[k].at[:, :, cell[0]], tr_half[k], late_sem.at[6 + k])
            for k in range(2)
        ]
        for copy in keep:
            copy.start()
    ring = [{"tensor": lax.rem(me + k, count)} for k in range(1, count)]
    everyone = (peers if reduce else []) + ring
    greet_all(everyone)
    sums_ref[0:2, :] = jnp.zeros_like(sums1_ref)
    sums_ref[2:4, :] = sums1_ref[...]

    def mix(layer, d_h_ref, t_ref, g_ref, h_ref, dt_ref, dg_ref, prev_ref, tile):
        dt, dg, prev = mix_back(d_h_ref[tile, :], t_ref[tile, :], g_ref[tile, :], h_ref[tile, :])
        dt_ref[tile, :] = dt
        dg_ref[tile, :] = dg
        prev_ref[tile, :] = prev
        for j, d in enumerate((dt, dg)):
            sums_ref[2 * layer + j : 2 * layer + j + 1, :] += jnp.sum(
                d.astype(f32), axis=0, keepdims=True
            )

    def products(layer, dt_ref, dg_ref, p_ref, start, size):
        tile = slice(start, start + size)

        def one(block, carry):
            lanes = pl.ds(pl.multiple_of(block * filters, filters), filters)
            p_ref[tile, lanes] = (
                dot(dt_ref[tile, :], w_ref[layer, 0, lanes, :], 1, 1)
                + dot(dg_ref[tile, :], w_ref[layer, 1, lanes, :], 1, 1)
            ).astype(bf16)
            return carry

        lax.fori_loop(0, count, one, 0)

    rows = words // chunks

    def tile_of(index):
        return pl.ds(pl.multiple_of(index * rows, rows), rows)

    half, quarter = words // 2, words // 4

    def own_part(part):
        tile = slice(part * (words // 2), (part + 1) * (words // 2))
        d_h1_ref[tile, :] += part1_ref[
            tile, pl.ds(pl.multiple_of(me * filters, filters), filters)
        ].astype(f32)

    loads[0].wait()
    products(1, dt1_ref, dg1_ref, part1_ref, 0, half)
    prev_load.wait()
    own_part(0)
    meet_all(everyone)
    if reduce:
        for k in range(4):
            item = DpSum(cell, peers, k % 2 == 0, dp_sems, 3 * k)
            if k < 2:
                item.src, item.half = hw_refs[k], hw_refs[k].at[:, :, cell[0]]
            else:
                item.src, item.half = tr_hbm[k - 2], tr_half[k - 2]
            item.in0, item.in1, item.mid = in0s[k], in1s[k], mids[k]
            if k >= 2:
                item.in2 = in2s[k - 2]
            items.append(item)
        for item in items[2:]:
            item.copy0().start()
    scatter = LineScatter(
        count, me, chunks, 3, part1_ref, d_h1_ref, from_left, from_right, sems
    )

    def step_fn(step, carry):
        scatter.step(step)

        @pl.when(step == 0)
        def rest():
            products(1, dt1_ref, dg1_ref, part1_ref, half, half)
            own_part(1)
            loads[1].wait()

        @pl.when((step > 0) & (step <= 8))
        def grads():
            weight_grad_piece(step - 1, whole1_ref, (dt1_ref, dg1_ref), hw_refs)

        @pl.when(step == 9)
        def late():
            for copy in loads[2:]:
                copy.wait()

        if reduce:

            @pl.when(step == 4)
            def encoder1():
                for copy in keep:
                    copy.wait()
                for item in items[2:]:
                    item.finish0()
                    item.copy1().start()

            @pl.when(step == 9)
            def highway0():
                for item in items[:2]:
                    item.copy0().start()

            @pl.when(step == 15)
            def highway1():
                for item in items[:2]:
                    item.finish0()
                    item.copy1().start()

            @pl.when(step == 20)
            def encoder2():
                for item in items[2:]:
                    item.finish1()
                    item.copy2().start()

        scatter.finished(
            step,
            lambda chunk: mix(
                0, d_h1_ref, t0_ref, g0_ref, h0_ref, dt0_ref, dg0_ref, prev0_ref, tile_of(chunk)
            ),
        )

        @pl.when(step == scatter.due(chunks // 2 - 1) + 1)
        def early():
            products(0, dt0_ref, dg0_ref, part0_ref, 0, half)

        @pl.when(step == scatter.due(3 * chunks // 4 - 1) + 1)
        def third_quarter():
            products(0, dt0_ref, dg0_ref, part0_ref, half, quarter)

        return carry

    lax.fori_loop(0, scatter.steps, step_fn, 0)
    products(0, dt0_ref, dg0_ref, part0_ref, half + quarter, quarter)
    for item in items[:2]:
        item.finish1()
    for item, out in zip(items[2:], tr_outs if reduce else ()):
        out[...] = item.finish2().astype(bf16)
    scatter.drain()


def highway_back(prev1, dt1, dg1, sums1, t0, g0, h0, whole1, weight, tra, trb, count, cid):
    words, filters = dt1.shape
    chunks = 8
    reduce = tra is not None
    rows = whole1.shape[1] // 8
    shape = jax.ShapeDtypeStruct
    out_shape = [
        shape(whole1.shape, bf16),
        shape((words, filters), f32),
        shape((words, filters), bf16),
        shape((words, filters), bf16),
        shape((4, filters), f32),
    ]
    operands = [prev1, dt1, dg1, sums1, t0, g0, h0, whole1, weight]
    in_specs = [ANY] + [VMEM] * 3 + [ANY] * 5
    hw_shape = (2, 2, 2, rows, filters)
    scratch = []
    if reduce:
        operands += [tra, trb]
        in_specs += [ANY] * 2
        tails = [hw_shape[-2:], hw_shape[-2:], tra.shape[-2:], trb.shape[-2:]]
        out_shape += [shape((2,) + tail, bf16) for tail in tails[:2]]
        out_shape += [shape(tail, bf16) for tail in tails[2:]]
        scratch += [pltpu.VMEM(hw_shape, bf16)] * 2
        scratch += [pltpu.VMEM((2, 2) + tail, bf16) for tail in tails[2:]]
        scratch += [pltpu.VMEM((2, 2) + tail, bf16) for tail in tails]
        scratch += [pltpu.VMEM((2,) + tail, bf16) for tail in tails + tails[2:]]
        scratch += [pltpu.VMEM(tail, bf16) for tail in tails[2:]]
        scratch += [DMA((12,))] * 2
    else:
        out_shape += [shape(hw_shape, bf16)] * 2
    scratch += [pltpu.VMEM(whole1.shape, bf16)] * 3
    scratch += [pltpu.VMEM((words, filters), f32)] * 4
    scratch += [pltpu.VMEM(whole1.shape, bf16), pltpu.VMEM(weight.shape, bf16), DMA((9,))]
    scratch += [DMA((count, chunks))] * 4
    return pl.pallas_call(
        functools.partial(highway_back_kernel, count, chunks, reduce),
        out_shape=tuple(out_shape),
        in_specs=in_specs,
        out_specs=tuple([VMEM] * len(out_shape)),
        scratch_shapes=scratch,
        compiler_params=params(cid, 58),
        name="highway_back",
    )(*operands)


class Spread:
    def __init__(self, sems, in_ref, got, mid, out_ref):
        self.dp_count, self.count = out_ref.shape[:2]
        self.sems, self.in_ref, self.got, self.mid, self.out_ref = sems, in_ref, got, mid, out_ref
        self.me = lax.axis_index("tensor")
        self.place = lax.axis_index("dp")

    def remote(self, src, dst, phase, hop, axis, peer):
        send, recv = self.sems[2 * phase : 2 * phase + 2]
        index = (hop - 1,) if phase < 2 else hop
        return pltpu.make_async_remote_copy(
            src_ref=src, dst_ref=dst, send_sem=send.at[index], recv_sem=recv.at[index],
            device_id={axis: peer}, device_id_type=MESH,
        )

    def scatter(self, hop):
        peer = lax.rem(self.place + hop, self.dp_count)
        return self.remote(self.in_ref.at[peer], self.got.at[hop - 1], 0, hop, "dp", peer)

    def across(self, hop):
        peer = lax.rem(self.me + hop, self.count)
        return self.remote(self.mid.at[self.me], self.mid.at[self.me], 1, hop, "tensor", peer)

    def around(self, hop, rank):
        peer = lax.rem(self.place + hop, self.dp_count)
        dst = self.out_ref.at[self.place, rank]
        return self.remote(self.mid.at[rank], dst, 2, (rank, hop - 1), "dp", peer)

    def hand_on(self, rank):
        self.loop(lambda hop: self.around(hop, rank).start(), self.dp_count)
        self.out_ref[self.place, rank] = self.mid[rank]

    def loop(self, fn, stop):
        def one(hop, carry):
            fn(hop)
            return carry

        lax.fori_loop(1, stop, one, 0)

    def first(self):
        self.loop(lambda hop: self.scatter(hop).start(), self.dp_count)

    def second(self):
        self.loop(lambda hop: self.scatter(hop).wait(), self.dp_count)
        total = lax.fori_loop(
            0,
            self.dp_count - 1,
            lambda k, acc: acc + self.got[k].astype(f32),
            self.in_ref[self.place].astype(f32),
        )
        self.mid[self.me] = total.astype(bf16)
        self.loop(lambda hop: self.across(hop).start(), self.count)
        self.hand_on(self.me)

    def third(self):
        def one(hop):
            self.across(hop).wait()
            self.hand_on(lax.rem(self.me + self.count - hop, self.count))

        self.loop(one, self.count)

    def finish(self):
        for rank in range(self.count):
            self.loop(lambda hop: self.around(hop, rank).wait(), self.dp_count)


def early_parts(rows):
    start = 0
    for source, (count, width) in enumerate(rows):
        for block in range(-(-width // LANES)):
            yield source, block, start, count, min(LANES, width - block * LANES)
            start += count


EARLY = ((4, 512), (1, 576), (10, 768))


def pack_early(ref, *sources):
    ref[...] = jnp.zeros_like(ref)
    for source, block, start, count, width in early_parts(EARLY):
        value = sources[source][0:count, block * LANES : block * LANES + width]
        for k in range(count):
            place = start + k
            ref[place // 16, place % 16 : place % 16 + 1, 0:width] = value[k : k + 1]


def unpack_early(ref, hwb_out, vec_out, upb_out, qv_out):
    for t in range(ref.shape[1]):
        for source, block, start, count, width in early_parts(EARLY):
            for k in range(count):
                place = start + k
                row = ref[place // 16, t, :, :].astype(f32)[place % 16 : place % 16 + 1, 0:width]
                lane = block * LANES
                if source == 0:
                    hwb_out[k : k + 1, t * 512 + lane : t * 512 + lane + width] = row
                elif source == 2 and k == 9:
                    upb_out[:, t * 768 + lane : t * 768 + lane + width] = row
                elif source == 2 and t == 0:
                    vec_out[k : k + 1, lane : lane + width] = row
                elif source == 1:
                    for out, low in ((0, 0), (1, 384)):
                        left, right = max(lane, low), min(lane + width, low + 192)
                        if left < right:
                            place_at = t * 192 + left - low
                            qv_out[out : out + 1, place_at : place_at + right - left] = row[
                                :, left - lane : right - lane
                            ]


def conv_backward_kernel(count, chars, cuts, *refs):
    (ids_ref, x_hbm, p_hbm, cw_ref, mask_ref, off_ref, log_ref, prev_ref, part_ref, whole_hbm,
     dt_ref, dg_ref) = refs[:12]
    refs = refs[12:]
    if cuts:
        mids_in = refs[:2]
        hb_sums, proj_sums, row_sums = refs[2:5]
        hw_out, convw_out, convb_out, table_out, hwb_out, vec_out, upb_out, qv_out = refs[5:13]
        dw_ref, table_ref, hw_a, hw_b = refs[13:17]
        in0s, in1s, mids, in2s = refs[17:19], refs[19:21], refs[21:23], refs[23:27]
        dp_sems = refs[27:29]
        spreads = [Spread(refs[33 + 10 * k : 39 + 10 * k], *refs[29 + 10 * k : 33 + 10 * k])
                   for k in range(2)]
        refs = refs[49:]
    else:
        dw_ref, table_ref, hw_a, hw_b = refs[:4]
        refs = refs[4:]
    (pad_ref, stage_ref, grad_ref, from_left, from_right, x_buf, p_buf, whole_ref, wb_ref,
     load_sem, whole_sem) = refs[:11]
    line_sems = refs[11:]
    me = lax.axis_index("tensor")
    words, filters = log_ref.shape
    tiles = words // WORD_TILE
    padded = ids_ref.shape[1] // WORD_TILE

    def load(index):
        slot = index % 2
        return [
            pltpu.make_async_copy(hbm.at[index], buf.at[slot], load_sem.at[k, slot])
            for k, (buf, hbm) in enumerate(((x_buf, x_hbm), (p_buf, p_hbm)))
        ]

    whole_copy = pltpu.make_async_copy(whole_hbm, whole_ref, whole_sem)
    whole_copy.start()
    for index in range(2):
        for copy in load(index):
            copy.start()
    ring = [{"tensor": lax.rem(me + k, count)} for k in range(1, count)]
    items = []
    if cuts:
        place = lax.axis_index("dp")
        dp_count = spreads[0].dp_count
        cell, dp_peers = dp_cell(place)
        ring += [{"dp": lax.rem(place + k, dp_count)} for k in range(1, dp_count)]
        for k in range(4):
            item = DpSum(cell, dp_peers, k % 2 == 0, dp_sems, 3 * k)
            item.in2 = in2s[k]
            if k < 2:
                item.src = (hw_a, hw_b)[k]
                item.half = item.src.at[:, :, cell[0]]
                item.in0, item.in1, item.mid = in0s[k], in1s[k], mids[k]
            else:
                item.mid = mids_in[k - 2]
            items.append(item)
        pack_early(spreads[0].in_ref, hb_sums, proj_sums, row_sums)
    greet_all(ring)
    taps = cw_ref.shape[0]
    wb_ref[...] = jnp.zeros_like(wb_ref)
    wb_ref[0:taps, :] = (cw_ref[...].astype(f32) * mask_ref[...]).astype(bf16)
    dw_ref[...] = jnp.zeros_like(dw_ref)
    table_ref[...] = jnp.zeros_like(table_ref)
    pad_ref[...] = jnp.zeros_like(pad_ref)
    grad_ref[...] = prev_ref[...] + part_ref[
        :, pl.ds(pl.multiple_of(me * filters, filters), filters)
    ].astype(f32)
    meet_all(ring)
    for item in items[2:]:
        item.copy2().start()
    if cuts:
        spreads[0].first()
    chunks = line_sems[0].shape[1]
    per = words // chunks // WORD_TILE
    scatter = LineScatter(
        count, me, chunks, 3, part_ref, grad_ref, from_left, from_right, line_sems
    )
    group = lax.broadcasted_iota(jnp.int32, (1, WORD_TILE, LANES), 2) // 16
    vocab = lax.broadcasted_iota(jnp.int32, (table_ref.shape[0], padded * WORD_TILE), 0)

    def tile_step(index):
        slot = index % 2
        for copy in load(index):
            copy.wait()
        tile = pl.ds(pl.multiple_of(index * WORD_TILE, WORD_TILE), WORD_TILE)
        pooled = log_ref[tile, :] - off_ref[...]
        sig = jax.nn.sigmoid(pooled)
        grad = grad_ref[tile, :] * (sig * (1.0 + pooled * (1.0 - sig)))
        d_conv = (grad[None] * p_buf[slot].astype(f32)).astype(bf16)
        d_conv = d_conv.reshape(chars * WORD_TILE, filters)
        dw_ref[...] += dot(x_buf[slot], d_conv, 0, 0)
        d_win = dot(d_conv, wb_ref[...], 1, 1).astype(bf16)
        pad_ref[6 : 6 + chars] = d_win.reshape(chars, WORD_TILE, LANES)
        d_emb = pad_ref[6 : 6 + padded]
        for tap in range(1, 7):
            d_emb = jnp.where(group == tap, pad_ref[6 - tap : 6 - tap + padded], d_emb)
        one_hot = jnp.where(vocab == ids_ref[pl.ds(index, 1), :], 1.0, 0.0).astype(bf16)
        table_ref[...] += dot(one_hot, d_emb.reshape(padded * WORD_TILE, LANES), 1, 0)

        @pl.when(index + 2 < tiles)
        def more():
            for copy in load(index + 2):
                copy.start()

    def step_fn(step, carry):
        scatter.step(step)

        @pl.when(step == 0)
        def whole():
            whole_copy.wait()

        @pl.when(step < 8)
        def grads():
            weight_grad_piece(step, whole_ref, (dt_ref, dg_ref), (hw_a, hw_b))

        if cuts:

            @pl.when(step == 4)
            def early2():
                spreads[0].second()

            @pl.when(step == 7)
            def early3():
                spreads[0].third()

            @pl.when(step == 8)
            def start0():
                for item in items[:2]:
                    item.copy0().start()

            @pl.when(step == cuts[0])
            def start1():
                for item in items[:2]:
                    item.finish0()
                    item.copy1().start()

            @pl.when(step == cuts[1])
            def start2():
                for item in items[:2]:
                    item.finish1()
                    item.copy2().start()

        for k in range(per):
            scatter.finished(step, lambda chunk: tile_step(chunk * per + k), k)
        return carry

    lax.fori_loop(0, scatter.due(chunks - 1) + per, step_fn, 0)
    if cuts:
        late = spreads[1]
        taps = table_ref[:, 0:16]
        for tap in range(1, 7):
            taps += table_ref[:, 16 * tap : 16 * tap + 16]
        stage_ref[...] = jnp.zeros_like(stage_ref)
        table_ref[:, 0:16] = taps
        for i in range(8):
            late.in_ref[i, :, 0:filters] = dw_ref[16 * i : 16 * i + 16, :].astype(bf16)
            for k in range(3):
                size = 16 if k < 2 else 1
                stage_ref[0:size, 16 * k : 16 * k + 16] = table_ref[
                    33 * i + 16 * k : 33 * i + 16 * k + size, 0:16
                ]
            late.in_ref[i, :, filters:] = stage_ref[...].astype(bf16)
        late.first()
        spreads[0].finish()
        unpack_early(spreads[0].out_ref, hwb_out, vec_out, upb_out, qv_out)
        late.second()
        late.third()
        for k in range(4):
            hw_out[k // 2, k % 2] = items[k].finish2().astype(bf16)
        late.finish()
        for t in range(count):
            lanes = slice(t * filters, (t + 1) * filters)
            for i in range(7):
                convw_out[16 * i : 16 * i + 16, lanes] = late.out_ref[i, t, :, 0:filters]
            convb_out[:, lanes] = late.out_ref[7, t, :, 0:filters].astype(f32)[0:1]
        for i in range(8):
            total = late.out_ref[i, 0, :, filters:].astype(f32)
            for t in range(1, count):
                total += late.out_ref[i, t, :, filters:].astype(f32)
            for k in range(3):
                size = 16 if k < 2 else 1
                table_out[33 * i + 16 * k : 33 * i + 16 * k + size, :] = total[
                    0:size, 16 * k : 16 * k + 16
                ]
    scatter.drain()


def conv_backward(ids, x, p, w, mask, off, logs, prev, part, whole, dt, dg, rest, count, cid):
    words, filters = logs.shape
    chars = p.shape[1]
    chunks = 8
    shape = jax.ShapeDtypeStruct
    hw_shape = (2, 2, 2, whole.shape[1] // 8, filters)
    operands = [ids, x, p, w, mask, off, logs, prev, part, whole, dt, dg] + list(rest)
    in_specs = [VMEM, ANY, ANY] + [VMEM] * 6 + [ANY, VMEM, VMEM] + [VMEM] * len(rest)
    sums = [(LANES, filters), (264, LANES)]
    scratch = []
    cuts = None
    if rest:
        cuts = (17, 28)
        tail = hw_shape[-2:]
        features = rest[-1].shape[-1]
        out_shape = [
            shape((2, 2) + tail, bf16),
            shape((112, count * filters), bf16),
            shape((1, count * filters), f32),
            shape((264, 16), f32),
            shape((4, count * filters), f32),
            shape((9, features), f32),
            shape((1, count * features), f32),
            shape((2, features), f32),
        ]
        scratch += [pltpu.VMEM(shape_of, f32) for shape_of in sums]
        scratch += [pltpu.VMEM(hw_shape, bf16)] * 2
        scratch += [pltpu.VMEM((2, 2) + tail, bf16)] * 2
        scratch += [pltpu.VMEM((2,) + tail, bf16)] * 4
        scratch += [pltpu.VMEM(tail, bf16)] * 4
        scratch += [DMA((12,))] * 2
        for small, kind in (((16, LANES), f32), ((16, filters + LANES), bf16)):
            scratch += [
                pltpu.VMEM((8,) + small, kind),
                pltpu.VMEM((7,) + small, kind),
                pltpu.VMEM((count,) + small, bf16),
                pltpu.VMEM((8, count) + small, bf16),
            ]
            scratch += [DMA((7,))] * 2 + [DMA((count - 1,))] * 2 + [DMA((count, 7))] * 2
    else:
        out_shape = [shape(shape_of, f32) for shape_of in sums] + [shape(hw_shape, bf16)] * 2
    scratch += [
        pltpu.VMEM((68, WORD_TILE, LANES), bf16),
        pltpu.VMEM((16, LANES), f32),
        pltpu.VMEM((words, filters), f32),
        pltpu.VMEM(part.shape, bf16),
        pltpu.VMEM(part.shape, bf16),
        pltpu.VMEM((2,) + x.shape[1:], bf16),
        pltpu.VMEM((2,) + p.shape[1:], bf16),
        pltpu.VMEM(whole.shape, bf16),
        pltpu.VMEM((LANES, filters), bf16),
        DMA((2, 2)),
        DMA,
    ]
    scratch += [DMA((count, chunks))] * 4
    return pl.pallas_call(
        functools.partial(conv_backward_kernel, count, chars, cuts),
        out_shape=tuple(out_shape),
        in_specs=in_specs,
        out_specs=tuple([VMEM] * len(out_shape)),
        scratch_shapes=scratch,
        compiler_params=params(cid, 58),
        name="conv_backward",
    )(*operands)


def small_kernel(dp_count, count, in_ref, out_ref, got, mid, *sems):
    me = lax.axis_index("tensor")
    place = lax.axis_index("dp")
    barrier = pltpu.get_barrier_semaphore()

    def greet(hop, carry):
        peer = lax.rem(place + hop, dp_count)
        pl.semaphore_signal(barrier, inc=1, device_id={"dp": peer}, device_id_type=MESH)
        return carry

    lax.fori_loop(1, dp_count, greet, 0)
    for hop in range(1, count):
        pl.semaphore_signal(
            barrier, inc=1, device_id={"tensor": lax.rem(me + hop, count)}, device_id_type=MESH
        )
    pl.semaphore_wait(barrier, dp_count + count - 2)
    spread = Spread(sems, in_ref, got, mid, out_ref)
    spread.first()
    spread.second()
    spread.third()
    spread.finish()


def sum_small(packed, dp_count, count, cid):
    shape = packed.shape[1:]
    return pl.pallas_call(
        functools.partial(small_kernel, dp_count, count),
        out_shape=jax.ShapeDtypeStruct((dp_count, count) + shape, bf16),
        in_specs=[VMEM],
        out_specs=VMEM,
        scratch_shapes=[
            pltpu.VMEM((dp_count - 1,) + shape, f32),
            pltpu.VMEM((count,) + shape, bf16),
            DMA((dp_count - 1,)),
            DMA((dp_count - 1,)),
            DMA((count - 1,)),
            DMA((count - 1,)),
            DMA((count, dp_count - 1)),
            DMA((count, dp_count - 1)),
        ],
        compiler_params=params(cid, 32),
        name="sum_small",
    )(packed)


def finish_kernel(units, three, *refs):
    (enc_out, table_out, conv_w_out, conv_b_out, hw_out, hw_b_out, proj_out, proj_b_out, gain_out,
     shift_out, qkv_out, qv_out, o_out, o_b_out, up_out, up_b_out, down_out,
     down_b_out) = refs[12:30]
    bufs, sem = refs[30:42], refs[42]
    loads = [
        pltpu.make_async_copy(src, dst, sem.at[k])
        for k, (src, dst) in enumerate(zip(refs[:12], bufs))
    ]
    for copy in loads:
        copy.start()
    for copy in loads:
        copy.wait()
    (enc, table, conv_w, mask, conv_b, hw, hw_b, rows, qv, up_b, tr_a, tr_b) = bufs
    filters = mask.shape[1]
    enc_out[0] = enc[...]
    table_out[...] = table[...].T[:, 0 : table_out.shape[1]]
    for start in range(0, conv_w.shape[1], filters):
        lanes = slice(start, start + filters)
        conv_w_out[:, lanes] = conv_w[:, lanes].astype(f32) * mask[...]
    conv_b_out[...] = conv_b[...].reshape(conv_b_out.shape)
    for layer in range(2):
        hw_b_out[layer] = hw_b[2 * layer : 2 * layer + 2, :]
        for j in range(2):
            hw_out[layer, j] = hw[layer, j].astype(f32)
    for k, out in enumerate((proj_b_out, o_b_out, down_b_out)):
        out[...] = rows[k : k + 1, :].reshape(out.shape)
    gain_out[...] = rows[3:6, :]
    shift_out[...] = rows[6:9, :]
    qv_out[...] = qv[...]
    up_b_out[...] = up_b[...].reshape(up_b_out.shape)
    up_out[...] = tr_a[:, 0:units].astype(f32)
    down_out[...] = tr_a[:, units:].astype(f32)
    proj_out[...] = tr_b[:, 0:filters].astype(f32)
    hidden = three // 3
    qkv = tr_b[:, filters : filters + three].astype(f32)
    for k in range(3):
        qkv_out[k] = qkv[:, k * hidden : (k + 1) * hidden]
    o_out[...] = tr_b[:, 1152 : 1152 + hidden].astype(f32).T


def finish(encoded, table, conv_w, mask, conv_b, hw, hw_b, rows, qv, up_b, tr_a, tr_b, vocab,
           units, three):
    features, depth, filters = rows.shape[1], tr_a.shape[0], mask.shape[1]
    shapes = [
        (table.shape[1], vocab), conv_w.shape, (conv_w.shape[1],), hw.shape,
        (2, 2, hw_b.shape[1]), (depth, filters), (features,), (3, features), (3, features),
        (3, depth, three // 3), qv.shape, (three // 3, depth), (features,), (depth, units),
        (up_b.shape[1],), (depth, tr_a.shape[1] - units), (features,),
    ]
    operands = (encoded, table, conv_w, mask, conv_b, hw, hw_b, rows, qv, up_b, tr_a, tr_b)
    (encoded, table, conv_w, conv_b, hw, hw_b, proj, proj_b, gain, shift, qkv, qv, o, o_b, up, up_b,
     down, down_b) = pl.pallas_call(
        functools.partial(finish_kernel, units, three),
        out_shape=tuple(
            [jax.ShapeDtypeStruct((1,) + encoded.shape, bf16)]
            + [jax.ShapeDtypeStruct(shape, f32) for shape in shapes]
        ),
        in_specs=[ANY] * 12,
        out_specs=(VMEM,) * 18,
        scratch_shapes=[pltpu.VMEM(part.shape, part.dtype) for part in operands] + [DMA((12,))],
        compiler_params=pltpu.CompilerParams(vmem_limit_bytes=58 * MIB),
        name="finish",
    )(*operands)
    return (
        jnp.transpose(encoded, (1, 0, 2)), table.T, conv_w, conv_b, hw, hw_b, proj.T, proj_b, gain,
        shift, jnp.transpose(qkv, (1, 0, 2)), qv, o, o_b, up, up_b, down.T, down_b,
    )


def body(
    char_ids,
    seq_lengths,
    char_table,
    conv_weight,
    conv_bias,
    highway_weight,
    highway_bias,
    proj_weight,
    proj_bias,
    norm_gain,
    norm_shift,
    qkv_weight,
    qv_bias,
    output_projection_weight,
    out_bias,
    up_weight,
    up_bias,
    down_weight,
    down_bias,
    out_grad,
):
    words, nseq, chars = char_ids.shape
    assert nseq == 1
    count = lax.axis_size("tensor")
    dp_count = lax.axis_size("dp")
    rank = lax.axis_index("tensor")
    vocab, char_dim = char_table.shape
    taps_dim, filters = conv_weight.shape
    features = proj_weight.shape[1]
    heads = qkv_weight.shape[2] // HEAD_DIM

    tiles = words // WORD_TILE
    ids_tiles = jnp.swapaxes(char_ids[:, 0].reshape(tiles, WORD_TILE, chars), 1, 2)
    ids_tiles = ids_tiles.reshape(tiles, chars * WORD_TILE)
    pattern = np.zeros((chars, WORD_TILE, LANES), np.float32)
    pattern[:, :, taps_dim] = 1.0
    for k in range(1, 7):
        pattern[chars - k, :, taps_dim + k] = 1.0

    widths = filter_widths(filters)
    off = jnp.asarray(np.log((chars - widths + 1).astype(np.float64)).astype(np.float32))[None]
    tap_of = np.arange(taps_dim)[:, None] // char_dim
    taps_mask = tap_of < widths[None]
    mask = jnp.asarray(taps_mask, f32)
    ends = np.zeros((LANES - taps_dim, filters), np.float32)
    ends[1:7] = np.where(widths[None] > np.arange(1, 7)[:, None], big_neg, 0.0)

    logs, whole0, whole1, top, x_tiles, p_tiles, t0, g0, h0, t1, g1, h1 = embed_forward(
        ids_tiles,
        char_table.T,
        jnp.asarray(pattern, bf16),
        (conv_weight, conv_bias, mask, jnp.asarray(ends)),
        off,
        highway_bias,
        highway_weight,
        count,
        chars,
        1,
    )
    encoded, prev1, dt1, dg1, sums1, tr_a, tr_b, row_sums, proj_sums = encoder(
        top,
        (
            proj_weight,
            jnp.transpose(qkv_weight, (1, 2, 0)).reshape(-1, features),
            output_projection_weight,
            up_weight,
            down_weight,
        ),
        (proj_bias, out_bias, down_bias, up_bias, norm_gain, norm_shift, qv_bias),
        out_grad[:, 0],
        seq_lengths,
        (t1, g1, h1),
        count,
        4,
    )

    back_args = (prev1, dt1, dg1, sums1, t0, g0, h0, whole1, highway_weight)
    conv_args = (ids_tiles, x_tiles, p_tiles, conv_weight, mask, off, logs)
    three = 3 * heads * HEAD_DIM
    units = up_weight.shape[1]
    if dp_count == 8 and (features // dp_count) % 16 == 0:
        part0, prev0, dt0, dg0, hw_bias_part, mid_a, mid_b, tr_a, tr_b = highway_back(
            *back_args, tr_a, tr_b, count, 9
        )
        (hw_w_grad, conv_w_grad, conv_b_grad, table_grad, hw_b_grad, rows, up_b_grad,
         qv_grad) = conv_backward(
            *conv_args, prev0, part0, whole0, dt0, dg0,
            (mid_a, mid_b, hw_bias_part, proj_sums, row_sums), count, 10,
        )
        return finish(
            encoded, table_grad, conv_w_grad, mask, conv_b_grad, hw_w_grad, hw_b_grad, rows,
            qv_grad, up_b_grad, tr_a, tr_b, vocab, units, three,
        )
    else:
        part0, prev0, dt0, dg0, hw_bias_part, *hw1 = highway_back(*back_args, None, None, count, 9)
        d_w_all, table_all, *hw0 = conv_backward(
            *conv_args, prev0, part0, whole0, dt0, dg0, (), count, 10
        )
        hw_sum = jnp.stack([part.reshape(-1, filters) for part in hw0 + hw1])
        hw_sum = lax.psum_scatter(hw_sum, "dp", scatter_dimension=1, tiled=True).astype(f32)
        tr_a, tr_b = [
            lax.psum_scatter(
                part.reshape(features, -1), "dp", scatter_dimension=0, tiled=True
            ).astype(f32)
            for part in (tr_a, tr_b)
        ]
        hw_w_grad = hw_sum.reshape(2, 2, -1, filters)
        pieces = [d_w_all[: taps_dim + 1], table_all, hw_bias_part, proj_sums, row_sums[:10]]
        flat = jnp.concatenate([part.reshape(-1) for part in pieces])
        width = -(-flat.size // (dp_count * 16 * LANES)) * LANES
        flat = jnp.pad(flat, (0, dp_count * 16 * width - flat.size))
        summed = sum_small(flat.reshape(dp_count, 16, width), dp_count, count, 11)
        summed = jnp.swapaxes(summed, 0, 1).reshape(count, -1).astype(f32)
        conv_size, table_size = pieces[0].size, table_all.size
        conv_all = summed[:, :conv_size].reshape(count, taps_dim + 1, filters)
        conv_all = jnp.swapaxes(conv_all, 0, 1)
        conv_w_grad = conv_all[:taps_dim].reshape(taps_dim, -1)
        conv_b_grad = conv_all[taps_dim].reshape(-1)
        table_all = jnp.sum(summed[:, conv_size : conv_size + table_size], axis=0)
        table_all = table_all.reshape(-1, LANES)
        early = summed[:, conv_size + table_size :]
        table_grad = jnp.sum(
            table_all[:vocab, :taps_dim].reshape(vocab, taps_dim // char_dim, char_dim), axis=1
        )
        hw_b_grad = jnp.swapaxes(early[:, : 4 * filters].reshape(count, 4, filters), 0, 1)
        early = early[:, 4 * filters :]
        qv_grad = jnp.swapaxes(early[:, :three].reshape(count, 3, -1), 0, 1)[::2].reshape(2, -1)
        rows = early[:, three : three + 10 * features].reshape(count, 10, features)
        up_b_grad = rows[:, 9].reshape(-1)
        rows = rows[0]

    conv_w_grad = jnp.where(np.tile(taps_mask, (1, count)), conv_w_grad, 0.0)
    hw_b_grad = hw_b_grad.reshape(2, 2, -1)
    up_w_grad = tr_a[:, :units]
    down_w_grad = tr_a[:, units:].T
    proj_w_grad = tr_b[:, :filters].T
    qkv_w_grad = tr_b[:, filters : filters + three].reshape(-1, 3, heads * HEAD_DIM)
    out_w_grad = tr_b[:, 1152 : 1152 + heads * HEAD_DIM].T
    proj_b_grad, out_b_grad, down_b_grad = rows[0], rows[1], rows[2]
    gain_grad, shift_grad = rows[3:6], rows[6:9]
    return (
        encoded[:, None],
        table_grad,
        conv_w_grad,
        conv_b_grad,
        hw_w_grad,
        hw_b_grad,
        proj_w_grad,
        proj_b_grad,
        gain_grad,
        shift_grad,
        qkv_w_grad,
        qv_grad,
        out_w_grad,
        out_b_grad,
        up_w_grad,
        up_b_grad,
        down_w_grad,
        down_b_grad,
    )


def solution(mesh):
    return jax.shard_map(
        body,
        mesh=mesh,
        in_specs=(
            P(None, "dp", None),
            P("dp"),
            P(),
            P(None, "tensor"),
            P("tensor"),
            P(None, None, None, "tensor"),
            P(None, None, "tensor"),
            P("tensor", None),
            P(),
            P(),
            P(),
            P(None, None, "tensor"),
            P(None, "tensor"),
            P("tensor", None),
            P(),
            P(None, "tensor"),
            P("tensor"),
            P("tensor", None),
            P(),
            P("tensor", "dp", None),
        ),
        out_specs=(
            P("tensor", "dp", None),
            P(),
            P(),
            P(),
            P(None, None, "dp", "tensor"),
            P(),
            P("tensor", "dp"),
            P(),
            P(),
            P(),
            P("dp", None, "tensor"),
            P(),
            P("tensor", "dp"),
            P(),
            P("dp", "tensor"),
            P(),
            P("tensor", "dp"),
            P(),
        ),
        check_vma=False,
    )
```
